32 devices in a mesh: dp: 4 (over x, core), ctx: 8 (over z, y).
Axes of the slice: x: 2, y: 2, z: 4, core: 2. Of those that a mesh axis runs over, the one named last changes fastest.
Arguments:
- activations: bfloat16 [4096, 4096], P(('dp', 'ctx')), parts along dimension 0
- routed: int32 [512], P('dp'), parts along dimension 0, may hold values from 0 to 1023, as said below
- balance: int32 [512], P('dp'), parts along dimension 0, may hold values from 0 to 7, as said below
- w_query: bfloat16 [4096, 4096], P(None, 'ctx')
- w_key: bfloat16 [4096, 1024], P(None, 'ctx')
- w_value: bfloat16 [4096, 1024], P(None, 'ctx'), may hold values from -0.09375 to 0.09375
- w_output: bfloat16 [4096, 4096], P('ctx'), may hold values from -0.09375 to 0.09375
- attn_gain: float32 [4096], replicated, may hold values from 0.25 to 1.75
- mlp_gain: float32 [4096], replicated, may hold values from 0.25 to 1.75
- w_gate: bfloat16 [4096, 8192], P(None, 'ctx'), may hold values from -0.09375 to 0.09375
- w_up: bfloat16 [4096, 8192], P(None, 'ctx'), may hold values from -0.09375 to 0.09375
- w_down: bfloat16 [8192, 4096], P('ctx'), may hold values from -0.0625 to 0.0625
- w_router: float32 [4096], replicated, may hold values from -0.09375 to 0.09375
Outputs:
- updated: bfloat16 [512, 4096], P(('dp', 'ctx')), parts along dimension 0
The draws below stay inside these ranges and needn't reach their ends.
There are 4 independent parts, one for each index of `dp`. The reference program is written for one: setup_inputs(seed, part) draws one part's arguments, and reference() takes and returns one part's arrays. A program takes and returns all parts, laid end to end along the dimension named above; an argument that names none is the same for every part. Nothing has to cross between parts.
Inputs may be any that keep to these rules, and one draw needn't show every extreme that they name: `routed`: strictly increasing positions; one device's 128 positions hold at most 32 of them, and some device's hold exactly 32. `balance`: each device index appears exactly 16 times.
All inputs are finite; a program needn't handle non-finite values.
Results may differ from the reference program's by a relative error of at most 0.015.
Values may be sent and summed in bfloat16 or wider, within the bound.
No kernel may reach another device: no remote copies, remote signals or barrier semaphores. Data moves between devices by JAX's collectives and lax.ppermute only.
A program may use at most 128 MiB of HBM per device.

```python
import math
import jax
import jax.numpy as jnp
from jax import lax

D = 4096
HEADS = 32
KV_HEADS = 8
HEAD_DIM = 128
FF = 8192
TOK_DEV = 128
SHARDS = 8
SEQ = 1024
ROUTED = 128
R_DEV = 16


def key_columns(key):
    return jax.random.normal(jax.random.fold_in(key, 303), (D, KV_HEADS * HEAD_DIM), jnp.float32) * D ** (-0.5)


def draw_w_key(key, part):
    return key_columns(key).astype(jnp.bfloat16)


def draw_w_query(key, part):
    noise = jax.random.normal(jax.random.fold_in(key, 505), (D, HEADS * HEAD_DIM), jnp.float32) * D ** (-0.5)
    return noise.astype(jnp.bfloat16)


def draw_activations(key, part):
    base_key = jax.random.fold_in(key, 404)
    key_one, key_two, key_three = jax.random.split(base_key, 3)
    column_scale = jnp.exp(jax.random.uniform(key_three, (1, D), jnp.float32, -0.6, 0.6))
    entries = jax.random.normal(key_one, (SEQ, D), jnp.float32)
    row_scale = jnp.exp(jax.random.uniform(key_two, (SEQ, 1), jnp.float32, math.log(0.3), math.log(3.0)))
    return (entries * row_scale * column_scale).astype(jnp.bfloat16)


def draw_routed(key, part):
    base_key = jax.random.fold_in(key, 101)
    key_delta, key_pick, key_sign, key_rank = jax.random.split(base_key, 4)
    pairs = SHARDS // 2
    delta = jax.random.randint(key_delta, (pairs,), -R_DEV, R_DEV + 1)
    chosen = jax.random.randint(key_pick, (), 0, pairs)
    delta = jnp.where(jnp.arange(pairs) == chosen, R_DEV, delta)
    signs = 2 * jax.random.randint(key_sign, (pairs,), 0, 2) - 1
    delta = delta * signs
    counts = jnp.stack([R_DEV + delta, R_DEV - delta], axis=1).reshape(SHARDS)
    shard_keys = jax.random.split(key_rank, SHARDS)

    def ranks(one_key):
        shuffled = jax.random.permutation(one_key, TOK_DEV)
        return jnp.argsort(shuffled)
    rank_table = jax.vmap(ranks)(shard_keys)
    picked = (rank_table < counts[:, None]).reshape(SEQ)
    return jnp.nonzero(picked, size=ROUTED)[0].astype(jnp.int32)


def draw_balance(key, part):
    shuffled = jax.random.permutation(jax.random.fold_in(key, 202), ROUTED)
    return (shuffled % SHARDS).astype(jnp.int32)


def levels(own_key, extent, pieces, smallest, largest):
    def one(dim, blocks):
        steps = jax.random.uniform(jax.random.fold_in(jax.random.fold_in(own_key, 6), dim), (blocks,), jnp.float32, smallest / len(pieces), largest / len(pieces))
        return jnp.repeat(jnp.exp(steps), extent[dim] // blocks).reshape((-1,) + (1,) * (len(extent) - dim - 1))

    level = one(*pieces[0])
    for cut in pieces[1:]:
        level = level * one(*cut)
    return level


def centred(own_key, shape, spread, most, shards=(), held_as=jnp.bfloat16):
    array = spread * jax.random.normal(own_key, shape, jnp.float32)
    if shards:
        array = array * levels(own_key, shape, shards, -0.22, 0.18)
    return jnp.clip(array, -most, most).astype(held_as)


def setup_inputs(seed: int = 0, part: int = 0) -> dict:
    arg_keys = jax.random.split(jax.random.key(seed), 14)
    own_keys = jax.random.split(jax.random.fold_in(arg_keys[13], part), 14)
    return {
        "activations": draw_activations(jax.random.fold_in(jax.random.fold_in(arg_keys[13], part), 71), part),
        "routed": draw_routed(jax.random.fold_in(jax.random.fold_in(arg_keys[13], part), 71), part),
        "balance": draw_balance(jax.random.fold_in(jax.random.fold_in(arg_keys[13], part), 71), part),
        "w_query": draw_w_query(jax.random.fold_in(arg_keys[13], 71), part),
        "w_key": draw_w_key(jax.random.fold_in(arg_keys[13], 71), part),
        "w_value": centred(arg_keys[5], (D, KV_HEADS * HEAD_DIM), D ** -0.5, 0.09375, ((1, 8),)),
        "w_output": centred(arg_keys[6], (HEADS * HEAD_DIM, D), (HEADS * HEAD_DIM) ** -0.5, 0.09375, ((0, 8),)),
        "attn_gain": jnp.clip(1.0 + 0.15 * jax.random.normal(arg_keys[7], (D,), jnp.float32), 0.25, 1.75),
        "mlp_gain": jnp.clip(1.0 + 0.15 * jax.random.normal(arg_keys[8], (D,), jnp.float32), 0.25, 1.75),
        "w_gate": centred(arg_keys[9], (D, FF), D ** -0.5, 0.09375, ((1, 8),)),
        "w_up": centred(arg_keys[10], (D, FF), D ** -0.5, 0.09375, ((1, 8),)),
        "w_down": centred(arg_keys[11], (FF, D), FF ** -0.5, 0.0625, ((0, 8),)),
        "w_router": centred(arg_keys[12], (D,), D ** -0.5, 0.09375, (), jnp.float32),
    }


rope_base = 500000.0
norm_eps = 1e-05

def rms_scale(values, gain):
    mean_sq = lax.optimization_barrier(jnp.mean(values * values, axis=-1, keepdims=True))
    return values * lax.rsqrt(mean_sq + norm_eps) * gain

def rotary(values, positions):
    half = values.shape[-1] // 2
    steps_f = jnp.arange(half, dtype=jnp.float32)
    freqs = jnp.exp(-jnp.log(jnp.float32(rope_base)) * (2.0 * steps_f / values.shape[-1]))
    angles = positions.astype(jnp.float32)[:, None] * freqs[None, :]
    cosine = jnp.cos(angles)[:, None, :]
    sine = jnp.sin(angles)[:, None, :]
    first = values[..., :half]
    second = values[..., half:]
    return jnp.concatenate([first * cosine - second * sine, second * cosine + first * sine], axis=-1)

def reference(activations, routed, balance, w_query, w_key, w_value, w_output, attn_gain, mlp_gain, w_gate, w_up, w_down, w_router):
    total = routed.shape[0]
    rows = jnp.take(activations, routed, axis=0)
    rows_f = rows.astype(jnp.float32)
    normed = rms_scale(rows_f, attn_gain).astype(jnp.bfloat16)
    query = jnp.dot(normed, w_query, preferred_element_type=jnp.float32).reshape(total, HEADS, HEAD_DIM)
    query = rotary(query, routed).astype(jnp.bfloat16)
    key_raw = jnp.dot(normed, w_key, preferred_element_type=jnp.float32).astype(jnp.bfloat16)
    value = jnp.dot(normed, w_value, preferred_element_type=jnp.float32).astype(jnp.bfloat16)
    value = jnp.transpose(value.reshape(total, HEAD_DIM, KV_HEADS), (0, 2, 1))
    key_heads = jnp.transpose(key_raw.astype(jnp.float32).reshape(total, HEAD_DIM, KV_HEADS), (0, 2, 1))
    keys = rotary(key_heads, routed).astype(jnp.bfloat16)
    allowed = routed[None, :] <= routed[:, None]
    group_size = HEADS // KV_HEADS
    scale = HEAD_DIM ** (-0.5)

    def one_head(head):
        q_head = lax.dynamic_index_in_dim(query, head, 1, keepdims=False)
        kv_index = head // group_size
        k_head = lax.dynamic_index_in_dim(keys, kv_index, 1, keepdims=False)
        v_head = lax.dynamic_index_in_dim(value, kv_index, 1, keepdims=False)
        scores = jnp.dot(q_head, k_head.T, preferred_element_type=jnp.float32) * scale
        scores = jnp.where(allowed, scores, -1e+30)
        row_max = lax.optimization_barrier(jnp.max(scores, axis=-1, keepdims=True))
        exp_scores = jnp.exp(scores - row_max)
        probs = (exp_scores / lax.optimization_barrier(jnp.sum(exp_scores, axis=-1, keepdims=True))).astype(jnp.bfloat16)
        return jnp.dot(probs, v_head, preferred_element_type=jnp.float32).astype(jnp.bfloat16)
    per_head = lax.map(one_head, jnp.arange(HEADS, dtype=jnp.int32))
    heads_out = jnp.transpose(per_head, (1, 0, 2)).reshape(total, HEADS * HEAD_DIM)
    attn = jnp.dot(heads_out, w_output, preferred_element_type=jnp.float32)
    hidden = rows_f + attn
    mnorm = rms_scale(hidden, mlp_gain).astype(jnp.bfloat16)
    gate = jnp.dot(mnorm, w_gate, preferred_element_type=jnp.float32)
    upward = jnp.dot(mnorm, w_up, preferred_element_type=jnp.float32)
    inner = (jax.nn.silu(gate) * upward).astype(jnp.bfloat16)
    mlp = jnp.dot(inner, w_down, preferred_element_type=jnp.float32)
    score = lax.optimization_barrier(jnp.sum(rows_f * w_router[None, :], axis=1, keepdims=True))
    block_out = (rows_f + score * (attn + mlp)).astype(jnp.bfloat16)
    owner_order = jnp.argsort(balance, stable=True)
    return jnp.take(block_out, owner_order, axis=0)
```

```python
import jax
import jax.numpy as jnp
from jax import lax
from jax.sharding import PartitionSpec as P

HEADS = 32
KV_HEADS = 8
HEAD_DIM = 128

rope_base = 500000.0
norm_eps = 1e-05


def rms_scale(values, gain):
    mean_sq = jnp.mean(values * values, axis=-1, keepdims=True)
    return values * lax.rsqrt(mean_sq + norm_eps) * gain


def plane_of(count):
    wide = max(y for y in range(1, count + 1) if count % y == 0 and 2 * y * y <= max(count, 2))
    return count // wide, wide


def shift(block, tall, wide, dz, dy):
    pairs = [
        (z * wide + y, (z + dz) % tall * wide + (y + dy) % wide)
        for z in range(tall)
        for y in range(wide)
    ]
    return lax.ppermute(block, "ctx", pairs)


def gather_blocks(block, tall, wide):
    blocks = {}
    for dz in range(tall):
        blocks[dz, 0] = block if dz == 0 else shift(block, tall, wide, dz, 0)
    for dz in range(tall):
        for dy in range(1, wide):
            blocks[dz, dy] = shift(blocks[dz, 0], tall, wide, 0, dy)
    return [blocks[dz, dy] for dz in range(tall) for dy in range(wide)]


def scatter_sum(parts, tall, wide):
    total = None
    for dz in [*range(1, tall), 0]:
        lane = parts[dz * wide].astype(jnp.float32)
        for dy in range(1, wide):
            lane = lane + shift(parts[dz * wide + dy], tall, wide, 0, dy).astype(jnp.float32)
        if dz:
            lane = shift(lane.astype(jnp.bfloat16), tall, wide, dz, 0).astype(jnp.float32)
        total = lane if total is None else total + lane
    return total


def onehot_dot(onehot, values):
    return jnp.dot(onehot, values, preferred_element_type=jnp.float32).astype(values.dtype)


def on_device(
    activations,
    routed,
    balance,
    w_query,
    w_key,
    w_value,
    w_output,
    attn_gain,
    mlp_gain,
    w_gate,
    w_up,
    w_down,
    w_router,
):
    shard_count = lax.axis_size("ctx")
    tall, wide = plane_of(shard_count)
    me = lax.axis_index("ctx")
    my_z, my_y = me // wide, me % wide
    tok_shard = activations.shape[0]
    total = routed.shape[0]
    share = total // shard_count
    capacity = 2 * share
    local_heads = w_query.shape[1] // HEAD_DIM
    group_size = HEADS // KV_HEADS
    bf16, f32 = jnp.bfloat16, jnp.float32

    row_ids = jnp.arange(total, dtype=jnp.int32)
    low = me * tok_shard
    my_first = jnp.sum((routed < low).astype(jnp.int32))
    local = routed - low
    is_here = (local >= 0) & (local < tok_shard)
    slots = jnp.arange(capacity, dtype=jnp.int32)
    hit = is_here[None, :] & (row_ids[None, :] - my_first == slots[:, None])
    token = jnp.sum(jnp.where(hit, local[None, :] + 1, 0), axis=1) - 1
    pick_out = (token[:, None] == jnp.arange(tok_shard, dtype=jnp.int32)[None, :]).astype(bf16)
    outgoing = onehot_dot(pick_out, activations)
    blocks = gather_blocks(outgoing, tall, wide)

    home = routed // tok_shard
    before = home[None, :] < home[:, None]
    in_block = row_ids - jnp.sum(before.astype(jnp.int32), axis=1)
    from_z, from_y = (my_z - home // wide) % tall, (my_y - home % wide) % wide
    slot_of_row = (from_z * wide + from_y) * capacity + in_block
    same = (balance[None, :] == balance[:, None]) & (row_ids[None, :] < row_ids[:, None])
    rank = jnp.sum(same.astype(jnp.int32), axis=1)
    to_z, to_y = (balance // wide - my_z) % tall, (balance % wide - my_y) % wide
    place_of_row = (to_z * wide + to_y) * share + rank
    placed = place_of_row[None, :] == row_ids[:, None]
    slot_at = jnp.sum(jnp.where(placed, slot_of_row[None, :], 0), axis=1)
    positions = jnp.sum(jnp.where(placed, routed[None, :], 0), axis=1)
    pick_rows = (
        slot_at[:, None] == jnp.arange(shard_count * capacity, dtype=jnp.int32)[None, :]
    ).astype(bf16)

    rows = onehot_dot(pick_rows, jnp.concatenate(blocks, axis=0))
    normed = rms_scale(rows.astype(f32), attn_gain).astype(bf16)

    half = HEAD_DIM // 2
    steps_f = jnp.arange(half, dtype=f32)
    freqs = jnp.exp(-jnp.log(f32(rope_base)) * (2.0 * steps_f / HEAD_DIM))
    q_angles = positions.astype(f32)[:, None] * freqs[None, :]
    q_cos, q_sin = jnp.cos(q_angles)[:, None, :], jnp.sin(q_angles)[:, None, :]
    k_angles = freqs[:, None] * routed.astype(f32)[None, :]
    k_cos, k_sin = jnp.cos(k_angles), jnp.sin(k_angles)

    key_part = jnp.dot(normed, w_key, preferred_element_type=f32).astype(bf16)
    value_part = jnp.dot(normed, w_value, preferred_element_type=f32).astype(bf16)
    depth = w_key.shape[1] // KV_HEADS
    kv_local = max(1, local_heads // group_size)
    in_order = placed.astype(bf16)
    kv_t = lax.dot_general(
        jnp.concatenate([key_part, value_part], axis=1),
        in_order,
        (((0,), (0,)), ((), ())),
        preferred_element_type=f32,
    ).astype(bf16)
    kv_t = jnp.transpose(kv_t.reshape(2, depth, KV_HEADS, total), (2, 0, 1, 3))
    if kv_local * shard_count == KV_HEADS:
        outbound = kv_t.reshape(shard_count, kv_local, 2, depth, total)
    else:
        firsts = [p * local_heads // group_size for p in range(shard_count)]
        outbound = jnp.stack([kv_t[g : g + kv_local] for g in firsts])
    inbound = lax.all_to_all(outbound, "ctx", 0, 0, tiled=True)
    inbound = jnp.transpose(inbound, (2, 1, 0, 3, 4)).reshape(2, kv_local, HEAD_DIM, total)
    key_t, value_t = inbound[0].astype(f32), inbound[1]
    key_a, key_b = key_t[:, :half], key_t[:, half:]
    key_t = jnp.concatenate(
        [key_a * k_cos - key_b * k_sin, key_b * k_cos + key_a * k_sin], axis=1
    ).astype(bf16)

    query = jnp.dot(normed, w_query, preferred_element_type=f32).reshape(
        total, local_heads, HEAD_DIM
    )
    query_a, query_b = query[..., :half], query[..., half:]
    query = jnp.concatenate(
        [query_a * q_cos - query_b * q_sin, query_b * q_cos + query_a * q_sin], axis=-1
    ).astype(bf16)
    query = query.reshape(total, kv_local, local_heads // kv_local, HEAD_DIM)
    scores = jnp.einsum("qgrd,gdk->grqk", query, key_t, preferred_element_type=f32)
    scores = scores * HEAD_DIM ** (-0.5)
    allowed = routed[None, :] <= positions[:, None]
    scores = jnp.where(allowed, scores, -1e30)
    exp_scores = jnp.exp(scores - jnp.max(scores, axis=-1, keepdims=True))
    probs = (exp_scores / jnp.sum(exp_scores, axis=-1, keepdims=True)).astype(bf16)
    heads_out = jnp.einsum("grqk,gdk->qgrd", probs, value_t, preferred_element_type=f32)
    heads_out = heads_out.astype(bf16).reshape(total, local_heads * HEAD_DIM)

    def split(partial):
        return [partial[r * share : (r + 1) * share] for r in range(shard_count)]

    attn_part = jnp.dot(heads_out, w_output, preferred_element_type=f32).astype(bf16)
    attn_own = scatter_sum(split(attn_part), tall, wide)
    own_rows = rows[:share].astype(f32)
    mnorm = rms_scale(own_rows + attn_own, mlp_gain).astype(bf16)
    piece = jnp.concatenate(gather_blocks(mnorm, tall, wide), axis=0)
    gate = jnp.dot(piece, w_gate, preferred_element_type=f32)
    upward = jnp.dot(piece, w_up, preferred_element_type=f32)
    inner = (jax.nn.silu(gate) * upward).astype(bf16)
    mlp_part = split(jnp.dot(inner, w_down, preferred_element_type=f32).astype(bf16))
    back = [
        mlp_part[(-dz) % tall * wide + (-dy) % wide] for dz in range(tall) for dy in range(wide)
    ]
    mlp_own = scatter_sum(back, tall, wide)
    router_score = jnp.sum(own_rows * w_router[None, :], axis=1, keepdims=True)
    return (own_rows + router_score * (attn_own + mlp_own)).astype(bf16)


def solution(mesh):
    in_specs = (
        P(("dp", "ctx"), None),
        P("dp"),
        P("dp"),
        P(None, "ctx"),
        P(None, "ctx"),
        P(None, "ctx"),
        P("ctx", None),
        P(),
        P(),
        P(None, "ctx"),
        P(None, "ctx"),
        P("ctx", None),
        P(),
    )
    out_specs = P(("dp", "ctx"), None)
    return jax.shard_map(
        on_device, mesh=mesh, in_specs=in_specs, out_specs=out_specs, check_vma=False
    )
```

```python
import functools

import jax
import jax.numpy as jnp
from jax import lax
from jax.experimental import pallas as pl
from jax.experimental.pallas import tpu as pltpu
from jax.sharding import PartitionSpec as P

HEADS = 32
KV_HEADS = 8
HEAD_DIM = 128

rope_base = 500000.0
norm_eps = 1e-05

bf16, f32, i32 = jnp.bfloat16, jnp.float32, jnp.int32
VMEM = pl.BlockSpec(memory_space=pltpu.VMEM)


def plane_of(count):
    wide = max(y for y in range(1, count + 1) if count % y == 0 and 2 * y * y <= max(count, 2))
    return count // wide, wide


def shift(block, tall, wide, dz, dy):
    pairs = [
        (z * wide + y, (z + dz) % tall * wide + (y + dy) % wide)
        for z in range(tall)
        for y in range(wide)
    ]
    return lax.ppermute(block, "ctx", pairs)


def gather_blocks(block, tall, wide):
    blocks = {}
    for dz in range(tall):
        blocks[dz, 0] = block if dz == 0 else shift(block, tall, wide, dz, 0)
    for dz in range(tall):
        for dy in range(1, wide):
            blocks[dz, dy] = shift(blocks[dz, 0], tall, wide, 0, dy)
    return [blocks[dz, dy] for dz in range(tall) for dy in range(wide)]


def scatter_sum(parts, tall, wide):
    total = None
    for dz in [*range(1, tall), 0]:
        lane = parts[dz * wide].astype(f32)
        for dy in range(1, wide):
            lane = lane + shift(parts[dz * wide + dy], tall, wide, 0, dy).astype(f32)
        if dz:
            lane = shift(lane.astype(bf16), tall, wide, dz, 0).astype(f32)
        total = lane if total is None else total + lane
    return total


def exchange(parts, tall, wide):
    rows = [[parts[dz * wide + dy] for dz in range(tall)] for dy in range(wide)]
    lanes = [jnp.stack(rows[0])]
    lanes += [shift(jnp.stack(rows[dy]), tall, wide, 0, dy) for dy in range(1, wide)]
    lanes = jnp.stack(lanes, axis=1)
    out = [lanes[0]] + [shift(lanes[dz], tall, wide, dz, 0) for dz in range(1, tall)]
    return jnp.stack(out)


def dot(a, b):
    return jnp.dot(a, b, preferred_element_type=f32)


def fetched(weight):
    return pltpu.with_memory_space_constraint(weight, pltpu.VMEM)


def kernel_call(body, outs, args, scratch=(), limit=16, flops=0):
    return pl.pallas_call(
        body,
        out_shape=[jax.ShapeDtypeStruct(s, d) for s, d in outs],
        in_specs=[VMEM] * len(args),
        out_specs=[VMEM] * len(outs),
        scratch_shapes=list(scratch),
        compiler_params=pltpu.CompilerParams(vmem_limit_bytes=limit << 20),
        cost_estimate=pl.CostEstimate(flops=flops, bytes_accessed=1 << 20, transcendentals=0),
    )(*args)


def tile_of(width, most):
    return width if width <= most else most


def kv_body(count, *refs):
    blocks = refs[:count]
    pick, order, columns, gain, w_key, w_value, normed, own, kv_out, rows = refs[count:]
    total, width = normed.shape
    tile = tile_of(width, 512)
    square = jnp.zeros((total, 1), f32)
    for start in range(0, width, tile):
        span = slice(start, start + tile)
        part = dot(pick[...], jnp.concatenate([b[:, span] for b in blocks], axis=0))
        rows[:, span] = part.astype(bf16)
        square += jnp.sum(part * part, axis=1, keepdims=True)
    own[...] = rows[: own.shape[0], :]
    factor = lax.rsqrt(square / width + norm_eps)
    for start in range(0, width, tile):
        span = slice(start, start + tile)
        part = rows[:, span].astype(f32) * factor * gain[:, span]
        normed[:, span] = part.astype(bf16)
    keys = dot(normed[...], w_key[...]).astype(bf16)
    values = dot(normed[...], w_value[...]).astype(bf16)
    both = jnp.concatenate([keys, values], axis=1)
    turned = lax.dot_general(
        columns[...], both, (((1,), (1,)), ((), ())), preferred_element_type=f32
    ).astype(bf16)
    kv_out[...] = dot(turned, order[...]).astype(bf16)


def query_body(normed, w_query, cosine, sine, query):
    raw = dot(normed[...], w_query[...])
    for head in range(query.shape[1] // HEAD_DIM):
        span = slice(head * HEAD_DIM, (head + 1) * HEAD_DIM)
        one = raw[:, span]
        turned = one * cosine[...] + pltpu.roll(one, HEAD_DIM // 2, 1) * sine[...]
        query[:, span] = turned.astype(bf16)


def attend_body(kv_local, query, key_t, value_t, cosine, sine, key_pos, query_pos, w_output, *rest):
    parts, heads_out = rest[:-1], rest[-1]
    half = HEAD_DIM // 2
    heads = query.shape[1] // HEAD_DIM
    allowed = key_pos[...] <= query_pos[...]
    for group in range(kv_local):
        base = group * HEAD_DIM
        first = key_t[base : base + half, :].astype(f32)
        second = key_t[base + half : base + HEAD_DIM, :].astype(f32)
        keys = jnp.concatenate(
            [first * cosine[...] - second * sine[...], second * cosine[...] + first * sine[...]],
            axis=0,
        ).astype(bf16)
        values = value_t[base : base + HEAD_DIM, :]
        for head in range(group * heads // kv_local, (group + 1) * heads // kv_local):
            span = slice(head * HEAD_DIM, (head + 1) * HEAD_DIM)
            scores = dot(query[:, span], keys) * HEAD_DIM ** (-0.5)
            scores = jnp.where(allowed, scores, -1e30)
            weights = jnp.exp(scores - jnp.max(scores, axis=1, keepdims=True))
            probs = (weights / jnp.sum(weights, axis=1, keepdims=True)).astype(bf16)
            heads_out[:, span] = lax.dot_general(
                probs, values, (((1,), (1,)), ((), ())), preferred_element_type=f32
            ).astype(bf16)
    spread(heads_out, w_output, parts)


def spread(left, weight, parts):
    width = weight.shape[1]
    tile = tile_of(width, 512)
    share = parts[0].shape[0]
    for start in range(0, width, tile):
        span = slice(start, start + tile)
        product = dot(left[...], weight[:, span]).astype(bf16)
        for index, part in enumerate(parts):
            part[:, span] = product[index * share : (index + 1) * share, :]


def mlp_body(count, *refs):
    blocks, (w_gate, w_up, w_down) = refs[:count], refs[count : count + 3]
    parts, (piece, inner) = refs[count + 3 : -2], refs[-2:]
    share = blocks[0].shape[0]
    for index, block in enumerate(blocks):
        piece[index * share : (index + 1) * share, :] = block[...]
    width = w_gate.shape[1]
    tile = tile_of(width, 256)
    for start in range(0, width, tile):
        span = slice(start, start + tile)
        gate = dot(piece[...], w_gate[:, span])
        upward = dot(piece[...], w_up[:, span])
        inner[:, span] = (gate / (1.0 + jnp.exp(-gate)) * upward).astype(bf16)
    spread(inner, w_down, parts)


def onehot_dot(onehot, values):
    return dot(onehot, values).astype(values.dtype)


def on_device(
    activations,
    routed,
    balance,
    w_query,
    w_key,
    w_value,
    w_output,
    attn_gain,
    mlp_gain,
    w_gate,
    w_up,
    w_down,
    w_router,
):
    shard_count = lax.axis_size("ctx")
    tall, wide = plane_of(shard_count)
    me = lax.axis_index("ctx")
    my_z, my_y = me // wide, me % wide
    tok_shard, model = activations.shape
    total = routed.shape[0]
    share = total // shard_count
    capacity = 2 * share
    local_heads = w_query.shape[1] // HEAD_DIM
    group_size = HEADS // KV_HEADS

    row_ids = jnp.arange(total, dtype=i32)
    low = me * tok_shard
    my_first = jnp.sum((routed < low).astype(i32))
    local = routed - low
    is_here = (local >= 0) & (local < tok_shard)
    slots = jnp.arange(capacity, dtype=i32)
    hit = is_here[None, :] & (row_ids[None, :] - my_first == slots[:, None])
    token = jnp.sum(jnp.where(hit, local[None, :] + 1, 0), axis=1) - 1
    pick_out = (token[:, None] == jnp.arange(tok_shard, dtype=i32)[None, :]).astype(bf16)
    outgoing = onehot_dot(pick_out, activations)
    blocks = gather_blocks(outgoing, tall, wide)

    home = routed // tok_shard
    before = home[None, :] < home[:, None]
    in_block = row_ids - jnp.sum(before.astype(i32), axis=1)
    from_z, from_y = (my_z - home // wide) % tall, (my_y - home % wide) % wide
    slot_of_row = (from_z * wide + from_y) * capacity + in_block
    same = (balance[None, :] == balance[:, None]) & (row_ids[None, :] < row_ids[:, None])
    rank = jnp.sum(same.astype(i32), axis=1)
    to_z, to_y = (balance // wide - my_z) % tall, (balance % wide - my_y) % wide
    place_of_row = (to_z * wide + to_y) * share + rank
    placed = place_of_row[None, :] == row_ids[:, None]
    slot_at = jnp.sum(jnp.where(placed, slot_of_row[None, :], 0), axis=1)
    positions = jnp.sum(jnp.where(placed, routed[None, :], 0), axis=1)
    pick_rows = (
        slot_at[:, None] == jnp.arange(shard_count * capacity, dtype=i32)[None, :]
    ).astype(bf16)
    in_order = placed.astype(bf16)

    half = HEAD_DIM // 2
    steps_f = jnp.arange(half, dtype=f32)
    freqs = jnp.exp(-jnp.log(f32(rope_base)) * (2.0 * steps_f / HEAD_DIM))
    q_angles = positions.astype(f32)[:, None] * freqs[None, :]
    q_cos, q_sin = jnp.cos(q_angles), jnp.sin(q_angles)
    q_cos = jnp.concatenate([q_cos, q_cos], axis=1)
    q_sin = jnp.concatenate([-q_sin, q_sin], axis=1)
    k_angles = freqs[:, None] * routed.astype(f32)[None, :]
    k_cos, k_sin = jnp.cos(k_angles), jnp.sin(k_angles)

    key_cols = w_key.shape[1]
    depth = key_cols // KV_HEADS
    kv_local = max(1, local_heads // group_size)
    at = jnp.arange(2 * key_cols, dtype=i32)
    head_at, side_at, entry_at = at // (2 * depth), at // depth % 2, at % depth
    column_at = side_at * key_cols + entry_at * KV_HEADS + head_at
    columns = (column_at[:, None] == at[None, :]).astype(bf16)
    normed, own, kv_out = kernel_call(
        functools.partial(kv_body, len(blocks)),
        [((total, model), bf16), ((share, model), bf16), ((2 * key_cols, total), bf16)],
        [
            *blocks,
            pick_rows,
            in_order,
            columns,
            attn_gain.reshape(1, model),
            fetched(w_key),
            fetched(w_value),
        ],
        [pltpu.VMEM((total, model), bf16)],
        flops=2 * total * model * 512,
    )
    kv_heads = kv_out.reshape(KV_HEADS, 2 * depth, total)
    sent = []
    for dz in range(tall):
        for dy in range(wide):
            peer = (my_z + dz) % tall * wide + (my_y + dy) % wide
            first = peer * local_heads // group_size
            sent.append(lax.dynamic_slice_in_dim(kv_heads, first, kv_local, 0))
    arrived = exchange(sent, tall, wide)
    from_where = jnp.arange(shard_count, dtype=i32)
    arrived_at = (my_z - from_where // wide) % tall * wide + (my_y - from_where % wide) % wide
    arrived = arrived.reshape(shard_count, kv_local * 2 * depth * total)
    in_turn = (arrived_at[:, None] == from_where[None, :]).astype(bf16)
    arrived = onehot_dot(in_turn, arrived).reshape(shard_count, kv_local, 2, depth, total)
    arrived = jnp.transpose(arrived, (2, 1, 0, 3, 4)).reshape(2, kv_local * HEAD_DIM, total)

    (query,) = kernel_call(
        query_body,
        [((total, local_heads * HEAD_DIM), bf16)],
        [normed, fetched(w_query), q_cos, q_sin],
        flops=2 * total * model * local_heads * HEAD_DIM,
    )
    share_block = ((share, model), bf16)
    attn_parts = kernel_call(
        functools.partial(attend_body, kv_local),
        [share_block] * shard_count,
        [
            query,
            arrived[0],
            arrived[1],
            k_cos,
            k_sin,
            routed.reshape(1, total),
            positions.reshape(total, 1),
            fetched(w_output),
        ],
        [pltpu.VMEM((total, local_heads * HEAD_DIM), bf16)],
        flops=2 * total * model * local_heads * HEAD_DIM,
    )
    attn_own = scatter_sum(attn_parts, tall, wide)
    own_rows = own.astype(f32)
    hidden = own_rows + attn_own
    mean_sq = jnp.mean(hidden * hidden, axis=-1, keepdims=True)
    mnorm = (hidden * lax.rsqrt(mean_sq + norm_eps) * mlp_gain).astype(bf16)
    pieces = gather_blocks(mnorm, tall, wide)
    hidden_units = w_gate.shape[1]
    mlp_parts = kernel_call(
        functools.partial(mlp_body, shard_count),
        [share_block] * shard_count,
        [*pieces, fetched(w_gate), fetched(w_up), fetched(w_down)],
        [pltpu.VMEM((total, model), bf16), pltpu.VMEM((total, hidden_units), bf16)],
        flops=6 * total * model * hidden_units,
    )
    back = [
        mlp_parts[(-dz) % tall * wide + (-dy) % wide] for dz in range(tall) for dy in range(wide)
    ]
    mlp_own = scatter_sum(back, tall, wide)
    router_score = jnp.sum(own_rows * w_router[None, :], axis=1, keepdims=True)
    return (own_rows + router_score * (attn_own + mlp_own)).astype(bf16)


def solution(mesh):
    in_specs = (
        P(("dp", "ctx"), None),
        P("dp"),
        P("dp"),
        P(None, "ctx"),
        P(None, "ctx"),
        P(None, "ctx"),
        P("ctx", None),
        P(),
        P(),
        P(None, "ctx"),
        P(None, "ctx"),
        P("ctx", None),
        P(),
    )
    out_specs = P(("dp", "ctx"), None)
    return jax.shard_map(
        on_device, mesh=mesh, in_specs=in_specs, out_specs=out_specs, check_vma=False
    )
```

```python
import functools

import jax
import jax.numpy as jnp
import numpy as np
from jax import lax
from jax.experimental import pallas as pl
from jax.experimental.pallas import tpu as pltpu
from jax.sharding import PartitionSpec as P

HEADS = 32
KV_HEADS = 8
HEAD_DIM = 128

rope_base = 500000.0
norm_eps = 1e-05

bf16, f32, i32 = jnp.bfloat16, jnp.float32, jnp.int32
VMEM = pl.BlockSpec(memory_space=pltpu.VMEM)


def plane_of(count):
    wide = max(y for y in range(1, count + 1) if count % y == 0 and 2 * y * y <= max(count, 2))
    return count // wide, wide


def shift(block, tall, wide, dz, dy, keep=None):
    pairs = [
        (z * wide + y, (z + dz) % tall * wide + (y + dy) % wide)
        for z in range(tall)
        for y in range(wide)
        if keep is None or keep(z)
    ]
    return lax.ppermute(block, "ctx", pairs)


def gather_blocks(block, tall, wide, relay=False):
    blocks = {(0, 0): block}
    for dz in range(1, tall):
        if not (relay and tall == 4 and dz == 2):
            blocks[dz, 0] = shift(block, tall, wide, dz, 0)
    if relay and tall == 4:
        up = shift(blocks[1, 0], tall, wide, 1, 0, lambda z: z in (1, 2))
        down = shift(blocks[3, 0], tall, wide, -1, 0, lambda z: z in (1, 2))
        blocks[2, 0] = up + down
    for dz in [0, 1, *range(tall - 1, 1, -1)]:
        for dy in range(1, wide):
            blocks[dz, dy] = shift(blocks[dz, 0], tall, wide, 0, dy)
    return [blocks[dz, dy] for dz in range(tall) for dy in range(wide)]


def sum_order(tall):
    order = [tall // 2, *range(1, tall // 2), *range(tall // 2 + 1, tall), 0]
    return order[: tall // 2], order[tall // 2 :]


def sum_shapes(tall, wide, share, model):
    kept = [((share, model), bf16)] * tall
    return kept + [((tall // 2 * share, model), bf16)] * (2 * (wide - 1))


def store_parts(parts, tall, wide, span, product, back):
    share = parts[0].shape[0]
    sign = -1 if back else 1

    def rows(dz, dy):
        at = sign * dz % tall * wide + sign * dy % wide
        return product[at * share : (at + 1) * share, :]

    for dz in range(tall):
        parts[dz][:, span] = rows(dz, 0)
    for dy in range(1, wide):
        for which, group in enumerate(sum_order(tall)):
            out = parts[tall + 2 * (dy - 1) + which]
            for place, dz in enumerate(group):
                out[place * share : (place + 1) * share, span] = rows(dz, dy)


def scatter_sum(parts, tall, wide):
    share = parts[0].shape[0]
    crossed = [shift(p, tall, wide, 0, i // 2 + 1) for i, p in enumerate(parts[tall:])]
    total = None
    for which, group in enumerate(sum_order(tall)):
        for place, dz in enumerate(group):
            lane = parts[dz].astype(f32)
            for dy in range(1, wide):
                other = crossed[2 * (dy - 1) + which]
                lane = lane + other[place * share : (place + 1) * share].astype(f32)
            if dz:
                lane = shift(lane.astype(bf16), tall, wide, dz, 0).astype(f32)
            total = lane if total is None else total + lane
    return total


def dot(a, b):
    return jnp.dot(a, b, preferred_element_type=f32)


def fetched(weight):
    return pltpu.with_memory_space_constraint(weight, pltpu.VMEM)


def kernel_call(body, outs, args, scratch=(), limit=14, flops=0, specs=None):
    return pl.pallas_call(
        body,
        out_shape=[jax.ShapeDtypeStruct(s, d) for s, d in outs],
        in_specs=specs or [VMEM] * len(args),
        out_specs=[VMEM] * len(outs),
        scratch_shapes=list(scratch),
        compiler_params=pltpu.CompilerParams(vmem_limit_bytes=limit << 20),
        cost_estimate=pl.CostEstimate(flops=flops, bytes_accessed=1 << 20, transcendentals=0),
    )(*args)


def load_body(count, *refs):
    sources, copies, sems = refs[1 : 1 + count], refs[1 + count : -2], refs[-1]
    moves = [
        pltpu.make_async_copy(a, b, sems.at[i]) for i, (a, b) in enumerate(zip(sources, copies))
    ]
    for move in moves:
        move.start()
    for move in moves:
        move.wait()
    refs[-2][...] = jnp.zeros_like(refs[-2])


def load(after, *arrays):
    size = sum(a.size * a.dtype.itemsize for a in arrays)
    *copies, token = pl.pallas_call(
        functools.partial(load_body, len(arrays)),
        out_shape=[pltpu.VMEM(a.shape, a.dtype) for a in arrays]
        + [jax.ShapeDtypeStruct((8, 128), f32)],
        in_specs=[pl.BlockSpec(memory_space=pl.ANY)] * (1 + len(arrays)),
        out_specs=[VMEM] * (1 + len(arrays)),
        scratch_shapes=[pltpu.SemaphoreType.DMA((len(arrays),))],
        compiler_params=pltpu.CompilerParams(vmem_limit_bytes=2 << 20),
        cost_estimate=pl.CostEstimate(flops=0, bytes_accessed=2 * size, transcendentals=0),
    )(after, *[pltpu.with_memory_space_constraint(a, pltpu.HBM) for a in arrays])
    return [fetched(c) for c in copies] + [token]


def tile_of(width, most):
    return width if width <= most else most


def iota(shape, axis):
    return lax.broadcasted_iota(i32, shape, axis).astype(f32)


def pick(onehot, values):
    return dot(onehot, values).astype(values.dtype)


def send_body(me, routed, activations, outgoing):
    capacity, tokens, total = outgoing.shape[0], activations.shape[0], routed.shape[1]
    low = (me[0] * tokens).astype(f32)
    where = routed[...].astype(f32)
    first = jnp.sum(jnp.where(where < low, 1.0, 0.0), axis=1, keepdims=True)
    here = (where >= low) & (where < low + tokens)
    slot = jnp.where(here, iota((1, total), 1) - first, -1.0)
    hit = slot == iota((capacity, total), 0)
    token = jnp.sum(jnp.where(hit, where - low + 1.0, 0.0), axis=1, keepdims=True) - 1.0
    onehot = jnp.where(token == iota((capacity, tokens), 1), 1.0, 0.0).astype(bf16)
    width = activations.shape[1]
    tile = tile_of(width, 1024)
    for start in range(0, width, tile):
        span = slice(start, start + tile)
        outgoing[:, span] = pick(onehot, activations[:, span])


def map_body(tall, wide, tokens, heads_of, me, routed, balance, notes, *outs):
    pick_rows, in_order, columns, unmix, positions = outs
    count, total = tall * wide, routed.shape[1]
    share, capacity = total // count, pick_rows.shape[1] // count
    outbound, inbound = columns.shape[0], unmix.shape[0]
    my_z, my_y = lax.div(me[0], wide), lax.rem(me[0], wide)
    where, owner = routed[...].astype(f32), balance[...].astype(f32)
    lane = iota((1, total), 1)
    slot, place = jnp.zeros((1, total), f32), jnp.zeros((1, total), f32)
    out_base, out_block = notes[:outbound, 0:1], notes[:outbound, 1:2]
    in_base, in_source = notes[:inbound, 2:3], notes[:inbound, 3:4]
    for s in range(count):
        z, y = divmod(s, wide)
        from_block = lax.rem(my_z - z + tall, tall) * wide + lax.rem(my_y - y + wide, wide)
        to_block = lax.rem(z - my_z + tall, tall) * wide + lax.rem(y - my_y + wide, wide)
        peer = lax.rem(my_z + z, tall) * wide + lax.rem(my_y + y, wide)
        before = where < s * tokens
        first = jnp.sum(jnp.where(before, 1.0, 0.0), axis=1, keepdims=True)
        inside = (where < (s + 1) * tokens) & jnp.logical_not(before)
        start = (from_block * capacity).astype(f32)
        slot += jnp.where(inside, lane - first + start, 0.0)
        place += jnp.where(owner == s, (to_block * share).astype(f32), 0.0)
        out_base += jnp.where(out_block == s, heads_of(peer).astype(f32), 0.0)
        in_base += jnp.where(in_source == s, (from_block * (outbound // count)).astype(f32), 0.0)
    mine = owner == iota((count, total), 0)
    earlier = jnp.where(iota((total, total), 0) < iota((total, total), 1), 1.0, 0.0)
    rank = dot(jnp.where(mine, 1.0, 0.0).astype(bf16), earlier.astype(bf16))
    place += jnp.sum(jnp.where(mine, rank, 0.0), axis=0, keepdims=True)
    placed = place == iota((total, total), 0)
    in_order[...] = jnp.where(placed, 1.0, 0.0).astype(bf16)
    positions[...] = jnp.sum(jnp.where(placed, where, 0.0), axis=1, keepdims=True)
    slot_at = jnp.sum(jnp.where(placed, slot, 0.0), axis=1, keepdims=True)
    pick_rows[...] = jnp.where(slot_at == iota(pick_rows.shape, 1), 1.0, 0.0).astype(bf16)
    columns[...] = jnp.where(out_base == iota(columns.shape, 1), 1.0, 0.0).astype(bf16)
    unmix[...] = jnp.where(in_base == iota(unmix.shape, 1), 1.0, 0.0).astype(bf16)


def kv_body(count, *refs):
    blocks = refs[:count]
    pick_rows, order, columns, gain, w_key, w_value = refs[count : count + 6]
    (normed, own, *sent), rows = refs[-3 - count : -1], refs[-1]
    total, width = normed.shape
    tile = tile_of(width, 512)
    square = jnp.zeros((total, 1), f32)
    for start in range(0, width, tile):
        span = slice(start, start + tile)
        part = dot(pick_rows[...], jnp.concatenate([b[:, span] for b in blocks], axis=0))
        rows[:, span] = part.astype(bf16)
        square += jnp.sum(part * part, axis=1, keepdims=True)
    own[...] = rows[: own.shape[0], :]
    factor = lax.rsqrt(square / width + norm_eps)
    for start in range(0, width, tile):
        span = slice(start, start + tile)
        part = rows[:, span].astype(f32) * factor * gain[:, span]
        normed[:, span] = part.astype(bf16)
    keys = dot(normed[...], w_key[...]).astype(bf16)
    values = dot(normed[...], w_value[...]).astype(bf16)
    both = jnp.concatenate([keys, values], axis=1)
    turned = lax.dot_general(
        columns[...], both, (((1,), (1,)), ((), ())), preferred_element_type=f32
    ).astype(bf16)
    turned = dot(turned, order[...])
    each = turned.shape[0] // len(sent)
    for index, part in enumerate(sent):
        part[...] = turned[index * each : (index + 1) * each, :].astype(bf16)


def query_body(normed, w_query, cosine, sine, query):
    raw = dot(normed[...], w_query[...])
    for head in range(query.shape[1] // HEAD_DIM):
        span = slice(head * HEAD_DIM, (head + 1) * HEAD_DIM)
        one = raw[:, span]
        turned = one * cosine[...] + pltpu.roll(one, HEAD_DIM // 2, 1) * sine[...]
        query[:, span] = turned.astype(bf16)


def attend_body(plane, kv_local, *refs):
    count = plane[0] * plane[1]
    arrived, rest = refs[:count], refs[count:]
    query, unmix, cosine, sine, key_pos, query_pos, w_output = rest[:7]
    parts, heads_out = rest[7:-1], rest[-1]
    half = HEAD_DIM // 2
    heads = query.shape[1] // HEAD_DIM
    mixed = jnp.concatenate([a[...].astype(f32) for a in arrived], axis=0).astype(bf16)
    both = dot(unmix[...], mixed)
    allowed = key_pos[...].astype(f32) <= query_pos[...]
    for group in range(kv_local):
        base = group * HEAD_DIM
        first, second = both[base : base + half], both[base + half : base + HEAD_DIM]
        keys = jnp.concatenate(
            [first * cosine[...] - second * sine[...], second * cosine[...] + first * sine[...]],
            axis=0,
        ).astype(bf16)
        base += kv_local * HEAD_DIM
        values = both[base : base + HEAD_DIM].astype(bf16)
        for head in range(group * heads // kv_local, (group + 1) * heads // kv_local):
            span = slice(head * HEAD_DIM, (head + 1) * HEAD_DIM)
            scores = dot(query[:, span], keys) * HEAD_DIM ** (-0.5)
            scores = jnp.where(allowed, scores, -1e30)
            weights = jnp.exp(scores - jnp.max(scores, axis=1, keepdims=True))
            probs = (weights / jnp.sum(weights, axis=1, keepdims=True)).astype(bf16)
            heads_out[:, span] = lax.dot_general(
                probs, values, (((1,), (1,)), ((), ())), preferred_element_type=f32
            ).astype(bf16)
    spread(heads_out, w_output, parts, plane, False)


def spread(left, weight, parts, plane, back):
    width = weight.shape[1]
    tile = tile_of(width, 512)
    for start in range(0, width, tile):
        span = slice(start, start + tile)
        product = dot(left[...], weight[:, span]).astype(bf16)
        store_parts(parts, *plane, span, product, back)


def mlp_body(plane, *refs):
    count = plane[0] * plane[1]
    blocks, (w_gate, w_up, w_down) = refs[:count], refs[count : count + 3]
    parts, (piece, inner) = refs[count + 3 : -2], refs[-2:]
    share = blocks[0].shape[0]
    for index, block in enumerate(blocks):
        piece[index * share : (index + 1) * share, :] = block[...]
    width = w_gate.shape[1]
    tile = tile_of(width, 256)
    for start in range(0, width, tile):
        span = slice(start, start + tile)
        gate = dot(piece[...], w_gate[:, span])
        upward = dot(piece[...], w_up[:, span])
        inner[:, span] = (gate / (1.0 + jnp.exp(-gate)) * upward).astype(bf16)
    spread(inner, w_down, parts, plane, True)


def on_device(
    activations,
    routed,
    balance,
    w_query,
    w_key,
    w_value,
    w_output,
    attn_gain,
    mlp_gain,
    w_gate,
    w_up,
    w_down,
    w_router,
):
    count = lax.axis_size("ctx")
    plane = tall, wide = plane_of(count)
    me = lax.axis_index("ctx").astype(i32).reshape(1)
    tokens, model = activations.shape
    total = routed.shape[0]
    share = total // count
    capacity = 2 * share
    local_heads = w_query.shape[1] // HEAD_DIM
    group_size = HEADS // KV_HEADS
    kv_local = max(1, local_heads // group_size)
    key_cols = w_key.shape[1]
    depth = key_cols // KV_HEADS
    scalar = pl.BlockSpec(memory_space=pltpu.SMEM)
    routed, balance = routed.reshape(1, total), balance.reshape(1, total)

    (outgoing,) = kernel_call(
        send_body,
        [((capacity, model), bf16)],
        [me, routed, activations],
        specs=[scalar, VMEM, VMEM],
        flops=2 * capacity * tokens * model,
    )
    blocks = gather_blocks(outgoing, tall, wide, relay=True)
    attn_gain, w_key, w_value, w_query, _ = load(
        outgoing, attn_gain.reshape(1, model), w_key, w_value, w_query
    )
    near = blocks[wide]
    w_output, *tokens_1 = load(near, w_output)
    w_gate, *tokens_2 = load(near, w_gate)
    w_up, *tokens_3 = load(near, w_up)
    w_down, *tokens_4 = load(near, w_down)
    loaded = tokens_1 + tokens_2 + tokens_3 + tokens_4

    each = kv_local * 2 * depth
    notes = np.zeros((max(count * each, 2 * kv_local * HEAD_DIM), 4), np.float32)
    block, local, side, entry = np.indices((count, kv_local, 2, depth)).reshape(4, -1)
    notes[: count * each, 0] = side * key_cols + entry * KV_HEADS + local
    notes[: count * each, 1] = block
    side, local, source, entry = np.indices((2, kv_local, count, depth)).reshape(4, -1)
    notes[: 2 * kv_local * HEAD_DIM, 2] = (local * 2 + side) * depth + entry
    notes[: 2 * kv_local * HEAD_DIM, 3] = source
    pick_rows, in_order, columns, unmix, positions = kernel_call(
        functools.partial(
            map_body, tall, wide, tokens, lambda peer: lax.div(peer * local_heads, group_size)
        ),
        [
            ((total, count * capacity), bf16),
            ((total, total), bf16),
            ((count * each, 2 * key_cols), bf16),
            ((2 * kv_local * HEAD_DIM, count * each), bf16),
            ((total, 1), f32),
        ],
        [me, routed, balance, notes],
        specs=[scalar, VMEM, VMEM, VMEM],
    )

    half = HEAD_DIM // 2
    steps_f = jnp.arange(half, dtype=f32)
    freqs = jnp.exp(-jnp.log(f32(rope_base)) * (2.0 * steps_f / HEAD_DIM))
    q_angles = positions * freqs[None, :]
    q_cos, q_sin = jnp.cos(q_angles), jnp.sin(q_angles)
    q_cos = jnp.concatenate([q_cos, q_cos], axis=1)
    q_sin = jnp.concatenate([-q_sin, q_sin], axis=1)
    k_angles = freqs[:, None] * routed.astype(f32)
    k_cos, k_sin = jnp.cos(k_angles), jnp.sin(k_angles)

    normed, own, *sent = kernel_call(
        functools.partial(kv_body, count),
        [((total, model), bf16), ((share, model), bf16)] + [((each, total), bf16)] * count,
        [*blocks, pick_rows, in_order, columns, attn_gain, w_key, w_value, *loaded],
        [pltpu.VMEM((total, model), bf16)],
        flops=2 * total * model * 512,
    )
    arrived = [
        part if r == 0 else shift(part, tall, wide, *divmod(r, wide)) for r, part in enumerate(sent)
    ]
    (query,) = kernel_call(
        query_body,
        [((total, local_heads * HEAD_DIM), bf16)],
        [normed, w_query, q_cos, q_sin],
        flops=2 * total * model * local_heads * HEAD_DIM,
    )
    part_shapes = sum_shapes(tall, wide, share, model)
    attn_parts = kernel_call(
        functools.partial(attend_body, plane, kv_local),
        part_shapes,
        [*arrived, query, unmix, k_cos, k_sin, routed, positions, w_output],
        [pltpu.VMEM((total, local_heads * HEAD_DIM), bf16)],
        flops=2 * total * model * local_heads * HEAD_DIM,
    )
    attn_own = scatter_sum(attn_parts, tall, wide)
    own_rows = own.astype(f32)
    hidden = own_rows + attn_own
    mean_sq = jnp.mean(hidden * hidden, axis=-1, keepdims=True)
    mnorm = (hidden * lax.rsqrt(mean_sq + norm_eps) * mlp_gain).astype(bf16)
    pieces = gather_blocks(mnorm, tall, wide)
    hidden_units = w_gate.shape[1]
    mlp_parts = kernel_call(
        functools.partial(mlp_body, plane),
        part_shapes,
        [*pieces, w_gate, w_up, w_down],
        [pltpu.VMEM((total, model), bf16), pltpu.VMEM((total, hidden_units), bf16)],
        flops=6 * total * model * hidden_units,
    )
    mlp_own = scatter_sum(mlp_parts, tall, wide)
    router_score = jnp.sum(own_rows * w_router[None, :], axis=1, keepdims=True)
    return (own_rows + router_score * (attn_own + mlp_own)).astype(bf16)


def solution(mesh):
    in_specs = (
        P(("dp", "ctx"), None),
        P("dp"),
        P("dp"),
        P(None, "ctx"),
        P(None, "ctx"),
        P(None, "ctx"),
        P("ctx", None),
        P(),
        P(),
        P(None, "ctx"),
        P(None, "ctx"),
        P("ctx", None),
        P(),
    )
    out_specs = P(("dp", "ctx"), None)
    return jax.shard_map(
        on_device, mesh=mesh, in_specs=in_specs, out_specs=out_specs, check_vma=False
    )
```

```python
import functools

import jax
import jax.numpy as jnp
import numpy as np
from jax import lax
from jax.experimental import pallas as pl
from jax.experimental.pallas import tpu as pltpu
from jax.sharding import PartitionSpec as P

HEADS = 32
KV_HEADS = 8
HEAD_DIM = 128

rope_base = 500000.0
norm_eps = 1e-05

bf16, f32, i32 = jnp.bfloat16, jnp.float32, jnp.int32
VMEM = pl.BlockSpec(memory_space=pltpu.VMEM)


def plane_of(count):
    wide = max(y for y in range(1, count + 1) if count % y == 0 and 2 * y * y <= max(count, 2))
    return count // wide, wide


def shift(block, tall, wide, dz, dy, keep=None):
    pairs = [
        (z * wide + y, (z + dz) % tall * wide + (y + dy) % wide)
        for z in range(tall)
        for y in range(wide)
        if keep is None or keep(z)
    ]
    return lax.ppermute(block, "ctx", pairs)


def tie_body(count, *refs):
    total = refs[0][...]
    for ref in refs[1:count]:
        total = total + ref[...]
    refs[-1][...] = total


def tie(blocks, tokens):
    return kernel_call(
        functools.partial(tie_body, len(blocks)),
        [(blocks[0].shape, blocks[0].dtype)],
        [*blocks, *tokens],
        specs=[VMEM] * len(blocks) + [pl.BlockSpec(memory_space=pl.ANY)] * len(tokens),
    )[0]


def gather_rows(block, tall, wide, tokens_1, tokens_2):
    blocks = {(0, 0): block}
    for dz in range(1, tall):
        if tall != 4 or dz != 2:
            blocks[dz, 0] = shift(block, tall, wide, dz, 0)
    blocks[1, 0] = tie([blocks[1, 0]], tokens_1)
    if tall == 4:
        up = shift(blocks[1, 0], tall, wide, 1, 0, lambda z: z in (1, 2))
        down = shift(blocks[3, 0], tall, wide, -1, 0, lambda z: z in (1, 2))
        blocks[2, 0] = tie([up, down], tokens_2)
    else:
        blocks[tall - 1, 0] = tie([blocks[tall - 1, 0]], tokens_2)
    for dz in [0, 1, *range(tall - 1, 1, -1)]:
        for dy in range(1, wide):
            blocks[dz, dy] = shift(blocks[dz, 0], tall, wide, 0, dy)
    return [blocks[dz, dy] for dz in range(tall) for dy in range(wide)]


def stack_body(count, *refs):
    share = refs[0].shape[0]
    for index, ref in enumerate(refs[:count]):
        refs[-1][index * share : (index + 1) * share, :] = ref[...]


def gather_half(block, tall, wide, tokens=()):
    mine = [block if dz == 0 else shift(block, tall, wide, dz, 0) for dz in range(tall)]
    share = block.shape[0]
    shape = ((tall * share, block.shape[1]), block.dtype)
    (mine,) = kernel_call(
        functools.partial(stack_body, tall),
        [shape],
        [*mine, *tokens],
        specs=[VMEM] * tall + [pl.BlockSpec(memory_space=pl.ANY)] * len(tokens),
    )
    return [mine] + [shift(mine, tall, wide, 0, dy) for dy in range(1, wide)]


def sum_half(parts, tall, wide):
    share = parts[0].shape[0] // tall
    lanes = parts[0].astype(f32)
    for dy in range(1, wide):
        lanes = lanes + shift(parts[dy], tall, wide, 0, dy).astype(f32)
    total = lanes[:share]
    for dz in [tall // 2, *range(1, tall // 2), *range(tall // 2 + 1, tall)]:
        one = lanes[dz * share : (dz + 1) * share].astype(bf16)
        total = total + shift(one, tall, wide, dz, 0).astype(f32)
    return total


def sum_order(tall):
    order = [tall // 2, *range(1, tall // 2), *range(tall // 2 + 1, tall), 0]
    return order[: tall // 2], order[tall // 2 :]


def sum_shapes(tall, wide, share, model):
    kept = [((share, model), bf16)] * tall
    return kept + [((tall // 2 * share, model), bf16)] * (2 * (wide - 1))


def store_parts(parts, tall, wide, span, product, back):
    share = parts[0].shape[0]
    sign = -1 if back else 1

    def rows(dz, dy):
        at = sign * dz % tall * wide + sign * dy % wide
        return product[at * share : (at + 1) * share, :]

    for dz in range(tall):
        parts[dz][:, span] = rows(dz, 0)
    for dy in range(1, wide):
        for which, group in enumerate(sum_order(tall)):
            out = parts[tall + 2 * (dy - 1) + which]
            for place, dz in enumerate(group):
                out[place * share : (place + 1) * share, span] = rows(dz, dy)


def scatter_sum(parts, tall, wide):
    share = parts[0].shape[0]
    crossed = [shift(p, tall, wide, 0, i // 2 + 1) for i, p in enumerate(parts[tall:])]
    total = None
    for which, group in enumerate(sum_order(tall)):
        for place, dz in enumerate(group):
            lane = parts[dz].astype(f32)
            for dy in range(1, wide):
                other = crossed[2 * (dy - 1) + which]
                lane = lane + other[place * share : (place + 1) * share].astype(f32)
            if dz:
                lane = shift(lane.astype(bf16), tall, wide, dz, 0).astype(f32)
            total = lane if total is None else total + lane
    return total


def dot(a, b):
    return jnp.dot(a, b, preferred_element_type=f32)


def fetched(weight):
    return pltpu.with_memory_space_constraint(weight, pltpu.VMEM)


def kernel_call(body, outs, args, scratch=(), limit=14, flops=0, specs=None):
    return pl.pallas_call(
        body,
        out_shape=[jax.ShapeDtypeStruct(s, d) for s, d in outs],
        in_specs=specs or [VMEM] * len(args),
        out_specs=[VMEM] * len(outs),
        scratch_shapes=list(scratch),
        compiler_params=pltpu.CompilerParams(vmem_limit_bytes=limit << 20),
        cost_estimate=pl.CostEstimate(flops=flops, bytes_accessed=1 << 20, transcendentals=0),
    )(*args)


def load_body(count, *refs):
    sources, copies, sems = refs[1 : 1 + count], refs[1 + count : -2], refs[-1]
    moves = [
        pltpu.make_async_copy(a, b, sems.at[i]) for i, (a, b) in enumerate(zip(sources, copies))
    ]
    for move in moves:
        move.start()
    for move in moves:
        move.wait()
    refs[-2][...] = jnp.zeros_like(refs[-2])


def load(after, *arrays):
    size = sum(a.size * a.dtype.itemsize for a in arrays)
    *copies, token = pl.pallas_call(
        functools.partial(load_body, len(arrays)),
        out_shape=[pltpu.VMEM(a.shape, a.dtype) for a in arrays]
        + [jax.ShapeDtypeStruct((8, 128), f32)],
        in_specs=[pl.BlockSpec(memory_space=pl.ANY)] * (1 + len(arrays)),
        out_specs=[VMEM] * (1 + len(arrays)),
        scratch_shapes=[pltpu.SemaphoreType.DMA((len(arrays),))],
        compiler_params=pltpu.CompilerParams(vmem_limit_bytes=2 << 20),
        cost_estimate=pl.CostEstimate(flops=0, bytes_accessed=2 * size, transcendentals=0),
    )(after, *[pltpu.with_memory_space_constraint(a, pltpu.HBM) for a in arrays])
    return [fetched(c) for c in copies] + [token]


def tile_of(width, most):
    return width if width <= most else most


def iota(shape, axis):
    return lax.broadcasted_iota(i32, shape, axis).astype(f32)


def pick(onehot, values):
    return dot(onehot, values).astype(values.dtype)


def send_body(me, routed, activations, outgoing):
    capacity, tokens, total = outgoing.shape[0], activations.shape[0], routed.shape[1]
    low = (me[0] * tokens).astype(f32)
    where = routed[...].astype(f32)
    first = jnp.sum(jnp.where(where < low, 1.0, 0.0), axis=1, keepdims=True)
    here = (where >= low) & (where < low + tokens)
    slot = jnp.where(here, iota((1, total), 1) - first, -1.0)
    hit = slot == iota((capacity, total), 0)
    token = jnp.sum(jnp.where(hit, where - low + 1.0, 0.0), axis=1, keepdims=True) - 1.0
    onehot = jnp.where(token == iota((capacity, tokens), 1), 1.0, 0.0).astype(bf16)
    width = activations.shape[1]
    tile = tile_of(width, 1024)
    for start in range(0, width, tile):
        span = slice(start, start + tile)
        outgoing[:, span] = pick(onehot, activations[:, span])


def map_body(tall, wide, tokens, heads_of, me, routed, balance, notes, *outs):
    pick_rows, in_order, columns, unmix, positions = outs
    count, total = tall * wide, routed.shape[1]
    share, capacity = total // count, pick_rows.shape[1] // count
    outbound, inbound = columns.shape[0], unmix.shape[0]
    my_z, my_y = lax.div(me[0], wide), lax.rem(me[0], wide)
    where, owner = routed[...].astype(f32), balance[...].astype(f32)
    lane = iota((1, total), 1)
    slot, place = jnp.zeros((1, total), f32), jnp.zeros((1, total), f32)
    out_base, out_block = notes[:outbound, 0:1], notes[:outbound, 1:2]
    in_base, in_source = notes[:inbound, 2:3], notes[:inbound, 3:4]
    for s in range(count):
        z, y = divmod(s, wide)
        from_block = lax.rem(my_z - z + tall, tall) * wide + lax.rem(my_y - y + wide, wide)
        to_block = lax.rem(z - my_z + tall, tall) * wide + lax.rem(y - my_y + wide, wide)
        peer = lax.rem(my_z + z, tall) * wide + lax.rem(my_y + y, wide)
        before = where < s * tokens
        first = jnp.sum(jnp.where(before, 1.0, 0.0), axis=1, keepdims=True)
        inside = (where < (s + 1) * tokens) & jnp.logical_not(before)
        start = (from_block * capacity).astype(f32)
        slot += jnp.where(inside, lane - first + start, 0.0)
        place += jnp.where(owner == s, (to_block * share).astype(f32), 0.0)
        out_base += jnp.where(out_block == s, heads_of(peer).astype(f32), 0.0)
        in_base += jnp.where(in_source == s, (from_block * (outbound // count)).astype(f32), 0.0)
    mine = owner == iota((count, total), 0)
    earlier = jnp.where(iota((total, total), 0) < iota((total, total), 1), 1.0, 0.0)
    rank = dot(jnp.where(mine, 1.0, 0.0).astype(bf16), earlier.astype(bf16))
    place += jnp.sum(jnp.where(mine, rank, 0.0), axis=0, keepdims=True)
    placed = place == iota((total, total), 0)
    in_order[...] = jnp.where(placed, 1.0, 0.0).astype(bf16)
    positions[...] = jnp.sum(jnp.where(placed, where, 0.0), axis=1, keepdims=True)
    slot_at = jnp.sum(jnp.where(placed, slot, 0.0), axis=1, keepdims=True)
    pick_rows[...] = jnp.where(slot_at == iota(pick_rows.shape, 1), 1.0, 0.0).astype(bf16)
    columns[...] = jnp.where(out_base == iota(columns.shape, 1), 1.0, 0.0).astype(bf16)
    unmix[...] = jnp.where(in_base == iota(unmix.shape, 1), 1.0, 0.0).astype(bf16)


def kv_body(count, *refs):
    blocks = refs[:count]
    pick_rows, order, columns, gain, w_key, w_value = refs[count : count + 6]
    (normed, own, *sent), rows = refs[-3 - count : -1], refs[-1]
    total, width = normed.shape
    tile = tile_of(width, 512)
    square = jnp.zeros((total, 1), f32)
    for start in range(0, width, tile):
        span = slice(start, start + tile)
        part = dot(pick_rows[...], jnp.concatenate([b[:, span] for b in blocks], axis=0))
        rows[:, span] = part.astype(bf16)
        square += jnp.sum(part * part, axis=1, keepdims=True)
    own[...] = rows[: own.shape[0], :]
    factor = lax.rsqrt(square / width + norm_eps)
    for start in range(0, width, tile):
        span = slice(start, start + tile)
        part = rows[:, span].astype(f32) * factor * gain[:, span]
        normed[:, span] = part.astype(bf16)
    keys = dot(normed[...], w_key[...]).astype(bf16)
    values = dot(normed[...], w_value[...]).astype(bf16)
    both = jnp.concatenate([keys, values], axis=1)
    turned = lax.dot_general(
        columns[...], both, (((1,), (1,)), ((), ())), preferred_element_type=f32
    ).astype(bf16)
    turned = dot(turned, order[...])
    each = turned.shape[0] // len(sent)
    for index, part in enumerate(sent):
        part[...] = turned[index * each : (index + 1) * each, :].astype(bf16)


def query_body(normed, w_query, cosine, sine, query):
    raw = dot(normed[...], w_query[...])
    for head in range(query.shape[1] // HEAD_DIM):
        span = slice(head * HEAD_DIM, (head + 1) * HEAD_DIM)
        one = raw[:, span]
        turned = one * cosine[...] + pltpu.roll(one, HEAD_DIM // 2, 1) * sine[...]
        query[:, span] = turned.astype(bf16)


def attend_body(plane, kv_local, *refs):
    count = plane[0] * plane[1]
    arrived, rest = refs[:count], refs[count:]
    query, unmix, cosine, sine, key_pos, query_pos, w_output = rest[:7]
    parts, heads_out = rest[7:-1], rest[-1]
    half = HEAD_DIM // 2
    heads = query.shape[1] // HEAD_DIM
    mixed = jnp.concatenate([a[...].astype(f32) for a in arrived], axis=0).astype(bf16)
    both = dot(unmix[...], mixed)
    allowed = key_pos[...].astype(f32) <= query_pos[...]
    for group in range(kv_local):
        base = group * HEAD_DIM
        first, second = both[base : base + half], both[base + half : base + HEAD_DIM]
        keys = jnp.concatenate(
            [first * cosine[...] - second * sine[...], second * cosine[...] + first * sine[...]],
            axis=0,
        ).astype(bf16)
        base += kv_local * HEAD_DIM
        values = both[base : base + HEAD_DIM].astype(bf16)
        for head in range(group * heads // kv_local, (group + 1) * heads // kv_local):
            span = slice(head * HEAD_DIM, (head + 1) * HEAD_DIM)
            scores = dot(query[:, span], keys) * HEAD_DIM ** (-0.5)
            scores = jnp.where(allowed, scores, -1e30)
            weights = jnp.exp(scores - jnp.max(scores, axis=1, keepdims=True))
            probs = (weights / jnp.sum(weights, axis=1, keepdims=True)).astype(bf16)
            heads_out[:, span] = lax.dot_general(
                probs, values, (((1,), (1,)), ((), ())), preferred_element_type=f32
            ).astype(bf16)
    tall, wide = plane
    width = w_output.shape[1]
    tile = tile_of(width // 2, 512)
    share = parts[0].shape[0] // tall
    for start in range(0, width, tile):
        product = dot(heads_out[...], w_output[:, start : start + tile]).astype(bf16)
        which, local = divmod(start, width // 2)
        for dy in range(wide):
            for dz in range(tall):
                block = product[(dz * wide + dy) * share : (dz * wide + dy + 1) * share, :]
                part = parts[which * wide + dy]
                part[dz * share : (dz + 1) * share, local : local + tile] = block


def scale_body(hidden_1, hidden_2, gain, out):
    width = hidden_2.shape[1]
    square = jnp.sum(hidden_1[...] * hidden_1[...], axis=1, keepdims=True)
    square += jnp.sum(hidden_2[...] * hidden_2[...], axis=1, keepdims=True)
    factor = lax.rsqrt(square / (2 * width) + norm_eps)
    high = factor.astype(bf16).astype(f32)
    out[:, :width] = (hidden_2[...] * gain[...]).astype(bf16)
    lane = lax.broadcasted_iota(i32, (out.shape[0], 128), 1)
    out[:, width:] = jnp.where(lane < 64, high, factor - high).astype(bf16)


def half_body(plane, *refs):
    tall, wide = plane
    blocks, (w_gate, w_up, gate, upward, piece) = refs[:wide], refs[wide:]
    fill(blocks, piece, tall, wide)
    depth, width = piece.shape[1], w_gate.shape[1]
    tile = tile_of(width, 256)
    for start in range(0, width, tile):
        span = slice(start, start + tile)
        gate[:, span] = dot(piece[...], w_gate[:depth, span])
        upward[:, span] = dot(piece[...], w_up[:depth, span])


def fill(blocks, piece, tall, wide):
    share = blocks[0].shape[0] // tall
    for dz in range(tall):
        for dy in range(wide):
            at = (dz * wide + dy) * share
            piece[at : at + share, :] = blocks[dy][dz * share : (dz + 1) * share, :]


def mlp_body(plane, *refs):
    tall, wide = plane
    blocks, (gate_1, up_1, w_gate, w_up, w_down) = refs[:wide], refs[wide : wide + 5]
    parts, (piece, inner) = refs[wide + 5 : -2], refs[-2:]
    fill(blocks, piece, tall, wide)
    depth, width = w_gate.shape[0] // 2, w_gate.shape[1]
    factor = piece[:, depth : depth + 1].astype(f32) + piece[:, depth + 64 : depth + 65].astype(f32)
    tile = tile_of(width, 256)
    for start in range(0, width, tile):
        span = slice(start, start + tile)
        gate = (gate_1[:, span] + dot(piece[:, :depth], w_gate[depth:, span])) * factor
        upward = (up_1[:, span] + dot(piece[:, :depth], w_up[depth:, span])) * factor
        inner[:, span] = (gate / (1.0 + jnp.exp(-gate)) * upward).astype(bf16)
    width = w_down.shape[1]
    tile = tile_of(width, 512)
    for start in range(0, width, tile):
        span = slice(start, start + tile)
        product = dot(inner[...], w_down[:, span]).astype(bf16)
        store_parts(parts, *plane, span, product, True)


def on_device(
    activations,
    routed,
    balance,
    w_query,
    w_key,
    w_value,
    w_output,
    attn_gain,
    mlp_gain,
    w_gate,
    w_up,
    w_down,
    w_router,
):
    count = lax.axis_size("ctx")
    plane = tall, wide = plane_of(count)
    me = lax.axis_index("ctx").astype(i32).reshape(1)
    tokens, model = activations.shape
    total = routed.shape[0]
    share = total // count
    capacity = 2 * share
    local_heads = w_query.shape[1] // HEAD_DIM
    group_size = HEADS // KV_HEADS
    kv_local = max(1, local_heads // group_size)
    key_cols = w_key.shape[1]
    depth = key_cols // KV_HEADS
    scalar = pl.BlockSpec(memory_space=pltpu.SMEM)
    routed, balance = routed.reshape(1, total), balance.reshape(1, total)

    (outgoing,) = kernel_call(
        send_body,
        [((capacity, model), bf16)],
        [me, routed, activations],
        specs=[scalar, VMEM, VMEM],
        flops=2 * capacity * tokens * model,
    )
    attn_gain, w_key, w_value, w_query, token_1 = load(
        outgoing, attn_gain.reshape(1, model), w_key, w_value, w_query
    )
    w_gate, token_2 = load(outgoing, w_gate)
    w_output, token_3 = load(token_2, w_output)
    w_up, token_4 = load(token_3, w_up)

    each = kv_local * 2 * depth
    notes = np.zeros((max(count * each, 2 * kv_local * HEAD_DIM), 4), np.float32)
    block, local, side, entry = np.indices((count, kv_local, 2, depth)).reshape(4, -1)
    notes[: count * each, 0] = side * key_cols + entry * KV_HEADS + local
    notes[: count * each, 1] = block
    side, local, source, entry = np.indices((2, kv_local, count, depth)).reshape(4, -1)
    notes[: 2 * kv_local * HEAD_DIM, 2] = (local * 2 + side) * depth + entry
    notes[: 2 * kv_local * HEAD_DIM, 3] = source
    pick_rows, in_order, columns, unmix, positions = kernel_call(
        functools.partial(
            map_body, tall, wide, tokens, lambda peer: lax.div(peer * local_heads, group_size)
        ),
        [
            ((total, count * capacity), bf16),
            ((total, total), bf16),
            ((count * each, 2 * key_cols), bf16),
            ((2 * kv_local * HEAD_DIM, count * each), bf16),
            ((total, 1), f32),
        ],
        [me, routed, balance, notes],
        specs=[scalar, VMEM, VMEM, VMEM],
    )
    blocks = gather_rows(outgoing, tall, wide, [token_1, token_2, positions], [token_3, token_4])

    half = HEAD_DIM // 2
    steps_f = jnp.arange(half, dtype=f32)
    freqs = jnp.exp(-jnp.log(f32(rope_base)) * (2.0 * steps_f / HEAD_DIM))
    q_angles = positions * freqs[None, :]
    q_cos, q_sin = jnp.cos(q_angles), jnp.sin(q_angles)
    q_cos = jnp.concatenate([q_cos, q_cos], axis=1)
    q_sin = jnp.concatenate([-q_sin, q_sin], axis=1)
    k_angles = freqs[:, None] * routed.astype(f32)
    k_cos, k_sin = jnp.cos(k_angles), jnp.sin(k_angles)

    normed, own, *sent = kernel_call(
        functools.partial(kv_body, count),
        [((total, model), bf16), ((share, model), bf16)] + [((each, total), bf16)] * count,
        [*blocks, pick_rows, in_order, columns, attn_gain, w_key, w_value],
        [pltpu.VMEM((total, model), bf16)],
        flops=2 * total * model * 512,
    )
    arrived = [
        part if r == 0 else shift(part, tall, wide, *divmod(r, wide)) for r, part in enumerate(sent)
    ]
    (query,) = kernel_call(
        query_body,
        [((total, local_heads * HEAD_DIM), bf16)],
        [normed, w_query, q_cos, q_sin],
        flops=2 * total * model * local_heads * HEAD_DIM,
    )
    half_width = model // 2
    parts = kernel_call(
        functools.partial(attend_body, plane, kv_local),
        [((tall * share, half_width), bf16)] * (2 * wide),
        [*arrived, query, unmix, k_cos, k_sin, routed, positions, w_output],
        [pltpu.VMEM((total, local_heads * HEAD_DIM), bf16)],
        flops=2 * total * model * local_heads * HEAD_DIM,
    )
    w_down, token_5 = load(parts[0], w_down)
    own_rows = own.astype(f32)
    attn_1 = sum_half(parts[:wide], tall, wide)
    hidden_1 = own_rows[:, :half_width] + attn_1
    scaled_1 = (hidden_1 * mlp_gain[:half_width]).astype(bf16)
    pieces_1 = gather_half(scaled_1, tall, wide, [token_5])
    attn_2 = sum_half(parts[wide:], tall, wide)
    hidden_2 = own_rows[:, half_width:] + attn_2
    (scaled_2,) = kernel_call(
        scale_body,
        [((share, half_width + 128), bf16)],
        [hidden_1, hidden_2, mlp_gain[half_width:].reshape(1, half_width)],
    )
    pieces_2 = gather_half(scaled_2, tall, wide)
    hidden_units = w_gate.shape[1]
    gate_1, up_1 = kernel_call(
        functools.partial(half_body, plane),
        [((total, hidden_units), f32)] * 2,
        [*pieces_1, w_gate, w_up],
        [pltpu.VMEM((total, half_width), bf16)],
        flops=2 * total * model * hidden_units,
    )
    mlp_parts = kernel_call(
        functools.partial(mlp_body, plane),
        sum_shapes(tall, wide, share, model),
        [*pieces_2, gate_1, up_1, w_gate, w_up, w_down],
        [pltpu.VMEM((total, half_width + 128), bf16), pltpu.VMEM((total, hidden_units), bf16)],
        flops=4 * total * model * hidden_units,
    )
    attn_own = jnp.concatenate([attn_1, attn_2], axis=1)
    mlp_own = scatter_sum(mlp_parts, tall, wide)
    router_score = jnp.sum(own_rows * w_router[None, :], axis=1, keepdims=True)
    return (own_rows + router_score * (attn_own + mlp_own)).astype(bf16)


def solution(mesh):
    in_specs = (
        P(("dp", "ctx"), None),
        P("dp"),
        P("dp"),
        P(None, "ctx"),
        P(None, "ctx"),
        P(None, "ctx"),
        P("ctx", None),
        P(),
        P(),
        P(None, "ctx"),
        P(None, "ctx"),
        P("ctx", None),
        P(),
    )
    out_specs = P(("dp", "ctx"), None)
    return jax.shard_map(
        on_device, mesh=mesh, in_specs=in_specs, out_specs=out_specs, check_vma=False
    )
```

```python
import functools

import jax
import jax.numpy as jnp
import numpy as np
from jax import lax
from jax.experimental import pallas as pl
from jax.experimental.pallas import tpu as pltpu
from jax.sharding import PartitionSpec as P

HEADS = 32
KV_HEADS = 8
HEAD_DIM = 128

rope_base = 500000.0
norm_eps = 1e-05

bf16, f32, i32 = jnp.bfloat16, jnp.float32, jnp.int32
VMEM = pl.BlockSpec(memory_space=pltpu.VMEM)


def plane_of(count):
    wide = max(y for y in range(1, count + 1) if count % y == 0 and 2 * y * y <= max(count, 2))
    return count // wide, wide


def shift(block, tall, wide, dz, dy, keep=None):
    pairs = [
        (z * wide + y, (z + dz) % tall * wide + (y + dy) % wide)
        for z in range(tall)
        for y in range(wide)
        if keep is None or keep(z)
    ]
    return lax.ppermute(block, "ctx", pairs)


def tie_body(count, *refs):
    total = refs[0][...]
    for ref in refs[1:count]:
        total = total + ref[...]
    refs[-1][...] = total


def tie(blocks, tokens):
    return kernel_call(
        functools.partial(tie_body, len(blocks)),
        [(blocks[0].shape, blocks[0].dtype)],
        [*blocks, *tokens],
        specs=[VMEM] * len(blocks) + [pl.BlockSpec(memory_space=pl.ANY)] * len(tokens),
    )[0]


def gather_rows(block, tall, wide, tokens_1, tokens_2):
    blocks = {(0, 0): block}
    for dz in range(1, tall):
        if tall != 4 or dz != 2:
            blocks[dz, 0] = shift(block, tall, wide, dz, 0)
    blocks[1, 0] = tie([blocks[1, 0]], tokens_1)
    if tall == 4:
        up = shift(blocks[1, 0], tall, wide, 1, 0, lambda z: z in (1, 2))
        down = shift(blocks[3, 0], tall, wide, -1, 0, lambda z: z in (1, 2))
        blocks[2, 0] = tie([up, down], tokens_2)
    else:
        blocks[tall - 1, 0] = tie([blocks[tall - 1, 0]], tokens_2)
    for dz in [0, 1, *range(tall - 1, 1, -1)]:
        for dy in range(1, wide):
            blocks[dz, dy] = shift(blocks[dz, 0], tall, wide, 0, dy)
    return [blocks[dz, dy] for dz in range(tall) for dy in range(wide)]


def gather_blocks(block, tall, wide):
    blocks = {(dz, 0): shift(block, tall, wide, dz, 0) if dz else block for dz in range(tall)}
    for dz in range(tall):
        for dy in range(1, wide):
            blocks[dz, dy] = shift(blocks[dz, 0], tall, wide, 0, dy)
    return [blocks[dz, dy] for dz in range(tall) for dy in range(wide)]


def sum_order(tall):
    order = [tall // 2, *range(1, tall // 2), *range(tall // 2 + 1, tall), 0]
    return order[: tall // 2], order[tall // 2 :]


def sum_shapes(tall, wide, share, model):
    kept = [((share, model), bf16)] * tall
    return kept + [((tall // 2 * share, model), bf16)] * (2 * (wide - 1))


def store_parts(parts, tall, wide, span, product, back):
    share = parts[0].shape[0]
    sign = -1 if back else 1

    def rows(dz, dy):
        at = sign * dz % tall * wide + sign * dy % wide
        return product[at * share : (at + 1) * share, :]

    for dz in range(tall):
        parts[dz][:, span] = rows(dz, 0)
    for dy in range(1, wide):
        for which, group in enumerate(sum_order(tall)):
            out = parts[tall + 2 * (dy - 1) + which]
            for place, dz in enumerate(group):
                out[place * share : (place + 1) * share, span] = rows(dz, dy)


def scatter_sum(parts, tall, wide, tokens=()):
    share = parts[0].shape[0]
    crossed = [shift(p, tall, wide, 0, i // 2 + 1) for i, p in enumerate(parts[tall:])]
    if tokens:
        crossed[1] = tie([crossed[1]], tokens)
    total = None
    for which, group in enumerate(sum_order(tall)):
        for place, dz in enumerate(group):
            lane = parts[dz].astype(f32)
            for dy in range(1, wide):
                other = crossed[2 * (dy - 1) + which]
                lane = lane + other[place * share : (place + 1) * share].astype(f32)
            if dz:
                lane = shift(lane.astype(bf16), tall, wide, dz, 0).astype(f32)
            total = lane if total is None else total + lane
    return total


def dot(a, b):
    return jnp.dot(a, b, preferred_element_type=f32)


def fetched(weight):
    return pltpu.with_memory_space_constraint(weight, pltpu.VMEM)


def kernel_call(body, outs, args, scratch=(), limit=14, flops=0, specs=None):
    return pl.pallas_call(
        body,
        out_shape=[jax.ShapeDtypeStruct(s, d) for s, d in outs],
        in_specs=specs or [VMEM] * len(args),
        out_specs=[VMEM] * len(outs),
        scratch_shapes=list(scratch),
        compiler_params=pltpu.CompilerParams(vmem_limit_bytes=limit << 20),
        cost_estimate=pl.CostEstimate(flops=flops, bytes_accessed=1 << 20, transcendentals=0),
    )(*args)


def load_body(count, *refs):
    sources, copies, sems = refs[1 : 1 + count], refs[1 + count : -2], refs[-1]
    moves = [
        pltpu.make_async_copy(a, b, sems.at[i]) for i, (a, b) in enumerate(zip(sources, copies))
    ]
    for move in moves:
        move.start()
    for move in moves:
        move.wait()
    refs[-2][...] = jnp.zeros_like(refs[-2])


def load(after, *arrays):
    size = sum(a.size * a.dtype.itemsize for a in arrays)
    *copies, token = pl.pallas_call(
        functools.partial(load_body, len(arrays)),
        out_shape=[pltpu.VMEM(a.shape, a.dtype) for a in arrays]
        + [jax.ShapeDtypeStruct((8, 128), f32)],
        in_specs=[pl.BlockSpec(memory_space=pl.ANY)] * (1 + len(arrays)),
        out_specs=[VMEM] * (1 + len(arrays)),
        scratch_shapes=[pltpu.SemaphoreType.DMA((len(arrays),))],
        compiler_params=pltpu.CompilerParams(vmem_limit_bytes=2 << 20),
        cost_estimate=pl.CostEstimate(flops=0, bytes_accessed=2 * size, transcendentals=0),
    )(after, *[pltpu.with_memory_space_constraint(a, pltpu.HBM) for a in arrays])
    return [fetched(c) for c in copies] + [token]


def tile_of(width, most):
    return width if width <= most else most


def iota(shape, axis):
    return lax.broadcasted_iota(i32, shape, axis).astype(f32)


def pick(onehot, values):
    return dot(onehot, values).astype(values.dtype)


def send_body(me, routed, activations, outgoing):
    capacity, tokens, total = outgoing.shape[0], activations.shape[0], routed.shape[1]
    low = (me[0] * tokens).astype(f32)
    where = routed[...].astype(f32)
    first = jnp.sum(jnp.where(where < low, 1.0, 0.0), axis=1, keepdims=True)
    here = (where >= low) & (where < low + tokens)
    slot = jnp.where(here, iota((1, total), 1) - first, -1.0)
    hit = slot == iota((capacity, total), 0)
    token = jnp.sum(jnp.where(hit, where - low + 1.0, 0.0), axis=1, keepdims=True) - 1.0
    onehot = jnp.where(token == iota((capacity, tokens), 1), 1.0, 0.0).astype(bf16)
    width = activations.shape[1]
    tile = tile_of(width, 1024)
    for start in range(0, width, tile):
        span = slice(start, start + tile)
        outgoing[:, span] = pick(onehot, activations[:, span])


def map_body(tall, wide, tokens, heads_of, me, routed, balance, notes, *outs):
    pick_rows, in_order, columns, unmix, positions = outs
    count, total = tall * wide, routed.shape[1]
    share, capacity = total // count, pick_rows.shape[1] // count
    outbound, inbound = columns.shape[0], unmix.shape[0]
    my_z, my_y = lax.div(me[0], wide), lax.rem(me[0], wide)
    where, owner = routed[...].astype(f32), balance[...].astype(f32)
    lane = iota((1, total), 1)
    slot, place = jnp.zeros((1, total), f32), jnp.zeros((1, total), f32)
    out_base, out_block = notes[:outbound, 0:1], notes[:outbound, 1:2]
    in_base, in_source = notes[:inbound, 2:3], notes[:inbound, 3:4]
    for s in range(count):
        z, y = divmod(s, wide)
        from_block = lax.rem(my_z - z + tall, tall) * wide + lax.rem(my_y - y + wide, wide)
        to_block = lax.rem(z - my_z + tall, tall) * wide + lax.rem(y - my_y + wide, wide)
        peer = lax.rem(my_z + z, tall) * wide + lax.rem(my_y + y, wide)
        before = where < s * tokens
        first = jnp.sum(jnp.where(before, 1.0, 0.0), axis=1, keepdims=True)
        inside = (where < (s + 1) * tokens) & jnp.logical_not(before)
        start = (from_block * capacity).astype(f32)
        slot += jnp.where(inside, lane - first + start, 0.0)
        place += jnp.where(owner == s, (to_block * share).astype(f32), 0.0)
        out_base += jnp.where(out_block == s, heads_of(peer).astype(f32), 0.0)
        in_base += jnp.where(in_source == s, (from_block * (outbound // count)).astype(f32), 0.0)
    mine = owner == iota((count, total), 0)
    earlier = jnp.where(iota((total, total), 0) < iota((total, total), 1), 1.0, 0.0)
    rank = dot(jnp.where(mine, 1.0, 0.0).astype(bf16), earlier.astype(bf16))
    place += jnp.sum(jnp.where(mine, rank, 0.0), axis=0, keepdims=True)
    placed = place == iota((total, total), 0)
    in_order[...] = jnp.where(placed, 1.0, 0.0).astype(bf16)
    at = jnp.sum(jnp.where(placed, where, 0.0), axis=1, keepdims=True)
    positions[...] = jnp.broadcast_to(at, positions.shape)
    slot_at = jnp.sum(jnp.where(placed, slot, 0.0), axis=1, keepdims=True)
    pick_rows[...] = jnp.where(slot_at == iota(pick_rows.shape, 1), 1.0, 0.0).astype(bf16)
    columns[...] = jnp.where(out_base == iota(columns.shape, 1), 1.0, 0.0).astype(bf16)
    unmix[...] = jnp.where(in_base == iota(unmix.shape, 1), 1.0, 0.0).astype(bf16)


def kv_body(count, *refs):
    blocks = refs[:count]
    pick_rows, order, columns, gain, w_key, w_value = refs[count : count + 6]
    (normed, own, *sent), rows = refs[-3 - count : -1], refs[-1]
    total, width = normed.shape
    tile = tile_of(width, 512)
    square = jnp.zeros((total, 1), f32)
    for start in range(0, width, tile):
        span = slice(start, start + tile)
        part = dot(pick_rows[...], jnp.concatenate([b[:, span] for b in blocks], axis=0))
        rows[:, span] = part.astype(bf16)
        square += jnp.sum(part * part, axis=1, keepdims=True)
    own[...] = rows[: own.shape[0], :]
    factor = lax.rsqrt(square / width + norm_eps)
    for start in range(0, width, tile):
        span = slice(start, start + tile)
        part = rows[:, span].astype(f32) * factor * gain[:, span]
        normed[:, span] = part.astype(bf16)
    keys = dot(normed[...], w_key[...]).astype(bf16)
    values = dot(normed[...], w_value[...]).astype(bf16)
    both = jnp.concatenate([keys, values], axis=1)
    turned = lax.dot_general(
        columns[...], both, (((1,), (1,)), ((), ())), preferred_element_type=f32
    ).astype(bf16)
    turned = dot(turned, order[...])
    each = turned.shape[0] // len(sent)
    for index, part in enumerate(sent):
        part[...] = turned[index * each : (index + 1) * each, :].astype(bf16)


def query_body(normed, w_query, cosine, sine, query):
    raw = dot(normed[...], w_query[...])
    for head in range(query.shape[1] // HEAD_DIM):
        span = slice(head * HEAD_DIM, (head + 1) * HEAD_DIM)
        one = raw[:, span]
        turned = one * cosine[...] + pltpu.roll(one, HEAD_DIM // 2, 1) * sine[...]
        query[:, span] = turned.astype(bf16)


def attend_body(plane, kv_local, *refs):
    count = plane[0] * plane[1]
    arrived, rest = refs[:count], refs[count:]
    query, unmix, cosine, sine, key_pos, query_pos, w_output = rest[:7]
    parts, heads_out = rest[7:-1], rest[-1]
    half = HEAD_DIM // 2
    heads = query.shape[1] // HEAD_DIM
    mixed = jnp.concatenate([a[...].astype(f32) for a in arrived], axis=0).astype(bf16)
    both = dot(unmix[...], mixed)
    allowed = key_pos[...].astype(f32) <= query_pos[:, 0:1]
    for group in range(kv_local):
        base = group * HEAD_DIM
        first, second = both[base : base + half], both[base + half : base + HEAD_DIM]
        keys = jnp.concatenate(
            [first * cosine[...] - second * sine[...], second * cosine[...] + first * sine[...]],
            axis=0,
        ).astype(bf16)
        base += kv_local * HEAD_DIM
        values = both[base : base + HEAD_DIM].astype(bf16)
        for head in range(group * heads // kv_local, (group + 1) * heads // kv_local):
            span = slice(head * HEAD_DIM, (head + 1) * HEAD_DIM)
            scores = dot(query[:, span], keys) * HEAD_DIM ** (-0.5)
            scores = jnp.where(allowed, scores, -1e30)
            weights = jnp.exp(scores - jnp.max(scores, axis=1, keepdims=True))
            probs = (weights / jnp.sum(weights, axis=1, keepdims=True)).astype(bf16)
            heads_out[:, span] = lax.dot_general(
                probs, values, (((1,), (1,)), ((), ())), preferred_element_type=f32
            ).astype(bf16)
    spread(heads_out, w_output, parts, plane, False)


def spread(left, weight, parts, plane, back):
    width = weight.shape[1]
    tile = tile_of(width, 512)
    for start in range(0, width, tile):
        span = slice(start, start + tile)
        product = dot(left[...], weight[:, span]).astype(bf16)
        store_parts(parts, *plane, span, product, back)


def mlp_body(plane, *refs):
    count = plane[0] * plane[1]
    blocks, (w_gate, w_up, w_down) = refs[:count], refs[count : count + 3]
    parts, (piece, inner) = refs[count + 3 : -2], refs[-2:]
    share = blocks[0].shape[0]
    for index, block in enumerate(blocks):
        piece[index * share : (index + 1) * share, :] = block[...]
    width = w_gate.shape[1]
    tile = tile_of(width, 256)
    for start in range(0, width, tile):
        span = slice(start, start + tile)
        gate = dot(piece[...], w_gate[:, span])
        upward = dot(piece[...], w_up[:, span])
        inner[:, span] = (gate / (1.0 + jnp.exp(-gate)) * upward).astype(bf16)
    spread(inner, w_down, parts, plane, True)


def on_device(
    activations,
    routed,
    balance,
    w_query,
    w_key,
    w_value,
    w_output,
    attn_gain,
    mlp_gain,
    w_gate,
    w_up,
    w_down,
    w_router,
):
    count = lax.axis_size("ctx")
    plane = tall, wide = plane_of(count)
    me = lax.axis_index("ctx").astype(i32).reshape(1)
    tokens, model = activations.shape
    total = routed.shape[0]
    share = total // count
    capacity = 2 * share
    local_heads = w_query.shape[1] // HEAD_DIM
    group_size = HEADS // KV_HEADS
    kv_local = max(1, local_heads // group_size)
    key_cols = w_key.shape[1]
    depth = key_cols // KV_HEADS
    scalar = pl.BlockSpec(memory_space=pltpu.SMEM)
    routed, balance = routed.reshape(1, total), balance.reshape(1, total)

    (outgoing,) = kernel_call(
        send_body,
        [((capacity, model), bf16)],
        [me, routed, activations],
        specs=[scalar, VMEM, VMEM],
        flops=2 * capacity * tokens * model,
    )
    attn_gain, w_key, w_value, w_query, token_1 = load(
        outgoing, attn_gain.reshape(1, model), w_key, w_value, w_query
    )
    w_gate, token_2 = load(outgoing, w_gate)
    w_output, token_3 = load(token_2, w_output)
    w_up, token_4 = load(token_3, w_up)

    each = kv_local * 2 * depth
    notes = np.zeros((max(count * each, 2 * kv_local * HEAD_DIM), 4), np.float32)
    block, local, side, entry = np.indices((count, kv_local, 2, depth)).reshape(4, -1)
    notes[: count * each, 0] = side * key_cols + entry * KV_HEADS + local
    notes[: count * each, 1] = block
    side, local, source, entry = np.indices((2, kv_local, count, depth)).reshape(4, -1)
    notes[: 2 * kv_local * HEAD_DIM, 2] = (local * 2 + side) * depth + entry
    notes[: 2 * kv_local * HEAD_DIM, 3] = source
    pick_rows, in_order, columns, unmix, positions = kernel_call(
        functools.partial(
            map_body, tall, wide, tokens, lambda peer: lax.div(peer * local_heads, group_size)
        ),
        [
            ((total, count * capacity), bf16),
            ((total, total), bf16),
            ((count * each, 2 * key_cols), bf16),
            ((2 * kv_local * HEAD_DIM, count * each), bf16),
            ((total, HEAD_DIM // 2), f32),
        ],
        [me, routed, balance, notes],
        specs=[scalar, VMEM, VMEM, VMEM],
    )
    blocks = gather_rows(outgoing, tall, wide, [token_1, token_2, positions], [token_3, token_4])

    half = HEAD_DIM // 2
    steps_f = jnp.arange(half, dtype=f32)
    freqs = jnp.exp(-jnp.log(f32(rope_base)) * (2.0 * steps_f / HEAD_DIM))
    q_angles = positions * freqs[None, :]
    q_cos, q_sin = jnp.cos(q_angles), jnp.sin(q_angles)
    q_cos = jnp.concatenate([q_cos, q_cos], axis=1)
    q_sin = jnp.concatenate([-q_sin, q_sin], axis=1)
    k_angles = freqs[:, None] * routed.astype(f32)
    k_cos, k_sin = jnp.cos(k_angles), jnp.sin(k_angles)

    normed, own, *sent = kernel_call(
        functools.partial(kv_body, count),
        [((total, model), bf16), ((share, model), bf16)] + [((each, total), bf16)] * count,
        [*blocks, pick_rows, in_order, columns, attn_gain, w_key, w_value],
        [pltpu.VMEM((total, model), bf16)],
        flops=2 * total * model * 512,
    )
    arrived = [
        part if r == 0 else shift(part, tall, wide, *divmod(r, wide)) for r, part in enumerate(sent)
    ]
    (query,) = kernel_call(
        query_body,
        [((total, local_heads * HEAD_DIM), bf16)],
        [normed, w_query, q_cos, q_sin],
        flops=2 * total * model * local_heads * HEAD_DIM,
    )
    part_shapes = sum_shapes(tall, wide, share, model)
    attn_parts = kernel_call(
        functools.partial(attend_body, plane, kv_local),
        part_shapes,
        [*arrived, query, unmix, k_cos, k_sin, routed, positions, w_output],
        [pltpu.VMEM((total, local_heads * HEAD_DIM), bf16)],
        flops=2 * total * model * local_heads * HEAD_DIM,
    )
    w_down, token_5 = load(attn_parts[0], w_down)
    attn_own = scatter_sum(attn_parts, tall, wide, [token_5])
    own_rows = own.astype(f32)
    hidden = own_rows + attn_own
    mean_sq = jnp.mean(hidden * hidden, axis=-1, keepdims=True)
    mnorm = (hidden * lax.rsqrt(mean_sq + norm_eps) * mlp_gain).astype(bf16)
    pieces = gather_blocks(mnorm, tall, wide)
    hidden_units = w_gate.shape[1]
    mlp_parts = kernel_call(
        functools.partial(mlp_body, plane),
        part_shapes,
        [*pieces, w_gate, w_up, w_down],
        [pltpu.VMEM((total, model), bf16), pltpu.VMEM((total, hidden_units), bf16)],
        flops=6 * total * model * hidden_units,
    )
    mlp_own = scatter_sum(mlp_parts, tall, wide)
    router_score = jnp.sum(own_rows * w_router[None, :], axis=1, keepdims=True)
    return (own_rows + router_score * (attn_own + mlp_own)).astype(bf16)


def solution(mesh):
    in_specs = (
        P(("dp", "ctx"), None),
        P("dp"),
        P("dp"),
        P(None, "ctx"),
        P(None, "ctx"),
        P(None, "ctx"),
        P("ctx", None),
        P(),
        P(),
        P(None, "ctx"),
        P(None, "ctx"),
        P("ctx", None),
        P(),
    )
    out_specs = P(("dp", "ctx"), None)
    return jax.shard_map(
        on_device, mesh=mesh, in_specs=in_specs, out_specs=out_specs, check_vma=False
    )
```

```python
import functools

import jax
import jax.numpy as jnp
import numpy as np
from jax import lax
from jax.experimental import pallas as pl
from jax.experimental.pallas import tpu as pltpu
from jax.sharding import PartitionSpec as P

HEADS = 32
KV_HEADS = 8
HEAD_DIM = 128

rope_base = 500000.0
norm_eps = 1e-05

bf16, f32, i32 = jnp.bfloat16, jnp.float32, jnp.int32
VMEM = pl.BlockSpec(memory_space=pltpu.VMEM)


def plane_of(count):
    wide = max(y for y in range(1, count + 1) if count % y == 0 and 2 * y * y <= max(count, 2))
    return count // wide, wide


def shift(block, tall, wide, dz, dy, keep=None):
    pairs = [
        (z * wide + y, (z + dz) % tall * wide + (y + dy) % wide)
        for z in range(tall)
        for y in range(wide)
        if keep is None or keep(z)
    ]
    return lax.ppermute(block, "ctx", pairs)


def tie_body(count, *refs):
    total = refs[0][...]
    for ref in refs[1:count]:
        total = total + ref[...]
    refs[-1][...] = total


def tie(blocks, tokens):
    return kernel_call(
        functools.partial(tie_body, len(blocks)),
        [(blocks[0].shape, blocks[0].dtype)],
        [*blocks, *tokens],
        specs=[VMEM] * len(blocks) + [pl.BlockSpec(memory_space=pl.ANY)] * len(tokens),
    )[0]


def gather_rows(block, tall, wide, tokens):
    blocks = {(0, 0): block}
    for dz in range(1, tall):
        if tall != 4 or dz != 2:
            blocks[dz, 0] = shift(block, tall, wide, dz, 0)
    blocks[1, 0] = tie([blocks[1, 0]], tokens)
    if tall == 4:
        up = shift(blocks[1, 0], tall, wide, 1, 0, lambda z: z in (1, 2))
        down = shift(blocks[3, 0], tall, wide, -1, 0, lambda z: z in (1, 2))
        blocks[2, 0] = up + down
    for dz in [0, 1, *range(tall - 1, 1, -1)]:
        for dy in range(1, wide):
            blocks[dz, dy] = shift(blocks[dz, 0], tall, wide, 0, dy)
    return [blocks[dz, dy] for dz in range(tall) for dy in range(wide)]


def gather_blocks(block, tall, wide):
    blocks = {(dz, 0): shift(block, tall, wide, dz, 0) if dz else block for dz in range(tall)}
    for dz in range(tall):
        for dy in range(1, wide):
            blocks[dz, dy] = shift(blocks[dz, 0], tall, wide, 0, dy)
    return [blocks[dz, dy] for dz in range(tall) for dy in range(wide)]


def sum_order(tall):
    order = [tall // 2, *range(1, tall // 2), *range(tall // 2 + 1, tall), 0]
    return order[: tall // 2], order[tall // 2 :]


def sum_shapes(tall, wide, share, model):
    kept = [((share, model), bf16)] * tall
    return kept + [((tall // 2 * share, model), bf16)] * (2 * (wide - 1))


def store_parts(parts, tall, wide, span, product, back):
    share = parts[0].shape[0]
    sign = -1 if back else 1

    def rows(dz, dy):
        at = sign * dz % tall * wide + sign * dy % wide
        return product[at * share : (at + 1) * share, :]

    for dz in range(tall):
        parts[dz][:, span] = rows(dz, 0)
    for dy in range(1, wide):
        for which, group in enumerate(sum_order(tall)):
            out = parts[tall + 2 * (dy - 1) + which]
            for place, dz in enumerate(group):
                out[place * share : (place + 1) * share, span] = rows(dz, dy)


def scatter_sum(parts, tall, wide, tokens=()):
    share = parts[0].shape[0]
    crossed = [shift(p, tall, wide, 0, i // 2 + 1) for i, p in enumerate(parts[tall:])]
    if tokens:
        crossed[1] = tie([crossed[1]], tokens)
    total = None
    for which, group in enumerate(sum_order(tall)):
        for place, dz in enumerate(group):
            lane = parts[dz].astype(f32)
            for dy in range(1, wide):
                other = crossed[2 * (dy - 1) + which]
                lane = lane + other[place * share : (place + 1) * share].astype(f32)
            if dz:
                lane = shift(lane.astype(bf16), tall, wide, dz, 0).astype(f32)
            total = lane if total is None else total + lane
    return total


def dot(a, b):
    return jnp.dot(a, b, preferred_element_type=f32)


def from_hbm(weight):
    return pltpu.with_memory_space_constraint(weight, pltpu.HBM)


def fetched(weight):
    return pltpu.with_memory_space_constraint(weight, pltpu.VMEM)


def kernel_call(body, outs, args, scratch=(), limit=14, flops=0, specs=None):
    return pl.pallas_call(
        body,
        out_shape=[jax.ShapeDtypeStruct(s, d) for s, d in outs],
        in_specs=specs or [VMEM] * len(args),
        out_specs=[VMEM] * len(outs),
        scratch_shapes=list(scratch),
        compiler_params=pltpu.CompilerParams(vmem_limit_bytes=limit << 20),
        cost_estimate=pl.CostEstimate(flops=flops, bytes_accessed=1 << 20, transcendentals=0),
    )(*args)


def load_body(count, *refs):
    sources, copies, sems = refs[1 : 1 + count], refs[1 + count : -2], refs[-1]
    moves = [
        pltpu.make_async_copy(a, b, sems.at[i]) for i, (a, b) in enumerate(zip(sources, copies))
    ]
    for move in moves:
        move.start()
    for move in moves:
        move.wait()
    refs[-2][...] = jnp.zeros_like(refs[-2])


def load(after, *arrays):
    size = sum(a.size * a.dtype.itemsize for a in arrays)
    *copies, token = pl.pallas_call(
        functools.partial(load_body, len(arrays)),
        out_shape=[pltpu.VMEM(a.shape, a.dtype) for a in arrays]
        + [jax.ShapeDtypeStruct((8, 128), f32)],
        in_specs=[pl.BlockSpec(memory_space=pl.ANY)] * (1 + len(arrays)),
        out_specs=[VMEM] * (1 + len(arrays)),
        scratch_shapes=[pltpu.SemaphoreType.DMA((len(arrays),))],
        compiler_params=pltpu.CompilerParams(vmem_limit_bytes=2 << 20),
        cost_estimate=pl.CostEstimate(flops=0, bytes_accessed=2 * size, transcendentals=0),
    )(after, *[from_hbm(a) for a in arrays])
    return [fetched(c) for c in copies] + [token]


def tile_of(width, most):
    return width if width <= most else most


def iota(shape, axis):
    return lax.broadcasted_iota(i32, shape, axis).astype(f32)


def pick(onehot, values):
    return dot(onehot, values).astype(values.dtype)


def send_body(me, routed, activations, outgoing):
    capacity, tokens, total = outgoing.shape[0], activations.shape[0], routed.shape[1]
    low = (me[0] * tokens).astype(f32)
    where = routed[...].astype(f32)
    first = jnp.sum(jnp.where(where < low, 1.0, 0.0), axis=1, keepdims=True)
    here = (where >= low) & (where < low + tokens)
    slot = jnp.where(here, iota((1, total), 1) - first, -1.0)
    hit = slot == iota((capacity, total), 0)
    token = jnp.sum(jnp.where(hit, where - low + 1.0, 0.0), axis=1, keepdims=True) - 1.0
    onehot = jnp.where(token == iota((capacity, tokens), 1), 1.0, 0.0).astype(bf16)
    width = activations.shape[1]
    tile = tile_of(width, 1024)
    for start in range(0, width, tile):
        span = slice(start, start + tile)
        outgoing[:, span] = pick(onehot, activations[:, span])


def map_body(tall, wide, tokens, heads_of, me, routed, balance, notes, *outs):
    pick_rows, in_order, columns, unmix, positions = outs
    count, total = tall * wide, routed.shape[1]
    share, capacity = total // count, pick_rows.shape[1] // count
    outbound, inbound = columns.shape[0], unmix.shape[0]
    my_z, my_y = lax.div(me[0], wide), lax.rem(me[0], wide)
    where, owner = routed[...].astype(f32), balance[...].astype(f32)
    lane = iota((1, total), 1)
    slot, place = jnp.zeros((1, total), f32), jnp.zeros((1, total), f32)
    out_base, out_block = notes[:outbound, 0:1], notes[:outbound, 1:2]
    in_base, in_source = notes[:inbound, 2:3], notes[:inbound, 3:4]
    for s in range(count):
        z, y = divmod(s, wide)
        from_block = lax.rem(my_z - z + tall, tall) * wide + lax.rem(my_y - y + wide, wide)
        to_block = lax.rem(z - my_z + tall, tall) * wide + lax.rem(y - my_y + wide, wide)
        before = where < s * tokens
        first = jnp.sum(jnp.where(before, 1.0, 0.0), axis=1, keepdims=True)
        inside = (where < (s + 1) * tokens) & jnp.logical_not(before)
        start = (from_block * capacity).astype(f32)
        slot += jnp.where(inside, lane - first + start, 0.0)
        place += jnp.where(owner == s, (to_block * share).astype(f32), 0.0)
        out_base += jnp.where(out_block == s, float(heads_of(s)), 0.0)
        in_base += jnp.where(in_source == s, float(s * (outbound // count)), 0.0)
    mine = owner == iota((count, total), 0)
    earlier = jnp.where(iota((total, total), 0) < iota((total, total), 1), 1.0, 0.0)
    rank = dot(jnp.where(mine, 1.0, 0.0).astype(bf16), earlier.astype(bf16))
    place += jnp.sum(jnp.where(mine, rank, 0.0), axis=0, keepdims=True)
    placed = place == iota((total, total), 0)
    in_order[...] = jnp.where(placed, 1.0, 0.0).astype(bf16)
    at = jnp.sum(jnp.where(placed, where, 0.0), axis=1, keepdims=True)
    positions[...] = jnp.broadcast_to(at, positions.shape)
    slot_at = jnp.sum(jnp.where(placed, slot, 0.0), axis=1, keepdims=True)
    pick_rows[...] = jnp.where(slot_at == iota(pick_rows.shape, 1), 1.0, 0.0).astype(bf16)
    columns[...] = jnp.where(out_base == iota(columns.shape, 1), 1.0, 0.0).astype(bf16)
    unmix[...] = jnp.where(in_base == iota(unmix.shape, 1), 1.0, 0.0).astype(bf16)


def kv_body(count, *refs):
    blocks = refs[:count]
    pick_rows, order, columns, gain, w_key, w_value = refs[count : count + 6]
    normed, own, sent, rows = refs[-4:]
    total, width = normed.shape
    tile = tile_of(width, 512)
    square = jnp.zeros((total, 1), f32)
    for start in range(0, width, tile):
        span = slice(start, start + tile)
        part = dot(pick_rows[...], jnp.concatenate([b[:, span] for b in blocks], axis=0))
        rows[:, span] = part.astype(bf16)
        square += jnp.sum(part * part, axis=1, keepdims=True)
    own[...] = rows[: own.shape[0], :]
    factor = lax.rsqrt(square / width + norm_eps)
    for start in range(0, width, tile):
        span = slice(start, start + tile)
        part = rows[:, span].astype(f32) * factor * gain[:, span]
        normed[:, span] = part.astype(bf16)
    keys = dot(normed[...], w_key[...]).astype(bf16)
    values = dot(normed[...], w_value[...]).astype(bf16)
    both = jnp.concatenate([keys, values], axis=1)
    turned = lax.dot_general(
        columns[...], both, (((1,), (1,)), ((), ())), preferred_element_type=f32
    ).astype(bf16)
    sent[...] = dot(turned, order[...]).astype(bf16)


def query_body(normed, w_query, cosine, sine, query, weight, sems):
    depth = weight.shape[0] // 4
    moves = []
    for index in range(4):
        piece = pl.ds(index * depth, depth)
        moves.append(
            pltpu.make_async_copy(w_query.at[piece], weight.at[piece], sems.at[index])
        )
        moves[-1].start()
    raw = jnp.zeros(query.shape, f32)
    for index, move in enumerate(moves):
        move.wait()
        piece = slice(index * depth, (index + 1) * depth)
        raw += dot(normed[:, piece], weight[piece, :])
    for head in range(query.shape[1] // HEAD_DIM):
        span = slice(head * HEAD_DIM, (head + 1) * HEAD_DIM)
        one = raw[:, span]
        turned = one * cosine[...] + pltpu.roll(one, HEAD_DIM // 2, 1) * sine[...]
        query[:, span] = turned.astype(bf16)


def attend_body(plane, kv_local, *refs):
    arrived, query, unmix, cosine, sine, key_pos, query_pos, w_output = refs[:8]
    parts, (heads_out, weight, sems) = refs[8:-3], refs[-3:]
    width = weight.shape[1] // 4
    moves = []
    for index in range(4):
        piece = pl.ds(index * width, width)
        moves.append(
            pltpu.make_async_copy(w_output.at[:, piece], weight.at[:, piece], sems.at[index])
        )
        moves[-1].start()
    half = HEAD_DIM // 2
    heads = query.shape[1] // HEAD_DIM
    both = dot(unmix[...], arrived[...])
    allowed = key_pos[...].astype(f32) <= query_pos[:, 0:1]
    for group in range(kv_local):
        base = group * HEAD_DIM
        first, second = both[base : base + half], both[base + half : base + HEAD_DIM]
        keys = jnp.concatenate(
            [first * cosine[...] - second * sine[...], second * cosine[...] + first * sine[...]],
            axis=0,
        ).astype(bf16)
        base += kv_local * HEAD_DIM
        values = both[base : base + HEAD_DIM].astype(bf16)
        for head in range(group * heads // kv_local, (group + 1) * heads // kv_local):
            span = slice(head * HEAD_DIM, (head + 1) * HEAD_DIM)
            scores = dot(query[:, span], keys) * HEAD_DIM ** (-0.5)
            scores = jnp.where(allowed, scores, -1e30)
            weights = jnp.exp(scores - jnp.max(scores, axis=1, keepdims=True))
            probs = (weights / jnp.sum(weights, axis=1, keepdims=True)).astype(bf16)
            heads_out[:, span] = lax.dot_general(
                probs, values, (((1,), (1,)), ((), ())), preferred_element_type=f32
            ).astype(bf16)
    spread(heads_out, weight, parts, plane, False, moves)


def spread(left, weight, parts, plane, back, moves=()):
    width = weight.shape[1]
    tile = tile_of(width, 512)
    for start in range(0, width, tile):
        if moves and start % (width // len(moves)) == 0:
            moves[start // (width // len(moves))].wait()
        span = slice(start, start + tile)
        product = dot(left[...], weight[:, span]).astype(bf16)
        store_parts(parts, *plane, span, product, back)


def mlp_body(plane, *refs):
    count = plane[0] * plane[1]
    blocks, (w_gate, w_up, w_down) = refs[:count], refs[count : count + 3]
    parts, (piece, inner) = refs[count + 3 : -2], refs[-2:]
    share = blocks[0].shape[0]
    for index, block in enumerate(blocks):
        piece[index * share : (index + 1) * share, :] = block[...]
    width = w_gate.shape[1]
    tile = tile_of(width, 256)
    for start in range(0, width, tile):
        span = slice(start, start + tile)
        gate = dot(piece[...], w_gate[:, span])
        upward = dot(piece[...], w_up[:, span])
        inner[:, span] = (gate / (1.0 + jnp.exp(-gate)) * upward).astype(bf16)
    spread(inner, w_down, parts, plane, True)


def on_device(
    activations,
    routed,
    balance,
    w_query,
    w_key,
    w_value,
    w_output,
    attn_gain,
    mlp_gain,
    w_gate,
    w_up,
    w_down,
    w_router,
):
    count = lax.axis_size("ctx")
    plane = tall, wide = plane_of(count)
    me = lax.axis_index("ctx").astype(i32).reshape(1)
    tokens, model = activations.shape
    total = routed.shape[0]
    share = total // count
    capacity = 2 * share
    local_heads = w_query.shape[1] // HEAD_DIM
    group_size = HEADS // KV_HEADS
    kv_local = max(1, local_heads // group_size)
    key_cols = w_key.shape[1]
    depth = key_cols // KV_HEADS
    scalar = pl.BlockSpec(memory_space=pltpu.SMEM)
    routed, balance = routed.reshape(1, total), balance.reshape(1, total)

    (outgoing,) = kernel_call(
        send_body,
        [((capacity, model), bf16)],
        [me, routed, activations],
        specs=[scalar, VMEM, VMEM],
        flops=2 * capacity * tokens * model,
    )
    attn_gain, w_key, w_value, token_1 = load(
        outgoing, attn_gain.reshape(1, model), w_key, w_value
    )

    each = kv_local * 2 * depth
    notes = np.zeros((max(count * each, 2 * kv_local * HEAD_DIM), 4), np.float32)
    block, local, side, entry = np.indices((count, kv_local, 2, depth)).reshape(4, -1)
    notes[: count * each, 0] = side * key_cols + entry * KV_HEADS + local
    notes[: count * each, 1] = block
    side, local, source, entry = np.indices((2, kv_local, count, depth)).reshape(4, -1)
    notes[: 2 * kv_local * HEAD_DIM, 2] = (local * 2 + side) * depth + entry
    notes[: 2 * kv_local * HEAD_DIM, 3] = source
    pick_rows, in_order, columns, unmix, positions = kernel_call(
        functools.partial(
            map_body, tall, wide, tokens, lambda peer: peer * local_heads // group_size
        ),
        [
            ((total, count * capacity), bf16),
            ((total, total), bf16),
            ((count * each, 2 * key_cols), bf16),
            ((2 * kv_local * HEAD_DIM, count * each), bf16),
            ((total, HEAD_DIM // 2), f32),
        ],
        [me, routed, balance, notes],
        specs=[scalar, VMEM, VMEM, VMEM],
    )
    blocks = gather_rows(outgoing, tall, wide, [token_1, positions])

    half = HEAD_DIM // 2
    steps_f = jnp.arange(half, dtype=f32)
    freqs = jnp.exp(-jnp.log(f32(rope_base)) * (2.0 * steps_f / HEAD_DIM))
    q_angles = positions * freqs[None, :]
    q_cos, q_sin = jnp.cos(q_angles), jnp.sin(q_angles)
    q_cos = jnp.concatenate([q_cos, q_cos], axis=1)
    q_sin = jnp.concatenate([-q_sin, q_sin], axis=1)
    k_angles = freqs[:, None] * routed.astype(f32)
    k_cos, k_sin = jnp.cos(k_angles), jnp.sin(k_angles)

    normed, own, sent = kernel_call(
        functools.partial(kv_body, count),
        [((total, model), bf16), ((share, model), bf16), ((count * each, total), bf16)],
        [*blocks, pick_rows, in_order, columns, attn_gain, w_key, w_value],
        [pltpu.VMEM((total, model), bf16)],
        flops=2 * total * model * 512,
    )
    arrived = lax.all_to_all(sent.reshape(count, each, total), "ctx", 0, 0, tiled=True)
    arrived = arrived.reshape(count * each, total)
    in_hbm = pl.BlockSpec(memory_space=pl.ANY)
    heads_wide = local_heads * HEAD_DIM
    (query,) = kernel_call(
        query_body,
        [((total, heads_wide), bf16)],
        [normed, from_hbm(w_query), q_cos, q_sin],
        [pltpu.VMEM((model, heads_wide), bf16), pltpu.SemaphoreType.DMA((4,))],
        flops=2 * total * model * heads_wide,
        specs=[VMEM, in_hbm, VMEM, VMEM],
    )
    part_shapes = sum_shapes(tall, wide, share, model)
    attn_parts = kernel_call(
        functools.partial(attend_body, plane, kv_local),
        part_shapes,
        [arrived, query, unmix, k_cos, k_sin, routed, positions, from_hbm(w_output)],
        [
            pltpu.VMEM((total, heads_wide), bf16),
            pltpu.VMEM((heads_wide, model), bf16),
            pltpu.SemaphoreType.DMA((4,)),
        ],
        flops=2 * total * model * heads_wide,
        specs=[VMEM] * 7 + [in_hbm],
    )
    w_down, token_5 = load(attn_parts[0], w_down)
    attn_own = scatter_sum(attn_parts, tall, wide, [token_5])
    own_rows = own.astype(f32)
    hidden = own_rows + attn_own
    mean_sq = jnp.mean(hidden * hidden, axis=-1, keepdims=True)
    mnorm = (hidden * lax.rsqrt(mean_sq + norm_eps) * mlp_gain).astype(bf16)
    pieces = gather_blocks(mnorm, tall, wide)
    w_gate, _ = load(mnorm, w_gate)
    w_up, _ = load(mnorm, w_up)
    hidden_units = w_gate.shape[1]
    mlp_parts = kernel_call(
        functools.partial(mlp_body, plane),
        part_shapes,
        [*pieces, w_gate, w_up, w_down],
        [pltpu.VMEM((total, model), bf16), pltpu.VMEM((total, hidden_units), bf16)],
        flops=6 * total * model * hidden_units,
    )
    mlp_own = scatter_sum(mlp_parts, tall, wide)
    router_score = jnp.sum(own_rows * w_router[None, :], axis=1, keepdims=True)
    return (own_rows + router_score * (attn_own + mlp_own)).astype(bf16)


def solution(mesh):
    in_specs = (
        P(("dp", "ctx"), None),
        P("dp"),
        P("dp"),
        P(None, "ctx"),
        P(None, "ctx"),
        P(None, "ctx"),
        P("ctx", None),
        P(),
        P(),
        P(None, "ctx"),
        P(None, "ctx"),
        P("ctx", None),
        P(),
    )
    out_specs = P(("dp", "ctx"), None)
    return jax.shard_map(
        on_device, mesh=mesh, in_specs=in_specs, out_specs=out_specs, check_vma=False
    )
```

```python
import functools

import jax
import jax.numpy as jnp
import numpy as np
from jax import lax
from jax.experimental import pallas as pl
from jax.experimental.pallas import tpu as pltpu
from jax.sharding import PartitionSpec as P

HEADS = 32
KV_HEADS = 8
HEAD_DIM = 128

rope_base = 500000.0
norm_eps = 1e-05

bf16, f32, i32 = jnp.bfloat16, jnp.float32, jnp.int32
VMEM = pl.BlockSpec(memory_space=pltpu.VMEM)


def plane_of(count):
    wide = max(y for y in range(1, count + 1) if count % y == 0 and 2 * y * y <= max(count, 2))
    return count // wide, wide


def shift(block, tall, wide, dz, dy, keep=None):
    pairs = [
        (z * wide + y, (z + dz) % tall * wide + (y + dy) % wide)
        for z in range(tall)
        for y in range(wide)
        if keep is None or keep(z)
    ]
    return lax.ppermute(block, "ctx", pairs)


def tie_body(count, *refs):
    total = refs[0][...]
    for ref in refs[1:count]:
        total = total + ref[...]
    refs[-1][...] = total


def tie(blocks, tokens):
    return kernel_call(
        functools.partial(tie_body, len(blocks)),
        [(blocks[0].shape, blocks[0].dtype)],
        [*blocks, *tokens],
        specs=[VMEM] * len(blocks) + [pl.BlockSpec(memory_space=pl.ANY)] * len(tokens),
    )[0]


def gather_rows(block, tall, wide, tokens):
    blocks = {(0, 0): block}
    for dz in range(1, tall):
        if tall != 4 or dz != 2:
            blocks[dz, 0] = shift(block, tall, wide, dz, 0)
    for dy in range(1, wide):
        blocks[0, dy] = shift(block, tall, wide, 0, dy)
    blocks[1, 0] = tie([blocks[1, 0]], [*tokens, *(blocks[0, dy] for dy in range(1, wide))])
    if tall == 4:
        up = shift(blocks[1, 0], tall, wide, 1, 0, lambda z: z in (1, 2))
        down = shift(blocks[3, 0], tall, wide, -1, 0, lambda z: z in (1, 2))
        blocks[2, 0] = up + down
    for dz in [1, *range(tall - 1, 1, -1)]:
        for dy in range(1, wide):
            blocks[dz, dy] = shift(blocks[dz, 0], tall, wide, 0, dy)
    return [blocks[dz, dy] for dz in range(tall) for dy in range(wide)]


def gather_blocks(block, tall, wide):
    blocks = {(dz, 0): shift(block, tall, wide, dz, 0) if dz else block for dz in range(tall)}
    for dz in range(tall):
        for dy in range(1, wide):
            blocks[dz, dy] = shift(blocks[dz, 0], tall, wide, 0, dy)
    return [blocks[dz, dy] for dz in range(tall) for dy in range(wide)]


def sum_order(tall):
    order = [tall // 2, *range(1, tall // 2), *range(tall // 2 + 1, tall), 0]
    return order[: tall // 2], order[tall // 2 :]


def sum_shapes(tall, wide, share, model):
    kept = [((share, model), bf16)] * tall
    return kept + [((tall // 2 * share, model), bf16)] * (2 * (wide - 1))


def store_parts(parts, tall, wide, span, product, back):
    share = parts[0].shape[0]
    sign = -1 if back else 1

    def rows(dz, dy):
        at = sign * dz % tall * wide + sign * dy % wide
        return product[at * share : (at + 1) * share, :]

    for dz in range(tall):
        parts[dz][:, span] = rows(dz, 0)
    for dy in range(1, wide):
        for which, group in enumerate(sum_order(tall)):
            out = parts[tall + 2 * (dy - 1) + which]
            for place, dz in enumerate(group):
                out[place * share : (place + 1) * share, span] = rows(dz, dy)


def scatter_sum(parts, tall, wide, loads=()):
    share = parts[0].shape[0]
    loaded = []
    crossed = [shift(p, tall, wide, 0, i // 2 + 1) for i, p in enumerate(parts[tall:])]
    if loads:
        *copy, token = load(parts[0], loads[0])
        loaded += copy
        crossed[1] = tie([crossed[1]], [token])
    total = None
    for which, group in enumerate(sum_order(tall)):
        for place, dz in enumerate(group):
            lane = parts[dz].astype(f32)
            for dy in range(1, wide):
                other = crossed[2 * (dy - 1) + which]
                lane = lane + other[place * share : (place + 1) * share].astype(f32)
            if dz:
                sent = lane.astype(bf16)
                lane = shift(sent, tall, wide, dz, 0)
                if loads and dz == tall - 1:
                    *copy, token = load(sent, loads[1])
                    loaded += copy
                    lane = tie([lane], [token])
                lane = lane.astype(f32)
            total = lane if total is None else total + lane
    return (total, *loaded) if loads else total


def dot(a, b):
    return jnp.dot(a, b, preferred_element_type=f32)


def from_hbm(weight):
    return pltpu.with_memory_space_constraint(weight, pltpu.HBM)


def fetched(weight):
    return pltpu.with_memory_space_constraint(weight, pltpu.VMEM)


def kernel_call(body, outs, args, scratch=(), limit=14, flops=0, specs=None):
    return pl.pallas_call(
        body,
        out_shape=[jax.ShapeDtypeStruct(s, d) for s, d in outs],
        in_specs=specs or [VMEM] * len(args),
        out_specs=[VMEM] * len(outs),
        scratch_shapes=list(scratch),
        compiler_params=pltpu.CompilerParams(vmem_limit_bytes=limit << 20),
        cost_estimate=pl.CostEstimate(flops=flops, bytes_accessed=1 << 20, transcendentals=0),
    )(*args)


def load_body(count, *refs):
    sources, copies, sems = refs[1 : 1 + count], refs[1 + count : -2], refs[-1]
    moves = [
        pltpu.make_async_copy(a, b, sems.at[i]) for i, (a, b) in enumerate(zip(sources, copies))
    ]
    for move in moves:
        move.start()
    for move in moves:
        move.wait()
    refs[-2][...] = jnp.zeros_like(refs[-2])


def load(after, *arrays):
    size = sum(a.size * a.dtype.itemsize for a in arrays)
    *copies, token = pl.pallas_call(
        functools.partial(load_body, len(arrays)),
        out_shape=[pltpu.VMEM(a.shape, a.dtype) for a in arrays]
        + [jax.ShapeDtypeStruct((8, 128), f32)],
        in_specs=[pl.BlockSpec(memory_space=pl.ANY)] * (1 + len(arrays)),
        out_specs=[VMEM] * (1 + len(arrays)),
        scratch_shapes=[pltpu.SemaphoreType.DMA((len(arrays),))],
        compiler_params=pltpu.CompilerParams(vmem_limit_bytes=2 << 20),
        cost_estimate=pl.CostEstimate(flops=0, bytes_accessed=2 * size, transcendentals=0),
    )(after, *[from_hbm(a) for a in arrays])
    return [fetched(c) for c in copies] + [token]


def tile_of(width, most):
    return width if width <= most else most


def iota(shape, axis):
    return lax.broadcasted_iota(i32, shape, axis).astype(f32)


def pick(onehot, values):
    return dot(onehot, values).astype(values.dtype)


def send_body(me, routed_in, activations_in, outgoing, routed, activations, sems):
    first_move = pltpu.make_async_copy(routed_in, routed, sems.at[0])
    second_move = pltpu.make_async_copy(activations_in, activations, sems.at[1])
    first_move.start()
    second_move.start()
    first_move.wait()
    capacity, tokens, total = outgoing.shape[0], activations.shape[0], routed.shape[1]
    low = (me[0] * tokens).astype(f32)
    where = routed[...].astype(f32)
    first = jnp.sum(jnp.where(where < low, 1.0, 0.0), axis=1, keepdims=True)
    here = (where >= low) & (where < low + tokens)
    slot = jnp.where(here, iota((1, total), 1) - first, -1.0)
    hit = slot == iota((capacity, total), 0)
    token = jnp.sum(jnp.where(hit, where - low + 1.0, 0.0), axis=1, keepdims=True) - 1.0
    onehot = jnp.where(token == iota((capacity, tokens), 1), 1.0, 0.0).astype(bf16)
    second_move.wait()
    width = activations.shape[1]
    tile = tile_of(width, 1024)
    for start in range(0, width, tile):
        span = slice(start, start + tile)
        outgoing[:, span] = pick(onehot, activations[:, span])


def map_body(tall, wide, tokens, heads_of, me, routed, balance, notes, *outs):
    pick_rows, in_order, columns, unmix, positions = outs
    count, total = tall * wide, routed.shape[1]
    share, capacity = total // count, pick_rows.shape[1] // count
    outbound, inbound = columns.shape[0], unmix.shape[0]
    my_z, my_y = lax.div(me[0], wide), lax.rem(me[0], wide)
    where, owner = routed[...].astype(f32), balance[...].astype(f32)
    lane = iota((1, total), 1)
    slot, place = jnp.zeros((1, total), f32), jnp.zeros((1, total), f32)
    out_base, out_block = notes[:outbound, 0:1], notes[:outbound, 1:2]
    in_base, in_source = notes[:inbound, 2:3], notes[:inbound, 3:4]
    for s in range(count):
        z, y = divmod(s, wide)
        from_block = lax.rem(my_z - z + tall, tall) * wide + lax.rem(my_y - y + wide, wide)
        to_block = lax.rem(z - my_z + tall, tall) * wide + lax.rem(y - my_y + wide, wide)
        before = where < s * tokens
        first = jnp.sum(jnp.where(before, 1.0, 0.0), axis=1, keepdims=True)
        inside = (where < (s + 1) * tokens) & jnp.logical_not(before)
        start = (from_block * capacity).astype(f32)
        slot += jnp.where(inside, lane - first + start, 0.0)
        place += jnp.where(owner == s, (to_block * share).astype(f32), 0.0)
        out_base += jnp.where(out_block == s, float(heads_of(s)), 0.0)
        in_base += jnp.where(in_source == s, float(s * (outbound // count)), 0.0)
    mine = owner == iota((count, total), 0)
    earlier = jnp.where(iota((total, total), 0) < iota((total, total), 1), 1.0, 0.0)
    rank = dot(jnp.where(mine, 1.0, 0.0).astype(bf16), earlier.astype(bf16))
    place += jnp.sum(jnp.where(mine, rank, 0.0), axis=0, keepdims=True)
    placed = place == iota((total, total), 0)
    in_order[...] = jnp.where(placed, 1.0, 0.0).astype(bf16)
    at = jnp.sum(jnp.where(placed, where, 0.0), axis=1, keepdims=True)
    positions[...] = jnp.broadcast_to(at, positions.shape)
    slot_at = jnp.sum(jnp.where(placed, slot, 0.0), axis=1, keepdims=True)
    pick_rows[...] = jnp.where(slot_at == iota(pick_rows.shape, 1), 1.0, 0.0).astype(bf16)
    columns[...] = jnp.where(out_base == iota(columns.shape, 1), 1.0, 0.0).astype(bf16)
    unmix[...] = jnp.where(in_base == iota(unmix.shape, 1), 1.0, 0.0).astype(bf16)


def kv_body(count, *refs):
    blocks = refs[:count]
    pick_rows, order, columns, gain, w_key, w_value = refs[count : count + 6]
    normed, own, sent, rows = refs[-4:]
    total, width = normed.shape
    tile = tile_of(width, 512)
    square = jnp.zeros((total, 1), f32)
    for start in range(0, width, tile):
        span = slice(start, start + tile)
        part = dot(pick_rows[...], jnp.concatenate([b[:, span] for b in blocks], axis=0))
        rows[:, span] = part.astype(bf16)
        square += jnp.sum(part * part, axis=1, keepdims=True)
    own[...] = rows[: own.shape[0], :]
    factor = lax.rsqrt(square / width + norm_eps)
    for start in range(0, width, tile):
        span = slice(start, start + tile)
        part = rows[:, span].astype(f32) * factor * gain[:, span]
        normed[:, span] = part.astype(bf16)
    keys = dot(normed[...], w_key[...]).astype(bf16)
    values = dot(normed[...], w_value[...]).astype(bf16)
    both = jnp.concatenate([keys, values], axis=1)
    turned = lax.dot_general(
        columns[...], both, (((1,), (1,)), ((), ())), preferred_element_type=f32
    ).astype(bf16)
    sent[...] = dot(turned, order[...]).astype(bf16)


def query_body(normed, w_query, cosine, sine, query, weight, sems):
    depth = weight.shape[0] // 4
    moves = []
    for index in range(4):
        piece = pl.ds(index * depth, depth)
        moves.append(
            pltpu.make_async_copy(w_query.at[piece], weight.at[piece], sems.at[index])
        )
        moves[-1].start()
    raw = jnp.zeros(query.shape, f32)
    for index, move in enumerate(moves):
        move.wait()
        piece = slice(index * depth, (index + 1) * depth)
        raw += dot(normed[:, piece], weight[piece, :])
    for head in range(query.shape[1] // HEAD_DIM):
        span = slice(head * HEAD_DIM, (head + 1) * HEAD_DIM)
        one = raw[:, span]
        turned = one * cosine[...] + pltpu.roll(one, HEAD_DIM // 2, 1) * sine[...]
        query[:, span] = turned.astype(bf16)


def attend_body(plane, kv_local, *refs):
    arrived, query, unmix, cosine, sine, key_pos, query_pos, w_output = refs[:8]
    parts, (heads_out, weight, sems) = refs[8:-3], refs[-3:]
    width = weight.shape[1] // 4
    moves = []
    for index in range(4):
        piece = pl.ds(index * width, width)
        moves.append(
            pltpu.make_async_copy(w_output.at[:, piece], weight.at[:, piece], sems.at[index])
        )
        moves[-1].start()
    half = HEAD_DIM // 2
    heads = query.shape[1] // HEAD_DIM
    both = dot(unmix[...], arrived[...])
    allowed = key_pos[...].astype(f32) <= query_pos[:, 0:1]
    for group in range(kv_local):
        base = group * HEAD_DIM
        first, second = both[base : base + half], both[base + half : base + HEAD_DIM]
        keys = jnp.concatenate(
            [first * cosine[...] - second * sine[...], second * cosine[...] + first * sine[...]],
            axis=0,
        ).astype(bf16)
        base += kv_local * HEAD_DIM
        values = both[base : base + HEAD_DIM].astype(bf16)
        for head in range(group * heads // kv_local, (group + 1) * heads // kv_local):
            span = slice(head * HEAD_DIM, (head + 1) * HEAD_DIM)
            scores = dot(query[:, span], keys) * HEAD_DIM ** (-0.5)
            scores = jnp.where(allowed, scores, -1e30)
            weights = jnp.exp(scores - jnp.max(scores, axis=1, keepdims=True))
            probs = (weights / jnp.sum(weights, axis=1, keepdims=True)).astype(bf16)
            heads_out[:, span] = lax.dot_general(
                probs, values, (((1,), (1,)), ((), ())), preferred_element_type=f32
            ).astype(bf16)
    spread(heads_out, weight, parts, plane, False, moves)


def spread(left, weight, parts, plane, back, moves=()):
    width = weight.shape[1]
    tile = tile_of(width, 512)
    for start in range(0, width, tile):
        if moves and start % (width // len(moves)) == 0:
            moves[start // (width // len(moves))].wait()
        span = slice(start, start + tile)
        product = dot(left[...], weight[:, span]).astype(bf16)
        store_parts(parts, *plane, span, product, back)


def mlp_body(plane, *refs):
    count = plane[0] * plane[1]
    blocks, (w_gate, w_up, w_down) = refs[:count], refs[count : count + 3]
    parts, (piece, inner) = refs[count + 3 : -2], refs[-2:]
    share = blocks[0].shape[0]
    for index, block in enumerate(blocks):
        piece[index * share : (index + 1) * share, :] = block[...]
    width = w_gate.shape[1]
    tile = tile_of(width, 256)
    for start in range(0, width, tile):
        span = slice(start, start + tile)
        gate = dot(piece[...], w_gate[:, span])
        upward = dot(piece[...], w_up[:, span])
        inner[:, span] = (gate / (1.0 + jnp.exp(-gate)) * upward).astype(bf16)
    spread(inner, w_down, parts, plane, True)


def on_device(
    activations,
    routed,
    balance,
    w_query,
    w_key,
    w_value,
    w_output,
    attn_gain,
    mlp_gain,
    w_gate,
    w_up,
    w_down,
    w_router,
):
    count = lax.axis_size("ctx")
    plane = tall, wide = plane_of(count)
    me = lax.axis_index("ctx").astype(i32).reshape(1)
    tokens, model = activations.shape
    total = routed.shape[0]
    share = total // count
    capacity = 2 * share
    local_heads = w_query.shape[1] // HEAD_DIM
    group_size = HEADS // KV_HEADS
    kv_local = max(1, local_heads // group_size)
    key_cols = w_key.shape[1]
    depth = key_cols // KV_HEADS
    scalar = pl.BlockSpec(memory_space=pltpu.SMEM)
    in_hbm = pl.BlockSpec(memory_space=pl.ANY)
    routed, balance = routed.reshape(1, total), balance.reshape(1, total)

    (outgoing,) = kernel_call(
        send_body,
        [((capacity, model), bf16)],
        [me, from_hbm(routed), from_hbm(activations)],
        [
            pltpu.VMEM(routed.shape, i32),
            pltpu.VMEM(activations.shape, bf16),
            pltpu.SemaphoreType.DMA((2,)),
        ],
        specs=[scalar, in_hbm, in_hbm],
        flops=2 * capacity * tokens * model,
    )
    attn_gain, w_key, w_value, token_1 = load(
        outgoing, attn_gain.reshape(1, model), w_key, w_value
    )

    each = kv_local * 2 * depth
    notes = np.zeros((max(count * each, 2 * kv_local * HEAD_DIM), 4), np.float32)
    block, local, side, entry = np.indices((count, kv_local, 2, depth)).reshape(4, -1)
    notes[: count * each, 0] = side * key_cols + entry * KV_HEADS + local
    notes[: count * each, 1] = block
    side, local, source, entry = np.indices((2, kv_local, count, depth)).reshape(4, -1)
    notes[: 2 * kv_local * HEAD_DIM, 2] = (local * 2 + side) * depth + entry
    notes[: 2 * kv_local * HEAD_DIM, 3] = source
    pick_rows, in_order, columns, unmix, positions = kernel_call(
        functools.partial(
            map_body, tall, wide, tokens, lambda peer: peer * local_heads // group_size
        ),
        [
            ((total, count * capacity), bf16),
            ((total, total), bf16),
            ((count * each, 2 * key_cols), bf16),
            ((2 * kv_local * HEAD_DIM, count * each), bf16),
            ((total, HEAD_DIM // 2), f32),
        ],
        [me, routed, balance, notes],
        specs=[scalar, VMEM, VMEM, VMEM],
    )
    blocks = gather_rows(outgoing, tall, wide, [token_1, positions])

    half = HEAD_DIM // 2
    steps_f = jnp.arange(half, dtype=f32)
    freqs = jnp.exp(-jnp.log(f32(rope_base)) * (2.0 * steps_f / HEAD_DIM))
    q_angles = positions * freqs[None, :]
    q_cos, q_sin = jnp.cos(q_angles), jnp.sin(q_angles)
    q_cos = jnp.concatenate([q_cos, q_cos], axis=1)
    q_sin = jnp.concatenate([-q_sin, q_sin], axis=1)
    k_angles = freqs[:, None] * routed.astype(f32)
    k_cos, k_sin = jnp.cos(k_angles), jnp.sin(k_angles)

    normed, own, sent = kernel_call(
        functools.partial(kv_body, count),
        [((total, model), bf16), ((share, model), bf16), ((count * each, total), bf16)],
        [*blocks, pick_rows, in_order, columns, attn_gain, w_key, w_value],
        [pltpu.VMEM((total, model), bf16)],
        flops=2 * total * model * 512,
    )
    arrived = lax.all_to_all(sent.reshape(count, each, total), "ctx", 0, 0, tiled=True)
    arrived = arrived.reshape(count * each, total)
    heads_wide = local_heads * HEAD_DIM
    (query,) = kernel_call(
        query_body,
        [((total, heads_wide), bf16)],
        [normed, from_hbm(w_query), q_cos, q_sin],
        [pltpu.VMEM((model, heads_wide), bf16), pltpu.SemaphoreType.DMA((4,))],
        flops=2 * total * model * heads_wide,
        specs=[VMEM, in_hbm, VMEM, VMEM],
    )
    part_shapes = sum_shapes(tall, wide, share, model)
    attn_parts = kernel_call(
        functools.partial(attend_body, plane, kv_local),
        part_shapes,
        [arrived, query, unmix, k_cos, k_sin, routed, positions, from_hbm(w_output)],
        [
            pltpu.VMEM((total, heads_wide), bf16),
            pltpu.VMEM((heads_wide, model), bf16),
            pltpu.SemaphoreType.DMA((4,)),
        ],
        flops=2 * total * model * heads_wide,
        specs=[VMEM] * 7 + [in_hbm],
    )
    attn_own, w_down, w_gate = scatter_sum(attn_parts, tall, wide, [w_down, w_gate])
    own_rows = own.astype(f32)
    hidden = own_rows + attn_own
    mean_sq = jnp.mean(hidden * hidden, axis=-1, keepdims=True)
    mnorm = (hidden * lax.rsqrt(mean_sq + norm_eps) * mlp_gain).astype(bf16)
    pieces = gather_blocks(mnorm, tall, wide)
    w_up, _ = load(mnorm, w_up)
    hidden_units = w_gate.shape[1]
    mlp_parts = kernel_call(
        functools.partial(mlp_body, plane),
        part_shapes,
        [*pieces, w_gate, w_up, w_down],
        [pltpu.VMEM((total, model), bf16), pltpu.VMEM((total, hidden_units), bf16)],
        flops=6 * total * model * hidden_units,
    )
    mlp_own = scatter_sum(mlp_parts, tall, wide)
    router_score = jnp.sum(own_rows * w_router[None, :], axis=1, keepdims=True)
    return (own_rows + router_score * (attn_own + mlp_own)).astype(bf16)


def solution(mesh):
    in_specs = (
        P(("dp", "ctx"), None),
        P("dp"),
        P("dp"),
        P(None, "ctx"),
        P(None, "ctx"),
        P(None, "ctx"),
        P("ctx", None),
        P(),
        P(),
        P(None, "ctx"),
        P(None, "ctx"),
        P("ctx", None),
        P(),
    )
    out_specs = P(("dp", "ctx"), None)
    return jax.shard_map(
        on_device, mesh=mesh, in_specs=in_specs, out_specs=out_specs, check_vma=False
    )
```

```python
import functools

import jax
import jax.numpy as jnp
import numpy as np
from jax import lax
from jax.experimental import pallas as pl
from jax.experimental.pallas import tpu as pltpu
from jax.sharding import PartitionSpec as P

HEADS = 32
KV_HEADS = 8
HEAD_DIM = 128

rope_base = 500000.0
norm_eps = 1e-05

bf16, f32, i32 = jnp.bfloat16, jnp.float32, jnp.int32
VMEM = pl.BlockSpec(memory_space=pltpu.VMEM)


def plane_of(count):
    wide = 1
    while 8 * wide * wide <= count:
        wide *= 2
    return count // wide, wide


def swap(block, tall, wide, kz, ky, keep=None):
    pairs = [
        (z * wide + y, (z ^ kz) * wide + (y ^ ky))
        for z in range(tall)
        for y in range(wide)
        if keep is None or keep(z)
    ]
    return lax.ppermute(block, "ctx", pairs)


def tie_body(count, *refs):
    total = refs[0][...]
    for ref in refs[1:count]:
        total = total + ref[...]
    refs[-1][...] = total


def tie(blocks, tokens):
    return kernel_call(
        functools.partial(tie_body, len(blocks)),
        [(blocks[0].shape, blocks[0].dtype)],
        [*blocks, *tokens],
        specs=[VMEM] * len(blocks) + [pl.BlockSpec(memory_space=pl.ANY)] * len(tokens),
    )[0]


def gather_rows(block, tall, wide, tokens):
    blocks = {(0, 0): block}
    for ky in range(1, wide):
        blocks[0, ky] = swap(block, tall, wide, 0, ky)
    first = [*tokens, *(blocks[0, ky] for ky in range(1, wide))]
    if tall == 4:
        blocks[1, 0] = tie([swap(block, tall, wide, 1, 0)], first)
        blocks[3, 0] = swap(block, tall, wide, 3, 0)
        inner = swap(blocks[1, 0], tall, wide, 3, 0, lambda z: z in (1, 2))
        outer = swap(blocks[3, 0], tall, wide, 1, 0, lambda z: z in (1, 2))
        for ky in range(1, wide):
            blocks[1, ky] = swap(blocks[1, 0], tall, wide, 0, ky)
            blocks[3, ky] = swap(blocks[3, 0], tall, wide, 0, ky)
        blocks[2, 0] = tie([inner, outer], [blocks[1, ky] for ky in range(1, wide)])
        rest = [2]
    else:
        for kz in range(1, tall):
            blocks[kz, 0] = swap(block, tall, wide, kz, 0)
        blocks[1, 0] = tie([blocks[1, 0]], first)
        rest = range(1, tall)
    for kz in rest:
        for ky in range(1, wide):
            blocks[kz, ky] = swap(blocks[kz, 0], tall, wide, 0, ky)
    return [blocks[kz, ky] for kz in range(tall) for ky in range(wide)]


def gather_blocks(block, tall, wide):
    blocks = {(kz, 0): swap(block, tall, wide, kz, 0) if kz else block for kz in range(tall)}
    for kz in range(tall):
        for ky in range(1, wide):
            blocks[kz, ky] = swap(blocks[kz, 0], tall, wide, 0, ky)
    return [blocks[kz, ky] for kz in range(tall) for ky in range(wide)]


def sum_order(tall):
    order = [*range(tall - 1, -1, -1)]
    return order[: tall // 2], order[tall // 2 :]


def sum_shapes(tall, wide, share, model):
    kept = [((share, model), bf16)] * tall
    return kept + [((tall // 2 * share, model), bf16)] * (2 * (wide - 1))


def store_parts(parts, tall, wide, span, product):
    share = parts[0].shape[0]

    def rows(kz, ky):
        at = kz * wide + ky
        return product[at * share : (at + 1) * share, :]

    for kz in range(tall):
        parts[kz][:, span] = rows(kz, 0)
    for ky in range(1, wide):
        for which, group in enumerate(sum_order(tall)):
            out = parts[tall + 2 * (ky - 1) + which]
            for place, kz in enumerate(group):
                out[place * share : (place + 1) * share, span] = rows(kz, ky)


def scatter_sum(parts, tall, wide, loads=()):
    share = parts[0].shape[0]
    loaded = []
    crossed = [swap(p, tall, wide, 0, i // 2 + 1) for i, p in enumerate(parts[tall:])]
    if loads:
        *copy, token = load(parts[0], loads[0])
        loaded += copy
        crossed[0] = tie([crossed[0]], [token])
    total = None
    for which, group in enumerate(sum_order(tall)):
        for place, kz in enumerate(group):
            lane = parts[kz].astype(f32)
            for ky in range(1, wide):
                other = crossed[2 * (ky - 1) + which]
                lane = lane + other[place * share : (place + 1) * share].astype(f32)
            if kz:
                sent = lane.astype(bf16)
                lane = swap(sent, tall, wide, kz, 0)
                if loads and kz == 1:
                    *copy, token = load(sent, loads[1])
                    loaded += copy
                    lane = tie([lane], [token])
                lane = lane.astype(f32)
            total = lane if total is None else total + lane
    return (total, *loaded) if loads else total


def dot(a, b):
    return jnp.dot(a, b, preferred_element_type=f32)


def from_hbm(weight):
    return pltpu.with_memory_space_constraint(weight, pltpu.HBM)


def fetched(weight):
    return pltpu.with_memory_space_constraint(weight, pltpu.VMEM)


def kernel_call(body, outs, args, scratch=(), limit=14, flops=0, specs=None):
    return pl.pallas_call(
        body,
        out_shape=[jax.ShapeDtypeStruct(s, d) for s, d in outs],
        in_specs=specs or [VMEM] * len(args),
        out_specs=[VMEM] * len(outs),
        scratch_shapes=list(scratch),
        compiler_params=pltpu.CompilerParams(vmem_limit_bytes=limit << 20),
        cost_estimate=pl.CostEstimate(flops=flops, bytes_accessed=1 << 20, transcendentals=0),
    )(*args)


def load_body(count, *refs):
    sources, copies, sems = refs[1 : 1 + count], refs[1 + count : -2], refs[-1]
    moves = [
        pltpu.make_async_copy(a, b, sems.at[i]) for i, (a, b) in enumerate(zip(sources, copies))
    ]
    for move in moves:
        move.start()
    for move in moves:
        move.wait()
    refs[-2][...] = jnp.zeros_like(refs[-2])


def load(after, *arrays):
    size = sum(a.size * a.dtype.itemsize for a in arrays)
    *copies, token = pl.pallas_call(
        functools.partial(load_body, len(arrays)),
        out_shape=[pltpu.VMEM(a.shape, a.dtype) for a in arrays]
        + [jax.ShapeDtypeStruct((8, 128), f32)],
        in_specs=[pl.BlockSpec(memory_space=pl.ANY)] * (1 + len(arrays)),
        out_specs=[VMEM] * (1 + len(arrays)),
        scratch_shapes=[pltpu.SemaphoreType.DMA((len(arrays),))],
        compiler_params=pltpu.CompilerParams(vmem_limit_bytes=2 << 20),
        cost_estimate=pl.CostEstimate(flops=0, bytes_accessed=2 * size, transcendentals=0),
    )(after, *[from_hbm(a) for a in arrays])
    return [fetched(c) for c in copies] + [token]


def tile_of(width, most):
    return width if width <= most else most


def iota(shape, axis):
    return lax.broadcasted_iota(i32, shape, axis).astype(f32)


def pick(onehot, values):
    return dot(onehot, values).astype(values.dtype)


def send_body(me, routed_in, activations_in, outgoing, routed, activations, sems):
    first_move = pltpu.make_async_copy(routed_in, routed, sems.at[0])
    second_move = pltpu.make_async_copy(activations_in, activations, sems.at[1])
    first_move.start()
    second_move.start()
    first_move.wait()
    capacity, tokens, total = outgoing.shape[0], activations.shape[0], routed.shape[1]
    low = (me[0] * tokens).astype(f32)
    where = routed[...].astype(f32)
    first = jnp.sum(jnp.where(where < low, 1.0, 0.0), axis=1, keepdims=True)
    here = (where >= low) & (where < low + tokens)
    slot = jnp.where(here, iota((1, total), 1) - first, -1.0)
    hit = slot == iota((capacity, total), 0)
    token = jnp.sum(jnp.where(hit, where - low + 1.0, 0.0), axis=1, keepdims=True) - 1.0
    onehot = jnp.where(token == iota((capacity, tokens), 1), 1.0, 0.0).astype(bf16)
    second_move.wait()
    width = activations.shape[1]
    tile = tile_of(width, 1024)
    for start in range(0, width, tile):
        span = slice(start, start + tile)
        outgoing[:, span] = pick(onehot, activations[:, span])


def map_body(tall, wide, tokens, heads_of, me, routed, balance, notes, *outs):
    pick_rows, in_order, columns, unmix, positions = outs
    count, total = tall * wide, routed.shape[1]
    share, capacity = total // count, pick_rows.shape[1] // count
    outbound, inbound = columns.shape[0], unmix.shape[0]
    my_z, my_y = lax.div(me[0], wide), lax.rem(me[0], wide)
    where, owner = routed[...].astype(f32), balance[...].astype(f32)
    lane = iota((1, total), 1)
    slot, place = jnp.zeros((1, total), f32), jnp.zeros((1, total), f32)
    out_base, out_block = notes[:outbound, 0:1], notes[:outbound, 1:2]
    in_base, in_source = notes[:inbound, 2:3], notes[:inbound, 3:4]
    for s in range(count):
        z, y = divmod(s, wide)
        pair = (my_z ^ z) * wide + (my_y ^ y)
        before = where < s * tokens
        first = jnp.sum(jnp.where(before, 1.0, 0.0), axis=1, keepdims=True)
        inside = (where < (s + 1) * tokens) & jnp.logical_not(before)
        start = (pair * capacity).astype(f32)
        slot += jnp.where(inside, lane - first + start, 0.0)
        place += jnp.where(owner == s, (pair * share).astype(f32), 0.0)
        out_base += jnp.where(out_block == s, float(heads_of(s)), 0.0)
        in_base += jnp.where(in_source == s, float(s * (outbound // count)), 0.0)
    mine = owner == iota((count, total), 0)
    earlier = jnp.where(iota((total, total), 0) < iota((total, total), 1), 1.0, 0.0)
    rank = dot(jnp.where(mine, 1.0, 0.0).astype(bf16), earlier.astype(bf16))
    place += jnp.sum(jnp.where(mine, rank, 0.0), axis=0, keepdims=True)
    placed = place == iota((total, total), 0)
    in_order[...] = jnp.where(placed, 1.0, 0.0).astype(bf16)
    at = jnp.sum(jnp.where(placed, where, 0.0), axis=1, keepdims=True)
    positions[...] = jnp.broadcast_to(at, positions.shape)
    slot_at = jnp.sum(jnp.where(placed, slot, 0.0), axis=1, keepdims=True)
    pick_rows[...] = jnp.where(slot_at == iota(pick_rows.shape, 1), 1.0, 0.0).astype(bf16)
    columns[...] = jnp.where(out_base == iota(columns.shape, 1), 1.0, 0.0).astype(bf16)
    unmix[...] = jnp.where(in_base == iota(unmix.shape, 1), 1.0, 0.0).astype(bf16)


def kv_body(count, *refs):
    blocks = refs[:count]
    pick_rows, order, columns, gain, w_key, w_value = refs[count : count + 6]
    normed, own, sent, rows = refs[-4:]
    total, width = normed.shape
    tile = tile_of(width, 512)
    square = jnp.zeros((total, 1), f32)
    for start in range(0, width, tile):
        span = slice(start, start + tile)
        part = dot(pick_rows[...], jnp.concatenate([b[:, span] for b in blocks], axis=0))
        rows[:, span] = part.astype(bf16)
        square += jnp.sum(part * part, axis=1, keepdims=True)
    own[...] = rows[: own.shape[0], :]
    factor = lax.rsqrt(square / width + norm_eps)
    for start in range(0, width, tile):
        span = slice(start, start + tile)
        part = rows[:, span].astype(f32) * factor * gain[:, span]
        normed[:, span] = part.astype(bf16)
    keys = dot(normed[...], w_key[...]).astype(bf16)
    values = dot(normed[...], w_value[...]).astype(bf16)
    both = jnp.concatenate([keys, values], axis=1)
    turned = lax.dot_general(
        columns[...], both, (((1,), (1,)), ((), ())), preferred_element_type=f32
    ).astype(bf16)
    sent[...] = dot(turned, order[...]).astype(bf16)


def query_body(normed, w_query, cosine, sine, query, weight, sems):
    depth = weight.shape[0] // 4
    moves = []
    for index in range(4):
        piece = pl.ds(index * depth, depth)
        moves.append(
            pltpu.make_async_copy(w_query.at[piece], weight.at[piece], sems.at[index])
        )
        moves[-1].start()
    raw = jnp.zeros(query.shape, f32)
    for index, move in enumerate(moves):
        move.wait()
        piece = slice(index * depth, (index + 1) * depth)
        raw += dot(normed[:, piece], weight[piece, :])
    for head in range(query.shape[1] // HEAD_DIM):
        span = slice(head * HEAD_DIM, (head + 1) * HEAD_DIM)
        one = raw[:, span]
        turned = one * cosine[...] + pltpu.roll(one, HEAD_DIM // 2, 1) * sine[...]
        query[:, span] = turned.astype(bf16)


def attend_body(plane, kv_local, *refs):
    arrived, query, unmix, cosine, sine, key_pos, query_pos, w_output = refs[:8]
    parts, (heads_out, weight, sems) = refs[8:-3], refs[-3:]
    width = weight.shape[1] // 4
    moves = []
    for index in range(4):
        piece = pl.ds(index * width, width)
        moves.append(
            pltpu.make_async_copy(w_output.at[:, piece], weight.at[:, piece], sems.at[index])
        )
        moves[-1].start()
    half = HEAD_DIM // 2
    heads = query.shape[1] // HEAD_DIM
    both = dot(unmix[...], arrived[...])
    allowed = key_pos[...].astype(f32) <= query_pos[:, 0:1]
    for group in range(kv_local):
        base = group * HEAD_DIM
        first, second = both[base : base + half], both[base + half : base + HEAD_DIM]
        keys = jnp.concatenate(
            [first * cosine[...] - second * sine[...], second * cosine[...] + first * sine[...]],
            axis=0,
        ).astype(bf16)
        base += kv_local * HEAD_DIM
        values = both[base : base + HEAD_DIM].astype(bf16)
        for head in range(group * heads // kv_local, (group + 1) * heads // kv_local):
            span = slice(head * HEAD_DIM, (head + 1) * HEAD_DIM)
            scores = dot(query[:, span], keys) * HEAD_DIM ** (-0.5)
            scores = jnp.where(allowed, scores, -1e30)
            weights = jnp.exp(scores - jnp.max(scores, axis=1, keepdims=True))
            probs = (weights / jnp.sum(weights, axis=1, keepdims=True)).astype(bf16)
            heads_out[:, span] = lax.dot_general(
                probs, values, (((1,), (1,)), ((), ())), preferred_element_type=f32
            ).astype(bf16)
    spread(heads_out, weight, parts, plane, moves)


def spread(left, weight, parts, plane, moves=()):
    width = weight.shape[1]
    tile = tile_of(width, 512)
    for start in range(0, width, tile):
        if moves and start % (width // len(moves)) == 0:
            moves[start // (width // len(moves))].wait()
        span = slice(start, start + tile)
        product = dot(left[...], weight[:, span]).astype(bf16)
        store_parts(parts, *plane, span, product)


def mlp_body(plane, *refs):
    count = plane[0] * plane[1]
    blocks, (w_gate, w_up, w_down) = refs[:count], refs[count : count + 3]
    parts, (piece, inner) = refs[count + 3 : -2], refs[-2:]
    share = blocks[0].shape[0]
    for index, block in enumerate(blocks):
        piece[index * share : (index + 1) * share, :] = block[...]
    width = w_gate.shape[1]
    tile = tile_of(width, 256)
    for start in range(0, width, tile):
        span = slice(start, start + tile)
        gate = dot(piece[...], w_gate[:, span])
        upward = dot(piece[...], w_up[:, span])
        inner[:, span] = (gate / (1.0 + jnp.exp(-gate)) * upward).astype(bf16)
    spread(inner, w_down, parts, plane)


def on_device(
    activations,
    routed,
    balance,
    w_query,
    w_key,
    w_value,
    w_output,
    attn_gain,
    mlp_gain,
    w_gate,
    w_up,
    w_down,
    w_router,
):
    count = lax.axis_size("ctx")
    plane = tall, wide = plane_of(count)
    me = lax.axis_index("ctx").astype(i32).reshape(1)
    tokens, model = activations.shape
    total = routed.shape[0]
    share = total // count
    capacity = 2 * share
    local_heads = w_query.shape[1] // HEAD_DIM
    group_size = HEADS // KV_HEADS
    kv_local = max(1, local_heads // group_size)
    key_cols = w_key.shape[1]
    depth = key_cols // KV_HEADS
    scalar = pl.BlockSpec(memory_space=pltpu.SMEM)
    in_hbm = pl.BlockSpec(memory_space=pl.ANY)
    routed, balance = routed.reshape(1, total), balance.reshape(1, total)

    (outgoing,) = kernel_call(
        send_body,
        [((capacity, model), bf16)],
        [me, from_hbm(routed), from_hbm(activations)],
        [
            pltpu.VMEM(routed.shape, i32),
            pltpu.VMEM(activations.shape, bf16),
            pltpu.SemaphoreType.DMA((2,)),
        ],
        specs=[scalar, in_hbm, in_hbm],
        flops=2 * capacity * tokens * model,
    )
    attn_gain, w_key, w_value, token_1 = load(
        outgoing, attn_gain.reshape(1, model), w_key, w_value
    )

    each = kv_local * 2 * depth
    notes = np.zeros((max(count * each, 2 * kv_local * HEAD_DIM), 4), np.float32)
    block, local, side, entry = np.indices((count, kv_local, 2, depth)).reshape(4, -1)
    notes[: count * each, 0] = side * key_cols + entry * KV_HEADS + local
    notes[: count * each, 1] = block
    side, local, source, entry = np.indices((2, kv_local, count, depth)).reshape(4, -1)
    notes[: 2 * kv_local * HEAD_DIM, 2] = (local * 2 + side) * depth + entry
    notes[: 2 * kv_local * HEAD_DIM, 3] = source
    pick_rows, in_order, columns, unmix, positions = kernel_call(
        functools.partial(
            map_body, tall, wide, tokens, lambda peer: peer * local_heads // group_size
        ),
        [
            ((total, count * capacity), bf16),
            ((total, total), bf16),
            ((count * each, 2 * key_cols), bf16),
            ((2 * kv_local * HEAD_DIM, count * each), bf16),
            ((total, HEAD_DIM // 2), f32),
        ],
        [me, routed, balance, notes],
        specs=[scalar, VMEM, VMEM, VMEM],
    )
    blocks = gather_rows(outgoing, tall, wide, [token_1, positions])

    half = HEAD_DIM // 2
    steps_f = jnp.arange(half, dtype=f32)
    freqs = jnp.exp(-jnp.log(f32(rope_base)) * (2.0 * steps_f / HEAD_DIM))
    q_angles = positions * freqs[None, :]
    q_cos, q_sin = jnp.cos(q_angles), jnp.sin(q_angles)
    q_cos = jnp.concatenate([q_cos, q_cos], axis=1)
    q_sin = jnp.concatenate([-q_sin, q_sin], axis=1)
    k_angles = freqs[:, None] * routed.astype(f32)
    k_cos, k_sin = jnp.cos(k_angles), jnp.sin(k_angles)

    normed, own, sent = kernel_call(
        functools.partial(kv_body, count),
        [((total, model), bf16), ((share, model), bf16), ((count * each, total), bf16)],
        [*blocks, pick_rows, in_order, columns, attn_gain, w_key, w_value],
        [pltpu.VMEM((total, model), bf16)],
        flops=2 * total * model * 512,
    )
    arrived = lax.all_to_all(sent.reshape(count, each, total), "ctx", 0, 0, tiled=True)
    arrived = arrived.reshape(count * each, total)
    heads_wide = local_heads * HEAD_DIM
    (query,) = kernel_call(
        query_body,
        [((total, heads_wide), bf16)],
        [normed, from_hbm(w_query), q_cos, q_sin],
        [pltpu.VMEM((model, heads_wide), bf16), pltpu.SemaphoreType.DMA((4,))],
        flops=2 * total * model * heads_wide,
        specs=[VMEM, in_hbm, VMEM, VMEM],
    )
    part_shapes = sum_shapes(tall, wide, share, model)
    attn_parts = kernel_call(
        functools.partial(attend_body, plane, kv_local),
        part_shapes,
        [arrived, query, unmix, k_cos, k_sin, routed, positions, from_hbm(w_output)],
        [
            pltpu.VMEM((total, heads_wide), bf16),
            pltpu.VMEM((heads_wide, model), bf16),
            pltpu.SemaphoreType.DMA((4,)),
        ],
        flops=2 * total * model * heads_wide,
        specs=[VMEM] * 7 + [in_hbm],
    )
    attn_own, w_down, w_gate = scatter_sum(attn_parts, tall, wide, [w_down, w_gate])
    own_rows = own.astype(f32)
    hidden = own_rows + attn_own
    mean_sq = jnp.mean(hidden * hidden, axis=-1, keepdims=True)
    mnorm = (hidden * lax.rsqrt(mean_sq + norm_eps) * mlp_gain).astype(bf16)
    pieces = gather_blocks(mnorm, tall, wide)
    w_up, _ = load(mnorm, w_up)
    hidden_units = w_gate.shape[1]
    mlp_parts = kernel_call(
        functools.partial(mlp_body, plane),
        part_shapes,
        [*pieces, w_gate, w_up, w_down],
        [pltpu.VMEM((total, model), bf16), pltpu.VMEM((total, hidden_units), bf16)],
        flops=6 * total * model * hidden_units,
    )
    mlp_own = scatter_sum(mlp_parts, tall, wide)
    router_score = jnp.sum(own_rows * w_router[None, :], axis=1, keepdims=True)
    return (own_rows + router_score * (attn_own + mlp_own)).astype(bf16)


def solution(mesh):
    in_specs = (
        P(("dp", "ctx"), None),
        P("dp"),
        P("dp"),
        P(None, "ctx"),
        P(None, "ctx"),
        P(None, "ctx"),
        P("ctx", None),
        P(),
        P(),
        P(None, "ctx"),
        P(None, "ctx"),
        P("ctx", None),
        P(),
    )
    out_specs = P(("dp", "ctx"), None)
    return jax.shard_map(
        on_device, mesh=mesh, in_specs=in_specs, out_specs=out_specs, check_vma=False
    )
```

```python
import functools

import jax
import jax.numpy as jnp
import numpy as np
from jax import lax
from jax.experimental import pallas as pl
from jax.experimental.pallas import tpu as pltpu
from jax.sharding import PartitionSpec as P

HEADS = 32
KV_HEADS = 8
HEAD_DIM = 128

rope_base = 500000.0
norm_eps = 1e-05

bf16, f32, i32 = jnp.bfloat16, jnp.float32, jnp.int32
VMEM = pl.BlockSpec(memory_space=pltpu.VMEM)


def plane_of(count):
    wide = max(y for y in range(1, count + 1) if count % y == 0 and 2 * y * y <= max(count, 2))
    return count // wide, wide


def shift(block, tall, wide, dz, dy, keep=None):
    pairs = [
        (z * wide + y, (z + dz) % tall * wide + (y + dy) % wide)
        for z in range(tall)
        for y in range(wide)
        if keep is None or keep(z)
    ]
    return lax.ppermute(block, "ctx", pairs)


def tie_body(count, *refs):
    total = refs[0][...]
    for ref in refs[1:count]:
        total = total + ref[...]
    refs[-1][...] = total


def tie(blocks, tokens):
    return kernel_call(
        functools.partial(tie_body, len(blocks)),
        [(blocks[0].shape, blocks[0].dtype)],
        [*blocks, *tokens],
        specs=[VMEM] * len(blocks) + [pl.BlockSpec(memory_space=pl.ANY)] * len(tokens),
    )[0]


def gather_rows(block, tall, wide, tokens):
    blocks = {(0, 0): block}
    for dz in range(1, tall):
        if tall != 4 or dz != 2:
            blocks[dz, 0] = shift(block, tall, wide, dz, 0)
    for dy in range(1, wide):
        blocks[0, dy] = shift(block, tall, wide, 0, dy)
        if tall == 4:
            blocks[3, dy] = shift(blocks[3, 0], tall, wide, 0, dy)
    early = [b for (_, dy), b in blocks.items() if dy]
    blocks[1, 0] = tie([blocks[1, 0]], [*tokens, *early])
    if tall == 4:
        up = shift(blocks[1, 0], tall, wide, 1, 0, lambda z: z in (1, 2))
        down = shift(blocks[3, 0], tall, wide, -1, 0, lambda z: z in (1, 2))
        blocks[2, 0] = up + down
    for dz in range(1, tall):
        for dy in range(1, wide):
            if (dz, dy) not in blocks:
                blocks[dz, dy] = shift(blocks[dz, 0], tall, wide, 0, dy)
    return [blocks[dz, dy] for dz in range(tall) for dy in range(wide)]


def pack_body(tall, *refs):
    wide = len(refs) - tall
    each = refs[0].shape[0] // tall
    for dz in range(tall):
        values = [ref[...].astype(f32)[dz * each : (dz + 1) * each] for ref in refs[:wide]]
        refs[wide + dz][...] = jnp.concatenate(values, axis=0).astype(bf16)


def exchange(parts, tall, wide):
    shape = ((parts[0].shape[0] // tall * wide, parts[0].shape[1]), bf16)
    crossed = [parts[0]] + [shift(parts[dy], tall, wide, 0, dy) for dy in range(1, wide)]
    packed = kernel_call(functools.partial(pack_body, tall), [shape] * tall, crossed)
    return [packed[0]] + [shift(packed[dz], tall, wide, dz, 0) for dz in range(1, tall)]


def gather_blocks(block, tall, wide):
    blocks = {(dz, 0): shift(block, tall, wide, dz, 0) if dz else block for dz in range(tall)}
    for dz in range(tall):
        for dy in range(1, wide):
            blocks[dz, dy] = shift(blocks[dz, 0], tall, wide, 0, dy)
    return [blocks[dz, dy] for dz in range(tall) for dy in range(wide)]


def sum_order(tall):
    order = [tall // 2, *range(1, tall // 2), *range(tall // 2 + 1, tall), 0]
    return order[: tall // 2], order[tall // 2 :]


def sum_shapes(tall, wide, share, model):
    kept = [((share, model), bf16)] * tall
    return kept + [((tall // 2 * share, model), bf16)] * (2 * (wide - 1))


def store_parts(parts, tall, wide, span, product, back):
    share = parts[0].shape[0]
    sign = -1 if back else 1

    def rows(dz, dy):
        at = sign * dz % tall * wide + sign * dy % wide
        return product[at * share : (at + 1) * share, :]

    for dz in range(tall):
        parts[dz][:, span] = rows(dz, 0)
    for dy in range(1, wide):
        for which, group in enumerate(sum_order(tall)):
            out = parts[tall + 2 * (dy - 1) + which]
            for place, dz in enumerate(group):
                out[place * share : (place + 1) * share, span] = rows(dz, dy)


def scatter_sum(parts, tall, wide, loads=()):
    share = parts[0].shape[0]
    loaded = []
    crossed = [shift(p, tall, wide, 0, i // 2 + 1) for i, p in enumerate(parts[tall:])]
    if loads:
        *copy, token = load(parts[0], loads[0])
        loaded += copy
        crossed[1] = tie([crossed[1]], [token])
    total = None
    for which, group in enumerate(sum_order(tall)):
        for place, dz in enumerate(group):
            lane = parts[dz].astype(f32)
            for dy in range(1, wide):
                other = crossed[2 * (dy - 1) + which]
                lane = lane + other[place * share : (place + 1) * share].astype(f32)
            if dz:
                sent = lane.astype(bf16)
                lane = shift(sent, tall, wide, dz, 0)
                if len(loads) > 1 and dz == tall - 1:
                    *copy, token = load(sent, loads[1])
                    loaded += copy
                    lane = tie([lane], [token])
                lane = lane.astype(f32)
            total = lane if total is None else total + lane
    return (total, *loaded) if loads else total


def dot(a, b):
    return jnp.dot(a, b, preferred_element_type=f32)


def from_hbm(weight):
    return pltpu.with_memory_space_constraint(weight, pltpu.HBM)


def fetched(weight):
    return pltpu.with_memory_space_constraint(weight, pltpu.VMEM)


def kernel_call(body, outs, args, scratch=(), limit=14, flops=0, specs=None):
    return pl.pallas_call(
        body,
        out_shape=[jax.ShapeDtypeStruct(s, d) for s, d in outs],
        in_specs=specs or [VMEM] * len(args),
        out_specs=[VMEM] * len(outs),
        scratch_shapes=list(scratch),
        compiler_params=pltpu.CompilerParams(vmem_limit_bytes=limit << 20),
        cost_estimate=pl.CostEstimate(flops=flops, bytes_accessed=1 << 20, transcendentals=0),
    )(*args)


def load_body(count, *refs):
    sources, copies, sems = refs[1 : 1 + count], refs[1 + count : -2], refs[-1]
    moves = [
        pltpu.make_async_copy(a, b, sems.at[i]) for i, (a, b) in enumerate(zip(sources, copies))
    ]
    for move in moves:
        move.start()
    for move in moves:
        move.wait()
    refs[-2][...] = jnp.zeros_like(refs[-2])


def load(after, *arrays):
    size = sum(a.size * a.dtype.itemsize for a in arrays)
    *copies, token = pl.pallas_call(
        functools.partial(load_body, len(arrays)),
        out_shape=[pltpu.VMEM(a.shape, a.dtype) for a in arrays]
        + [jax.ShapeDtypeStruct((8, 128), f32)],
        in_specs=[pl.BlockSpec(memory_space=pl.ANY)] * (1 + len(arrays)),
        out_specs=[VMEM] * (1 + len(arrays)),
        scratch_shapes=[pltpu.SemaphoreType.DMA((len(arrays),))],
        compiler_params=pltpu.CompilerParams(vmem_limit_bytes=2 << 20),
        cost_estimate=pl.CostEstimate(flops=0, bytes_accessed=2 * size, transcendentals=0),
    )(after, *[from_hbm(a) for a in arrays])
    return [fetched(c) for c in copies] + [token]


def tile_of(width, most):
    return width if width <= most else most


def iota(shape, axis):
    return lax.broadcasted_iota(i32, shape, axis).astype(f32)


def pick(onehot, values):
    return dot(onehot, values).astype(values.dtype)


def send_body(me, routed_in, activations_in, outgoing, routed, activations, sems):
    first_move = pltpu.make_async_copy(routed_in, routed, sems.at[0])
    second_move = pltpu.make_async_copy(activations_in, activations, sems.at[1])
    first_move.start()
    second_move.start()
    first_move.wait()
    capacity, tokens, total = outgoing.shape[0], activations.shape[0], routed.shape[1]
    low = (me[0] * tokens).astype(f32)
    where = routed[...].astype(f32)
    first = jnp.sum(jnp.where(where < low, 1.0, 0.0), axis=1, keepdims=True)
    here = (where >= low) & (where < low + tokens)
    slot = jnp.where(here, iota((1, total), 1) - first, -1.0)
    hit = slot == iota((capacity, total), 0)
    token = jnp.sum(jnp.where(hit, where - low + 1.0, 0.0), axis=1, keepdims=True) - 1.0
    onehot = jnp.where(token == iota((capacity, tokens), 1), 1.0, 0.0).astype(bf16)
    second_move.wait()
    width = activations.shape[1]
    tile = tile_of(width, 1024)
    for start in range(0, width, tile):
        span = slice(start, start + tile)
        outgoing[:, span] = pick(onehot, activations[:, span])


def map_body(tall, wide, tokens, heads_of, me, routed, balance, notes, *outs):
    pick_rows, in_order, columns, unmix, positions = outs
    count, total = tall * wide, routed.shape[1]
    share, capacity = total // count, pick_rows.shape[1] // count
    outbound, inbound = columns.shape[0], unmix.shape[0]
    my_z, my_y = lax.div(me[0], wide), lax.rem(me[0], wide)
    where, owner = routed[...].astype(f32), balance[...].astype(f32)
    lane = iota((1, total), 1)
    slot, place = jnp.zeros((1, total), f32), jnp.zeros((1, total), f32)
    out_base, out_block = notes[:outbound, 0:1], notes[:outbound, 1:2]
    in_base, in_source = notes[:inbound, 2:3], notes[:inbound, 3:4]
    for s in range(count):
        z, y = divmod(s, wide)
        from_block = lax.rem(my_z - z + tall, tall) * wide + lax.rem(my_y - y + wide, wide)
        to_block = lax.rem(z - my_z + tall, tall) * wide + lax.rem(y - my_y + wide, wide)
        peer = lax.rem(my_z + z, tall) * wide + lax.rem(my_y + y, wide)
        before = where < s * tokens
        first = jnp.sum(jnp.where(before, 1.0, 0.0), axis=1, keepdims=True)
        inside = (where < (s + 1) * tokens) & jnp.logical_not(before)
        start = (from_block * capacity).astype(f32)
        slot += jnp.where(inside, lane - first + start, 0.0)
        place += jnp.where(owner == s, (to_block * share).astype(f32), 0.0)
        out_base += jnp.where(out_block == y * tall + z, heads_of(peer).astype(f32), 0.0)
        in_base += jnp.where(in_source == s, (from_block * (outbound // count)).astype(f32), 0.0)
    mine = owner == iota((count, total), 0)
    earlier = jnp.where(iota((total, total), 0) < iota((total, total), 1), 1.0, 0.0)
    rank = dot(jnp.where(mine, 1.0, 0.0).astype(bf16), earlier.astype(bf16))
    place += jnp.sum(jnp.where(mine, rank, 0.0), axis=0, keepdims=True)
    placed = place == iota((total, total), 0)
    in_order[...] = jnp.where(placed, 1.0, 0.0).astype(bf16)
    at = jnp.sum(jnp.where(placed, where, 0.0), axis=1, keepdims=True)
    positions[...] = jnp.broadcast_to(at, positions.shape)
    slot_at = jnp.sum(jnp.where(placed, slot, 0.0), axis=1, keepdims=True)
    pick_rows[...] = jnp.where(slot_at == iota(pick_rows.shape, 1), 1.0, 0.0).astype(bf16)
    columns[...] = jnp.where(out_base == iota(columns.shape, 1), 1.0, 0.0).astype(bf16)
    unmix[...] = jnp.where(in_base == iota(unmix.shape, 1), 1.0, 0.0).astype(bf16)


def kv_body(count, extra, *refs):
    blocks = refs[:count]
    pick_rows, order, columns, gain, w_key, w_value = refs[count : count + 6]
    wide = len(refs) - count - 9 - extra
    normed, own, *sent, rows = refs[-3 - wide :]
    total, width = normed.shape
    tile = tile_of(width, 512)
    square = jnp.zeros((total, 1), f32)
    for start in range(0, width, tile):
        span = slice(start, start + tile)
        part = dot(pick_rows[...], jnp.concatenate([b[:, span] for b in blocks], axis=0))
        rows[:, span] = part.astype(bf16)
        square += jnp.sum(part * part, axis=1, keepdims=True)
    own[...] = rows[: own.shape[0], :]
    factor = lax.rsqrt(square / width + norm_eps)
    for start in range(0, width, tile):
        span = slice(start, start + tile)
        part = rows[:, span].astype(f32) * factor * gain[:, span]
        normed[:, span] = part.astype(bf16)
    keys = dot(normed[...], w_key[...]).astype(bf16)
    values = dot(normed[...], w_value[...]).astype(bf16)
    both = jnp.concatenate([keys, values], axis=1)
    turned = lax.dot_general(
        columns[...], both, (((1,), (1,)), ((), ())), preferred_element_type=f32
    ).astype(bf16)
    turned = dot(turned, order[...])
    each = turned.shape[0] // wide
    for dy in range(wide):
        sent[dy][...] = turned[dy * each : (dy + 1) * each].astype(bf16)


def query_body(normed, w_query, cosine, sine, query):
    raw = dot(normed[...], w_query[...])
    for head in range(query.shape[1] // HEAD_DIM):
        span = slice(head * HEAD_DIM, (head + 1) * HEAD_DIM)
        one = raw[:, span]
        turned = one * cosine[...] + pltpu.roll(one, HEAD_DIM // 2, 1) * sine[...]
        query[:, span] = turned.astype(bf16)


def attend_body(plane, kv_local, *refs):
    tall = plane[0]
    arrived, rest = refs[:tall], refs[tall:]
    query, unmix, cosine, sine, key_pos, query_pos, w_output = rest[:7]
    parts, heads_out = rest[7:-1], rest[-1]
    half = HEAD_DIM // 2
    heads = query.shape[1] // HEAD_DIM
    mixed = jnp.concatenate([a[...].astype(f32) for a in arrived], axis=0).astype(bf16)
    both = dot(unmix[...], mixed)
    allowed = key_pos[...].astype(f32) <= query_pos[:, 0:1]
    for group in range(kv_local):
        base = group * HEAD_DIM
        first, second = both[base : base + half], both[base + half : base + HEAD_DIM]
        keys = jnp.concatenate(
            [first * cosine[...] - second * sine[...], second * cosine[...] + first * sine[...]],
            axis=0,
        ).astype(bf16)
        base += kv_local * HEAD_DIM
        values = both[base : base + HEAD_DIM].astype(bf16)
        for head in range(group * heads // kv_local, (group + 1) * heads // kv_local):
            span = slice(head * HEAD_DIM, (head + 1) * HEAD_DIM)
            scores = dot(query[:, span], keys) * HEAD_DIM ** (-0.5)
            scores = jnp.where(allowed, scores, -1e30)
            weights = jnp.exp(scores - jnp.max(scores, axis=1, keepdims=True))
            probs = (weights / jnp.sum(weights, axis=1, keepdims=True)).astype(bf16)
            heads_out[:, span] = lax.dot_general(
                probs, values, (((1,), (1,)), ((), ())), preferred_element_type=f32
            ).astype(bf16)
    spread(heads_out, w_output, parts, plane, False)


def spread(left, weight, parts, plane, back):
    width = weight.shape[1]
    tile = tile_of(width, 512)
    for start in range(0, width, tile):
        span = slice(start, start + tile)
        product = dot(left[...], weight[:, span]).astype(bf16)
        store_parts(parts, *plane, span, product, back)


def mlp_body(plane, *refs):
    count = plane[0] * plane[1]
    blocks, (w_gate, w_up, w_down) = refs[:count], refs[count : count + 3]
    parts, (piece, inner) = refs[count + 3 : -2], refs[-2:]
    share = blocks[0].shape[0]
    for index, block in enumerate(blocks):
        piece[index * share : (index + 1) * share, :] = block[...]
    width = w_gate.shape[1]
    tile = tile_of(width, 256)
    for start in range(0, width, tile):
        span = slice(start, start + tile)
        gate = dot(piece[...], w_gate[:, span])
        upward = dot(piece[...], w_up[:, span])
        inner[:, span] = (gate / (1.0 + jnp.exp(-gate)) * upward).astype(bf16)
    spread(inner, w_down, parts, plane, True)


def on_device(
    activations,
    routed,
    balance,
    w_query,
    w_key,
    w_value,
    w_output,
    attn_gain,
    mlp_gain,
    w_gate,
    w_up,
    w_down,
    w_router,
):
    count = lax.axis_size("ctx")
    plane = tall, wide = plane_of(count)
    me = lax.axis_index("ctx").astype(i32).reshape(1)
    tokens, model = activations.shape
    total = routed.shape[0]
    share = total // count
    capacity = 2 * share
    local_heads = w_query.shape[1] // HEAD_DIM
    group_size = HEADS // KV_HEADS
    kv_local = max(1, local_heads // group_size)
    key_cols = w_key.shape[1]
    depth = key_cols // KV_HEADS
    scalar = pl.BlockSpec(memory_space=pltpu.SMEM)
    in_hbm = pl.BlockSpec(memory_space=pl.ANY)
    routed, balance = routed.reshape(1, total), balance.reshape(1, total)

    (outgoing,) = kernel_call(
        send_body,
        [((capacity, model), bf16)],
        [me, from_hbm(routed), from_hbm(activations)],
        [
            pltpu.VMEM(routed.shape, i32),
            pltpu.VMEM(activations.shape, bf16),
            pltpu.SemaphoreType.DMA((2,)),
        ],
        specs=[scalar, in_hbm, in_hbm],
        flops=2 * capacity * tokens * model,
    )
    attn_gain, w_key, w_value, w_query, token_1 = load(
        outgoing, attn_gain.reshape(1, model), w_key, w_value, w_query
    )

    each = kv_local * 2 * depth
    notes = np.zeros((max(count * each, 2 * kv_local * HEAD_DIM), 4), np.float32)
    block, local, side, entry = np.indices((count, kv_local, 2, depth)).reshape(4, -1)
    notes[: count * each, 0] = side * key_cols + entry * KV_HEADS + local
    notes[: count * each, 1] = block
    side, local, source, entry = np.indices((2, kv_local, count, depth)).reshape(4, -1)
    notes[: 2 * kv_local * HEAD_DIM, 2] = (local * 2 + side) * depth + entry
    notes[: 2 * kv_local * HEAD_DIM, 3] = source
    pick_rows, in_order, columns, unmix, positions = kernel_call(
        functools.partial(
            map_body, tall, wide, tokens, lambda peer: lax.div(peer * local_heads, group_size)
        ),
        [
            ((total, count * capacity), bf16),
            ((total, total), bf16),
            ((count * each, 2 * key_cols), bf16),
            ((2 * kv_local * HEAD_DIM, count * each), bf16),
            ((total, HEAD_DIM // 2), f32),
        ],
        [me, routed, balance, notes],
        specs=[scalar, VMEM, VMEM, VMEM],
    )
    blocks = gather_rows(outgoing, tall, wide, [token_1, positions])
    near = blocks[2 * wide]
    w_output, *token_2 = load(near, w_output)
    w_gate, *token_3 = load(near, w_gate)
    w_up, *token_4 = load(near, w_up)
    loaded = token_2 + token_3 + token_4

    half = HEAD_DIM // 2
    steps_f = jnp.arange(half, dtype=f32)
    freqs = jnp.exp(-jnp.log(f32(rope_base)) * (2.0 * steps_f / HEAD_DIM))
    q_angles = positions * freqs[None, :]
    q_cos, q_sin = jnp.cos(q_angles), jnp.sin(q_angles)
    q_cos = jnp.concatenate([q_cos, q_cos], axis=1)
    q_sin = jnp.concatenate([-q_sin, q_sin], axis=1)
    k_angles = freqs[:, None] * routed.astype(f32)
    k_cos, k_sin = jnp.cos(k_angles), jnp.sin(k_angles)

    normed, own, *sent = kernel_call(
        functools.partial(kv_body, count, len(loaded)),
        [((total, model), bf16), ((share, model), bf16)] + [((tall * each, total), bf16)] * wide,
        [*blocks, pick_rows, in_order, columns, attn_gain, w_key, w_value, *loaded],
        [pltpu.VMEM((total, model), bf16)],
        flops=2 * total * model * 512,
    )
    arrived = exchange(sent, tall, wide)
    heads_wide = local_heads * HEAD_DIM
    (query,) = kernel_call(
        query_body,
        [((total, heads_wide), bf16)],
        [normed, w_query, q_cos, q_sin],
        flops=2 * total * model * heads_wide,
    )
    part_shapes = sum_shapes(tall, wide, share, model)
    attn_parts = kernel_call(
        functools.partial(attend_body, plane, kv_local),
        part_shapes,
        [*arrived, query, unmix, k_cos, k_sin, routed, positions, w_output],
        [pltpu.VMEM((total, heads_wide), bf16)],
        flops=2 * total * model * heads_wide,
    )
    attn_own, w_down = scatter_sum(attn_parts, tall, wide, [w_down])
    own_rows = own.astype(f32)
    hidden = own_rows + attn_own
    mean_sq = jnp.mean(hidden * hidden, axis=-1, keepdims=True)
    mnorm = (hidden * lax.rsqrt(mean_sq + norm_eps) * mlp_gain).astype(bf16)
    pieces = gather_blocks(mnorm, tall, wide)
    hidden_units = w_gate.shape[1]
    mlp_parts = kernel_call(
        functools.partial(mlp_body, plane),
        part_shapes,
        [*pieces, w_gate, w_up, w_down],
        [pltpu.VMEM((total, model), bf16), pltpu.VMEM((total, hidden_units), bf16)],
        flops=6 * total * model * hidden_units,
    )
    mlp_own = scatter_sum(mlp_parts, tall, wide)
    router_score = jnp.sum(own_rows * w_router[None, :], axis=1, keepdims=True)
    return (own_rows + router_score * (attn_own + mlp_own)).astype(bf16)


def solution(mesh):
    in_specs = (
        P(("dp", "ctx"), None),
        P("dp"),
        P("dp"),
        P(None, "ctx"),
        P(None, "ctx"),
        P(None, "ctx"),
        P("ctx", None),
        P(),
        P(),
        P(None, "ctx"),
        P(None, "ctx"),
        P("ctx", None),
        P(),
    )
    out_specs = P(("dp", "ctx"), None)
    return jax.shard_map(
        on_device, mesh=mesh, in_specs=in_specs, out_specs=out_specs, check_vma=False
    )
```

```python
import functools

import jax
import jax.numpy as jnp
import numpy as np
from jax import lax
from jax.experimental import pallas as pl
from jax.experimental.pallas import tpu as pltpu
from jax.sharding import PartitionSpec as P

HEADS = 32
KV_HEADS = 8
HEAD_DIM = 128

rope_base = 500000.0
norm_eps = 1e-05

bf16, f32, i32 = jnp.bfloat16, jnp.float32, jnp.int32
VMEM = pl.BlockSpec(memory_space=pltpu.VMEM)


def plane_of(count):
    wide = max(y for y in range(1, count + 1) if count % y == 0 and 2 * y * y <= max(count, 2))
    return count // wide, wide


def shift(block, tall, wide, dz, dy, keep=None):
    pairs = [
        (z * wide + y, (z + dz) % tall * wide + (y + dy) % wide)
        for z in range(tall)
        for y in range(wide)
        if keep is None or keep(z)
    ]
    return lax.ppermute(block, "ctx", pairs)


def tie_body(count, *refs):
    total = refs[0][...]
    for ref in refs[1:count]:
        total = total + ref[...]
    refs[-1][...] = total


def tie(blocks, tokens):
    return kernel_call(
        functools.partial(tie_body, len(blocks)),
        [(blocks[0].shape, blocks[0].dtype)],
        [*blocks, *tokens],
        specs=[VMEM] * len(blocks) + [pl.BlockSpec(memory_space=pl.ANY)] * len(tokens),
    )[0]


def gather_rows(block, tall, wide, tokens):
    blocks = {(0, 0): block}
    for dy in range(1, wide):
        blocks[0, dy] = shift(block, tall, wide, 0, dy)
    first = [*tokens, *(blocks[0, dy] for dy in range(1, wide))]
    for dz in range(tall - 1, 0, -1):
        if tall != 4 or dz != 2:
            blocks[dz, 0] = shift(block, tall, wide, dz, 0)
    blocks[tall - 1, 0] = tie([blocks[tall - 1, 0]], first)
    if tall == 4:
        for dy in range(1, wide):
            blocks[3, dy] = shift(blocks[3, 0], tall, wide, 0, dy)
        up = shift(blocks[1, 0], tall, wide, 1, 0, lambda z: z in (1, 2))
        down = shift(blocks[3, 0], tall, wide, -1, 0, lambda z: z in (1, 2))
        blocks[2, 0] = tie([up, down], [blocks[3, dy] for dy in range(1, wide)])
    for dz in range(1, tall):
        for dy in range(1, wide):
            if (dz, dy) not in blocks:
                blocks[dz, dy] = shift(blocks[dz, 0], tall, wide, 0, dy)
    return [blocks[dz, dy] for dz in range(tall) for dy in range(wide)]


def pack_body(tall, *refs):
    wide = len(refs) - tall
    each = refs[0].shape[0] // tall
    for dz in range(tall):
        values = [ref[...].astype(f32)[dz * each : (dz + 1) * each] for ref in refs[:wide]]
        refs[wide + dz][...] = jnp.concatenate(values, axis=0).astype(bf16)


def exchange(parts, tall, wide):
    shape = ((parts[0].shape[0] // tall * wide, parts[0].shape[1]), bf16)
    crossed = [parts[0]] + [shift(parts[dy], tall, wide, 0, dy) for dy in range(1, wide)]
    packed = kernel_call(functools.partial(pack_body, tall), [shape] * tall, crossed)
    return [packed[0]] + [shift(packed[dz], tall, wide, dz, 0) for dz in range(1, tall)]


def gather_blocks(block, tall, wide):
    blocks = {(dz, 0): shift(block, tall, wide, dz, 0) if dz else block for dz in range(tall)}
    for dz in range(tall):
        for dy in range(1, wide):
            blocks[dz, dy] = shift(blocks[dz, 0], tall, wide, 0, dy)
    return [blocks[dz, dy] for dz in range(tall) for dy in range(wide)]


def sum_order(tall):
    order = [tall // 2, *range(1, tall // 2), *range(tall // 2 + 1, tall), 0]
    return order[: tall // 2], order[tall // 2 :]


def sum_shapes(tall, wide, share, model):
    kept = [((share, model), bf16)] * tall
    return kept + [((tall // 2 * share, model), bf16)] * (2 * (wide - 1))


def store_parts(parts, tall, wide, span, product, back):
    share = parts[0].shape[0]
    sign = -1 if back else 1

    def rows(dz, dy):
        at = sign * dz % tall * wide + sign * dy % wide
        return product[at * share : (at + 1) * share, :]

    for dz in range(tall):
        parts[dz][:, span] = rows(dz, 0)
    for dy in range(1, wide):
        for which, group in enumerate(sum_order(tall)):
            out = parts[tall + 2 * (dy - 1) + which]
            for place, dz in enumerate(group):
                out[place * share : (place + 1) * share, span] = rows(dz, dy)


def scatter_sum(parts, tall, wide, loads=()):
    share = parts[0].shape[0]
    loaded = []
    crossed = [shift(p, tall, wide, 0, i // 2 + 1) for i, p in enumerate(parts[tall:])]
    if loads:
        *copy, token = load(parts[0], loads[0])
        loaded += copy
        crossed[1] = tie([crossed[1]], [token])
    total = None
    for which, group in enumerate(sum_order(tall)):
        for place, dz in enumerate(group):
            lane = parts[dz].astype(f32)
            for dy in range(1, wide):
                other = crossed[2 * (dy - 1) + which]
                lane = lane + other[place * share : (place + 1) * share].astype(f32)
            if dz:
                sent = lane.astype(bf16)
                lane = shift(sent, tall, wide, dz, 0)
                if len(loads) > 1 and dz == tall - 1:
                    *copy, token = load(sent, loads[1])
                    loaded += copy
                    lane = tie([lane], [token])
                lane = lane.astype(f32)
            total = lane if total is None else total + lane
    return (total, *loaded) if loads else total


def dot(a, b):
    return jnp.dot(a, b, preferred_element_type=f32)


def from_hbm(weight):
    return pltpu.with_memory_space_constraint(weight, pltpu.HBM)


def fetched(weight):
    return pltpu.with_memory_space_constraint(weight, pltpu.VMEM)


def kernel_call(body, outs, args, scratch=(), limit=14, flops=0, specs=None):
    return pl.pallas_call(
        body,
        out_shape=[jax.ShapeDtypeStruct(s, d) for s, d in outs],
        in_specs=specs or [VMEM] * len(args),
        out_specs=[VMEM] * len(outs),
        scratch_shapes=list(scratch),
        compiler_params=pltpu.CompilerParams(vmem_limit_bytes=limit << 20),
        cost_estimate=pl.CostEstimate(flops=flops, bytes_accessed=1 << 20, transcendentals=0),
    )(*args)


def load_body(count, *refs):
    sources, copies, sems = refs[1 : 1 + count], refs[1 + count : -2], refs[-1]
    moves = [
        pltpu.make_async_copy(a, b, sems.at[i]) for i, (a, b) in enumerate(zip(sources, copies))
    ]
    for move in moves:
        move.start()
    for move in moves:
        move.wait()
    refs[-2][...] = jnp.zeros_like(refs[-2])


def load(after, *arrays):
    size = sum(a.size * a.dtype.itemsize for a in arrays)
    *copies, token = pl.pallas_call(
        functools.partial(load_body, len(arrays)),
        out_shape=[pltpu.VMEM(a.shape, a.dtype) for a in arrays]
        + [jax.ShapeDtypeStruct((8, 128), f32)],
        in_specs=[pl.BlockSpec(memory_space=pl.ANY)] * (1 + len(arrays)),
        out_specs=[VMEM] * (1 + len(arrays)),
        scratch_shapes=[pltpu.SemaphoreType.DMA((len(arrays),))],
        compiler_params=pltpu.CompilerParams(vmem_limit_bytes=2 << 20),
        cost_estimate=pl.CostEstimate(flops=0, bytes_accessed=2 * size, transcendentals=0),
    )(after, *[from_hbm(a) for a in arrays])
    return [fetched(c) for c in copies] + [token]


def tile_of(width, most):
    return width if width <= most else most


def iota(shape, axis):
    return lax.broadcasted_iota(i32, shape, axis).astype(f32)


def pick(onehot, values):
    return dot(onehot, values).astype(values.dtype)


def send_body(me, routed_in, activations_in, outgoing, routed, activations, sems):
    first_move = pltpu.make_async_copy(routed_in, routed, sems.at[0])
    second_move = pltpu.make_async_copy(activations_in, activations, sems.at[1])
    first_move.start()
    second_move.start()
    first_move.wait()
    capacity, tokens, total = outgoing.shape[0], activations.shape[0], routed.shape[1]
    low = (me[0] * tokens).astype(f32)
    where = routed[...].astype(f32)
    first = jnp.sum(jnp.where(where < low, 1.0, 0.0), axis=1, keepdims=True)
    here = (where >= low) & (where < low + tokens)
    slot = jnp.where(here, iota((1, total), 1) - first, -1.0)
    hit = slot == iota((capacity, total), 0)
    token = jnp.sum(jnp.where(hit, where - low + 1.0, 0.0), axis=1, keepdims=True) - 1.0
    onehot = jnp.where(token == iota((capacity, tokens), 1), 1.0, 0.0).astype(bf16)
    second_move.wait()
    width = activations.shape[1]
    tile = tile_of(width, 1024)
    for start in range(0, width, tile):
        span = slice(start, start + tile)
        outgoing[:, span] = pick(onehot, activations[:, span])


def map_body(tall, wide, tokens, heads_of, me, routed, balance, notes, *outs):
    pick_rows, in_order, columns, unmix, positions = outs
    count, total = tall * wide, routed.shape[1]
    share, capacity = total // count, pick_rows.shape[1] // count
    outbound, inbound = columns.shape[0], unmix.shape[0]
    my_z, my_y = lax.div(me[0], wide), lax.rem(me[0], wide)
    where, owner = routed[...].astype(f32), balance[...].astype(f32)
    lane = iota((1, total), 1)
    slot, place = jnp.zeros((1, total), f32), jnp.zeros((1, total), f32)
    out_base, out_block = notes[:outbound, 0:1], notes[:outbound, 1:2]
    in_base, in_source = notes[:inbound, 2:3], notes[:inbound, 3:4]
    for s in range(count):
        z, y = divmod(s, wide)
        from_block = lax.rem(my_z - z + tall, tall) * wide + lax.rem(my_y - y + wide, wide)
        to_block = lax.rem(z - my_z + tall, tall) * wide + lax.rem(y - my_y + wide, wide)
        peer = lax.rem(my_z + z, tall) * wide + lax.rem(my_y + y, wide)
        before = where < s * tokens
        first = jnp.sum(jnp.where(before, 1.0, 0.0), axis=1, keepdims=True)
        inside = (where < (s + 1) * tokens) & jnp.logical_not(before)
        start = (from_block * capacity).astype(f32)
        slot += jnp.where(inside, lane - first + start, 0.0)
        place += jnp.where(owner == s, (to_block * share).astype(f32), 0.0)
        out_base += jnp.where(out_block == y * tall + z, heads_of(peer).astype(f32), 0.0)
        in_base += jnp.where(in_source == s, (from_block * (outbound // count)).astype(f32), 0.0)
    mine = owner == iota((count, total), 0)
    earlier = jnp.where(iota((total, total), 0) < iota((total, total), 1), 1.0, 0.0)
    rank = dot(jnp.where(mine, 1.0, 0.0).astype(bf16), earlier.astype(bf16))
    place += jnp.sum(jnp.where(mine, rank, 0.0), axis=0, keepdims=True)
    placed = place == iota((total, total), 0)
    in_order[...] = jnp.where(placed, 1.0, 0.0).astype(bf16)
    at = jnp.sum(jnp.where(placed, where, 0.0), axis=1, keepdims=True)
    positions[...] = jnp.broadcast_to(at, positions.shape)
    slot_at = jnp.sum(jnp.where(placed, slot, 0.0), axis=1, keepdims=True)
    pick_rows[...] = jnp.where(slot_at == iota(pick_rows.shape, 1), 1.0, 0.0).astype(bf16)
    columns[...] = jnp.where(out_base == iota(columns.shape, 1), 1.0, 0.0).astype(bf16)
    unmix[...] = jnp.where(in_base == iota(unmix.shape, 1), 1.0, 0.0).astype(bf16)


def kv_body(count, extra, *refs):
    blocks = refs[:count]
    pick_rows, order, columns, gain, w_key, w_value = refs[count : count + 6]
    wide = len(refs) - count - 9 - extra
    normed, own, *sent, rows = refs[-3 - wide :]
    total, width = normed.shape
    tile = tile_of(width, 512)
    square = jnp.zeros((total, 1), f32)
    for start in range(0, width, tile):
        span = slice(start, start + tile)
        part = dot(pick_rows[...], jnp.concatenate([b[:, span] for b in blocks], axis=0))
        rows[:, span] = part.astype(bf16)
        square += jnp.sum(part * part, axis=1, keepdims=True)
    own[...] = rows[: own.shape[0], :]
    factor = lax.rsqrt(square / width + norm_eps)
    for start in range(0, width, tile):
        span = slice(start, start + tile)
        part = rows[:, span].astype(f32) * factor * gain[:, span]
        normed[:, span] = part.astype(bf16)
    keys = dot(normed[...], w_key[...]).astype(bf16)
    values = dot(normed[...], w_value[...]).astype(bf16)
    both = jnp.concatenate([keys, values], axis=1)
    turned = lax.dot_general(
        columns[...], both, (((1,), (1,)), ((), ())), preferred_element_type=f32
    ).astype(bf16)
    turned = dot(turned, order[...])
    each = turned.shape[0] // wide
    for dy in range(wide):
        sent[dy][...] = turned[dy * each : (dy + 1) * each].astype(bf16)


def query_body(normed, w_query, cosine, sine, query):
    raw = dot(normed[...], w_query[...])
    for head in range(query.shape[1] // HEAD_DIM):
        span = slice(head * HEAD_DIM, (head + 1) * HEAD_DIM)
        one = raw[:, span]
        turned = one * cosine[...] + pltpu.roll(one, HEAD_DIM // 2, 1) * sine[...]
        query[:, span] = turned.astype(bf16)


def attend_body(plane, kv_local, *refs):
    tall = plane[0]
    arrived, rest = refs[:tall], refs[tall:]
    query, unmix, cosine, sine, key_pos, query_pos, w_output = rest[:7]
    parts, heads_out = rest[7:-1], rest[-1]
    half = HEAD_DIM // 2
    heads = query.shape[1] // HEAD_DIM
    mixed = jnp.concatenate([a[...].astype(f32) for a in arrived], axis=0).astype(bf16)
    both = dot(unmix[...], mixed)
    allowed = key_pos[...].astype(f32) <= query_pos[:, 0:1]
    for group in range(kv_local):
        base = group * HEAD_DIM
        first, second = both[base : base + half], both[base + half : base + HEAD_DIM]
        keys = jnp.concatenate(
            [first * cosine[...] - second * sine[...], second * cosine[...] + first * sine[...]],
            axis=0,
        ).astype(bf16)
        base += kv_local * HEAD_DIM
        values = both[base : base + HEAD_DIM].astype(bf16)
        for head in range(group * heads // kv_local, (group + 1) * heads // kv_local):
            span = slice(head * HEAD_DIM, (head + 1) * HEAD_DIM)
            scores = dot(query[:, span], keys) * HEAD_DIM ** (-0.5)
            scores = jnp.where(allowed, scores, -1e30)
            weights = jnp.exp(scores - jnp.max(scores, axis=1, keepdims=True))
            probs = (weights / jnp.sum(weights, axis=1, keepdims=True)).astype(bf16)
            heads_out[:, span] = lax.dot_general(
                probs, values, (((1,), (1,)), ((), ())), preferred_element_type=f32
            ).astype(bf16)
    spread(heads_out, w_output, parts, plane, False)


def spread(left, weight, parts, plane, back):
    width = weight.shape[1]
    tile = tile_of(width, 512)
    for start in range(0, width, tile):
        span = slice(start, start + tile)
        product = dot(left[...], weight[:, span]).astype(bf16)
        store_parts(parts, *plane, span, product, back)


def mlp_body(plane, *refs):
    count = plane[0] * plane[1]
    blocks, (w_gate, w_up, w_down) = refs[:count], refs[count : count + 3]
    parts, (piece, inner) = refs[count + 3 : -2], refs[-2:]
    share = blocks[0].shape[0]
    for index, block in enumerate(blocks):
        piece[index * share : (index + 1) * share, :] = block[...]
    width = w_gate.shape[1]
    tile = tile_of(width, 256)
    for start in range(0, width, tile):
        span = slice(start, start + tile)
        gate = dot(piece[...], w_gate[:, span])
        upward = dot(piece[...], w_up[:, span])
        inner[:, span] = (gate / (1.0 + jnp.exp(-gate)) * upward).astype(bf16)
    spread(inner, w_down, parts, plane, True)


def on_device(
    activations,
    routed,
    balance,
    w_query,
    w_key,
    w_value,
    w_output,
    attn_gain,
    mlp_gain,
    w_gate,
    w_up,
    w_down,
    w_router,
):
    count = lax.axis_size("ctx")
    plane = tall, wide = plane_of(count)
    me = lax.axis_index("ctx").astype(i32).reshape(1)
    tokens, model = activations.shape
    total = routed.shape[0]
    share = total // count
    capacity = 2 * share
    local_heads = w_query.shape[1] // HEAD_DIM
    group_size = HEADS // KV_HEADS
    kv_local = max(1, local_heads // group_size)
    key_cols = w_key.shape[1]
    depth = key_cols // KV_HEADS
    scalar = pl.BlockSpec(memory_space=pltpu.SMEM)
    in_hbm = pl.BlockSpec(memory_space=pl.ANY)
    routed, balance = routed.reshape(1, total), balance.reshape(1, total)

    (outgoing,) = kernel_call(
        send_body,
        [((capacity, model), bf16)],
        [me, from_hbm(routed), from_hbm(activations)],
        [
            pltpu.VMEM(routed.shape, i32),
            pltpu.VMEM(activations.shape, bf16),
            pltpu.SemaphoreType.DMA((2,)),
        ],
        specs=[scalar, in_hbm, in_hbm],
        flops=2 * capacity * tokens * model,
    )
    attn_gain, w_key, w_value, w_query, token_1 = load(
        outgoing, attn_gain.reshape(1, model), w_key, w_value, w_query
    )

    each = kv_local * 2 * depth
    notes = np.zeros((max(count * each, 2 * kv_local * HEAD_DIM), 4), np.float32)
    block, local, side, entry = np.indices((count, kv_local, 2, depth)).reshape(4, -1)
    notes[: count * each, 0] = side * key_cols + entry * KV_HEADS + local
    notes[: count * each, 1] = block
    side, local, source, entry = np.indices((2, kv_local, count, depth)).reshape(4, -1)
    notes[: 2 * kv_local * HEAD_DIM, 2] = (local * 2 + side) * depth + entry
    notes[: 2 * kv_local * HEAD_DIM, 3] = source
    pick_rows, in_order, columns, unmix, positions = kernel_call(
        functools.partial(
            map_body, tall, wide, tokens, lambda peer: lax.div(peer * local_heads, group_size)
        ),
        [
            ((total, count * capacity), bf16),
            ((total, total), bf16),
            ((count * each, 2 * key_cols), bf16),
            ((2 * kv_local * HEAD_DIM, count * each), bf16),
            ((total, HEAD_DIM // 2), f32),
        ],
        [me, routed, balance, notes],
        specs=[scalar, VMEM, VMEM, VMEM],
    )
    blocks = gather_rows(outgoing, tall, wide, [token_1, positions])
    near = blocks[2 * wide]
    w_output, *token_2 = load(near, w_output)
    w_gate, *token_3 = load(near, w_gate)
    loaded = token_2 + token_3

    half = HEAD_DIM // 2
    steps_f = jnp.arange(half, dtype=f32)
    freqs = jnp.exp(-jnp.log(f32(rope_base)) * (2.0 * steps_f / HEAD_DIM))
    q_angles = positions * freqs[None, :]
    q_cos, q_sin = jnp.cos(q_angles), jnp.sin(q_angles)
    q_cos = jnp.concatenate([q_cos, q_cos], axis=1)
    q_sin = jnp.concatenate([-q_sin, q_sin], axis=1)
    k_angles = freqs[:, None] * routed.astype(f32)
    k_cos, k_sin = jnp.cos(k_angles), jnp.sin(k_angles)

    normed, own, *sent = kernel_call(
        functools.partial(kv_body, count, len(loaded)),
        [((total, model), bf16), ((share, model), bf16)] + [((tall * each, total), bf16)] * wide,
        [*blocks, pick_rows, in_order, columns, attn_gain, w_key, w_value, *loaded],
        [pltpu.VMEM((total, model), bf16)],
        flops=2 * total * model * 512,
    )
    arrived = exchange(sent, tall, wide)
    heads_wide = local_heads * HEAD_DIM
    (query,) = kernel_call(
        query_body,
        [((total, heads_wide), bf16)],
        [normed, w_query, q_cos, q_sin],
        flops=2 * total * model * heads_wide,
    )
    part_shapes = sum_shapes(tall, wide, share, model)
    attn_parts = kernel_call(
        functools.partial(attend_body, plane, kv_local),
        part_shapes,
        [*arrived, query, unmix, k_cos, k_sin, routed, positions, w_output],
        [pltpu.VMEM((total, heads_wide), bf16)],
        flops=2 * total * model * heads_wide,
    )
    attn_own, w_down = scatter_sum(attn_parts, tall, wide, [w_down])
    own_rows = own.astype(f32)
    hidden = own_rows + attn_own
    mean_sq = jnp.mean(hidden * hidden, axis=-1, keepdims=True)
    mnorm = (hidden * lax.rsqrt(mean_sq + norm_eps) * mlp_gain).astype(bf16)
    pieces = gather_blocks(mnorm, tall, wide)
    w_up, _ = load(mnorm, w_up)
    hidden_units = w_gate.shape[1]
    mlp_parts = kernel_call(
        functools.partial(mlp_body, plane),
        part_shapes,
        [*pieces, w_gate, w_up, w_down],
        [pltpu.VMEM((total, model), bf16), pltpu.VMEM((total, hidden_units), bf16)],
        flops=6 * total * model * hidden_units,
    )
    mlp_own = scatter_sum(mlp_parts, tall, wide)
    router_score = jnp.sum(own_rows * w_router[None, :], axis=1, keepdims=True)
    return (own_rows + router_score * (attn_own + mlp_own)).astype(bf16)


def solution(mesh):
    in_specs = (
        P(("dp", "ctx"), None),
        P("dp"),
        P("dp"),
        P(None, "ctx"),
        P(None, "ctx"),
        P(None, "ctx"),
        P("ctx", None),
        P(),
        P(),
        P(None, "ctx"),
        P(None, "ctx"),
        P("ctx", None),
        P(),
    )
    out_specs = P(("dp", "ctx"), None)
    return jax.shard_map(
        on_device, mesh=mesh, in_specs=in_specs, out_specs=out_specs, check_vma=False
    )
```

```python
import functools

import jax
import jax.numpy as jnp
import numpy as np
from jax import lax
from jax.experimental import pallas as pl
from jax.experimental.pallas import tpu as pltpu
from jax.sharding import PartitionSpec as P

HEADS = 32
KV_HEADS = 8
HEAD_DIM = 128

rope_base = 500000.0
norm_eps = 1e-05

bf16, f32, i32 = jnp.bfloat16, jnp.float32, jnp.int32
VMEM = pl.BlockSpec(memory_space=pltpu.VMEM)


def plane_of(count):
    wide = max(y for y in range(1, count + 1) if count % y == 0 and 2 * y * y <= max(count, 2))
    return count // wide, wide


def shift(block, tall, wide, dz, dy, keep=None):
    pairs = [
        (z * wide + y, (z + dz) % tall * wide + (y + dy) % wide)
        for z in range(tall)
        for y in range(wide)
        if keep is None or keep(z)
    ]
    return lax.ppermute(block, "ctx", pairs)


def tie_body(count, *refs):
    total = refs[0][...]
    for ref in refs[1:count]:
        total = total + ref[...]
    refs[-1][...] = total


def tie(blocks, tokens):
    return kernel_call(
        functools.partial(tie_body, len(blocks)),
        [(blocks[0].shape, blocks[0].dtype)],
        [*blocks, *tokens],
        specs=[VMEM] * len(blocks) + [pl.BlockSpec(memory_space=pl.ANY)] * len(tokens),
    )[0]


def gather_rows(block, tall, wide, tokens):
    blocks = {(0, 0): block}
    for dy in range(1, wide):
        blocks[0, dy] = shift(block, tall, wide, 0, dy)
    early = [blocks[0, dy] for dy in range(1, wide)]
    last = tall - 1
    blocks[last, 0] = tie([shift(block, tall, wide, last, 0)], early)
    for dy in range(1, wide):
        blocks[last, dy] = shift(blocks[last, 0], tall, wide, 0, dy)
    block = tie([block], [blocks[last, 0]])
    for dz in range(1, last):
        if tall != 4 or dz != 2:
            blocks[dz, 0] = shift(block, tall, wide, dz, 0)
    blocks[1, 0] = tie([blocks[1, 0]], tokens)
    if tall == 4:
        up = shift(blocks[1, 0], tall, wide, 1, 0, lambda z: z in (1, 2))
        held = tie([blocks[3, 0]], [blocks[1, 0]])
        down = shift(held, tall, wide, -1, 0, lambda z: z in (1, 2))
        blocks[2, 0] = tie([up, down], [blocks[3, dy] for dy in range(1, wide)])
    for dz in range(1, tall):
        for dy in range(1, wide):
            if (dz, dy) not in blocks:
                blocks[dz, dy] = shift(blocks[dz, 0], tall, wide, 0, dy)
    return [blocks[dz, dy] for dz in range(tall) for dy in range(wide)]


def pack_body(tall, *refs):
    wide = len(refs) - tall
    each = refs[0].shape[0] // tall
    for dz in range(tall):
        values = [ref[...].astype(f32)[dz * each : (dz + 1) * each] for ref in refs[:wide]]
        refs[wide + dz][...] = jnp.concatenate(values, axis=0).astype(bf16)


def exchange(parts, tall, wide):
    shape = ((parts[0].shape[0] // tall * wide, parts[0].shape[1]), bf16)
    crossed = [parts[0]] + [shift(parts[dy], tall, wide, 0, dy) for dy in range(1, wide)]
    packed = kernel_call(functools.partial(pack_body, tall), [shape] * tall, crossed)
    return [packed[0]] + [shift(packed[dz], tall, wide, dz, 0) for dz in range(1, tall)]


def gather_blocks(block, tall, wide):
    blocks = {(dz, 0): shift(block, tall, wide, dz, 0) if dz else block for dz in range(tall)}
    for dz in range(tall):
        for dy in range(1, wide):
            blocks[dz, dy] = shift(blocks[dz, 0], tall, wide, 0, dy)
    return [blocks[dz, dy] for dz in range(tall) for dy in range(wide)]


def sum_order(tall):
    order = [tall // 2, *range(1, tall // 2), *range(tall // 2 + 1, tall), 0]
    return order[: tall // 2], order[tall // 2 :]


def sum_shapes(tall, wide, share, model):
    kept = [((share, model), bf16)] * tall
    return kept + [((tall // 2 * share, model), bf16)] * (2 * (wide - 1))


def store_parts(parts, tall, wide, span, product, back):
    share = parts[0].shape[0]
    sign = -1 if back else 1

    def rows(dz, dy):
        at = sign * dz % tall * wide + sign * dy % wide
        return product[at * share : (at + 1) * share, :]

    for dz in range(tall):
        parts[dz][:, span] = rows(dz, 0)
    for dy in range(1, wide):
        for which, group in enumerate(sum_order(tall)):
            out = parts[tall + 2 * (dy - 1) + which]
            for place, dz in enumerate(group):
                out[place * share : (place + 1) * share, span] = rows(dz, dy)


def scatter_sum(parts, tall, wide, loads=()):
    share = parts[0].shape[0]
    loaded = []
    crossed = [shift(p, tall, wide, 0, i // 2 + 1) for i, p in enumerate(parts[tall:])]
    if loads:
        *copy, token = load(parts[0], loads[0])
        loaded += copy
        crossed[1] = tie([crossed[1]], [token])
    total = None
    for which, group in enumerate(sum_order(tall)):
        for place, dz in enumerate(group):
            lane = parts[dz].astype(f32)
            for dy in range(1, wide):
                other = crossed[2 * (dy - 1) + which]
                lane = lane + other[place * share : (place + 1) * share].astype(f32)
            if dz:
                sent = lane.astype(bf16)
                lane = shift(sent, tall, wide, dz, 0)
                if len(loads) > 1 and dz == tall - 1:
                    *copy, token = load(sent, loads[1])
                    loaded += copy
                    lane = tie([lane], [token])
                lane = lane.astype(f32)
            total = lane if total is None else total + lane
    return (total, *loaded) if loads else total


def dot(a, b):
    return jnp.dot(a, b, preferred_element_type=f32)


def from_hbm(weight):
    return pltpu.with_memory_space_constraint(weight, pltpu.HBM)


def fetched(weight):
    return pltpu.with_memory_space_constraint(weight, pltpu.VMEM)


def kernel_call(body, outs, args, scratch=(), limit=14, flops=0, specs=None):
    return pl.pallas_call(
        body,
        out_shape=[jax.ShapeDtypeStruct(s, d) for s, d in outs],
        in_specs=specs or [VMEM] * len(args),
        out_specs=[VMEM] * len(outs),
        scratch_shapes=list(scratch),
        compiler_params=pltpu.CompilerParams(vmem_limit_bytes=limit << 20),
        cost_estimate=pl.CostEstimate(flops=flops, bytes_accessed=1 << 20, transcendentals=0),
    )(*args)


def load_body(count, *refs):
    sources, copies, sems = refs[1 : 1 + count], refs[1 + count : -2], refs[-1]
    moves = [
        pltpu.make_async_copy(a, b, sems.at[i]) for i, (a, b) in enumerate(zip(sources, copies))
    ]
    for move in moves:
        move.start()
    for move in moves:
        move.wait()
    refs[-2][...] = jnp.zeros_like(refs[-2])


def load(after, *arrays):
    size = sum(a.size * a.dtype.itemsize for a in arrays)
    *copies, token = pl.pallas_call(
        functools.partial(load_body, len(arrays)),
        out_shape=[pltpu.VMEM(a.shape, a.dtype) for a in arrays]
        + [jax.ShapeDtypeStruct((8, 128), f32)],
        in_specs=[pl.BlockSpec(memory_space=pl.ANY)] * (1 + len(arrays)),
        out_specs=[VMEM] * (1 + len(arrays)),
        scratch_shapes=[pltpu.SemaphoreType.DMA((len(arrays),))],
        compiler_params=pltpu.CompilerParams(vmem_limit_bytes=2 << 20),
        cost_estimate=pl.CostEstimate(flops=0, bytes_accessed=2 * size, transcendentals=0),
    )(after, *[from_hbm(a) for a in arrays])
    return [fetched(c) for c in copies] + [token]


def tile_of(width, most):
    return width if width <= most else most


def iota(shape, axis):
    return lax.broadcasted_iota(i32, shape, axis).astype(f32)


def pick(onehot, values):
    return dot(onehot, values).astype(values.dtype)


def send_body(me, routed_in, activations_in, outgoing, routed, activations, sems):
    first_move = pltpu.make_async_copy(routed_in, routed, sems.at[0])
    second_move = pltpu.make_async_copy(activations_in, activations, sems.at[1])
    first_move.start()
    second_move.start()
    first_move.wait()
    capacity, tokens, total = outgoing.shape[0], activations.shape[0], routed.shape[1]
    low = (me[0] * tokens).astype(f32)
    where = routed[...].astype(f32)
    first = jnp.sum(jnp.where(where < low, 1.0, 0.0), axis=1, keepdims=True)
    here = (where >= low) & (where < low + tokens)
    slot = jnp.where(here, iota((1, total), 1) - first, -1.0)
    hit = slot == iota((capacity, total), 0)
    token = jnp.sum(jnp.where(hit, where - low + 1.0, 0.0), axis=1, keepdims=True) - 1.0
    onehot = jnp.where(token == iota((capacity, tokens), 1), 1.0, 0.0).astype(bf16)
    second_move.wait()
    width = activations.shape[1]
    tile = tile_of(width, 1024)
    for start in range(0, width, tile):
        span = slice(start, start + tile)
        outgoing[:, span] = pick(onehot, activations[:, span])


def map_body(tall, wide, tokens, heads_of, me, routed, balance, notes, *outs):
    pick_rows, in_order, columns, unmix, positions = outs
    count, total = tall * wide, routed.shape[1]
    share, capacity = total // count, pick_rows.shape[1] // count
    outbound, inbound = columns.shape[0], unmix.shape[0]
    my_z, my_y = lax.div(me[0], wide), lax.rem(me[0], wide)
    where, owner = routed[...].astype(f32), balance[...].astype(f32)
    lane = iota((1, total), 1)
    slot, place = jnp.zeros((1, total), f32), jnp.zeros((1, total), f32)
    out_base, out_block = notes[:outbound, 0:1], notes[:outbound, 1:2]
    in_base, in_source = notes[:inbound, 2:3], notes[:inbound, 3:4]
    for s in range(count):
        z, y = divmod(s, wide)
        from_block = lax.rem(my_z - z + tall, tall) * wide + lax.rem(my_y - y + wide, wide)
        to_block = lax.rem(z - my_z + tall, tall) * wide + lax.rem(y - my_y + wide, wide)
        peer = lax.rem(my_z + z, tall) * wide + lax.rem(my_y + y, wide)
        before = where < s * tokens
        first = jnp.sum(jnp.where(before, 1.0, 0.0), axis=1, keepdims=True)
        inside = (where < (s + 1) * tokens) & jnp.logical_not(before)
        start = (from_block * capacity).astype(f32)
        slot += jnp.where(inside, lane - first + start, 0.0)
        place += jnp.where(owner == s, (to_block * share).astype(f32), 0.0)
        out_base += jnp.where(out_block == y * tall + z, heads_of(peer).astype(f32), 0.0)
        in_base += jnp.where(in_source == s, (from_block * (outbound // count)).astype(f32), 0.0)
    mine = owner == iota((count, total), 0)
    earlier = jnp.where(iota((total, total), 0) < iota((total, total), 1), 1.0, 0.0)
    rank = dot(jnp.where(mine, 1.0, 0.0).astype(bf16), earlier.astype(bf16))
    place += jnp.sum(jnp.where(mine, rank, 0.0), axis=0, keepdims=True)
    placed = place == iota((total, total), 0)
    in_order[...] = jnp.where(placed, 1.0, 0.0).astype(bf16)
    at = jnp.sum(jnp.where(placed, where, 0.0), axis=1, keepdims=True)
    positions[...] = jnp.broadcast_to(at, positions.shape)
    slot_at = jnp.sum(jnp.where(placed, slot, 0.0), axis=1, keepdims=True)
    pick_rows[...] = jnp.where(slot_at == iota(pick_rows.shape, 1), 1.0, 0.0).astype(bf16)
    columns[...] = jnp.where(out_base == iota(columns.shape, 1), 1.0, 0.0).astype(bf16)
    unmix[...] = jnp.where(in_base == iota(unmix.shape, 1), 1.0, 0.0).astype(bf16)


def kv_body(count, extra, *refs):
    blocks = refs[:count]
    pick_rows, order, columns, gain, w_key, w_value = refs[count : count + 6]
    wide = len(refs) - count - 9 - extra
    normed, own, *sent, rows = refs[-3 - wide :]
    total, width = normed.shape
    tile = tile_of(width, 512)
    square = jnp.zeros((total, 1), f32)
    for start in range(0, width, tile):
        span = slice(start, start + tile)
        part = dot(pick_rows[...], jnp.concatenate([b[:, span] for b in blocks], axis=0))
        rows[:, span] = part.astype(bf16)
        square += jnp.sum(part * part, axis=1, keepdims=True)
    own[...] = rows[: own.shape[0], :]
    factor = lax.rsqrt(square / width + norm_eps)
    for start in range(0, width, tile):
        span = slice(start, start + tile)
        part = rows[:, span].astype(f32) * factor * gain[:, span]
        normed[:, span] = part.astype(bf16)
    keys = dot(normed[...], w_key[...]).astype(bf16)
    values = dot(normed[...], w_value[...]).astype(bf16)
    both = jnp.concatenate([keys, values], axis=1)
    turned = lax.dot_general(
        columns[...], both, (((1,), (1,)), ((), ())), preferred_element_type=f32
    ).astype(bf16)
    turned = dot(turned, order[...])
    each = turned.shape[0] // wide
    for dy in range(wide):
        sent[dy][...] = turned[dy * each : (dy + 1) * each].astype(bf16)


def query_body(normed, w_query, cosine, sine, query):
    raw = dot(normed[...], w_query[...])
    for head in range(query.shape[1] // HEAD_DIM):
        span = slice(head * HEAD_DIM, (head + 1) * HEAD_DIM)
        one = raw[:, span]
        turned = one * cosine[...] + pltpu.roll(one, HEAD_DIM // 2, 1) * sine[...]
        query[:, span] = turned.astype(bf16)


def attend_body(plane, kv_local, *refs):
    tall = plane[0]
    arrived, rest = refs[:tall], refs[tall:]
    query, unmix, cosine, sine, key_pos, query_pos, w_output = rest[:7]
    parts, heads_out = rest[7:-1], rest[-1]
    half = HEAD_DIM // 2
    heads = query.shape[1] // HEAD_DIM
    mixed = jnp.concatenate([a[...].astype(f32) for a in arrived], axis=0).astype(bf16)
    both = dot(unmix[...], mixed)
    allowed = key_pos[...].astype(f32) <= query_pos[:, 0:1]
    for group in range(kv_local):
        base = group * HEAD_DIM
        first, second = both[base : base + half], both[base + half : base + HEAD_DIM]
        keys = jnp.concatenate(
            [first * cosine[...] - second * sine[...], second * cosine[...] + first * sine[...]],
            axis=0,
        ).astype(bf16)
        base += kv_local * HEAD_DIM
        values = both[base : base + HEAD_DIM].astype(bf16)
        for head in range(group * heads // kv_local, (group + 1) * heads // kv_local):
            span = slice(head * HEAD_DIM, (head + 1) * HEAD_DIM)
            scores = dot(query[:, span], keys) * HEAD_DIM ** (-0.5)
            scores = jnp.where(allowed, scores, -1e30)
            weights = jnp.exp(scores - jnp.max(scores, axis=1, keepdims=True))
            probs = (weights / jnp.sum(weights, axis=1, keepdims=True)).astype(bf16)
            heads_out[:, span] = lax.dot_general(
                probs, values, (((1,), (1,)), ((), ())), preferred_element_type=f32
            ).astype(bf16)
    spread(heads_out, w_output, parts, plane, False)


def spread(left, weight, parts, plane, back):
    width = weight.shape[1]
    tile = tile_of(width, 512)
    for start in range(0, width, tile):
        span = slice(start, start + tile)
        product = dot(left[...], weight[:, span]).astype(bf16)
        store_parts(parts, *plane, span, product, back)


def mlp_body(plane, *refs):
    count = plane[0] * plane[1]
    blocks, (w_gate, w_up, w_down) = refs[:count], refs[count : count + 3]
    parts, (piece, inner) = refs[count + 3 : -2], refs[-2:]
    share = blocks[0].shape[0]
    for index, block in enumerate(blocks):
        piece[index * share : (index + 1) * share, :] = block[...]
    width = w_gate.shape[1]
    tile = tile_of(width, 256)
    for start in range(0, width, tile):
        span = slice(start, start + tile)
        gate = dot(piece[...], w_gate[:, span])
        upward = dot(piece[...], w_up[:, span])
        inner[:, span] = (gate / (1.0 + jnp.exp(-gate)) * upward).astype(bf16)
    spread(inner, w_down, parts, plane, True)


def on_device(
    activations,
    routed,
    balance,
    w_query,
    w_key,
    w_value,
    w_output,
    attn_gain,
    mlp_gain,
    w_gate,
    w_up,
    w_down,
    w_router,
):
    count = lax.axis_size("ctx")
    plane = tall, wide = plane_of(count)
    me = lax.axis_index("ctx").astype(i32).reshape(1)
    tokens, model = activations.shape
    total = routed.shape[0]
    share = total // count
    capacity = 2 * share
    local_heads = w_query.shape[1] // HEAD_DIM
    group_size = HEADS // KV_HEADS
    kv_local = max(1, local_heads // group_size)
    key_cols = w_key.shape[1]
    depth = key_cols // KV_HEADS
    scalar = pl.BlockSpec(memory_space=pltpu.SMEM)
    in_hbm = pl.BlockSpec(memory_space=pl.ANY)
    routed, balance = routed.reshape(1, total), balance.reshape(1, total)

    (outgoing,) = kernel_call(
        send_body,
        [((capacity, model), bf16)],
        [me, from_hbm(routed), from_hbm(activations)],
        [
            pltpu.VMEM(routed.shape, i32),
            pltpu.VMEM(activations.shape, bf16),
            pltpu.SemaphoreType.DMA((2,)),
        ],
        specs=[scalar, in_hbm, in_hbm],
        flops=2 * capacity * tokens * model,
    )
    attn_gain, w_key, w_value, w_query, token_1 = load(
        outgoing, attn_gain.reshape(1, model), w_key, w_value, w_query
    )

    each = kv_local * 2 * depth
    notes = np.zeros((max(count * each, 2 * kv_local * HEAD_DIM), 4), np.float32)
    block, local, side, entry = np.indices((count, kv_local, 2, depth)).reshape(4, -1)
    notes[: count * each, 0] = side * key_cols + entry * KV_HEADS + local
    notes[: count * each, 1] = block
    side, local, source, entry = np.indices((2, kv_local, count, depth)).reshape(4, -1)
    notes[: 2 * kv_local * HEAD_DIM, 2] = (local * 2 + side) * depth + entry
    notes[: 2 * kv_local * HEAD_DIM, 3] = source
    pick_rows, in_order, columns, unmix, positions = kernel_call(
        functools.partial(
            map_body, tall, wide, tokens, lambda peer: lax.div(peer * local_heads, group_size)
        ),
        [
            ((total, count * capacity), bf16),
            ((total, total), bf16),
            ((count * each, 2 * key_cols), bf16),
            ((2 * kv_local * HEAD_DIM, count * each), bf16),
            ((total, HEAD_DIM // 2), f32),
        ],
        [me, routed, balance, notes],
        specs=[scalar, VMEM, VMEM, VMEM],
    )
    blocks = gather_rows(outgoing, tall, wide, [token_1, positions])
    near = blocks[2 * wide]
    w_output, *token_2 = load(near, w_output)
    w_gate, *token_3 = load(near, w_gate)
    loaded = token_2 + token_3

    half = HEAD_DIM // 2
    steps_f = jnp.arange(half, dtype=f32)
    freqs = jnp.exp(-jnp.log(f32(rope_base)) * (2.0 * steps_f / HEAD_DIM))
    q_angles = positions * freqs[None, :]
    q_cos, q_sin = jnp.cos(q_angles), jnp.sin(q_angles)
    q_cos = jnp.concatenate([q_cos, q_cos], axis=1)
    q_sin = jnp.concatenate([-q_sin, q_sin], axis=1)
    k_angles = freqs[:, None] * routed.astype(f32)
    k_cos, k_sin = jnp.cos(k_angles), jnp.sin(k_angles)

    normed, own, *sent = kernel_call(
        functools.partial(kv_body, count, len(loaded)),
        [((total, model), bf16), ((share, model), bf16)] + [((tall * each, total), bf16)] * wide,
        [*blocks, pick_rows, in_order, columns, attn_gain, w_key, w_value, *loaded],
        [pltpu.VMEM((total, model), bf16)],
        flops=2 * total * model * 512,
    )
    arrived = exchange(sent, tall, wide)
    heads_wide = local_heads * HEAD_DIM
    (query,) = kernel_call(
        query_body,
        [((total, heads_wide), bf16)],
        [normed, w_query, q_cos, q_sin],
        flops=2 * total * model * heads_wide,
    )
    part_shapes = sum_shapes(tall, wide, share, model)
    attn_parts = kernel_call(
        functools.partial(attend_body, plane, kv_local),
        part_shapes,
        [*arrived, query, unmix, k_cos, k_sin, routed, positions, w_output],
        [pltpu.VMEM((total, heads_wide), bf16)],
        flops=2 * total * model * heads_wide,
    )
    attn_own, w_down = scatter_sum(attn_parts, tall, wide, [w_down])
    own_rows = own.astype(f32)
    hidden = own_rows + attn_own
    mean_sq = jnp.mean(hidden * hidden, axis=-1, keepdims=True)
    mnorm = (hidden * lax.rsqrt(mean_sq + norm_eps) * mlp_gain).astype(bf16)
    pieces = gather_blocks(mnorm, tall, wide)
    w_up, _ = load(mnorm, w_up)
    hidden_units = w_gate.shape[1]
    mlp_parts = kernel_call(
        functools.partial(mlp_body, plane),
        part_shapes,
        [*pieces, w_gate, w_up, w_down],
        [pltpu.VMEM((total, model), bf16), pltpu.VMEM((total, hidden_units), bf16)],
        flops=6 * total * model * hidden_units,
    )
    mlp_own = scatter_sum(mlp_parts, tall, wide)
    router_score = jnp.sum(own_rows * w_router[None, :], axis=1, keepdims=True)
    return (own_rows + router_score * (attn_own + mlp_own)).astype(bf16)


def solution(mesh):
    in_specs = (
        P(("dp", "ctx"), None),
        P("dp"),
        P("dp"),
        P(None, "ctx"),
        P(None, "ctx"),
        P(None, "ctx"),
        P("ctx", None),
        P(),
        P(),
        P(None, "ctx"),
        P(None, "ctx"),
        P("ctx", None),
        P(),
    )
    out_specs = P(("dp", "ctx"), None)
    return jax.shard_map(
        on_device, mesh=mesh, in_specs=in_specs, out_specs=out_specs, check_vma=False
    )
```

```python
import functools

import jax
import jax.numpy as jnp
import numpy as np
from jax import lax
from jax.experimental import pallas as pl
from jax.experimental.pallas import tpu as pltpu
from jax.sharding import PartitionSpec as P

HEADS = 32
KV_HEADS = 8
HEAD_DIM = 128

rope_base = 500000.0
norm_eps = 1e-05

bf16, f32, i32 = jnp.bfloat16, jnp.float32, jnp.int32
VMEM = pl.BlockSpec(memory_space=pltpu.VMEM)


def plane_of(count):
    wide = max(y for y in range(1, count + 1) if count % y == 0 and 2 * y * y <= max(count, 2))
    return count // wide, wide


def shift(block, tall, wide, dz, dy, keep=None):
    pairs = [
        (z * wide + y, (z + dz) % tall * wide + (y + dy) % wide)
        for z in range(tall)
        for y in range(wide)
        if keep is None or keep(z)
    ]
    return lax.ppermute(block, "ctx", pairs)


def tie_body(count, *refs):
    total = refs[0][...]
    for ref in refs[1:count]:
        total = total + ref[...]
    refs[-1][...] = total


def tie(blocks, tokens):
    return kernel_call(
        functools.partial(tie_body, len(blocks)),
        [(blocks[0].shape, blocks[0].dtype)],
        [*blocks, *tokens],
        specs=[VMEM] * len(blocks) + [pl.BlockSpec(memory_space=pl.ANY)] * len(tokens),
    )[0]


def gather_rows(block, tall, wide, tokens):
    blocks = {(0, 0): block}
    for dy in range(1, wide):
        blocks[0, dy] = shift(block, tall, wide, 0, dy)
    first = [*tokens, *(blocks[0, dy] for dy in range(1, wide))]
    for dz in range(tall - 1, 0, -1):
        if tall != 4 or dz != 2:
            blocks[dz, 0] = shift(block, tall, wide, dz, 0)
    blocks[tall - 1, 0] = tie([blocks[tall - 1, 0]], first)
    if tall == 4:
        for dy in range(1, wide):
            blocks[3, dy] = shift(blocks[3, 0], tall, wide, 0, dy)
        up = shift(blocks[1, 0], tall, wide, 1, 0, lambda z: z in (1, 2))
        down = shift(blocks[3, 0], tall, wide, -1, 0, lambda z: z in (1, 2))
        blocks[2, 0] = tie([up, down], [blocks[3, dy] for dy in range(1, wide)])
    for dz in range(1, tall):
        for dy in range(1, wide):
            if (dz, dy) not in blocks:
                blocks[dz, dy] = shift(blocks[dz, 0], tall, wide, 0, dy)
    return [blocks[dz, dy] for dz in range(tall) for dy in range(wide)]


def pack_body(tall, *refs):
    wide = len(refs) - tall
    each = refs[0].shape[0] // tall
    for dz in range(tall):
        values = [ref[...].astype(f32)[dz * each : (dz + 1) * each] for ref in refs[:wide]]
        refs[wide + dz][...] = jnp.concatenate(values, axis=0).astype(bf16)


def exchange(parts, tall, wide):
    shape = ((parts[0].shape[0] // tall * wide, parts[0].shape[1]), bf16)
    crossed = [parts[0]] + [shift(parts[dy], tall, wide, 0, dy) for dy in range(1, wide)]
    packed = kernel_call(functools.partial(pack_body, tall), [shape] * tall, crossed)
    return [packed[0]] + [shift(packed[dz], tall, wide, dz, 0) for dz in range(1, tall)]


def gather_blocks(block, tall, wide):
    blocks = {(dz, 0): shift(block, tall, wide, dz, 0) if dz else block for dz in range(tall)}
    for dy in range(1, wide):
        blocks[0, dy] = shift(block, tall, wide, 0, dy)
    blocks[1, 0] = tie([blocks[1, 0]], [blocks[0, dy] for dy in range(1, wide)])
    for dz in range(1, tall):
        for dy in range(1, wide):
            blocks[dz, dy] = shift(blocks[dz, 0], tall, wide, 0, dy)
    return [blocks[dz, dy] for dz in range(tall) for dy in range(wide)]


def sum_shapes(tall, wide, share, model):
    kept = [((share, model), bf16)] * tall
    return kept + [((tall * share, model), bf16)] * (wide - 1)


def store_parts(parts, tall, wide, span, product, back):
    share = parts[0].shape[0]
    sign = -1 if back else 1

    def rows(dz, dy):
        at = sign * dz % tall * wide + sign * dy % wide
        return product[at * share : (at + 1) * share, :]

    for dz in range(tall):
        parts[dz][:, span] = rows(dz, 0)
        for dy in range(1, wide):
            parts[tall + dy - 1][dz * share : (dz + 1) * share, span] = rows(dz, dy)


def scatter_sum(parts, tall, wide, loads=()):
    share = parts[0].shape[0]
    loaded = []
    crossed = [shift(p, tall, wide, 0, dy) for dy, p in enumerate(parts[tall:], 1)]
    if loads:
        *loaded, token = load(parts[0], *loads)
        crossed[0] = tie([crossed[0]], [token])
    total = None
    for dz in [tall // 2, *range(1, tall // 2), *range(tall // 2 + 1, tall), 0]:
        lane = parts[dz].astype(f32)
        for other in crossed:
            lane = lane + other[dz * share : (dz + 1) * share].astype(f32)
        if dz:
            lane = shift(lane.astype(bf16), tall, wide, dz, 0).astype(f32)
        total = lane if total is None else total + lane
    return (total, *loaded) if loads else total


def dot(a, b):
    return jnp.dot(a, b, preferred_element_type=f32)


def from_hbm(weight):
    return pltpu.with_memory_space_constraint(weight, pltpu.HBM)


def fetched(weight):
    return pltpu.with_memory_space_constraint(weight, pltpu.VMEM)


def kernel_call(body, outs, args, scratch=(), limit=14, flops=0, specs=None):
    return pl.pallas_call(
        body,
        out_shape=[jax.ShapeDtypeStruct(s, d) for s, d in outs],
        in_specs=specs or [VMEM] * len(args),
        out_specs=[VMEM] * len(outs),
        scratch_shapes=list(scratch),
        compiler_params=pltpu.CompilerParams(vmem_limit_bytes=limit << 20),
        cost_estimate=pl.CostEstimate(flops=flops, bytes_accessed=1 << 20, transcendentals=0),
    )(*args)


def load_body(count, *refs):
    sources, copies, sems = refs[1 : 1 + count], refs[1 + count : -2], refs[-1]
    moves = [
        pltpu.make_async_copy(a, b, sems.at[i]) for i, (a, b) in enumerate(zip(sources, copies))
    ]
    for move in moves:
        move.start()
    for move in moves:
        move.wait()
    refs[-2][...] = jnp.zeros_like(refs[-2])


def load(after, *arrays):
    size = sum(a.size * a.dtype.itemsize for a in arrays)
    *copies, token = pl.pallas_call(
        functools.partial(load_body, len(arrays)),
        out_shape=[pltpu.VMEM(a.shape, a.dtype) for a in arrays]
        + [jax.ShapeDtypeStruct((8, 128), f32)],
        in_specs=[pl.BlockSpec(memory_space=pl.ANY)] * (1 + len(arrays)),
        out_specs=[VMEM] * (1 + len(arrays)),
        scratch_shapes=[pltpu.SemaphoreType.DMA((len(arrays),))],
        compiler_params=pltpu.CompilerParams(vmem_limit_bytes=2 << 20),
        cost_estimate=pl.CostEstimate(flops=0, bytes_accessed=2 * size, transcendentals=0),
    )(after, *[from_hbm(a) for a in arrays])
    return [fetched(c) for c in copies] + [token]


def tile_of(width, most):
    return width if width <= most else most


def iota(shape, axis):
    return lax.broadcasted_iota(i32, shape, axis).astype(f32)


def pick(onehot, values):
    return dot(onehot, values).astype(values.dtype)


def send_body(me, routed_in, activations_in, outgoing, routed, activations, sems):
    first_move = pltpu.make_async_copy(routed_in, routed, sems.at[0])
    second_move = pltpu.make_async_copy(activations_in, activations, sems.at[1])
    first_move.start()
    second_move.start()
    first_move.wait()
    capacity, tokens, total = outgoing.shape[0], activations.shape[0], routed.shape[1]
    low = (me[0] * tokens).astype(f32)
    where = routed[...].astype(f32)
    first = jnp.sum(jnp.where(where < low, 1.0, 0.0), axis=1, keepdims=True)
    here = (where >= low) & (where < low + tokens)
    slot = jnp.where(here, iota((1, total), 1) - first, -1.0)
    hit = slot == iota((capacity, total), 0)
    token = jnp.sum(jnp.where(hit, where - low + 1.0, 0.0), axis=1, keepdims=True) - 1.0
    onehot = jnp.where(token == iota((capacity, tokens), 1), 1.0, 0.0).astype(bf16)
    second_move.wait()
    width = activations.shape[1]
    tile = tile_of(width, 1024)
    for start in range(0, width, tile):
        span = slice(start, start + tile)
        outgoing[:, span] = pick(onehot, activations[:, span])


def map_body(tall, wide, tokens, heads_of, me, routed, balance, notes, *outs):
    pick_rows, in_order, columns, unmix, positions = outs
    count, total = tall * wide, routed.shape[1]
    share, capacity = total // count, pick_rows.shape[1] // count
    outbound, inbound = columns.shape[0], unmix.shape[0]
    my_z, my_y = lax.div(me[0], wide), lax.rem(me[0], wide)
    where, owner = routed[...].astype(f32), balance[...].astype(f32)
    lane = iota((1, total), 1)
    slot, place = jnp.zeros((1, total), f32), jnp.zeros((1, total), f32)
    out_base, out_block = notes[:outbound, 0:1], notes[:outbound, 1:2]
    in_base, in_source = notes[:inbound, 2:3], notes[:inbound, 3:4]
    for s in range(count):
        z, y = divmod(s, wide)
        from_block = lax.rem(my_z - z + tall, tall) * wide + lax.rem(my_y - y + wide, wide)
        to_block = lax.rem(z - my_z + tall, tall) * wide + lax.rem(y - my_y + wide, wide)
        peer = lax.rem(my_z + z, tall) * wide + lax.rem(my_y + y, wide)
        before = where < s * tokens
        first = jnp.sum(jnp.where(before, 1.0, 0.0), axis=1, keepdims=True)
        inside = (where < (s + 1) * tokens) & jnp.logical_not(before)
        start = (from_block * capacity).astype(f32)
        slot += jnp.where(inside, lane - first + start, 0.0)
        place += jnp.where(owner == s, (to_block * share).astype(f32), 0.0)
        out_base += jnp.where(out_block == y * tall + z, heads_of(peer).astype(f32), 0.0)
        in_base += jnp.where(in_source == s, (from_block * (outbound // count)).astype(f32), 0.0)
    mine = owner == iota((count, total), 0)
    earlier = jnp.where(iota((total, total), 0) < iota((total, total), 1), 1.0, 0.0)
    rank = dot(jnp.where(mine, 1.0, 0.0).astype(bf16), earlier.astype(bf16))
    place += jnp.sum(jnp.where(mine, rank, 0.0), axis=0, keepdims=True)
    placed = place == iota((total, total), 0)
    in_order[...] = jnp.where(placed, 1.0, 0.0).astype(bf16)
    at = jnp.sum(jnp.where(placed, where, 0.0), axis=1, keepdims=True)
    positions[...] = jnp.broadcast_to(at, positions.shape)
    slot_at = jnp.sum(jnp.where(placed, slot, 0.0), axis=1, keepdims=True)
    pick_rows[...] = jnp.where(slot_at == iota(pick_rows.shape, 1), 1.0, 0.0).astype(bf16)
    columns[...] = jnp.where(out_base == iota(columns.shape, 1), 1.0, 0.0).astype(bf16)
    unmix[...] = jnp.where(in_base == iota(unmix.shape, 1), 1.0, 0.0).astype(bf16)


def kv_body(count, extra, *refs):
    blocks = refs[:count]
    pick_rows, order, columns, gain, w_key, w_value = refs[count : count + 6]
    wide = len(refs) - count - 9 - extra
    normed, own, *sent, rows = refs[-3 - wide :]
    total, width = normed.shape
    tile = tile_of(width, 512)
    square = jnp.zeros((total, 1), f32)
    for start in range(0, width, tile):
        span = slice(start, start + tile)
        part = dot(pick_rows[...], jnp.concatenate([b[:, span] for b in blocks], axis=0))
        rows[:, span] = part.astype(bf16)
        square += jnp.sum(part * part, axis=1, keepdims=True)
    own[...] = rows[: own.shape[0], :]
    factor = lax.rsqrt(square / width + norm_eps)
    for start in range(0, width, tile):
        span = slice(start, start + tile)
        part = rows[:, span].astype(f32) * factor * gain[:, span]
        normed[:, span] = part.astype(bf16)
    keys = dot(normed[...], w_key[...]).astype(bf16)
    values = dot(normed[...], w_value[...]).astype(bf16)
    both = jnp.concatenate([keys, values], axis=1)
    turned = lax.dot_general(
        columns[...], both, (((1,), (1,)), ((), ())), preferred_element_type=f32
    ).astype(bf16)
    turned = dot(turned, order[...])
    each = turned.shape[0] // wide
    for dy in range(wide):
        sent[dy][...] = turned[dy * each : (dy + 1) * each].astype(bf16)


def query_body(normed, w_query, cosine, sine, query):
    raw = dot(normed[...], w_query[...])
    for head in range(query.shape[1] // HEAD_DIM):
        span = slice(head * HEAD_DIM, (head + 1) * HEAD_DIM)
        one = raw[:, span]
        turned = one * cosine[...] + pltpu.roll(one, HEAD_DIM // 2, 1) * sine[...]
        query[:, span] = turned.astype(bf16)


def attend_body(plane, kv_local, *refs):
    tall = plane[0]
    arrived, rest = refs[:tall], refs[tall:]
    query, unmix, cosine, sine, key_pos, query_pos, w_output = rest[:7]
    parts, heads_out = rest[7:-1], rest[-1]
    half = HEAD_DIM // 2
    heads = query.shape[1] // HEAD_DIM
    mixed = jnp.concatenate([a[...].astype(f32) for a in arrived], axis=0).astype(bf16)
    both = dot(unmix[...], mixed)
    allowed = key_pos[...].astype(f32) <= query_pos[:, 0:1]
    for group in range(kv_local):
        base = group * HEAD_DIM
        first, second = both[base : base + half], both[base + half : base + HEAD_DIM]
        keys = jnp.concatenate(
            [first * cosine[...] - second * sine[...], second * cosine[...] + first * sine[...]],
            axis=0,
        ).astype(bf16)
        base += kv_local * HEAD_DIM
        values = both[base : base + HEAD_DIM].astype(bf16)
        for head in range(group * heads // kv_local, (group + 1) * heads // kv_local):
            span = slice(head * HEAD_DIM, (head + 1) * HEAD_DIM)
            scores = dot(query[:, span], keys) * HEAD_DIM ** (-0.5)
            scores = jnp.where(allowed, scores, -1e30)
            weights = jnp.exp(scores - jnp.max(scores, axis=1, keepdims=True))
            probs = (weights / jnp.sum(weights, axis=1, keepdims=True)).astype(bf16)
            heads_out[:, span] = lax.dot_general(
                probs, values, (((1,), (1,)), ((), ())), preferred_element_type=f32
            ).astype(bf16)
    spread(heads_out, w_output, parts, plane, False)


def spread(left, weight, parts, plane, back):
    width = weight.shape[1]
    tile = tile_of(width, 512)
    for start in range(0, width, tile):
        span = slice(start, start + tile)
        product = dot(left[...], weight[:, span]).astype(bf16)
        store_parts(parts, *plane, span, product, back)


def mlp_body(plane, *refs):
    count = plane[0] * plane[1]
    blocks, (w_gate, w_up, w_down) = refs[:count], refs[count : count + 3]
    parts, (piece, inner) = refs[count + 3 : -2], refs[-2:]
    share = blocks[0].shape[0]
    for index, block in enumerate(blocks):
        piece[index * share : (index + 1) * share, :] = block[...]
    width = w_gate.shape[1]
    tile = tile_of(width, 256)
    for start in range(0, width, tile):
        span = slice(start, start + tile)
        gate = dot(piece[...], w_gate[:, span])
        upward = dot(piece[...], w_up[:, span])
        inner[:, span] = (gate / (1.0 + jnp.exp(-gate)) * upward).astype(bf16)
    spread(inner, w_down, parts, plane, True)


def on_device(
    activations,
    routed,
    balance,
    w_query,
    w_key,
    w_value,
    w_output,
    attn_gain,
    mlp_gain,
    w_gate,
    w_up,
    w_down,
    w_router,
):
    count = lax.axis_size("ctx")
    plane = tall, wide = plane_of(count)
    me = lax.axis_index("ctx").astype(i32).reshape(1)
    tokens, model = activations.shape
    total = routed.shape[0]
    share = total // count
    capacity = 2 * share
    local_heads = w_query.shape[1] // HEAD_DIM
    group_size = HEADS // KV_HEADS
    kv_local = max(1, local_heads // group_size)
    key_cols = w_key.shape[1]
    depth = key_cols // KV_HEADS
    scalar = pl.BlockSpec(memory_space=pltpu.SMEM)
    in_hbm = pl.BlockSpec(memory_space=pl.ANY)
    routed, balance = routed.reshape(1, total), balance.reshape(1, total)

    (outgoing,) = kernel_call(
        send_body,
        [((capacity, model), bf16)],
        [me, from_hbm(routed), from_hbm(activations)],
        [
            pltpu.VMEM(routed.shape, i32),
            pltpu.VMEM(activations.shape, bf16),
            pltpu.SemaphoreType.DMA((2,)),
        ],
        specs=[scalar, in_hbm, in_hbm],
        flops=2 * capacity * tokens * model,
    )
    attn_gain, w_key, w_value, w_query, token_1 = load(
        outgoing, attn_gain.reshape(1, model), w_key, w_value, w_query
    )

    each = kv_local * 2 * depth
    notes = np.zeros((max(count * each, 2 * kv_local * HEAD_DIM), 4), np.float32)
    block, local, side, entry = np.indices((count, kv_local, 2, depth)).reshape(4, -1)
    notes[: count * each, 0] = side * key_cols + entry * KV_HEADS + local
    notes[: count * each, 1] = block
    side, local, source, entry = np.indices((2, kv_local, count, depth)).reshape(4, -1)
    notes[: 2 * kv_local * HEAD_DIM, 2] = (local * 2 + side) * depth + entry
    notes[: 2 * kv_local * HEAD_DIM, 3] = source
    pick_rows, in_order, columns, unmix, positions = kernel_call(
        functools.partial(
            map_body, tall, wide, tokens, lambda peer: lax.div(peer * local_heads, group_size)
        ),
        [
            ((total, count * capacity), bf16),
            ((total, total), bf16),
            ((count * each, 2 * key_cols), bf16),
            ((2 * kv_local * HEAD_DIM, count * each), bf16),
            ((total, HEAD_DIM // 2), f32),
        ],
        [me, routed, balance, notes],
        specs=[scalar, VMEM, VMEM, VMEM],
    )
    blocks = gather_rows(outgoing, tall, wide, [token_1, positions])
    near = blocks[2 * wide]
    w_output, *token_2 = load(near, w_output)
    w_gate, *token_3 = load(near, w_gate)
    loaded = token_2 + token_3

    half = HEAD_DIM // 2
    steps_f = jnp.arange(half, dtype=f32)
    freqs = jnp.exp(-jnp.log(f32(rope_base)) * (2.0 * steps_f / HEAD_DIM))
    q_angles = positions * freqs[None, :]
    q_cos, q_sin = jnp.cos(q_angles), jnp.sin(q_angles)
    q_cos = jnp.concatenate([q_cos, q_cos], axis=1)
    q_sin = jnp.concatenate([-q_sin, q_sin], axis=1)
    k_angles = freqs[:, None] * routed.astype(f32)
    k_cos, k_sin = jnp.cos(k_angles), jnp.sin(k_angles)

    normed, own, *sent = kernel_call(
        functools.partial(kv_body, count, len(loaded)),
        [((total, model), bf16), ((share, model), bf16)] + [((tall * each, total), bf16)] * wide,
        [*blocks, pick_rows, in_order, columns, attn_gain, w_key, w_value, *loaded],
        [pltpu.VMEM((total, model), bf16)],
        flops=2 * total * model * 512,
    )
    arrived = exchange(sent, tall, wide)
    heads_wide = local_heads * HEAD_DIM
    (query,) = kernel_call(
        query_body,
        [((total, heads_wide), bf16)],
        [normed, w_query, q_cos, q_sin],
        flops=2 * total * model * heads_wide,
    )
    part_shapes = sum_shapes(tall, wide, share, model)
    attn_parts = kernel_call(
        functools.partial(attend_body, plane, kv_local),
        part_shapes,
        [*arrived, query, unmix, k_cos, k_sin, routed, positions, w_output],
        [pltpu.VMEM((total, heads_wide), bf16)],
        flops=2 * total * model * heads_wide,
    )
    attn_own, w_down = scatter_sum(attn_parts, tall, wide, [w_down])
    own_rows = own.astype(f32)
    hidden = own_rows + attn_own
    mean_sq = jnp.mean(hidden * hidden, axis=-1, keepdims=True)
    mnorm = (hidden * lax.rsqrt(mean_sq + norm_eps) * mlp_gain).astype(bf16)
    pieces = gather_blocks(mnorm, tall, wide)
    w_up, _ = load(mnorm, w_up)
    hidden_units = w_gate.shape[1]
    mlp_parts = kernel_call(
        functools.partial(mlp_body, plane),
        part_shapes,
        [*pieces, w_gate, w_up, w_down],
        [pltpu.VMEM((total, model), bf16), pltpu.VMEM((total, hidden_units), bf16)],
        flops=6 * total * model * hidden_units,
    )
    mlp_own = scatter_sum(mlp_parts, tall, wide)
    router_score = jnp.sum(own_rows * w_router[None, :], axis=1, keepdims=True)
    return (own_rows + router_score * (attn_own + mlp_own)).astype(bf16)


def solution(mesh):
    in_specs = (
        P(("dp", "ctx"), None),
        P("dp"),
        P("dp"),
        P(None, "ctx"),
        P(None, "ctx"),
        P(None, "ctx"),
        P("ctx", None),
        P(),
        P(),
        P(None, "ctx"),
        P(None, "ctx"),
        P("ctx", None),
        P(),
    )
    out_specs = P(("dp", "ctx"), None)
    return jax.shard_map(
        on_device, mesh=mesh, in_specs=in_specs, out_specs=out_specs, check_vma=False
    )
```

```python
import functools

import jax
import jax.numpy as jnp
import numpy as np
from jax import lax
from jax.experimental import pallas as pl
from jax.experimental.pallas import tpu as pltpu
from jax.sharding import PartitionSpec as P

HEADS = 32
KV_HEADS = 8
HEAD_DIM = 128

rope_base = 500000.0
norm_eps = 1e-05

bf16, f32, i32 = jnp.bfloat16, jnp.float32, jnp.int32
VMEM = pl.BlockSpec(memory_space=pltpu.VMEM)


def plane_of(count):
    wide = max(y for y in range(1, count + 1) if count % y == 0 and 2 * y * y <= max(count, 2))
    return count // wide, wide


def shift(block, tall, wide, dz, dy, keep=None):
    pairs = [
        (z * wide + y, (z + dz) % tall * wide + (y + dy) % wide)
        for z in range(tall)
        for y in range(wide)
        if keep is None or keep(z)
    ]
    return lax.ppermute(block, "ctx", pairs)


def tie_body(count, *refs):
    total = refs[0][...]
    for ref in refs[1:count]:
        total = total + ref[...]
    refs[-1][...] = total


def tie(blocks, tokens):
    return kernel_call(
        functools.partial(tie_body, len(blocks)),
        [(blocks[0].shape, blocks[0].dtype)],
        [*blocks, *tokens],
        specs=[VMEM] * len(blocks) + [pl.BlockSpec(memory_space=pl.ANY)] * len(tokens),
    )[0]


def gather_rows(block, tall, wide, tokens):
    blocks = {(0, 0): block}
    for dy in range(1, wide):
        blocks[0, dy] = shift(block, tall, wide, 0, dy)
    first = [*tokens, *(blocks[0, dy] for dy in range(1, wide))]
    for dz in range(tall - 1, 0, -1):
        if tall != 4 or dz != 2:
            blocks[dz, 0] = shift(block, tall, wide, dz, 0)
    blocks[tall - 1, 0] = tie([blocks[tall - 1, 0]], first)
    if tall == 4:
        for dy in range(1, wide):
            blocks[3, dy] = shift(blocks[3, 0], tall, wide, 0, dy)
        up = shift(blocks[1, 0], tall, wide, 1, 0, lambda z: z in (1, 2))
        down = shift(blocks[3, 0], tall, wide, -1, 0, lambda z: z in (1, 2))
        blocks[2, 0] = tie([up, down], [blocks[3, dy] for dy in range(1, wide)])
    for dz in range(1, tall):
        for dy in range(1, wide):
            if (dz, dy) not in blocks:
                blocks[dz, dy] = shift(blocks[dz, 0], tall, wide, 0, dy)
    return [blocks[dz, dy] for dz in range(tall) for dy in range(wide)]


def pack_body(tall, *refs):
    wide = len(refs) - tall
    each = refs[0].shape[0] // tall
    for dz in range(tall):
        values = [ref[...].astype(f32)[dz * each : (dz + 1) * each] for ref in refs[:wide]]
        refs[wide + dz][...] = jnp.concatenate(values, axis=0).astype(bf16)


def exchange(parts, tall, wide):
    shape = ((parts[0].shape[0] // tall * wide, parts[0].shape[1]), bf16)
    crossed = [parts[0]] + [shift(parts[dy], tall, wide, 0, dy) for dy in range(1, wide)]
    packed = kernel_call(functools.partial(pack_body, tall), [shape] * tall, crossed)
    pairs = [
        [(z * wide + y, (z ^ kz) * wide + y) for z in range(tall) for y in range(wide)]
        for kz in range(tall)
    ]
    return [packed[0]] + [lax.ppermute(packed[k], "ctx", pairs[k]) for k in range(1, tall)]


def gather_blocks(block, tall, wide):
    blocks = {(dz, 0): shift(block, tall, wide, dz, 0) if dz else block for dz in range(tall)}
    for dz in range(tall):
        for dy in range(1, wide):
            blocks[dz, dy] = shift(blocks[dz, 0], tall, wide, 0, dy)
    return [blocks[dz, dy] for dz in range(tall) for dy in range(wide)]


def sum_groups(tall, fine):
    order = [tall // 2, *range(1, tall // 2), *range(tall // 2 + 1, tall), 0]
    half = [order[: tall // 2], order[tall // 2 :]]
    return [[dz] for dz in half[0]] + half[1:] if fine else half


def sum_shapes(tall, wide, share, model, fine):
    shapes = [((share, model), bf16)] * tall
    for group in sum_groups(tall, fine):
        shapes += [((len(group) * share, model), bf16)] * (wide - 1)
    return shapes


def store_parts(parts, tall, wide, span, product, last):
    share = parts[0].shape[0]
    sign = -1 if last else 1

    def rows(dz, dy):
        at = sign * dz % tall * wide + sign * dy % wide
        return product[at * share : (at + 1) * share, :]

    for dz in range(tall):
        parts[dz][:, span] = rows(dz, 0)
    for which, group in enumerate(sum_groups(tall, last)):
        for dy in range(1, wide):
            out = parts[tall + which * (wide - 1) + dy - 1]
            for place, dz in enumerate(group):
                out[place * share : (place + 1) * share, span] = rows(dz, dy)


def scatter_sum(parts, tall, wide, last, loads=()):
    share = parts[0].shape[0]
    others = wide - 1
    loaded = []
    crossed = [shift(p, tall, wide, 0, i % others + 1) for i, p in enumerate(parts[tall:])]
    if loads:
        *loaded, token = load(parts[0], *loads)
        crossed[others] = tie([crossed[others]], [token])
    total = None
    for which, group in enumerate(sum_groups(tall, last)):
        for place, dz in enumerate(group):
            lane = parts[dz].astype(f32)
            for other in crossed[which * others : (which + 1) * others]:
                lane = lane + other[place * share : (place + 1) * share].astype(f32)
            if dz:
                lane = shift(lane.astype(bf16), tall, wide, dz, 0).astype(f32)
            total = lane if total is None else total + lane
    return (total, *loaded) if loads else total


def dot(a, b):
    return jnp.dot(a, b, preferred_element_type=f32)


def from_hbm(weight):
    return pltpu.with_memory_space_constraint(weight, pltpu.HBM)


def fetched(weight):
    return pltpu.with_memory_space_constraint(weight, pltpu.VMEM)


def kernel_call(body, outs, args, scratch=(), limit=14, flops=0, specs=None):
    return pl.pallas_call(
        body,
        out_shape=[jax.ShapeDtypeStruct(s, d) for s, d in outs],
        in_specs=specs or [VMEM] * len(args),
        out_specs=[VMEM] * len(outs),
        scratch_shapes=list(scratch),
        compiler_params=pltpu.CompilerParams(vmem_limit_bytes=limit << 20),
        cost_estimate=pl.CostEstimate(flops=flops, bytes_accessed=1 << 20, transcendentals=0),
    )(*args)


def load_body(count, *refs):
    sources, copies, sems = refs[1 : 1 + count], refs[1 + count : -2], refs[-1]
    moves = [
        pltpu.make_async_copy(a, b, sems.at[i]) for i, (a, b) in enumerate(zip(sources, copies))
    ]
    for move in moves:
        move.start()
    for move in moves:
        move.wait()
    refs[-2][...] = jnp.zeros_like(refs[-2])


def load(after, *arrays):
    size = sum(a.size * a.dtype.itemsize for a in arrays)
    *copies, token = pl.pallas_call(
        functools.partial(load_body, len(arrays)),
        out_shape=[pltpu.VMEM(a.shape, a.dtype) for a in arrays]
        + [jax.ShapeDtypeStruct((8, 128), f32)],
        in_specs=[pl.BlockSpec(memory_space=pl.ANY)] * (1 + len(arrays)),
        out_specs=[VMEM] * (1 + len(arrays)),
        scratch_shapes=[pltpu.SemaphoreType.DMA((len(arrays),))],
        compiler_params=pltpu.CompilerParams(vmem_limit_bytes=2 << 20),
        cost_estimate=pl.CostEstimate(flops=0, bytes_accessed=2 * size, transcendentals=0),
    )(after, *[from_hbm(a) for a in arrays])
    return [fetched(c) for c in copies] + [token]


def tile_of(width, most):
    return width if width <= most else most


def iota(shape, axis):
    return lax.broadcasted_iota(i32, shape, axis).astype(f32)


def pick(onehot, values):
    return dot(onehot, values).astype(values.dtype)


def send_body(me, routed_in, activations_in, outgoing, routed, activations, sems):
    first_move = pltpu.make_async_copy(routed_in, routed, sems.at[0])
    second_move = pltpu.make_async_copy(activations_in, activations, sems.at[1])
    first_move.start()
    second_move.start()
    first_move.wait()
    capacity, tokens, total = outgoing.shape[0], activations.shape[0], routed.shape[1]
    low = (me[0] * tokens).astype(f32)
    where = routed[...].astype(f32)
    first = jnp.sum(jnp.where(where < low, 1.0, 0.0), axis=1, keepdims=True)
    here = (where >= low) & (where < low + tokens)
    slot = jnp.where(here, iota((1, total), 1) - first, -1.0)
    hit = slot == iota((capacity, total), 0)
    token = jnp.sum(jnp.where(hit, where - low + 1.0, 0.0), axis=1, keepdims=True) - 1.0
    onehot = jnp.where(token == iota((capacity, tokens), 1), 1.0, 0.0).astype(bf16)
    second_move.wait()
    width = activations.shape[1]
    tile = tile_of(width, 1024)
    for start in range(0, width, tile):
        span = slice(start, start + tile)
        outgoing[:, span] = pick(onehot, activations[:, span])


def map_body(tall, wide, tokens, heads_of, me, routed, balance, notes, *outs):
    pick_rows, in_order, columns, unmix, positions = outs
    count, total = tall * wide, routed.shape[1]
    share, capacity = total // count, pick_rows.shape[1] // count
    outbound, inbound = columns.shape[0], unmix.shape[0]
    my_z, my_y = lax.div(me[0], wide), lax.rem(me[0], wide)
    where, owner = routed[...].astype(f32), balance[...].astype(f32)
    lane = iota((1, total), 1)
    slot, place = jnp.zeros((1, total), f32), jnp.zeros((1, total), f32)
    out_base, out_block = notes[:outbound, 0:1], notes[:outbound, 1:2]
    in_base, in_source = notes[:inbound, 2:3], notes[:inbound, 3:4]
    for s in range(count):
        z, y = divmod(s, wide)
        from_block = lax.rem(my_z - z + tall, tall) * wide + lax.rem(my_y - y + wide, wide)
        to_block = lax.rem(z - my_z + tall, tall) * wide + lax.rem(y - my_y + wide, wide)
        peer = (my_z ^ z) * wide + lax.rem(my_y + y, wide)
        lot = (my_z ^ z) * wide + lax.rem(my_y - y + wide, wide)
        before = where < s * tokens
        first = jnp.sum(jnp.where(before, 1.0, 0.0), axis=1, keepdims=True)
        inside = (where < (s + 1) * tokens) & jnp.logical_not(before)
        start = (from_block * capacity).astype(f32)
        slot += jnp.where(inside, lane - first + start, 0.0)
        place += jnp.where(owner == s, (to_block * share).astype(f32), 0.0)
        out_base += jnp.where(out_block == y * tall + z, heads_of(peer).astype(f32), 0.0)
        in_base += jnp.where(in_source == s, (lot * (outbound // count)).astype(f32), 0.0)
    mine = owner == iota((count, total), 0)
    earlier = jnp.where(iota((total, total), 0) < iota((total, total), 1), 1.0, 0.0)
    rank = dot(jnp.where(mine, 1.0, 0.0).astype(bf16), earlier.astype(bf16))
    place += jnp.sum(jnp.where(mine, rank, 0.0), axis=0, keepdims=True)
    placed = place == iota((total, total), 0)
    in_order[...] = jnp.where(placed, 1.0, 0.0).astype(bf16)
    at = jnp.sum(jnp.where(placed, where, 0.0), axis=1, keepdims=True)
    positions[...] = jnp.broadcast_to(at, positions.shape)
    slot_at = jnp.sum(jnp.where(placed, slot, 0.0), axis=1, keepdims=True)
    pick_rows[...] = jnp.where(slot_at == iota(pick_rows.shape, 1), 1.0, 0.0).astype(bf16)
    columns[...] = jnp.where(out_base == iota(columns.shape, 1), 1.0, 0.0).astype(bf16)
    unmix[...] = jnp.where(in_base == iota(unmix.shape, 1), 1.0, 0.0).astype(bf16)


def kv_body(count, extra, *refs):
    blocks = refs[:count]
    pick_rows, order, columns, gain, w_key, w_value = refs[count : count + 6]
    wide = len(refs) - count - 9 - extra
    normed, own, *sent, rows = refs[-3 - wide :]
    total, width = normed.shape
    tile = tile_of(width, 512)
    square = jnp.zeros((total, 1), f32)
    for start in range(0, width, tile):
        span = slice(start, start + tile)
        part = dot(pick_rows[...], jnp.concatenate([b[:, span] for b in blocks], axis=0))
        rows[:, span] = part.astype(bf16)
        square += jnp.sum(part * part, axis=1, keepdims=True)
    own[...] = rows[: own.shape[0], :]
    factor = lax.rsqrt(square / width + norm_eps)
    for start in range(0, width, tile):
        span = slice(start, start + tile)
        part = rows[:, span].astype(f32) * factor * gain[:, span]
        normed[:, span] = part.astype(bf16)
    keys = dot(normed[...], w_key[...]).astype(bf16)
    values = dot(normed[...], w_value[...]).astype(bf16)
    both = jnp.concatenate([keys, values], axis=1)
    turned = lax.dot_general(
        columns[...], both, (((1,), (1,)), ((), ())), preferred_element_type=f32
    ).astype(bf16)
    turned = dot(turned, order[...])
    each = turned.shape[0] // wide
    for dy in range(wide):
        sent[dy][...] = turned[dy * each : (dy + 1) * each].astype(bf16)


def query_body(normed, w_query, cosine, sine, query):
    raw = dot(normed[...], w_query[...])
    for head in range(query.shape[1] // HEAD_DIM):
        span = slice(head * HEAD_DIM, (head + 1) * HEAD_DIM)
        one = raw[:, span]
        turned = one * cosine[...] + pltpu.roll(one, HEAD_DIM // 2, 1) * sine[...]
        query[:, span] = turned.astype(bf16)


def attend_body(plane, kv_local, *refs):
    tall = plane[0]
    arrived, rest = refs[:tall], refs[tall:]
    query, unmix, cosine, sine, key_pos, query_pos, w_output = rest[:7]
    parts, heads_out = rest[7:-1], rest[-1]
    half = HEAD_DIM // 2
    heads = query.shape[1] // HEAD_DIM
    mixed = jnp.concatenate([a[...].astype(f32) for a in arrived], axis=0).astype(bf16)
    both = dot(unmix[...], mixed)
    allowed = key_pos[...].astype(f32) <= query_pos[:, 0:1]
    for group in range(kv_local):
        base = group * HEAD_DIM
        first, second = both[base : base + half], both[base + half : base + HEAD_DIM]
        keys = jnp.concatenate(
            [first * cosine[...] - second * sine[...], second * cosine[...] + first * sine[...]],
            axis=0,
        ).astype(bf16)
        base += kv_local * HEAD_DIM
        values = both[base : base + HEAD_DIM].astype(bf16)
        for head in range(group * heads // kv_local, (group + 1) * heads // kv_local):
            span = slice(head * HEAD_DIM, (head + 1) * HEAD_DIM)
            scores = dot(query[:, span], keys) * HEAD_DIM ** (-0.5)
            scores = jnp.where(allowed, scores, -1e30)
            weights = jnp.exp(scores - jnp.max(scores, axis=1, keepdims=True))
            probs = (weights / jnp.sum(weights, axis=1, keepdims=True)).astype(bf16)
            heads_out[:, span] = lax.dot_general(
                probs, values, (((1,), (1,)), ((), ())), preferred_element_type=f32
            ).astype(bf16)
    spread(heads_out, w_output, parts, plane, False)


def spread(left, weight, parts, plane, back):
    width = weight.shape[1]
    tile = tile_of(width, 512)
    for start in range(0, width, tile):
        span = slice(start, start + tile)
        product = dot(left[...], weight[:, span]).astype(bf16)
        store_parts(parts, *plane, span, product, back)


def mlp_body(plane, *refs):
    count = plane[0] * plane[1]
    blocks, (w_gate, w_up, w_down) = refs[:count], refs[count : count + 3]
    parts, (piece, inner) = refs[count + 3 : -2], refs[-2:]
    share = blocks[0].shape[0]
    for index, block in enumerate(blocks):
        piece[index * share : (index + 1) * share, :] = block[...]
    width = w_gate.shape[1]
    tile = tile_of(width, 256)
    for start in range(0, width, tile):
        span = slice(start, start + tile)
        gate = dot(piece[...], w_gate[:, span])
        upward = dot(piece[...], w_up[:, span])
        inner[:, span] = (gate / (1.0 + jnp.exp(-gate)) * upward).astype(bf16)
    spread(inner, w_down, parts, plane, True)


def on_device(
    activations,
    routed,
    balance,
    w_query,
    w_key,
    w_value,
    w_output,
    attn_gain,
    mlp_gain,
    w_gate,
    w_up,
    w_down,
    w_router,
):
    count = lax.axis_size("ctx")
    plane = tall, wide = plane_of(count)
    me = lax.axis_index("ctx").astype(i32).reshape(1)
    tokens, model = activations.shape
    total = routed.shape[0]
    share = total // count
    capacity = 2 * share
    local_heads = w_query.shape[1] // HEAD_DIM
    group_size = HEADS // KV_HEADS
    kv_local = max(1, local_heads // group_size)
    key_cols = w_key.shape[1]
    depth = key_cols // KV_HEADS
    scalar = pl.BlockSpec(memory_space=pltpu.SMEM)
    in_hbm = pl.BlockSpec(memory_space=pl.ANY)
    routed, balance = routed.reshape(1, total), balance.reshape(1, total)

    (outgoing,) = kernel_call(
        send_body,
        [((capacity, model), bf16)],
        [me, from_hbm(routed), from_hbm(activations)],
        [
            pltpu.VMEM(routed.shape, i32),
            pltpu.VMEM(activations.shape, bf16),
            pltpu.SemaphoreType.DMA((2,)),
        ],
        specs=[scalar, in_hbm, in_hbm],
        flops=2 * capacity * tokens * model,
    )
    attn_gain, w_key, w_value, w_query, token_1 = load(
        outgoing, attn_gain.reshape(1, model), w_key, w_value, w_query
    )

    each = kv_local * 2 * depth
    notes = np.zeros((max(count * each, 2 * kv_local * HEAD_DIM), 4), np.float32)
    block, local, side, entry = np.indices((count, kv_local, 2, depth)).reshape(4, -1)
    notes[: count * each, 0] = side * key_cols + entry * KV_HEADS + local
    notes[: count * each, 1] = block
    side, local, source, entry = np.indices((2, kv_local, count, depth)).reshape(4, -1)
    notes[: 2 * kv_local * HEAD_DIM, 2] = (local * 2 + side) * depth + entry
    notes[: 2 * kv_local * HEAD_DIM, 3] = source
    pick_rows, in_order, columns, unmix, positions = kernel_call(
        functools.partial(
            map_body, tall, wide, tokens, lambda peer: lax.div(peer * local_heads, group_size)
        ),
        [
            ((total, count * capacity), bf16),
            ((total, total), bf16),
            ((count * each, 2 * key_cols), bf16),
            ((2 * kv_local * HEAD_DIM, count * each), bf16),
            ((total, HEAD_DIM // 2), f32),
        ],
        [me, routed, balance, notes],
        specs=[scalar, VMEM, VMEM, VMEM],
    )
    blocks = gather_rows(outgoing, tall, wide, [token_1, positions])
    near = blocks[2 * wide]
    w_output, *token_2 = load(near, w_output)
    w_gate, *token_3 = load(near, w_gate)
    loaded = token_2 + token_3

    half = HEAD_DIM // 2
    steps_f = jnp.arange(half, dtype=f32)
    freqs = jnp.exp(-jnp.log(f32(rope_base)) * (2.0 * steps_f / HEAD_DIM))
    q_angles = positions * freqs[None, :]
    q_cos, q_sin = jnp.cos(q_angles), jnp.sin(q_angles)
    q_cos = jnp.concatenate([q_cos, q_cos], axis=1)
    q_sin = jnp.concatenate([-q_sin, q_sin], axis=1)
    k_angles = freqs[:, None] * routed.astype(f32)
    k_cos, k_sin = jnp.cos(k_angles), jnp.sin(k_angles)

    normed, own, *sent = kernel_call(
        functools.partial(kv_body, count, len(loaded)),
        [((total, model), bf16), ((share, model), bf16)] + [((tall * each, total), bf16)] * wide,
        [*blocks, pick_rows, in_order, columns, attn_gain, w_key, w_value, *loaded],
        [pltpu.VMEM((total, model), bf16)],
        flops=2 * total * model * 512,
    )
    arrived = exchange(sent, tall, wide)
    heads_wide = local_heads * HEAD_DIM
    (query,) = kernel_call(
        query_body,
        [((total, heads_wide), bf16)],
        [normed, w_query, q_cos, q_sin],
        flops=2 * total * model * heads_wide,
    )
    attn_parts = kernel_call(
        functools.partial(attend_body, plane, kv_local),
        sum_shapes(tall, wide, share, model, False),
        [*arrived, query, unmix, k_cos, k_sin, routed, positions, w_output],
        [pltpu.VMEM((total, heads_wide), bf16)],
        flops=2 * total * model * heads_wide,
    )
    attn_own, w_down = scatter_sum(attn_parts, tall, wide, False, [w_down])
    own_rows = own.astype(f32)
    hidden = own_rows + attn_own
    mean_sq = jnp.mean(hidden * hidden, axis=-1, keepdims=True)
    mnorm = (hidden * lax.rsqrt(mean_sq + norm_eps) * mlp_gain).astype(bf16)
    pieces = gather_blocks(mnorm, tall, wide)
    w_up, _ = load(mnorm, w_up)
    hidden_units = w_gate.shape[1]
    mlp_parts = kernel_call(
        functools.partial(mlp_body, plane),
        sum_shapes(tall, wide, share, model, True),
        [*pieces, w_gate, w_up, w_down],
        [pltpu.VMEM((total, model), bf16), pltpu.VMEM((total, hidden_units), bf16)],
        flops=6 * total * model * hidden_units,
    )
    mlp_own = scatter_sum(mlp_parts, tall, wide, True)
    router_score = jnp.sum(own_rows * w_router[None, :], axis=1, keepdims=True)
    return (own_rows + router_score * (attn_own + mlp_own)).astype(bf16)


def solution(mesh):
    in_specs = (
        P(("dp", "ctx"), None),
        P("dp"),
        P("dp"),
        P(None, "ctx"),
        P(None, "ctx"),
        P(None, "ctx"),
        P("ctx", None),
        P(),
        P(),
        P(None, "ctx"),
        P(None, "ctx"),
        P("ctx", None),
        P(),
    )
    out_specs = P(("dp", "ctx"), None)
    return jax.shard_map(
        on_device, mesh=mesh, in_specs=in_specs, out_specs=out_specs, check_vma=False
    )
```

```python
import functools

import jax
import jax.numpy as jnp
import numpy as np
from jax import lax
from jax.experimental import pallas as pl
from jax.experimental.pallas import tpu as pltpu
from jax.sharding import PartitionSpec as P

HEADS = 32
KV_HEADS = 8
HEAD_DIM = 128

rope_base = 500000.0
norm_eps = 1e-05

bf16, f32, i32 = jnp.bfloat16, jnp.float32, jnp.int32
VMEM = pl.BlockSpec(memory_space=pltpu.VMEM)


def plane_of(count):
    wide = max(y for y in range(1, count + 1) if count % y == 0 and 2 * y * y <= max(count, 2))
    return count // wide, wide


def shift(block, tall, wide, dz, dy, keep=None):
    pairs = [
        (z * wide + y, (z + dz) % tall * wide + (y + dy) % wide)
        for z in range(tall)
        for y in range(wide)
        if keep is None or keep(z)
    ]
    return lax.ppermute(block, "ctx", pairs)


def tie_body(count, *refs):
    total = refs[0][...]
    for ref in refs[1:count]:
        total = total + ref[...]
    refs[-1][...] = total


def tie(blocks, tokens):
    return kernel_call(
        functools.partial(tie_body, len(blocks)),
        [(blocks[0].shape, blocks[0].dtype)],
        [*blocks, *tokens],
        specs=[VMEM] * len(blocks) + [pl.BlockSpec(memory_space=pl.ANY)] * len(tokens),
    )[0]


def lots_of(tall):
    return 5 if tall == 4 else tall


def lot_of(tall, my_z, z):
    if tall != 4:
        return lax.rem(my_z - z + tall, tall)
    ahead = z - my_z
    far = jnp.maximum(2 * jnp.abs(ahead) - 2, 0)
    return jnp.where(ahead == -1, 1, jnp.where(ahead == 1, 3, far))


def send(block, wide, moves, ky=0):
    pairs = [(a * wide + y, b * wide + (y + ky) % wide) for a, b in moves for y in range(wide)]
    return lax.ppermute(block, "ctx", pairs)


def gather_rows(block, tall, wide, tokens):
    blocks = {(0, 0): block}
    across = range(1, wide)
    for dy in across:
        blocks[0, dy] = shift(block, tall, wide, 0, dy)
    first = [*tokens, *(blocks[0, dy] for dy in across)]
    if tall != 4:
        for dz in range(1, tall):
            blocks[dz, 0] = shift(block, tall, wide, dz, 0)
        blocks[1, 0] = tie([blocks[1, 0]], first)
        for dz in range(1, tall):
            for dy in across:
                blocks[dz, dy] = shift(blocks[dz, 0], tall, wide, 0, dy)
    else:
        blocks[1, 0] = send(block, wide, [(0, 1), (1, 2), (2, 3)])
        blocks[3, 0] = tie([send(block, wide, [(1, 0), (2, 1), (3, 2)])], first)
        for dy in across:
            blocks[3, dy] = send(blocks[3, 0], wide, [(0, 0), (1, 1), (2, 2)], dy)
        down = send(blocks[3, 0], wide, [(1, 0), (2, 1)])
        for dy in across:
            blocks[1, dy] = send(blocks[1, 0], wide, [(1, 1), (2, 2), (3, 3)], dy)
        up = send(blocks[1, 0], wide, [(1, 2), (2, 3)])
        blocks[4, 0] = send(tie([block], [blocks[1, 0]]), wide, [(0, 3), (3, 0)])
        blocks[2, 0] = tie([up, down], [blocks[3, dy] for dy in across])
        for dy in across:
            blocks[2, dy] = shift(blocks[2, 0], tall, wide, 0, dy)
            blocks[4, dy] = send(blocks[4, 0], wide, [(0, 0), (3, 3)], dy)
    return [blocks[lot, dy] for lot in range(lots_of(tall)) for dy in range(wide)]


def pack_body(tall, *refs):
    wide = len(refs) - tall
    each = refs[0].shape[0] // tall
    for dz in range(tall):
        values = [ref[...].astype(f32)[dz * each : (dz + 1) * each] for ref in refs[:wide]]
        refs[wide + dz][...] = jnp.concatenate(values, axis=0).astype(bf16)


def exchange(parts, tall, wide):
    shape = ((parts[0].shape[0] // tall * wide, parts[0].shape[1]), bf16)
    crossed = [parts[0]] + [shift(parts[dy], tall, wide, 0, dy) for dy in range(1, wide)]
    packed = kernel_call(functools.partial(pack_body, tall), [shape] * tall, crossed)
    return [packed[0]] + [shift(packed[dz], tall, wide, dz, 0) for dz in range(1, tall)]


def gather_blocks(block, tall, wide):
    blocks = {(dz, 0): shift(block, tall, wide, dz, 0) if dz else block for dz in range(tall)}
    for dz in range(tall):
        for dy in range(1, wide):
            blocks[dz, dy] = shift(blocks[dz, 0], tall, wide, 0, dy)
    return [blocks[dz, dy] for dz in range(tall) for dy in range(wide)]


def sum_order(tall):
    order = [tall // 2, *range(1, tall // 2), *range(tall // 2 + 1, tall), 0]
    return order[: tall // 2], order[tall // 2 :]


def sum_shapes(tall, wide, share, model):
    kept = [((share, model), bf16)] * tall
    return kept + [((tall // 2 * share, model), bf16)] * (2 * (wide - 1))


def store_parts(parts, tall, wide, span, product, back):
    share = parts[0].shape[0]
    sign = -1 if back else 1

    def rows(dz, dy):
        at = sign * dz % tall * wide + sign * dy % wide
        return product[at * share : (at + 1) * share, :]

    for dz in range(tall):
        parts[dz][:, span] = rows(dz, 0)
    for dy in range(1, wide):
        for which, group in enumerate(sum_order(tall)):
            out = parts[tall + 2 * (dy - 1) + which]
            for place, dz in enumerate(group):
                out[place * share : (place + 1) * share, span] = rows(dz, dy)


def scatter_sum(parts, tall, wide, loads=()):
    share = parts[0].shape[0]
    loaded = []
    crossed = [shift(p, tall, wide, 0, i // 2 + 1) for i, p in enumerate(parts[tall:])]
    if loads:
        *copy, token = load(parts[0], loads[0])
        loaded += copy
        crossed[1] = tie([crossed[1]], [token])
    total = None
    for which, group in enumerate(sum_order(tall)):
        for place, dz in enumerate(group):
            lane = parts[dz].astype(f32)
            for dy in range(1, wide):
                other = crossed[2 * (dy - 1) + which]
                lane = lane + other[place * share : (place + 1) * share].astype(f32)
            if dz:
                sent = lane.astype(bf16)
                lane = shift(sent, tall, wide, dz, 0)
                if len(loads) > 1 and dz == tall - 1:
                    *copy, token = load(sent, loads[1])
                    loaded += copy
                    lane = tie([lane], [token])
                lane = lane.astype(f32)
            total = lane if total is None else total + lane
    return (total, *loaded) if loads else total


def dot(a, b):
    return jnp.dot(a, b, preferred_element_type=f32)


def from_hbm(weight):
    return pltpu.with_memory_space_constraint(weight, pltpu.HBM)


def fetched(weight):
    return pltpu.with_memory_space_constraint(weight, pltpu.VMEM)


def kernel_call(body, outs, args, scratch=(), limit=14, flops=0, specs=None):
    return pl.pallas_call(
        body,
        out_shape=[jax.ShapeDtypeStruct(s, d) for s, d in outs],
        in_specs=specs or [VMEM] * len(args),
        out_specs=[VMEM] * len(outs),
        scratch_shapes=list(scratch),
        compiler_params=pltpu.CompilerParams(vmem_limit_bytes=limit << 20),
        cost_estimate=pl.CostEstimate(flops=flops, bytes_accessed=1 << 20, transcendentals=0),
    )(*args)


def load_body(count, *refs):
    sources, copies, sems = refs[1 : 1 + count], refs[1 + count : -2], refs[-1]
    moves = [
        pltpu.make_async_copy(a, b, sems.at[i]) for i, (a, b) in enumerate(zip(sources, copies))
    ]
    for move in moves:
        move.start()
    for move in moves:
        move.wait()
    refs[-2][...] = jnp.zeros_like(refs[-2])


def load(after, *arrays):
    size = sum(a.size * a.dtype.itemsize for a in arrays)
    *copies, token = pl.pallas_call(
        functools.partial(load_body, len(arrays)),
        out_shape=[pltpu.VMEM(a.shape, a.dtype) for a in arrays]
        + [jax.ShapeDtypeStruct((8, 128), f32)],
        in_specs=[pl.BlockSpec(memory_space=pl.ANY)] * (1 + len(arrays)),
        out_specs=[VMEM] * (1 + len(arrays)),
        scratch_shapes=[pltpu.SemaphoreType.DMA((len(arrays),))],
        compiler_params=pltpu.CompilerParams(vmem_limit_bytes=2 << 20),
        cost_estimate=pl.CostEstimate(flops=0, bytes_accessed=2 * size, transcendentals=0),
    )(after, *[from_hbm(a) for a in arrays])
    return [fetched(c) for c in copies] + [token]


def tile_of(width, most):
    return width if width <= most else most


def iota(shape, axis):
    return lax.broadcasted_iota(i32, shape, axis).astype(f32)


def pick(onehot, values):
    return dot(onehot, values).astype(values.dtype)


def send_body(me, routed_in, activations_in, outgoing, routed, activations, sems):
    first_move = pltpu.make_async_copy(routed_in, routed, sems.at[0])
    second_move = pltpu.make_async_copy(activations_in, activations, sems.at[1])
    first_move.start()
    second_move.start()
    first_move.wait()
    capacity, tokens, total = outgoing.shape[0], activations.shape[0], routed.shape[1]
    low = (me[0] * tokens).astype(f32)
    where = routed[...].astype(f32)
    first = jnp.sum(jnp.where(where < low, 1.0, 0.0), axis=1, keepdims=True)
    here = (where >= low) & (where < low + tokens)
    slot = jnp.where(here, iota((1, total), 1) - first, -1.0)
    hit = slot == iota((capacity, total), 0)
    token = jnp.sum(jnp.where(hit, where - low + 1.0, 0.0), axis=1, keepdims=True) - 1.0
    onehot = jnp.where(token == iota((capacity, tokens), 1), 1.0, 0.0).astype(bf16)
    second_move.wait()
    width = activations.shape[1]
    tile = tile_of(width, 1024)
    for start in range(0, width, tile):
        span = slice(start, start + tile)
        outgoing[:, span] = pick(onehot, activations[:, span])


def map_body(tall, wide, tokens, heads_of, me, routed, balance, notes, *outs):
    pick_rows, in_order, columns, unmix, positions = outs
    count, total = tall * wide, routed.shape[1]
    share, capacity = total // count, pick_rows.shape[1] // (lots_of(tall) * wide)
    outbound, inbound = columns.shape[0], unmix.shape[0]
    my_z, my_y = lax.div(me[0], wide), lax.rem(me[0], wide)
    where, owner = routed[...].astype(f32), balance[...].astype(f32)
    lane = iota((1, total), 1)
    slot, place = jnp.zeros((1, total), f32), jnp.zeros((1, total), f32)
    out_base, out_block = notes[:outbound, 0:1], notes[:outbound, 1:2]
    in_base, in_source = notes[:inbound, 2:3], notes[:inbound, 3:4]
    for s in range(count):
        z, y = divmod(s, wide)
        from_block = lax.rem(my_z - z + tall, tall) * wide + lax.rem(my_y - y + wide, wide)
        to_block = lax.rem(z - my_z + tall, tall) * wide + lax.rem(y - my_y + wide, wide)
        peer = lax.rem(my_z + z, tall) * wide + lax.rem(my_y + y, wide)
        before = where < s * tokens
        first = jnp.sum(jnp.where(before, 1.0, 0.0), axis=1, keepdims=True)
        inside = (where < (s + 1) * tokens) & jnp.logical_not(before)
        lot = lot_of(tall, my_z, z) * wide + lax.rem(my_y - y + wide, wide)
        start = (lot * capacity).astype(f32)
        slot += jnp.where(inside, lane - first + start, 0.0)
        place += jnp.where(owner == s, (to_block * share).astype(f32), 0.0)
        out_base += jnp.where(out_block == y * tall + z, heads_of(peer).astype(f32), 0.0)
        in_base += jnp.where(in_source == s, (from_block * (outbound // count)).astype(f32), 0.0)
    mine = owner == iota((count, total), 0)
    earlier = jnp.where(iota((total, total), 0) < iota((total, total), 1), 1.0, 0.0)
    rank = dot(jnp.where(mine, 1.0, 0.0).astype(bf16), earlier.astype(bf16))
    place += jnp.sum(jnp.where(mine, rank, 0.0), axis=0, keepdims=True)
    placed = place == iota((total, total), 0)
    in_order[...] = jnp.where(placed, 1.0, 0.0).astype(bf16)
    at = jnp.sum(jnp.where(placed, where, 0.0), axis=1, keepdims=True)
    positions[...] = jnp.broadcast_to(at, positions.shape)
    slot_at = jnp.sum(jnp.where(placed, slot, 0.0), axis=1, keepdims=True)
    pick_rows[...] = jnp.where(slot_at == iota(pick_rows.shape, 1), 1.0, 0.0).astype(bf16)
    columns[...] = jnp.where(out_base == iota(columns.shape, 1), 1.0, 0.0).astype(bf16)
    unmix[...] = jnp.where(in_base == iota(unmix.shape, 1), 1.0, 0.0).astype(bf16)


def kv_body(count, extra, *refs):
    blocks = refs[:count]
    pick_rows, order, columns, gain, w_key, w_value = refs[count : count + 6]
    wide = len(refs) - count - 9 - extra
    normed, own, *sent, rows = refs[-3 - wide :]
    total, width = normed.shape
    tile = tile_of(width, 512)
    square = jnp.zeros((total, 1), f32)
    for start in range(0, width, tile):
        span = slice(start, start + tile)
        part = dot(pick_rows[...], jnp.concatenate([b[:, span] for b in blocks], axis=0))
        rows[:, span] = part.astype(bf16)
        square += jnp.sum(part * part, axis=1, keepdims=True)
    own[...] = rows[: own.shape[0], :]
    factor = lax.rsqrt(square / width + norm_eps)
    for start in range(0, width, tile):
        span = slice(start, start + tile)
        part = rows[:, span].astype(f32) * factor * gain[:, span]
        normed[:, span] = part.astype(bf16)
    keys = dot(normed[...], w_key[...]).astype(bf16)
    values = dot(normed[...], w_value[...]).astype(bf16)
    both = jnp.concatenate([keys, values], axis=1)
    turned = lax.dot_general(
        columns[...], both, (((1,), (1,)), ((), ())), preferred_element_type=f32
    ).astype(bf16)
    turned = dot(turned, order[...])
    each = turned.shape[0] // wide
    for dy in range(wide):
        sent[dy][...] = turned[dy * each : (dy + 1) * each].astype(bf16)


def query_body(normed, w_query, cosine, sine, query):
    raw = dot(normed[...], w_query[...])
    for head in range(query.shape[1] // HEAD_DIM):
        span = slice(head * HEAD_DIM, (head + 1) * HEAD_DIM)
        one = raw[:, span]
        turned = one * cosine[...] + pltpu.roll(one, HEAD_DIM // 2, 1) * sine[...]
        query[:, span] = turned.astype(bf16)


def attend_body(plane, kv_local, *refs):
    tall = plane[0]
    arrived, rest = refs[:tall], refs[tall:]
    query, unmix, cosine, sine, key_pos, query_pos, w_output = rest[:7]
    parts, heads_out = rest[7:-1], rest[-1]
    half = HEAD_DIM // 2
    heads = query.shape[1] // HEAD_DIM
    mixed = jnp.concatenate([a[...].astype(f32) for a in arrived], axis=0).astype(bf16)
    both = dot(unmix[...], mixed)
    allowed = key_pos[...].astype(f32) <= query_pos[:, 0:1]
    for group in range(kv_local):
        base = group * HEAD_DIM
        first, second = both[base : base + half], both[base + half : base + HEAD_DIM]
        keys = jnp.concatenate(
            [first * cosine[...] - second * sine[...], second * cosine[...] + first * sine[...]],
            axis=0,
        ).astype(bf16)
        base += kv_local * HEAD_DIM
        values = both[base : base + HEAD_DIM].astype(bf16)
        for head in range(group * heads // kv_local, (group + 1) * heads // kv_local):
            span = slice(head * HEAD_DIM, (head + 1) * HEAD_DIM)
            scores = dot(query[:, span], keys) * HEAD_DIM ** (-0.5)
            scores = jnp.where(allowed, scores, -1e30)
            weights = jnp.exp(scores - jnp.max(scores, axis=1, keepdims=True))
            probs = (weights / jnp.sum(weights, axis=1, keepdims=True)).astype(bf16)
            heads_out[:, span] = lax.dot_general(
                probs, values, (((1,), (1,)), ((), ())), preferred_element_type=f32
            ).astype(bf16)
    spread(heads_out, w_output, parts, plane, False)


def spread(left, weight, parts, plane, back):
    width = weight.shape[1]
    tile = tile_of(width, 512)
    for start in range(0, width, tile):
        span = slice(start, start + tile)
        product = dot(left[...], weight[:, span]).astype(bf16)
        store_parts(parts, *plane, span, product, back)


def mlp_body(plane, *refs):
    count = plane[0] * plane[1]
    blocks, (w_gate, w_up, w_down) = refs[:count], refs[count : count + 3]
    parts, (piece, inner) = refs[count + 3 : -2], refs[-2:]
    share = blocks[0].shape[0]
    for index, block in enumerate(blocks):
        piece[index * share : (index + 1) * share, :] = block[...]
    width = w_gate.shape[1]
    tile = tile_of(width, 256)
    for start in range(0, width, tile):
        span = slice(start, start + tile)
        gate = dot(piece[...], w_gate[:, span])
        upward = dot(piece[...], w_up[:, span])
        inner[:, span] = (gate / (1.0 + jnp.exp(-gate)) * upward).astype(bf16)
    spread(inner, w_down, parts, plane, True)


def on_device(
    activations,
    routed,
    balance,
    w_query,
    w_key,
    w_value,
    w_output,
    attn_gain,
    mlp_gain,
    w_gate,
    w_up,
    w_down,
    w_router,
):
    count = lax.axis_size("ctx")
    plane = tall, wide = plane_of(count)
    me = lax.axis_index("ctx").astype(i32).reshape(1)
    tokens, model = activations.shape
    total = routed.shape[0]
    share = total // count
    capacity = 2 * share
    local_heads = w_query.shape[1] // HEAD_DIM
    group_size = HEADS // KV_HEADS
    kv_local = max(1, local_heads // group_size)
    key_cols = w_key.shape[1]
    depth = key_cols // KV_HEADS
    scalar = pl.BlockSpec(memory_space=pltpu.SMEM)
    in_hbm = pl.BlockSpec(memory_space=pl.ANY)
    routed, balance = routed.reshape(1, total), balance.reshape(1, total)

    (outgoing,) = kernel_call(
        send_body,
        [((capacity, model), bf16)],
        [me, from_hbm(routed), from_hbm(activations)],
        [
            pltpu.VMEM(routed.shape, i32),
            pltpu.VMEM(activations.shape, bf16),
            pltpu.SemaphoreType.DMA((2,)),
        ],
        specs=[scalar, in_hbm, in_hbm],
        flops=2 * capacity * tokens * model,
    )
    attn_gain, w_key, w_value, w_query, token_1 = load(
        outgoing, attn_gain.reshape(1, model), w_key, w_value, w_query
    )

    each = kv_local * 2 * depth
    notes = np.zeros((max(count * each, 2 * kv_local * HEAD_DIM), 4), np.float32)
    block, local, side, entry = np.indices((count, kv_local, 2, depth)).reshape(4, -1)
    notes[: count * each, 0] = side * key_cols + entry * KV_HEADS + local
    notes[: count * each, 1] = block
    side, local, source, entry = np.indices((2, kv_local, count, depth)).reshape(4, -1)
    notes[: 2 * kv_local * HEAD_DIM, 2] = (local * 2 + side) * depth + entry
    notes[: 2 * kv_local * HEAD_DIM, 3] = source
    pick_rows, in_order, columns, unmix, positions = kernel_call(
        functools.partial(
            map_body, tall, wide, tokens, lambda peer: lax.div(peer * local_heads, group_size)
        ),
        [
            ((total, lots_of(tall) * wide * capacity), bf16),
            ((total, total), bf16),
            ((count * each, 2 * key_cols), bf16),
            ((2 * kv_local * HEAD_DIM, count * each), bf16),
            ((total, HEAD_DIM // 2), f32),
        ],
        [me, routed, balance, notes],
        specs=[scalar, VMEM, VMEM, VMEM],
    )
    blocks = gather_rows(outgoing, tall, wide, [token_1, positions])
    near = blocks[wide]
    w_output, *token_2 = load(near, w_output)
    w_gate, *token_3 = load(near, w_gate)
    loaded = token_2 + token_3

    half = HEAD_DIM // 2
    steps_f = jnp.arange(half, dtype=f32)
    freqs = jnp.exp(-jnp.log(f32(rope_base)) * (2.0 * steps_f / HEAD_DIM))
    q_angles = positions * freqs[None, :]
    q_cos, q_sin = jnp.cos(q_angles), jnp.sin(q_angles)
    q_cos = jnp.concatenate([q_cos, q_cos], axis=1)
    q_sin = jnp.concatenate([-q_sin, q_sin], axis=1)
    k_angles = freqs[:, None] * routed.astype(f32)
    k_cos, k_sin = jnp.cos(k_angles), jnp.sin(k_angles)

    normed, own, *sent = kernel_call(
        functools.partial(kv_body, len(blocks), len(loaded)),
        [((total, model), bf16), ((share, model), bf16)] + [((tall * each, total), bf16)] * wide,
        [*blocks, pick_rows, in_order, columns, attn_gain, w_key, w_value, *loaded],
        [pltpu.VMEM((total, model), bf16)],
        flops=2 * total * model * 512,
    )
    arrived = exchange(sent, tall, wide)
    heads_wide = local_heads * HEAD_DIM
    (query,) = kernel_call(
        query_body,
        [((total, heads_wide), bf16)],
        [normed, w_query, q_cos, q_sin],
        flops=2 * total * model * heads_wide,
    )
    part_shapes = sum_shapes(tall, wide, share, model)
    attn_parts = kernel_call(
        functools.partial(attend_body, plane, kv_local),
        part_shapes,
        [*arrived, query, unmix, k_cos, k_sin, routed, positions, w_output],
        [pltpu.VMEM((total, heads_wide), bf16)],
        flops=2 * total * model * heads_wide,
    )
    attn_own, w_down = scatter_sum(attn_parts, tall, wide, [w_down])
    own_rows = own.astype(f32)
    hidden = own_rows + attn_own
    mean_sq = jnp.mean(hidden * hidden, axis=-1, keepdims=True)
    mnorm = (hidden * lax.rsqrt(mean_sq + norm_eps) * mlp_gain).astype(bf16)
    pieces = gather_blocks(mnorm, tall, wide)
    w_up, _ = load(mnorm, w_up)
    hidden_units = w_gate.shape[1]
    mlp_parts = kernel_call(
        functools.partial(mlp_body, plane),
        part_shapes,
        [*pieces, w_gate, w_up, w_down],
        [pltpu.VMEM((total, model), bf16), pltpu.VMEM((total, hidden_units), bf16)],
        flops=6 * total * model * hidden_units,
    )
    mlp_own = scatter_sum(mlp_parts, tall, wide)
    router_score = jnp.sum(own_rows * w_router[None, :], axis=1, keepdims=True)
    return (own_rows + router_score * (attn_own + mlp_own)).astype(bf16)


def solution(mesh):
    in_specs = (
        P(("dp", "ctx"), None),
        P("dp"),
        P("dp"),
        P(None, "ctx"),
        P(None, "ctx"),
        P(None, "ctx"),
        P("ctx", None),
        P(),
        P(),
        P(None, "ctx"),
        P(None, "ctx"),
        P("ctx", None),
        P(),
    )
    out_specs = P(("dp", "ctx"), None)
    return jax.shard_map(
        on_device, mesh=mesh, in_specs=in_specs, out_specs=out_specs, check_vma=False
    )
```

```python
import functools

import jax
import jax.numpy as jnp
import numpy as np
from jax import lax
from jax.experimental import pallas as pl
from jax.experimental.pallas import tpu as pltpu
from jax.sharding import PartitionSpec as P

HEADS = 32
KV_HEADS = 8
HEAD_DIM = 128

rope_base = 500000.0
norm_eps = 1e-05

bf16, f32, i32 = jnp.bfloat16, jnp.float32, jnp.int32
VMEM = pl.BlockSpec(memory_space=pltpu.VMEM)


def plane_of(count):
    wide = max(y for y in range(1, count + 1) if count % y == 0 and 2 * y * y <= max(count, 2))
    return count // wide, wide


def shift(block, tall, wide, dz, dy, keep=None):
    pairs = [
        (z * wide + y, (z + dz) % tall * wide + (y + dy) % wide)
        for z in range(tall)
        for y in range(wide)
        if keep is None or keep(z)
    ]
    return lax.ppermute(block, "ctx", pairs)


def tie_body(count, *refs):
    total = refs[0][...]
    for ref in refs[1:count]:
        total = total + ref[...]
    refs[-1][...] = total


def tie(blocks, tokens):
    return kernel_call(
        functools.partial(tie_body, len(blocks)),
        [(blocks[0].shape, blocks[0].dtype)],
        [*blocks, *tokens],
        specs=[VMEM] * len(blocks) + [pl.BlockSpec(memory_space=pl.ANY)] * len(tokens),
    )[0]


def gather_rows(block, tall, wide, tokens):
    blocks = {(0, 0): block}
    for dy in range(1, wide):
        blocks[0, dy] = shift(block, tall, wide, 0, dy)
    first = [*tokens, *(blocks[0, dy] for dy in range(1, wide))]
    for dz in range(tall - 1, 0, -1):
        if tall != 4 or dz != 2:
            blocks[dz, 0] = shift(block, tall, wide, dz, 0)
    blocks[tall - 1, 0] = tie([blocks[tall - 1, 0]], first)
    if tall == 4:
        for dy in range(1, wide):
            blocks[3, dy] = shift(blocks[3, 0], tall, wide, 0, dy)
        up = shift(blocks[1, 0], tall, wide, 1, 0, lambda z: z in (1, 2))
        down = shift(blocks[3, 0], tall, wide, -1, 0, lambda z: z in (1, 2))
        blocks[2, 0] = tie([up, down], [blocks[3, dy] for dy in range(1, wide)])
    for dz in range(1, tall):
        for dy in range(1, wide):
            if (dz, dy) not in blocks:
                blocks[dz, dy] = shift(blocks[dz, 0], tall, wide, 0, dy)
    return [blocks[dz, dy] for dz in range(tall) for dy in range(wide)]


def pack_body(tall, *refs):
    wide = len(refs) - tall
    each = refs[0].shape[0] // tall
    for dz in range(tall):
        values = [ref[...].astype(f32)[dz * each : (dz + 1) * each] for ref in refs[:wide]]
        refs[wide + dz][...] = jnp.concatenate(values, axis=0).astype(bf16)


def exchange(parts, tall, wide):
    shape = ((parts[0].shape[0] // tall * wide, parts[0].shape[1]), bf16)
    crossed = [parts[0]] + [shift(parts[dy], tall, wide, 0, dy) for dy in range(1, wide)]
    packed = kernel_call(functools.partial(pack_body, tall), [shape] * tall, crossed)
    pairs = [
        [(z * wide + y, (z ^ kz) * wide + y) for z in range(tall) for y in range(wide)]
        for kz in range(tall)
    ]
    return [packed[0]] + [lax.ppermute(packed[k], "ctx", pairs[k]) for k in range(1, tall)]


def gather_blocks(block, tall, wide):
    blocks = {(dz, 0): shift(block, tall, wide, dz, 0) if dz else block for dz in range(tall)}
    for dz in range(tall):
        for dy in range(1, wide):
            blocks[dz, dy] = shift(blocks[dz, 0], tall, wide, 0, dy)
    return [blocks[dz, dy] for dz in range(tall) for dy in range(wide)]


def sum_groups(tall, fine):
    order = [tall // 2, *range(1, tall // 2), *range(tall // 2 + 1, tall), 0]
    return [[dz] for dz in order] if fine else [order[: tall // 2], order[tall // 2 :]]


def sum_shapes(tall, wide, share, model, fine):
    shapes = [((share, model), bf16)] * tall
    for group in sum_groups(tall, fine):
        shapes += [((len(group) * share, model), bf16)] * (wide - 1)
    return shapes


def store_parts(parts, tall, wide, span, product, last):
    share = parts[0].shape[0]
    sign = -1 if last else 1

    def rows(dz, dy):
        at = sign * dz % tall * wide + sign * dy % wide
        return product[at * share : (at + 1) * share, :]

    for dz in range(tall):
        parts[dz][:, span] = rows(dz, 0)
    for which, group in enumerate(sum_groups(tall, last)):
        for dy in range(1, wide):
            out = parts[tall + which * (wide - 1) + dy - 1]
            for place, dz in enumerate(group):
                out[place * share : (place + 1) * share, span] = rows(dz, dy)


def scatter_sum(parts, tall, wide, last, loads=()):
    share = parts[0].shape[0]
    others = wide - 1
    loaded = []
    crossed = [shift(p, tall, wide, 0, i % others + 1) for i, p in enumerate(parts[tall:])]
    if loads:
        *loaded, token = load(parts[0], *loads)
        crossed[others] = tie([crossed[others]], [token])
    total = None
    for which, group in enumerate(sum_groups(tall, last)):
        for place, dz in enumerate(group):
            lane = parts[dz].astype(f32)
            for other in crossed[which * others : (which + 1) * others]:
                lane = lane + other[place * share : (place + 1) * share].astype(f32)
            if dz:
                lane = shift(lane.astype(bf16), tall, wide, dz, 0).astype(f32)
            total = lane if total is None else total + lane
    return (total, *loaded) if loads else total


def dot(a, b):
    return jnp.dot(a, b, preferred_element_type=f32)


def from_hbm(weight):
    return pltpu.with_memory_space_constraint(weight, pltpu.HBM)


def fetched(weight):
    return pltpu.with_memory_space_constraint(weight, pltpu.VMEM)


def kernel_call(body, outs, args, scratch=(), limit=14, flops=0, specs=None):
    return pl.pallas_call(
        body,
        out_shape=[jax.ShapeDtypeStruct(s, d) for s, d in outs],
        in_specs=specs or [VMEM] * len(args),
        out_specs=[VMEM] * len(outs),
        scratch_shapes=list(scratch),
        compiler_params=pltpu.CompilerParams(vmem_limit_bytes=limit << 20),
        cost_estimate=pl.CostEstimate(flops=flops, bytes_accessed=1 << 20, transcendentals=0),
    )(*args)


def load_body(count, *refs):
    sources, copies, sems = refs[1 : 1 + count], refs[1 + count : -2], refs[-1]
    moves = [
        pltpu.make_async_copy(a, b, sems.at[i]) for i, (a, b) in enumerate(zip(sources, copies))
    ]
    for move in moves:
        move.start()
    for move in moves:
        move.wait()
    refs[-2][...] = jnp.zeros_like(refs[-2])


def load(after, *arrays):
    size = sum(a.size * a.dtype.itemsize for a in arrays)
    *copies, token = pl.pallas_call(
        functools.partial(load_body, len(arrays)),
        out_shape=[pltpu.VMEM(a.shape, a.dtype) for a in arrays]
        + [jax.ShapeDtypeStruct((8, 128), f32)],
        in_specs=[pl.BlockSpec(memory_space=pl.ANY)] * (1 + len(arrays)),
        out_specs=[VMEM] * (1 + len(arrays)),
        scratch_shapes=[pltpu.SemaphoreType.DMA((len(arrays),))],
        compiler_params=pltpu.CompilerParams(vmem_limit_bytes=2 << 20),
        cost_estimate=pl.CostEstimate(flops=0, bytes_accessed=2 * size, transcendentals=0),
    )(after, *[from_hbm(a) for a in arrays])
    return [fetched(c) for c in copies] + [token]


def tile_of(width, most):
    return width if width <= most else most


def iota(shape, axis):
    return lax.broadcasted_iota(i32, shape, axis).astype(f32)


def pick(onehot, values):
    return dot(onehot, values).astype(values.dtype)


def send_body(me, routed_in, activations_in, outgoing, routed, activations, sems):
    first_move = pltpu.make_async_copy(routed_in, routed, sems.at[0])
    first_move.start()
    width = activations.shape[1]
    tile = width // 4
    moves = []
    for index in range(4):
        piece = pl.ds(index * tile, tile)
        source, target = activations_in.at[:, piece], activations.at[:, piece]
        moves.append(pltpu.make_async_copy(source, target, sems.at[1 + index]))
        moves[-1].start()
    first_move.wait()
    capacity, tokens, total = outgoing.shape[0], activations.shape[0], routed.shape[1]
    low = (me[0] * tokens).astype(f32)
    where = routed[...].astype(f32)
    first = jnp.sum(jnp.where(where < low, 1.0, 0.0), axis=1, keepdims=True)
    here = (where >= low) & (where < low + tokens)
    slot = jnp.where(here, iota((1, total), 1) - first, -1.0)
    hit = slot == iota((capacity, total), 0)
    token = jnp.sum(jnp.where(hit, where - low + 1.0, 0.0), axis=1, keepdims=True) - 1.0
    onehot = jnp.where(token == iota((capacity, tokens), 1), 1.0, 0.0).astype(bf16)
    for index, move in enumerate(moves):
        move.wait()
        span = slice(index * tile, (index + 1) * tile)
        outgoing[:, span] = pick(onehot, activations[:, span])


def map_body(tall, wide, tokens, heads_of, me, routed, balance, notes, *outs):
    pick_rows, in_order, columns, unmix, positions = outs
    count, total = tall * wide, routed.shape[1]
    share, capacity = total // count, pick_rows.shape[1] // count
    outbound, inbound = columns.shape[0], unmix.shape[0]
    my_z, my_y = lax.div(me[0], wide), lax.rem(me[0], wide)
    where, owner = routed[...].astype(f32), balance[...].astype(f32)
    lane = iota((1, total), 1)
    slot, place = jnp.zeros((1, total), f32), jnp.zeros((1, total), f32)
    out_base, out_block = notes[:outbound, 0:1], notes[:outbound, 1:2]
    in_base, in_source = notes[:inbound, 2:3], notes[:inbound, 3:4]
    for s in range(count):
        z, y = divmod(s, wide)
        from_block = lax.rem(my_z - z + tall, tall) * wide + lax.rem(my_y - y + wide, wide)
        to_block = lax.rem(z - my_z + tall, tall) * wide + lax.rem(y - my_y + wide, wide)
        peer = (my_z ^ z) * wide + lax.rem(my_y + y, wide)
        lot = (my_z ^ z) * wide + lax.rem(my_y - y + wide, wide)
        before = where < s * tokens
        first = jnp.sum(jnp.where(before, 1.0, 0.0), axis=1, keepdims=True)
        inside = (where < (s + 1) * tokens) & jnp.logical_not(before)
        start = (from_block * capacity).astype(f32)
        slot += jnp.where(inside, lane - first + start, 0.0)
        place += jnp.where(owner == s, (to_block * share).astype(f32), 0.0)
        out_base += jnp.where(out_block == y * tall + z, heads_of(peer).astype(f32), 0.0)
        in_base += jnp.where(in_source == s, (lot * (outbound // count)).astype(f32), 0.0)
    mine = owner == iota((count, total), 0)
    earlier = jnp.where(iota((total, total), 0) < iota((total, total), 1), 1.0, 0.0)
    rank = dot(jnp.where(mine, 1.0, 0.0).astype(bf16), earlier.astype(bf16))
    place += jnp.sum(jnp.where(mine, rank, 0.0), axis=0, keepdims=True)
    placed = place == iota((total, total), 0)
    in_order[...] = jnp.where(placed, 1.0, 0.0).astype(bf16)
    at = jnp.sum(jnp.where(placed, where, 0.0), axis=1, keepdims=True)
    positions[...] = jnp.broadcast_to(at, positions.shape)
    slot_at = jnp.sum(jnp.where(placed, slot, 0.0), axis=1, keepdims=True)
    pick_rows[...] = jnp.where(slot_at == iota(pick_rows.shape, 1), 1.0, 0.0).astype(bf16)
    columns[...] = jnp.where(out_base == iota(columns.shape, 1), 1.0, 0.0).astype(bf16)
    unmix[...] = jnp.where(in_base == iota(unmix.shape, 1), 1.0, 0.0).astype(bf16)


def kv_body(count, extra, *refs):
    blocks = refs[:count]
    pick_rows, order, columns, gain, w_key, w_value = refs[count : count + 6]
    wide = len(refs) - count - 9 - extra
    normed, own, *sent, rows = refs[-3 - wide :]
    total, width = normed.shape
    tile = tile_of(width, 512)
    square = jnp.zeros((total, 1), f32)
    for start in range(0, width, tile):
        span = slice(start, start + tile)
        part = dot(pick_rows[...], jnp.concatenate([b[:, span] for b in blocks], axis=0))
        rows[:, span] = part.astype(bf16)
        square += jnp.sum(part * part, axis=1, keepdims=True)
    own[...] = rows[: own.shape[0], :]
    factor = lax.rsqrt(square / width + norm_eps)
    for start in range(0, width, tile):
        span = slice(start, start + tile)
        part = rows[:, span].astype(f32) * factor * gain[:, span]
        normed[:, span] = part.astype(bf16)
    keys = dot(normed[...], w_key[...]).astype(bf16)
    values = dot(normed[...], w_value[...]).astype(bf16)
    both = jnp.concatenate([keys, values], axis=1)
    turned = lax.dot_general(
        columns[...], both, (((1,), (1,)), ((), ())), preferred_element_type=f32
    ).astype(bf16)
    turned = dot(turned, order[...])
    each = turned.shape[0] // wide
    for dy in range(wide):
        sent[dy][...] = turned[dy * each : (dy + 1) * each].astype(bf16)


def query_body(normed, w_query, cosine, sine, query):
    raw = dot(normed[...], w_query[...])
    for head in range(query.shape[1] // HEAD_DIM):
        span = slice(head * HEAD_DIM, (head + 1) * HEAD_DIM)
        one = raw[:, span]
        turned = one * cosine[...] + pltpu.roll(one, HEAD_DIM // 2, 1) * sine[...]
        query[:, span] = turned.astype(bf16)


def attend_body(plane, kv_local, *refs):
    tall = plane[0]
    arrived, rest = refs[:tall], refs[tall:]
    query, unmix, cosine, sine, key_pos, query_pos, w_output = rest[:7]
    parts, heads_out = rest[7:-1], rest[-1]
    half = HEAD_DIM // 2
    heads = query.shape[1] // HEAD_DIM
    mixed = jnp.concatenate([a[...].astype(f32) for a in arrived], axis=0).astype(bf16)
    both = dot(unmix[...], mixed)
    allowed = key_pos[...].astype(f32) <= query_pos[:, 0:1]
    for group in range(kv_local):
        base = group * HEAD_DIM
        first, second = both[base : base + half], both[base + half : base + HEAD_DIM]
        keys = jnp.concatenate(
            [first * cosine[...] - second * sine[...], second * cosine[...] + first * sine[...]],
            axis=0,
        ).astype(bf16)
        base += kv_local * HEAD_DIM
        values = both[base : base + HEAD_DIM].astype(bf16)
        for head in range(group * heads // kv_local, (group + 1) * heads // kv_local):
            span = slice(head * HEAD_DIM, (head + 1) * HEAD_DIM)
            scores = dot(query[:, span], keys) * HEAD_DIM ** (-0.5)
            scores = jnp.where(allowed, scores, -1e30)
            weights = jnp.exp(scores - jnp.max(scores, axis=1, keepdims=True))
            probs = (weights / jnp.sum(weights, axis=1, keepdims=True)).astype(bf16)
            heads_out[:, span] = lax.dot_general(
                probs, values, (((1,), (1,)), ((), ())), preferred_element_type=f32
            ).astype(bf16)
    spread(heads_out, w_output, parts, plane, False)


def spread(left, weight, parts, plane, back):
    width = weight.shape[1]
    tile = tile_of(width, 512)
    for start in range(0, width, tile):
        span = slice(start, start + tile)
        product = dot(left[...], weight[:, span]).astype(bf16)
        store_parts(parts, *plane, span, product, back)


def mlp_body(plane, *refs):
    count = plane[0] * plane[1]
    blocks, (w_gate, w_up, w_down) = refs[:count], refs[count : count + 3]
    parts, (piece, inner) = refs[count + 3 : -2], refs[-2:]
    share = blocks[0].shape[0]
    for index, block in enumerate(blocks):
        piece[index * share : (index + 1) * share, :] = block[...]
    width = w_gate.shape[1]
    tile = tile_of(width, 256)
    for start in range(0, width, tile):
        span = slice(start, start + tile)
        gate = dot(piece[...], w_gate[:, span])
        upward = dot(piece[...], w_up[:, span])
        inner[:, span] = (gate / (1.0 + jnp.exp(-gate)) * upward).astype(bf16)
    spread(inner, w_down, parts, plane, True)


def on_device(
    activations,
    routed,
    balance,
    w_query,
    w_key,
    w_value,
    w_output,
    attn_gain,
    mlp_gain,
    w_gate,
    w_up,
    w_down,
    w_router,
):
    count = lax.axis_size("ctx")
    plane = tall, wide = plane_of(count)
    me = lax.axis_index("ctx").astype(i32).reshape(1)
    tokens, model = activations.shape
    total = routed.shape[0]
    share = total // count
    capacity = 2 * share
    local_heads = w_query.shape[1] // HEAD_DIM
    group_size = HEADS // KV_HEADS
    kv_local = max(1, local_heads // group_size)
    key_cols = w_key.shape[1]
    depth = key_cols // KV_HEADS
    scalar = pl.BlockSpec(memory_space=pltpu.SMEM)
    in_hbm = pl.BlockSpec(memory_space=pl.ANY)
    routed, balance = routed.reshape(1, total), balance.reshape(1, total)

    (outgoing,) = kernel_call(
        send_body,
        [((capacity, model), bf16)],
        [me, from_hbm(routed), from_hbm(activations)],
        [
            pltpu.VMEM(routed.shape, i32),
            pltpu.VMEM(activations.shape, bf16),
            pltpu.SemaphoreType.DMA((5,)),
        ],
        specs=[scalar, in_hbm, in_hbm],
        flops=2 * capacity * tokens * model,
    )
    attn_gain, w_key, w_value, w_query, token_1 = load(
        outgoing, attn_gain.reshape(1, model), w_key, w_value, w_query
    )

    each = kv_local * 2 * depth
    notes = np.zeros((max(count * each, 2 * kv_local * HEAD_DIM), 4), np.float32)
    block, local, side, entry = np.indices((count, kv_local, 2, depth)).reshape(4, -1)
    notes[: count * each, 0] = side * key_cols + entry * KV_HEADS + local
    notes[: count * each, 1] = block
    side, local, source, entry = np.indices((2, kv_local, count, depth)).reshape(4, -1)
    notes[: 2 * kv_local * HEAD_DIM, 2] = (local * 2 + side) * depth + entry
    notes[: 2 * kv_local * HEAD_DIM, 3] = source
    pick_rows, in_order, columns, unmix, positions = kernel_call(
        functools.partial(
            map_body, tall, wide, tokens, lambda peer: lax.div(peer * local_heads, group_size)
        ),
        [
            ((total, count * capacity), bf16),
            ((total, total), bf16),
            ((count * each, 2 * key_cols), bf16),
            ((2 * kv_local * HEAD_DIM, count * each), bf16),
            ((total, HEAD_DIM // 2), f32),
        ],
        [me, routed, balance, notes],
        specs=[scalar, VMEM, VMEM, VMEM],
    )
    blocks = gather_rows(outgoing, tall, wide, [token_1, positions])
    near = blocks[2 * wide]
    w_output, *token_2 = load(near, w_output)
    w_gate, *token_3 = load(near, w_gate)
    loaded = token_2 + token_3

    half = HEAD_DIM // 2
    steps_f = jnp.arange(half, dtype=f32)
    freqs = jnp.exp(-jnp.log(f32(rope_base)) * (2.0 * steps_f / HEAD_DIM))
    q_angles = positions * freqs[None, :]
    q_cos, q_sin = jnp.cos(q_angles), jnp.sin(q_angles)
    q_cos = jnp.concatenate([q_cos, q_cos], axis=1)
    q_sin = jnp.concatenate([-q_sin, q_sin], axis=1)
    k_angles = freqs[:, None] * routed.astype(f32)
    k_cos, k_sin = jnp.cos(k_angles), jnp.sin(k_angles)

    normed, own, *sent = kernel_call(
        functools.partial(kv_body, count, len(loaded)),
        [((total, model), bf16), ((share, model), bf16)] + [((tall * each, total), bf16)] * wide,
        [*blocks, pick_rows, in_order, columns, attn_gain, w_key, w_value, *loaded],
        [pltpu.VMEM((total, model), bf16)],
        flops=2 * total * model * 512,
    )
    arrived = exchange(sent, tall, wide)
    heads_wide = local_heads * HEAD_DIM
    (query,) = kernel_call(
        query_body,
        [((total, heads_wide), bf16)],
        [normed, w_query, q_cos, q_sin],
        flops=2 * total * model * heads_wide,
    )
    attn_parts = kernel_call(
        functools.partial(attend_body, plane, kv_local),
        sum_shapes(tall, wide, share, model, False),
        [*arrived, query, unmix, k_cos, k_sin, routed, positions, w_output],
        [pltpu.VMEM((total, heads_wide), bf16)],
        flops=2 * total * model * heads_wide,
    )
    attn_own, w_down = scatter_sum(attn_parts, tall, wide, False, [w_down])
    own_rows = own.astype(f32)
    hidden = own_rows + attn_own
    mean_sq = jnp.mean(hidden * hidden, axis=-1, keepdims=True)
    mnorm = (hidden * lax.rsqrt(mean_sq + norm_eps) * mlp_gain).astype(bf16)
    pieces = gather_blocks(mnorm, tall, wide)
    w_up, _ = load(mnorm, w_up)
    hidden_units = w_gate.shape[1]
    mlp_parts = kernel_call(
        functools.partial(mlp_body, plane),
        sum_shapes(tall, wide, share, model, True),
        [*pieces, w_gate, w_up, w_down],
        [pltpu.VMEM((total, model), bf16), pltpu.VMEM((total, hidden_units), bf16)],
        flops=6 * total * model * hidden_units,
    )
    mlp_own = scatter_sum(mlp_parts, tall, wide, True)
    router_score = jnp.sum(own_rows * w_router[None, :], axis=1, keepdims=True)
    return (own_rows + router_score * (attn_own + mlp_own)).astype(bf16)


def solution(mesh):
    in_specs = (
        P(("dp", "ctx"), None),
        P("dp"),
        P("dp"),
        P(None, "ctx"),
        P(None, "ctx"),
        P(None, "ctx"),
        P("ctx", None),
        P(),
        P(),
        P(None, "ctx"),
        P(None, "ctx"),
        P("ctx", None),
        P(),
    )
    out_specs = P(("dp", "ctx"), None)
    return jax.shard_map(
        on_device, mesh=mesh, in_specs=in_specs, out_specs=out_specs, check_vma=False
    )
```

```python
import functools

import jax
import jax.numpy as jnp
import numpy as np
from jax import lax
from jax.experimental import pallas as pl
from jax.experimental.pallas import tpu as pltpu
from jax.sharding import PartitionSpec as P

HEADS = 32
KV_HEADS = 8
HEAD_DIM = 128

rope_base = 500000.0
norm_eps = 1e-05

bf16, f32, i32 = jnp.bfloat16, jnp.float32, jnp.int32
VMEM = pl.BlockSpec(memory_space=pltpu.VMEM)


def plane_of(count):
    wide = max(y for y in range(1, count + 1) if count % y == 0 and 2 * y * y <= max(count, 2))
    return count // wide, wide


def shift(block, tall, wide, dz, dy, keep=None):
    pairs = [
        (z * wide + y, (z + dz) % tall * wide + (y + dy) % wide)
        for z in range(tall)
        for y in range(wide)
        if keep is None or keep(z)
    ]
    return lax.ppermute(block, "ctx", pairs)


def tie_body(count, *refs):
    total = refs[0][...]
    for ref in refs[1:count]:
        total = total + ref[...]
    refs[-1][...] = total


def tie(blocks, tokens):
    return kernel_call(
        functools.partial(tie_body, len(blocks)),
        [(blocks[0].shape, blocks[0].dtype)],
        [*blocks, *tokens],
        specs=[VMEM] * len(blocks) + [pl.BlockSpec(memory_space=pl.ANY)] * len(tokens),
    )[0]


def gather_rows(block, tall, wide, tokens):
    blocks = {(0, 0): block}
    for dy in range(1, wide):
        blocks[0, dy] = shift(block, tall, wide, 0, dy)
    first = [*tokens, *(blocks[0, dy] for dy in range(1, wide))]
    for dz in range(tall - 1, 0, -1):
        if tall != 4 or dz != 2:
            blocks[dz, 0] = shift(block, tall, wide, dz, 0)
    blocks[tall - 1, 0] = tie([blocks[tall - 1, 0]], first)
    if tall == 4:
        for dy in range(1, wide):
            blocks[3, dy] = shift(blocks[3, 0], tall, wide, 0, dy)
        up = shift(blocks[1, 0], tall, wide, 1, 0, lambda z: z in (1, 2))
        down = shift(blocks[3, 0], tall, wide, -1, 0, lambda z: z in (1, 2))
        blocks[2, 0] = tie([up, down], [blocks[3, dy] for dy in range(1, wide)])
    for dz in range(1, tall):
        for dy in range(1, wide):
            if (dz, dy) not in blocks:
                blocks[dz, dy] = shift(blocks[dz, 0], tall, wide, 0, dy)
    return [blocks[dz, dy] for dz in range(tall) for dy in range(wide)]


def pack_body(tall, *refs):
    wide = len(refs) - tall
    each = refs[0].shape[0] // tall
    for dz in range(tall):
        values = [ref[...].astype(f32)[dz * each : (dz + 1) * each] for ref in refs[:wide]]
        refs[wide + dz][...] = jnp.concatenate(values, axis=0).astype(bf16)


def exchange(parts, tall, wide):
    shape = ((parts[0].shape[0] // tall * wide, parts[0].shape[1]), bf16)
    crossed = [parts[0]] + [shift(parts[dy], tall, wide, 0, dy) for dy in range(1, wide)]
    packed = kernel_call(functools.partial(pack_body, tall), [shape] * tall, crossed)
    pairs = [
        [(z * wide + y, (z ^ kz) * wide + y) for z in range(tall) for y in range(wide)]
        for kz in range(tall)
    ]
    return [packed[0]] + [lax.ppermute(packed[k], "ctx", pairs[k]) for k in range(1, tall)]


def gather_blocks(block, tall, wide):
    blocks = {(dz, 0): shift(block, tall, wide, dz, 0) if dz else block for dz in range(tall)}
    for dz in range(tall):
        for dy in range(1, wide):
            blocks[dz, dy] = shift(blocks[dz, 0], tall, wide, 0, dy)
    return [blocks[dz, dy] for dz in range(tall) for dy in range(wide)]


def sum_order(tall):
    return [tall // 2, *range(1, tall // 2), *range(tall // 2 + 1, tall), 0]


def store_parts(parts, tall, wide, span, product, back):
    share = parts[0].shape[0]
    sign = -1 if back else 1
    for dz in range(tall):
        for dy in range(wide):
            at = sign * dz % tall * wide + sign * dy % wide
            parts[dz * wide + dy][:, span] = product[at * share : (at + 1) * share, :]


def scatter_sum(parts, tall, wide):
    total = None
    for dz in sum_order(tall):
        lane = parts[dz * wide].astype(f32)
        for dy in range(1, wide):
            lane = lane + shift(parts[dz * wide + dy], tall, wide, 0, dy).astype(f32)
        if dz:
            lane = shift(lane.astype(bf16), tall, wide, dz, 0).astype(f32)
        total = lane if total is None else total + lane
    return total


def dot(a, b):
    return jnp.dot(a, b, preferred_element_type=f32)


def from_hbm(weight):
    return pltpu.with_memory_space_constraint(weight, pltpu.HBM)


def fetched(weight):
    return pltpu.with_memory_space_constraint(weight, pltpu.VMEM)


def kernel_call(body, outs, args, scratch=(), limit=14, flops=0, specs=None):
    return pl.pallas_call(
        body,
        out_shape=[jax.ShapeDtypeStruct(s, d) for s, d in outs],
        in_specs=specs or [VMEM] * len(args),
        out_specs=[VMEM] * len(outs),
        scratch_shapes=list(scratch),
        compiler_params=pltpu.CompilerParams(vmem_limit_bytes=limit << 20),
        cost_estimate=pl.CostEstimate(flops=flops, bytes_accessed=1 << 20, transcendentals=0),
    )(*args)


def load_body(count, *refs):
    sources, copies, sems = refs[1 : 1 + count], refs[1 + count : -2], refs[-1]
    moves = [
        pltpu.make_async_copy(a, b, sems.at[i]) for i, (a, b) in enumerate(zip(sources, copies))
    ]
    for move in moves:
        move.start()
    for move in moves:
        move.wait()
    refs[-2][...] = jnp.zeros_like(refs[-2])


def load(after, *arrays):
    size = sum(a.size * a.dtype.itemsize for a in arrays)
    *copies, token = pl.pallas_call(
        functools.partial(load_body, len(arrays)),
        out_shape=[pltpu.VMEM(a.shape, a.dtype) for a in arrays]
        + [jax.ShapeDtypeStruct((8, 128), f32)],
        in_specs=[pl.BlockSpec(memory_space=pl.ANY)] * (1 + len(arrays)),
        out_specs=[VMEM] * (1 + len(arrays)),
        scratch_shapes=[pltpu.SemaphoreType.DMA((len(arrays),))],
        compiler_params=pltpu.CompilerParams(vmem_limit_bytes=2 << 20),
        cost_estimate=pl.CostEstimate(flops=0, bytes_accessed=2 * size, transcendentals=0),
    )(after, *[from_hbm(a) for a in arrays])
    return [fetched(c) for c in copies] + [token]


def tile_of(width, most):
    return width if width <= most else most


def iota(shape, axis):
    return lax.broadcasted_iota(i32, shape, axis).astype(f32)


def pick(onehot, values):
    return dot(onehot, values).astype(values.dtype)


def send_body(me, routed_in, activations_in, outgoing, routed, activations, sems):
    first_move = pltpu.make_async_copy(routed_in, routed, sems.at[0])
    second_move = pltpu.make_async_copy(activations_in, activations, sems.at[1])
    first_move.start()
    second_move.start()
    first_move.wait()
    capacity, tokens, total = outgoing.shape[0], activations.shape[0], routed.shape[1]
    low = (me[0] * tokens).astype(f32)
    where = routed[...].astype(f32)
    first = jnp.sum(jnp.where(where < low, 1.0, 0.0), axis=1, keepdims=True)
    here = (where >= low) & (where < low + tokens)
    slot = jnp.where(here, iota((1, total), 1) - first, -1.0)
    hit = slot == iota((capacity, total), 0)
    token = jnp.sum(jnp.where(hit, where - low + 1.0, 0.0), axis=1, keepdims=True) - 1.0
    onehot = jnp.where(token == iota((capacity, tokens), 1), 1.0, 0.0).astype(bf16)
    second_move.wait()
    width = activations.shape[1]
    tile = tile_of(width, 1024)
    for start in range(0, width, tile):
        span = slice(start, start + tile)
        outgoing[:, span] = pick(onehot, activations[:, span])


def map_body(tall, wide, tokens, heads_of, me, routed, balance, notes, *outs):
    pick_rows, in_order, columns, unmix, positions = outs
    count, total = tall * wide, routed.shape[1]
    share, capacity = total // count, pick_rows.shape[1] // count
    outbound, inbound = columns.shape[0], unmix.shape[0]
    my_z, my_y = lax.div(me[0], wide), lax.rem(me[0], wide)
    where, owner = routed[...].astype(f32), balance[...].astype(f32)
    lane = iota((1, total), 1)
    slot, place = jnp.zeros((1, total), f32), jnp.zeros((1, total), f32)
    out_base, out_block = notes[:outbound, 0:1], notes[:outbound, 1:2]
    in_base, in_source = notes[:inbound, 2:3], notes[:inbound, 3:4]
    for s in range(count):
        z, y = divmod(s, wide)
        from_block = lax.rem(my_z - z + tall, tall) * wide + lax.rem(my_y - y + wide, wide)
        to_block = lax.rem(z - my_z + tall, tall) * wide + lax.rem(y - my_y + wide, wide)
        peer = (my_z ^ z) * wide + lax.rem(my_y + y, wide)
        lot = (my_z ^ z) * wide + lax.rem(my_y - y + wide, wide)
        before = where < s * tokens
        first = jnp.sum(jnp.where(before, 1.0, 0.0), axis=1, keepdims=True)
        inside = (where < (s + 1) * tokens) & jnp.logical_not(before)
        start = (from_block * capacity).astype(f32)
        slot += jnp.where(inside, lane - first + start, 0.0)
        place += jnp.where(owner == s, (to_block * share).astype(f32), 0.0)
        out_base += jnp.where(out_block == y * tall + z, heads_of(peer).astype(f32), 0.0)
        in_base += jnp.where(in_source == s, (lot * (outbound // count)).astype(f32), 0.0)
    mine = owner == iota((count, total), 0)
    earlier = jnp.where(iota((total, total), 0) < iota((total, total), 1), 1.0, 0.0)
    rank = dot(jnp.where(mine, 1.0, 0.0).astype(bf16), earlier.astype(bf16))
    place += jnp.sum(jnp.where(mine, rank, 0.0), axis=0, keepdims=True)
    placed = place == iota((total, total), 0)
    in_order[...] = jnp.where(placed, 1.0, 0.0).astype(bf16)
    at = jnp.sum(jnp.where(placed, where, 0.0), axis=1, keepdims=True)
    positions[...] = jnp.broadcast_to(at, positions.shape)
    slot_at = jnp.sum(jnp.where(placed, slot, 0.0), axis=1, keepdims=True)
    pick_rows[...] = jnp.where(slot_at == iota(pick_rows.shape, 1), 1.0, 0.0).astype(bf16)
    columns[...] = jnp.where(out_base == iota(columns.shape, 1), 1.0, 0.0).astype(bf16)
    unmix[...] = jnp.where(in_base == iota(unmix.shape, 1), 1.0, 0.0).astype(bf16)


def kv_body(count, extra, *refs):
    blocks = refs[:count]
    pick_rows, order, columns, gain, w_key, w_value = refs[count : count + 6]
    wide = len(refs) - count - 9 - extra
    normed, own, *sent, rows = refs[-3 - wide :]
    total, width = normed.shape
    tile = tile_of(width, 512)
    square = jnp.zeros((total, 1), f32)
    for start in range(0, width, tile):
        span = slice(start, start + tile)
        part = dot(pick_rows[...], jnp.concatenate([b[:, span] for b in blocks], axis=0))
        rows[:, span] = part.astype(bf16)
        square += jnp.sum(part * part, axis=1, keepdims=True)
    own[...] = rows[: own.shape[0], :]
    factor = lax.rsqrt(square / width + norm_eps)
    for start in range(0, width, tile):
        span = slice(start, start + tile)
        part = rows[:, span].astype(f32) * factor * gain[:, span]
        normed[:, span] = part.astype(bf16)
    keys = dot(normed[...], w_key[...]).astype(bf16)
    values = dot(normed[...], w_value[...]).astype(bf16)
    both = jnp.concatenate([keys, values], axis=1)
    turned = lax.dot_general(
        columns[...], both, (((1,), (1,)), ((), ())), preferred_element_type=f32
    ).astype(bf16)
    turned = dot(turned, order[...])
    each = turned.shape[0] // wide
    for dy in range(wide):
        sent[dy][...] = turned[dy * each : (dy + 1) * each].astype(bf16)


def query_body(normed, w_query, cosine, sine, query):
    raw = dot(normed[...], w_query[...])
    for head in range(query.shape[1] // HEAD_DIM):
        span = slice(head * HEAD_DIM, (head + 1) * HEAD_DIM)
        one = raw[:, span]
        turned = one * cosine[...] + pltpu.roll(one, HEAD_DIM // 2, 1) * sine[...]
        query[:, span] = turned.astype(bf16)


def attend_body(plane, kv_local, *refs):
    tall = plane[0]
    arrived, rest = refs[:tall], refs[tall:]
    query, unmix, cosine, sine, key_pos, query_pos, w_output = rest[:7]
    parts, heads_out = rest[7:-1], rest[-1]
    half = HEAD_DIM // 2
    heads = query.shape[1] // HEAD_DIM
    mixed = jnp.concatenate([a[...].astype(f32) for a in arrived], axis=0).astype(bf16)
    both = dot(unmix[...], mixed)
    allowed = key_pos[...].astype(f32) <= query_pos[:, 0:1]
    for group in range(kv_local):
        base = group * HEAD_DIM
        first, second = both[base : base + half], both[base + half : base + HEAD_DIM]
        keys = jnp.concatenate(
            [first * cosine[...] - second * sine[...], second * cosine[...] + first * sine[...]],
            axis=0,
        ).astype(bf16)
        base += kv_local * HEAD_DIM
        values = both[base : base + HEAD_DIM].astype(bf16)
        for head in range(group * heads // kv_local, (group + 1) * heads // kv_local):
            span = slice(head * HEAD_DIM, (head + 1) * HEAD_DIM)
            scores = dot(query[:, span], keys) * HEAD_DIM ** (-0.5)
            scores = jnp.where(allowed, scores, -1e30)
            weights = jnp.exp(scores - jnp.max(scores, axis=1, keepdims=True))
            probs = (weights / jnp.sum(weights, axis=1, keepdims=True)).astype(bf16)
            heads_out[:, span] = lax.dot_general(
                probs, values, (((1,), (1,)), ((), ())), preferred_element_type=f32
            ).astype(bf16)
    spread(heads_out, w_output, parts, plane, False)


def spread(left, weight, parts, plane, back):
    width = weight.shape[1]
    tile = tile_of(width, 512)
    for start in range(0, width, tile):
        span = slice(start, start + tile)
        product = dot(left[...], weight[:, span]).astype(bf16)
        store_parts(parts, *plane, span, product, back)


def mlp_body(plane, *refs):
    count = plane[0] * plane[1]
    blocks, (w_gate, w_up, w_down) = refs[:count], refs[count : count + 3]
    parts, (piece, inner) = refs[count + 3 : -2], refs[-2:]
    share = blocks[0].shape[0]
    for index, block in enumerate(blocks):
        piece[index * share : (index + 1) * share, :] = block[...]
    width = w_gate.shape[1]
    tile = tile_of(width, 256)
    for start in range(0, width, tile):
        span = slice(start, start + tile)
        gate = dot(piece[...], w_gate[:, span])
        upward = dot(piece[...], w_up[:, span])
        inner[:, span] = (gate / (1.0 + jnp.exp(-gate)) * upward).astype(bf16)
    spread(inner, w_down, parts, plane, True)


def on_device(
    activations,
    routed,
    balance,
    w_query,
    w_key,
    w_value,
    w_output,
    attn_gain,
    mlp_gain,
    w_gate,
    w_up,
    w_down,
    w_router,
):
    count = lax.axis_size("ctx")
    plane = tall, wide = plane_of(count)
    me = lax.axis_index("ctx").astype(i32).reshape(1)
    tokens, model = activations.shape
    total = routed.shape[0]
    share = total // count
    capacity = 2 * share
    local_heads = w_query.shape[1] // HEAD_DIM
    group_size = HEADS // KV_HEADS
    kv_local = max(1, local_heads // group_size)
    key_cols = w_key.shape[1]
    depth = key_cols // KV_HEADS
    scalar = pl.BlockSpec(memory_space=pltpu.SMEM)
    in_hbm = pl.BlockSpec(memory_space=pl.ANY)
    routed, balance = routed.reshape(1, total), balance.reshape(1, total)

    (outgoing,) = kernel_call(
        send_body,
        [((capacity, model), bf16)],
        [me, from_hbm(routed), from_hbm(activations)],
        [
            pltpu.VMEM(routed.shape, i32),
            pltpu.VMEM(activations.shape, bf16),
            pltpu.SemaphoreType.DMA((2,)),
        ],
        specs=[scalar, in_hbm, in_hbm],
        flops=2 * capacity * tokens * model,
    )
    attn_gain, w_key, w_value, w_query, token_1 = load(
        outgoing, attn_gain.reshape(1, model), w_key, w_value, w_query
    )
    w_down, token_5 = load(token_1, w_down)

    each = kv_local * 2 * depth
    notes = np.zeros((max(count * each, 2 * kv_local * HEAD_DIM), 4), np.float32)
    block, local, side, entry = np.indices((count, kv_local, 2, depth)).reshape(4, -1)
    notes[: count * each, 0] = side * key_cols + entry * KV_HEADS + local
    notes[: count * each, 1] = block
    side, local, source, entry = np.indices((2, kv_local, count, depth)).reshape(4, -1)
    notes[: 2 * kv_local * HEAD_DIM, 2] = (local * 2 + side) * depth + entry
    notes[: 2 * kv_local * HEAD_DIM, 3] = source
    pick_rows, in_order, columns, unmix, positions = kernel_call(
        functools.partial(
            map_body, tall, wide, tokens, lambda peer: lax.div(peer * local_heads, group_size)
        ),
        [
            ((total, count * capacity), bf16),
            ((total, total), bf16),
            ((count * each, 2 * key_cols), bf16),
            ((2 * kv_local * HEAD_DIM, count * each), bf16),
            ((total, HEAD_DIM // 2), f32),
        ],
        [me, routed, balance, notes],
        specs=[scalar, VMEM, VMEM, VMEM],
    )
    blocks = gather_rows(outgoing, tall, wide, [token_1, token_5, positions])
    near = blocks[2 * wide]
    w_output, *token_2 = load(near, w_output)
    w_gate, *token_3 = load(near, w_gate)
    loaded = token_2 + token_3

    half = HEAD_DIM // 2
    steps_f = jnp.arange(half, dtype=f32)
    freqs = jnp.exp(-jnp.log(f32(rope_base)) * (2.0 * steps_f / HEAD_DIM))
    q_angles = positions * freqs[None, :]
    q_cos, q_sin = jnp.cos(q_angles), jnp.sin(q_angles)
    q_cos = jnp.concatenate([q_cos, q_cos], axis=1)
    q_sin = jnp.concatenate([-q_sin, q_sin], axis=1)
    k_angles = freqs[:, None] * routed.astype(f32)
    k_cos, k_sin = jnp.cos(k_angles), jnp.sin(k_angles)

    normed, own, *sent = kernel_call(
        functools.partial(kv_body, count, len(loaded)),
        [((total, model), bf16), ((share, model), bf16)] + [((tall * each, total), bf16)] * wide,
        [*blocks, pick_rows, in_order, columns, attn_gain, w_key, w_value, *loaded],
        [pltpu.VMEM((total, model), bf16)],
        flops=2 * total * model * 512,
    )
    arrived = exchange(sent, tall, wide)
    heads_wide = local_heads * HEAD_DIM
    (query,) = kernel_call(
        query_body,
        [((total, heads_wide), bf16)],
        [normed, w_query, q_cos, q_sin],
        flops=2 * total * model * heads_wide,
    )
    attn_parts = kernel_call(
        functools.partial(attend_body, plane, kv_local),
        [((share, model), bf16)] * count,
        [*arrived, query, unmix, k_cos, k_sin, routed, positions, w_output],
        [pltpu.VMEM((total, heads_wide), bf16)],
        flops=2 * total * model * heads_wide,
    )
    attn_own = scatter_sum(attn_parts, tall, wide)
    own_rows = own.astype(f32)
    hidden = own_rows + attn_own
    mean_sq = jnp.mean(hidden * hidden, axis=-1, keepdims=True)
    mnorm = (hidden * lax.rsqrt(mean_sq + norm_eps) * mlp_gain).astype(bf16)
    pieces = gather_blocks(mnorm, tall, wide)
    w_up, _ = load(mnorm, w_up)
    hidden_units = w_gate.shape[1]
    mlp_parts = kernel_call(
        functools.partial(mlp_body, plane),
        [((share, model), bf16)] * count,
        [*pieces, w_gate, w_up, w_down],
        [pltpu.VMEM((total, model), bf16), pltpu.VMEM((total, hidden_units), bf16)],
        flops=6 * total * model * hidden_units,
    )
    mlp_own = scatter_sum(mlp_parts, tall, wide)
    router_score = jnp.sum(own_rows * w_router[None, :], axis=1, keepdims=True)
    return (own_rows + router_score * (attn_own + mlp_own)).astype(bf16)


def solution(mesh):
    in_specs = (
        P(("dp", "ctx"), None),
        P("dp"),
        P("dp"),
        P(None, "ctx"),
        P(None, "ctx"),
        P(None, "ctx"),
        P("ctx", None),
        P(),
        P(),
        P(None, "ctx"),
        P(None, "ctx"),
        P("ctx", None),
        P(),
    )
    out_specs = P(("dp", "ctx"), None)
    return jax.shard_map(
        on_device, mesh=mesh, in_specs=in_specs, out_specs=out_specs, check_vma=False
    )
```

```python
import functools

import jax
import jax.numpy as jnp
import numpy as np
from jax import lax
from jax.experimental import pallas as pl
from jax.experimental.pallas import tpu as pltpu
from jax.sharding import PartitionSpec as P

HEADS = 32
KV_HEADS = 8
HEAD_DIM = 128

rope_base = 500000.0
norm_eps = 1e-05

bf16, f32, i32 = jnp.bfloat16, jnp.float32, jnp.int32
VMEM = pl.BlockSpec(memory_space=pltpu.VMEM)


def plane_of(count):
    wide = max(y for y in range(1, count + 1) if count % y == 0 and 2 * y * y <= max(count, 2))
    return count // wide, wide


def shift(block, tall, wide, dz, dy, keep=None):
    pairs = [
        (z * wide + y, (z + dz) % tall * wide + (y + dy) % wide)
        for z in range(tall)
        for y in range(wide)
        if keep is None or keep(z)
    ]
    return lax.ppermute(block, "ctx", pairs)


def tie_body(count, *refs):
    total = refs[0][...]
    for ref in refs[1:count]:
        total = total + ref[...]
    refs[-1][...] = total


def tie(blocks, tokens):
    return kernel_call(
        functools.partial(tie_body, len(blocks)),
        [(blocks[0].shape, blocks[0].dtype)],
        [*blocks, *tokens],
        specs=[VMEM] * len(blocks) + [pl.BlockSpec(memory_space=pl.ANY)] * len(tokens),
    )[0]


def gather_rows(block, tall, wide, tokens):
    blocks = {(0, 0): block}
    for dy in range(1, wide):
        blocks[0, dy] = shift(block, tall, wide, 0, dy)
    first = [*tokens, *(blocks[0, dy] for dy in range(1, wide))]
    for dz in range(tall - 1, 0, -1):
        if tall != 4 or dz != 2:
            blocks[dz, 0] = shift(block, tall, wide, dz, 0)
    blocks[tall - 1, 0] = tie([blocks[tall - 1, 0]], first)
    if tall == 4:
        for dy in range(1, wide):
            blocks[3, dy] = shift(blocks[3, 0], tall, wide, 0, dy)
        up = shift(blocks[1, 0], tall, wide, 1, 0, lambda z: z in (1, 2))
        down = shift(blocks[3, 0], tall, wide, -1, 0, lambda z: z in (1, 2))
        blocks[2, 0] = tie([up, down], [blocks[3, dy] for dy in range(1, wide)])
    for dz in range(1, tall):
        for dy in range(1, wide):
            if (dz, dy) not in blocks:
                blocks[dz, dy] = shift(blocks[dz, 0], tall, wide, 0, dy)
    return [blocks[dz, dy] for dz in range(tall) for dy in range(wide)]


def pack_body(tall, *refs):
    wide = len(refs) - tall
    each = refs[0].shape[0] // tall
    for dz in range(tall):
        values = [ref[...].astype(f32)[dz * each : (dz + 1) * each] for ref in refs[:wide]]
        refs[wide + dz][...] = jnp.concatenate(values, axis=0).astype(bf16)


def exchange(parts, tall, wide):
    shape = ((parts[0].shape[0] // tall * wide, parts[0].shape[1]), bf16)
    crossed = [parts[0]] + [shift(parts[dy], tall, wide, 0, dy) for dy in range(1, wide)]
    packed = kernel_call(functools.partial(pack_body, tall), [shape] * tall, crossed)
    return [packed[0]] + [shift(packed[dz], tall, wide, dz, 0) for dz in range(1, tall)]


def gather_blocks(block, tall, wide):
    blocks = {(dz, 0): shift(block, tall, wide, dz, 0) if dz else block for dz in range(tall)}
    for dz in range(tall):
        for dy in range(1, wide):
            blocks[dz, dy] = shift(blocks[dz, 0], tall, wide, 0, dy)
    return [blocks[dz, dy] for dz in range(tall) for dy in range(wide)]


def sum_order(tall):
    return [tall // 2, *range(1, tall // 2), *range(tall // 2 + 1, tall), 0]


def store_parts(parts, tall, wide, span, product, back):
    share = parts[0].shape[0]
    sign = -1 if back else 1
    for dz in range(tall):
        for dy in range(wide):
            at = sign * dz % tall * wide + sign * dy % wide
            parts[dz * wide + dy][:, span] = product[at * share : (at + 1) * share, :]


def scatter_sum(parts, tall, wide):
    total = None
    for dz in sum_order(tall):
        lane = parts[dz * wide].astype(f32)
        for dy in range(1, wide):
            lane = lane + shift(parts[dz * wide + dy], tall, wide, 0, dy).astype(f32)
        if dz:
            lane = shift(lane.astype(bf16), tall, wide, dz, 0).astype(f32)
        total = lane if total is None else total + lane
    return total


def dot(a, b):
    return jnp.dot(a, b, preferred_element_type=f32)


def from_hbm(weight):
    return pltpu.with_memory_space_constraint(weight, pltpu.HBM)


def fetched(weight):
    return pltpu.with_memory_space_constraint(weight, pltpu.VMEM)


def kernel_call(body, outs, args, scratch=(), limit=14, flops=0, specs=None):
    return pl.pallas_call(
        body,
        out_shape=[jax.ShapeDtypeStruct(s, d) for s, d in outs],
        in_specs=specs or [VMEM] * len(args),
        out_specs=[VMEM] * len(outs),
        scratch_shapes=list(scratch),
        compiler_params=pltpu.CompilerParams(vmem_limit_bytes=limit << 20),
        cost_estimate=pl.CostEstimate(flops=flops, bytes_accessed=1 << 20, transcendentals=0),
    )(*args)


def load_body(count, *refs):
    sources, copies, sems = refs[1 : 1 + count], refs[1 + count : -2], refs[-1]
    moves = [
        pltpu.make_async_copy(a, b, sems.at[i]) for i, (a, b) in enumerate(zip(sources, copies))
    ]
    for move in moves:
        move.start()
    for move in moves:
        move.wait()
    refs[-2][...] = jnp.zeros_like(refs[-2])


def load(after, *arrays):
    size = sum(a.size * a.dtype.itemsize for a in arrays)
    *copies, token = pl.pallas_call(
        functools.partial(load_body, len(arrays)),
        out_shape=[pltpu.VMEM(a.shape, a.dtype) for a in arrays]
        + [jax.ShapeDtypeStruct((8, 128), f32)],
        in_specs=[pl.BlockSpec(memory_space=pl.ANY)] * (1 + len(arrays)),
        out_specs=[VMEM] * (1 + len(arrays)),
        scratch_shapes=[pltpu.SemaphoreType.DMA((len(arrays),))],
        compiler_params=pltpu.CompilerParams(vmem_limit_bytes=2 << 20),
        cost_estimate=pl.CostEstimate(flops=0, bytes_accessed=2 * size, transcendentals=0),
    )(after, *[from_hbm(a) for a in arrays])
    return [fetched(c) for c in copies] + [token]


def tile_of(width, most):
    return width if width <= most else most


def iota(shape, axis):
    return lax.broadcasted_iota(i32, shape, axis).astype(f32)


def pick(onehot, values):
    return dot(onehot, values).astype(values.dtype)


def send_body(me, routed_in, activations_in, outgoing, routed, activations, sems):
    first_move = pltpu.make_async_copy(routed_in, routed, sems.at[0])
    second_move = pltpu.make_async_copy(activations_in, activations, sems.at[1])
    first_move.start()
    second_move.start()
    first_move.wait()
    capacity, tokens, total = outgoing.shape[0], activations.shape[0], routed.shape[1]
    low = (me[0] * tokens).astype(f32)
    where = routed[...].astype(f32)
    first = jnp.sum(jnp.where(where < low, 1.0, 0.0), axis=1, keepdims=True)
    here = (where >= low) & (where < low + tokens)
    slot = jnp.where(here, iota((1, total), 1) - first, -1.0)
    hit = slot == iota((capacity, total), 0)
    token = jnp.sum(jnp.where(hit, where - low + 1.0, 0.0), axis=1, keepdims=True) - 1.0
    onehot = jnp.where(token == iota((capacity, tokens), 1), 1.0, 0.0).astype(bf16)
    second_move.wait()
    width = activations.shape[1]
    tile = tile_of(width, 1024)
    for start in range(0, width, tile):
        span = slice(start, start + tile)
        outgoing[:, span] = pick(onehot, activations[:, span])


def map_body(tall, wide, tokens, heads_of, me, routed, balance, notes, *outs):
    pick_rows, in_order, columns, unmix, positions = outs
    count, total = tall * wide, routed.shape[1]
    share, capacity = total // count, pick_rows.shape[1] // count
    outbound, inbound = columns.shape[0], unmix.shape[0]
    my_z, my_y = lax.div(me[0], wide), lax.rem(me[0], wide)
    where, owner = routed[...].astype(f32), balance[...].astype(f32)
    lane = iota((1, total), 1)
    slot, place = jnp.zeros((1, total), f32), jnp.zeros((1, total), f32)
    out_base, out_block = notes[:outbound, 0:1], notes[:outbound, 1:2]
    in_base, in_source = notes[:inbound, 2:3], notes[:inbound, 3:4]
    for s in range(count):
        z, y = divmod(s, wide)
        from_block = lax.rem(my_z - z + tall, tall) * wide + lax.rem(my_y - y + wide, wide)
        to_block = lax.rem(z - my_z + tall, tall) * wide + lax.rem(y - my_y + wide, wide)
        peer = lax.rem(my_z + z, tall) * wide + lax.rem(my_y + y, wide)
        before = where < s * tokens
        first = jnp.sum(jnp.where(before, 1.0, 0.0), axis=1, keepdims=True)
        inside = (where < (s + 1) * tokens) & jnp.logical_not(before)
        start = (from_block * capacity).astype(f32)
        slot += jnp.where(inside, lane - first + start, 0.0)
        place += jnp.where(owner == s, (to_block * share).astype(f32), 0.0)
        out_base += jnp.where(out_block == y * tall + z, heads_of(peer).astype(f32), 0.0)
        in_base += jnp.where(in_source == s, (from_block * (outbound // count)).astype(f32), 0.0)
    mine = owner == iota((count, total), 0)
    earlier = jnp.where(iota((total, total), 0) < iota((total, total), 1), 1.0, 0.0)
    rank = dot(jnp.where(mine, 1.0, 0.0).astype(bf16), earlier.astype(bf16))
    place += jnp.sum(jnp.where(mine, rank, 0.0), axis=0, keepdims=True)
    placed = place == iota((total, total), 0)
    in_order[...] = jnp.where(placed, 1.0, 0.0).astype(bf16)
    at = jnp.sum(jnp.where(placed, where, 0.0), axis=1, keepdims=True)
    positions[...] = jnp.broadcast_to(at, positions.shape)
    slot_at = jnp.sum(jnp.where(placed, slot, 0.0), axis=1, keepdims=True)
    pick_rows[...] = jnp.where(slot_at == iota(pick_rows.shape, 1), 1.0, 0.0).astype(bf16)
    columns[...] = jnp.where(out_base == iota(columns.shape, 1), 1.0, 0.0).astype(bf16)
    unmix[...] = jnp.where(in_base == iota(unmix.shape, 1), 1.0, 0.0).astype(bf16)


def kv_body(count, extra, *refs):
    blocks = refs[:count]
    pick_rows, order, columns, gain, w_key, w_value = refs[count : count + 6]
    wide = len(refs) - count - 9 - extra
    normed, own, *sent, rows = refs[-3 - wide :]
    total, width = normed.shape
    tile = tile_of(width, 512)
    square = jnp.zeros((total, 1), f32)
    for start in range(0, width, tile):
        span = slice(start, start + tile)
        part = dot(pick_rows[...], jnp.concatenate([b[:, span] for b in blocks], axis=0))
        rows[:, span] = part.astype(bf16)
        square += jnp.sum(part * part, axis=1, keepdims=True)
    own[...] = rows[: own.shape[0], :]
    factor = lax.rsqrt(square / width + norm_eps)
    for start in range(0, width, tile):
        span = slice(start, start + tile)
        part = rows[:, span].astype(f32) * factor * gain[:, span]
        normed[:, span] = part.astype(bf16)
    keys = dot(normed[...], w_key[...]).astype(bf16)
    values = dot(normed[...], w_value[...]).astype(bf16)
    both = jnp.concatenate([keys, values], axis=1)
    turned = lax.dot_general(
        columns[...], both, (((1,), (1,)), ((), ())), preferred_element_type=f32
    ).astype(bf16)
    turned = dot(turned, order[...])
    each = turned.shape[0] // wide
    for dy in range(wide):
        sent[dy][...] = turned[dy * each : (dy + 1) * each].astype(bf16)


def query_body(normed, w_query, cosine, sine, query):
    raw = dot(normed[...], w_query[...])
    for head in range(query.shape[1] // HEAD_DIM):
        span = slice(head * HEAD_DIM, (head + 1) * HEAD_DIM)
        one = raw[:, span]
        turned = one * cosine[...] + pltpu.roll(one, HEAD_DIM // 2, 1) * sine[...]
        query[:, span] = turned.astype(bf16)


def attend_body(plane, kv_local, *refs):
    tall = plane[0]
    arrived, rest = refs[:tall], refs[tall:]
    query, unmix, cosine, sine, key_pos, query_pos, w_output = rest[:7]
    parts, heads_out = rest[7:-1], rest[-1]
    half = HEAD_DIM // 2
    heads = query.shape[1] // HEAD_DIM
    mixed = jnp.concatenate([a[...].astype(f32) for a in arrived], axis=0).astype(bf16)
    both = dot(unmix[...], mixed)
    allowed = key_pos[...].astype(f32) <= query_pos[:, 0:1]
    for group in range(kv_local):
        base = group * HEAD_DIM
        first, second = both[base : base + half], both[base + half : base + HEAD_DIM]
        keys = jnp.concatenate(
            [first * cosine[...] - second * sine[...], second * cosine[...] + first * sine[...]],
            axis=0,
        ).astype(bf16)
        base += kv_local * HEAD_DIM
        values = both[base : base + HEAD_DIM].astype(bf16)
        for head in range(group * heads // kv_local, (group + 1) * heads // kv_local):
            span = slice(head * HEAD_DIM, (head + 1) * HEAD_DIM)
            scores = dot(query[:, span], keys) * HEAD_DIM ** (-0.5)
            scores = jnp.where(allowed, scores, -1e30)
            weights = jnp.exp(scores - jnp.max(scores, axis=1, keepdims=True))
            probs = (weights / jnp.sum(weights, axis=1, keepdims=True)).astype(bf16)
            heads_out[:, span] = lax.dot_general(
                probs, values, (((1,), (1,)), ((), ())), preferred_element_type=f32
            ).astype(bf16)
    spread(heads_out, w_output, parts, plane, False)


def spread(left, weight, parts, plane, back):
    width = weight.shape[1]
    tile = tile_of(width, 512)
    for start in range(0, width, tile):
        span = slice(start, start + tile)
        product = dot(left[...], weight[:, span]).astype(bf16)
        store_parts(parts, *plane, span, product, back)


def mlp_body(plane, *refs):
    count = plane[0] * plane[1]
    blocks, (w_gate, w_up, w_down) = refs[:count], refs[count : count + 3]
    parts, (piece, inner) = refs[count + 3 : -2], refs[-2:]
    share = blocks[0].shape[0]
    for index, block in enumerate(blocks):
        piece[index * share : (index + 1) * share, :] = block[...]
    width = w_gate.shape[1]
    tile = tile_of(width, 256)
    for start in range(0, width, tile):
        span = slice(start, start + tile)
        gate = dot(piece[...], w_gate[:, span])
        upward = dot(piece[...], w_up[:, span])
        inner[:, span] = (gate / (1.0 + jnp.exp(-gate)) * upward).astype(bf16)
    spread(inner, w_down, parts, plane, True)


def on_device(
    activations,
    routed,
    balance,
    w_query,
    w_key,
    w_value,
    w_output,
    attn_gain,
    mlp_gain,
    w_gate,
    w_up,
    w_down,
    w_router,
):
    count = lax.axis_size("ctx")
    plane = tall, wide = plane_of(count)
    me = lax.axis_index("ctx").astype(i32).reshape(1)
    tokens, model = activations.shape
    total = routed.shape[0]
    share = total // count
    capacity = 2 * share
    local_heads = w_query.shape[1] // HEAD_DIM
    group_size = HEADS // KV_HEADS
    kv_local = max(1, local_heads // group_size)
    key_cols = w_key.shape[1]
    depth = key_cols // KV_HEADS
    scalar = pl.BlockSpec(memory_space=pltpu.SMEM)
    in_hbm = pl.BlockSpec(memory_space=pl.ANY)
    routed, balance = routed.reshape(1, total), balance.reshape(1, total)

    (outgoing,) = kernel_call(
        send_body,
        [((capacity, model), bf16)],
        [me, from_hbm(routed), from_hbm(activations)],
        [
            pltpu.VMEM(routed.shape, i32),
            pltpu.VMEM(activations.shape, bf16),
            pltpu.SemaphoreType.DMA((2,)),
        ],
        specs=[scalar, in_hbm, in_hbm],
        flops=2 * capacity * tokens * model,
    )
    attn_gain, w_key, w_value, w_query, token_1 = load(
        outgoing, attn_gain.reshape(1, model), w_key, w_value, w_query
    )
    w_down, token_5 = load(token_1, w_down)

    each = kv_local * 2 * depth
    notes = np.zeros((max(count * each, 2 * kv_local * HEAD_DIM), 4), np.float32)
    block, local, side, entry = np.indices((count, kv_local, 2, depth)).reshape(4, -1)
    notes[: count * each, 0] = side * key_cols + entry * KV_HEADS + local
    notes[: count * each, 1] = block
    side, local, source, entry = np.indices((2, kv_local, count, depth)).reshape(4, -1)
    notes[: 2 * kv_local * HEAD_DIM, 2] = (local * 2 + side) * depth + entry
    notes[: 2 * kv_local * HEAD_DIM, 3] = source
    pick_rows, in_order, columns, unmix, positions = kernel_call(
        functools.partial(
            map_body, tall, wide, tokens, lambda peer: lax.div(peer * local_heads, group_size)
        ),
        [
            ((total, count * capacity), bf16),
            ((total, total), bf16),
            ((count * each, 2 * key_cols), bf16),
            ((2 * kv_local * HEAD_DIM, count * each), bf16),
            ((total, HEAD_DIM // 2), f32),
        ],
        [me, routed, balance, notes],
        specs=[scalar, VMEM, VMEM, VMEM],
    )
    blocks = gather_rows(outgoing, tall, wide, [token_1, token_5, positions])
    near = blocks[2 * wide]
    w_output, *token_2 = load(near, w_output)
    w_gate, *token_3 = load(near, w_gate)
    loaded = token_2 + token_3

    half = HEAD_DIM // 2
    steps_f = jnp.arange(half, dtype=f32)
    freqs = jnp.exp(-jnp.log(f32(rope_base)) * (2.0 * steps_f / HEAD_DIM))
    q_angles = positions * freqs[None, :]
    q_cos, q_sin = jnp.cos(q_angles), jnp.sin(q_angles)
    q_cos = jnp.concatenate([q_cos, q_cos], axis=1)
    q_sin = jnp.concatenate([-q_sin, q_sin], axis=1)
    k_angles = freqs[:, None] * routed.astype(f32)
    k_cos, k_sin = jnp.cos(k_angles), jnp.sin(k_angles)

    normed, own, *sent = kernel_call(
        functools.partial(kv_body, count, len(loaded)),
        [((total, model), bf16), ((share, model), bf16)] + [((tall * each, total), bf16)] * wide,
        [*blocks, pick_rows, in_order, columns, attn_gain, w_key, w_value, *loaded],
        [pltpu.VMEM((total, model), bf16)],
        flops=2 * total * model * 512,
    )
    arrived = exchange(sent, tall, wide)
    heads_wide = local_heads * HEAD_DIM
    (query,) = kernel_call(
        query_body,
        [((total, heads_wide), bf16)],
        [normed, w_query, q_cos, q_sin],
        flops=2 * total * model * heads_wide,
    )
    attn_parts = kernel_call(
        functools.partial(attend_body, plane, kv_local),
        [((share, model), bf16)] * count,
        [*arrived, query, unmix, k_cos, k_sin, routed, positions, w_output],
        [pltpu.VMEM((total, heads_wide), bf16)],
        flops=2 * total * model * heads_wide,
    )
    attn_own = scatter_sum(attn_parts, tall, wide)
    own_rows = own.astype(f32)
    hidden = own_rows + attn_own
    mean_sq = jnp.mean(hidden * hidden, axis=-1, keepdims=True)
    mnorm = (hidden * lax.rsqrt(mean_sq + norm_eps) * mlp_gain).astype(bf16)
    pieces = gather_blocks(mnorm, tall, wide)
    w_up, _ = load(mnorm, w_up)
    hidden_units = w_gate.shape[1]
    mlp_parts = kernel_call(
        functools.partial(mlp_body, plane),
        [((share, model), bf16)] * count,
        [*pieces, w_gate, w_up, w_down],
        [pltpu.VMEM((total, model), bf16), pltpu.VMEM((total, hidden_units), bf16)],
        flops=6 * total * model * hidden_units,
    )
    mlp_own = scatter_sum(mlp_parts, tall, wide)
    router_score = jnp.sum(own_rows * w_router[None, :], axis=1, keepdims=True)
    return (own_rows + router_score * (attn_own + mlp_own)).astype(bf16)


def solution(mesh):
    in_specs = (
        P(("dp", "ctx"), None),
        P("dp"),
        P("dp"),
        P(None, "ctx"),
        P(None, "ctx"),
        P(None, "ctx"),
        P("ctx", None),
        P(),
        P(),
        P(None, "ctx"),
        P(None, "ctx"),
        P("ctx", None),
        P(),
    )
    out_specs = P(("dp", "ctx"), None)
    return jax.shard_map(
        on_device, mesh=mesh, in_specs=in_specs, out_specs=out_specs, check_vma=False
    )
```

```python
import functools

import jax
import jax.numpy as jnp
import numpy as np
from jax import lax
from jax.experimental import pallas as pl
from jax.experimental.pallas import tpu as pltpu
from jax.sharding import PartitionSpec as P

HEADS = 32
KV_HEADS = 8
HEAD_DIM = 128

rope_base = 500000.0
norm_eps = 1e-05

bf16, f32, i32 = jnp.bfloat16, jnp.float32, jnp.int32
VMEM = pl.BlockSpec(memory_space=pltpu.VMEM)


def plane_of(count):
    wide = max(y for y in range(1, count + 1) if count % y == 0 and 2 * y * y <= max(count, 2))
    return count // wide, wide


def shift(block, tall, wide, dz, dy, keep=None):
    pairs = [
        (z * wide + y, (z + dz) % tall * wide + (y + dy) % wide)
        for z in range(tall)
        for y in range(wide)
        if keep is None or keep(z)
    ]
    return lax.ppermute(block, "ctx", pairs)


def tie_body(count, *refs):
    total = refs[0][...]
    for ref in refs[1:count]:
        total = total + ref[...]
    refs[-1][...] = total


def tie(blocks, tokens):
    return kernel_call(
        functools.partial(tie_body, len(blocks)),
        [(blocks[0].shape, blocks[0].dtype)],
        [*blocks, *tokens],
        specs=[VMEM] * len(blocks) + [pl.BlockSpec(memory_space=pl.ANY)] * len(tokens),
    )[0]


def gather_rows(block, tall, wide, tokens):
    blocks = {(0, 0): block}
    for dy in range(1, wide):
        blocks[0, dy] = shift(block, tall, wide, 0, dy)
    first = [*tokens, *(blocks[0, dy] for dy in range(1, wide))]
    for dz in range(tall - 1, 0, -1):
        if tall != 4 or dz != 2:
            blocks[dz, 0] = shift(block, tall, wide, dz, 0)
    blocks[tall - 1, 0] = tie([blocks[tall - 1, 0]], first)
    if tall == 4:
        for dy in range(1, wide):
            blocks[3, dy] = shift(blocks[3, 0], tall, wide, 0, dy)
        up = shift(blocks[1, 0], tall, wide, 1, 0, lambda z: z in (1, 2))
        down = shift(blocks[3, 0], tall, wide, -1, 0, lambda z: z in (1, 2))
        blocks[2, 0] = tie([up, down], [blocks[3, dy] for dy in range(1, wide)])
    for dz in range(1, tall):
        for dy in range(1, wide):
            if (dz, dy) not in blocks:
                blocks[dz, dy] = shift(blocks[dz, 0], tall, wide, 0, dy)
    return [blocks[dz, dy] for dz in range(tall) for dy in range(wide)]


def pack_body(tall, *refs):
    wide = len(refs) - tall
    each = refs[0].shape[0] // tall
    for dz in range(tall):
        values = [ref[...].astype(f32)[dz * each : (dz + 1) * each] for ref in refs[:wide]]
        refs[wide + dz][...] = jnp.concatenate(values, axis=0).astype(bf16)


def exchange(parts, tall, wide):
    shape = ((parts[0].shape[0] // tall * wide, parts[0].shape[1]), bf16)
    crossed = [parts[0]] + [shift(parts[dy], tall, wide, 0, dy) for dy in range(1, wide)]
    packed = kernel_call(functools.partial(pack_body, tall), [shape] * tall, crossed)
    pairs = [
        [(z * wide + y, (z ^ kz) * wide + y) for z in range(tall) for y in range(wide)]
        for kz in range(tall)
    ]
    return [packed[0]] + [lax.ppermute(packed[k], "ctx", pairs[k]) for k in range(1, tall)]


def gather_blocks(block, tall, wide):
    blocks = {(dz, 0): shift(block, tall, wide, dz, 0) if dz else block for dz in range(tall)}
    for dz in range(tall):
        for dy in range(1, wide):
            blocks[dz, dy] = shift(blocks[dz, 0], tall, wide, 0, dy)
    return [blocks[dz, dy] for dz in range(tall) for dy in range(wide)]


def sum_order(tall):
    return [tall // 2, *range(1, tall // 2), *range(tall // 2 + 1, tall), 0]


def store_parts(parts, tall, wide, span, product, back):
    share = parts[0].shape[0]
    sign = -1 if back else 1
    for dz in range(tall):
        for dy in range(wide):
            at = sign * dz % tall * wide + sign * dy % wide
            parts[dz * wide + dy][:, span] = product[at * share : (at + 1) * share, :]


def scatter_sum(parts, tall, wide):
    total = None
    for dz in sum_order(tall):
        lane = parts[dz * wide].astype(f32)
        for dy in range(1, wide):
            lane = lane + shift(parts[dz * wide + dy], tall, wide, 0, dy).astype(f32)
        if dz:
            lane = shift(lane.astype(bf16), tall, wide, dz, 0).astype(f32)
        total = lane if total is None else total + lane
    return total


def dot(a, b):
    return jnp.dot(a, b, preferred_element_type=f32)


def from_hbm(weight):
    return pltpu.with_memory_space_constraint(weight, pltpu.HBM)


def fetched(weight):
    return pltpu.with_memory_space_constraint(weight, pltpu.VMEM)


def kernel_call(body, outs, args, scratch=(), limit=14, flops=0, specs=None):
    return pl.pallas_call(
        body,
        out_shape=[jax.ShapeDtypeStruct(s, d) for s, d in outs],
        in_specs=specs or [VMEM] * len(args),
        out_specs=[VMEM] * len(outs),
        scratch_shapes=list(scratch),
        compiler_params=pltpu.CompilerParams(vmem_limit_bytes=limit << 20),
        cost_estimate=pl.CostEstimate(flops=flops, bytes_accessed=1 << 20, transcendentals=0),
    )(*args)


def load_body(count, *refs):
    sources, copies, sems = refs[1 : 1 + count], refs[1 + count : -2], refs[-1]
    moves = [
        pltpu.make_async_copy(a, b, sems.at[i]) for i, (a, b) in enumerate(zip(sources, copies))
    ]
    for move in moves:
        move.start()
    for move in moves:
        move.wait()
    refs[-2][...] = jnp.zeros_like(refs[-2])


def load(after, *arrays):
    size = sum(a.size * a.dtype.itemsize for a in arrays)
    *copies, token = pl.pallas_call(
        functools.partial(load_body, len(arrays)),
        out_shape=[pltpu.VMEM(a.shape, a.dtype) for a in arrays]
        + [jax.ShapeDtypeStruct((8, 128), f32)],
        in_specs=[pl.BlockSpec(memory_space=pl.ANY)] * (1 + len(arrays)),
        out_specs=[VMEM] * (1 + len(arrays)),
        scratch_shapes=[pltpu.SemaphoreType.DMA((len(arrays),))],
        compiler_params=pltpu.CompilerParams(vmem_limit_bytes=2 << 20),
        cost_estimate=pl.CostEstimate(flops=0, bytes_accessed=2 * size, transcendentals=0),
    )(after, *[from_hbm(a) for a in arrays])
    return [fetched(c) for c in copies] + [token]


def tile_of(width, most):
    return width if width <= most else most


def iota(shape, axis):
    return lax.broadcasted_iota(i32, shape, axis).astype(f32)


def pick(onehot, values):
    return dot(onehot, values).astype(values.dtype)


def send_body(me, routed_in, activations_in, outgoing, routed, activations, sems):
    first_move = pltpu.make_async_copy(routed_in, routed, sems.at[0])
    second_move = pltpu.make_async_copy(activations_in, activations, sems.at[1])
    first_move.start()
    second_move.start()
    first_move.wait()
    capacity, tokens, total = outgoing.shape[0], activations.shape[0], routed.shape[1]
    low = (me[0] * tokens).astype(f32)
    where = routed[...].astype(f32)
    first = jnp.sum(jnp.where(where < low, 1.0, 0.0), axis=1, keepdims=True)
    here = (where >= low) & (where < low + tokens)
    slot = jnp.where(here, iota((1, total), 1) - first, -1.0)
    hit = slot == iota((capacity, total), 0)
    token = jnp.sum(jnp.where(hit, where - low + 1.0, 0.0), axis=1, keepdims=True) - 1.0
    onehot = jnp.where(token == iota((capacity, tokens), 1), 1.0, 0.0).astype(bf16)
    second_move.wait()
    width = activations.shape[1]
    tile = tile_of(width, 1024)
    for start in range(0, width, tile):
        span = slice(start, start + tile)
        outgoing[:, span] = pick(onehot, activations[:, span])


def map_body(tall, wide, tokens, heads_of, me, routed, balance, notes, *outs):
    pick_rows, in_order, columns, unmix, positions = outs
    count, total = tall * wide, routed.shape[1]
    share, capacity = total // count, pick_rows.shape[1] // count
    outbound, inbound = columns.shape[0], unmix.shape[0]
    my_z, my_y = lax.div(me[0], wide), lax.rem(me[0], wide)
    where, owner = routed[...].astype(f32), balance[...].astype(f32)
    lane = iota((1, total), 1)
    slot, place = jnp.zeros((1, total), f32), jnp.zeros((1, total), f32)
    out_base, out_block = notes[:outbound, 0:1], notes[:outbound, 1:2]
    in_base, in_source = notes[:inbound, 2:3], notes[:inbound, 3:4]
    for s in range(count):
        z, y = divmod(s, wide)
        from_block = lax.rem(my_z - z + tall, tall) * wide + lax.rem(my_y - y + wide, wide)
        to_block = lax.rem(z - my_z + tall, tall) * wide + lax.rem(y - my_y + wide, wide)
        peer = (my_z ^ z) * wide + lax.rem(my_y + y, wide)
        lot = (my_z ^ z) * wide + lax.rem(my_y - y + wide, wide)
        before = where < s * tokens
        first = jnp.sum(jnp.where(before, 1.0, 0.0), axis=1, keepdims=True)
        inside = (where < (s + 1) * tokens) & jnp.logical_not(before)
        start = (from_block * capacity).astype(f32)
        slot += jnp.where(inside, lane - first + start, 0.0)
        place += jnp.where(owner == s, (to_block * share).astype(f32), 0.0)
        out_base += jnp.where(out_block == y * tall + z, heads_of(peer).astype(f32), 0.0)
        in_base += jnp.where(in_source == s, (lot * (outbound // count)).astype(f32), 0.0)
    mine = owner == iota((count, total), 0)
    earlier = jnp.where(iota((total, total), 0) < iota((total, total), 1), 1.0, 0.0)
    rank = dot(jnp.where(mine, 1.0, 0.0).astype(bf16), earlier.astype(bf16))
    place += jnp.sum(jnp.where(mine, rank, 0.0), axis=0, keepdims=True)
    placed = place == iota((total, total), 0)
    in_order[...] = jnp.where(placed, 1.0, 0.0).astype(bf16)
    at = jnp.sum(jnp.where(placed, where, 0.0), axis=1, keepdims=True)
    positions[...] = jnp.broadcast_to(at, positions.shape)
    slot_at = jnp.sum(jnp.where(placed, slot, 0.0), axis=1, keepdims=True)
    pick_rows[...] = jnp.where(slot_at == iota(pick_rows.shape, 1), 1.0, 0.0).astype(bf16)
    columns[...] = jnp.where(out_base == iota(columns.shape, 1), 1.0, 0.0).astype(bf16)
    unmix[...] = jnp.where(in_base == iota(unmix.shape, 1), 1.0, 0.0).astype(bf16)


def kv_body(count, extra, *refs):
    blocks = refs[:count]
    pick_rows, order, columns, gain, w_key, w_value = refs[count : count + 6]
    wide = len(refs) - count - 9 - extra
    scaled, own, factor, *sent = refs[-3 - wide :]
    total, width = scaled.shape
    tile = tile_of(width, 512)
    square = jnp.zeros((total, 1), f32)
    for start in range(0, width, tile):
        span = slice(start, start + tile)
        part = dot(pick_rows[...], jnp.concatenate([b[:, span] for b in blocks], axis=0))
        own[:, span] = part[: own.shape[0], :].astype(bf16)
        scaled[:, span] = (part * gain[:, span]).astype(bf16)
        square += jnp.sum(part * part, axis=1, keepdims=True)
    rooted = lax.rsqrt(square / width + norm_eps)
    factor[...] = jnp.broadcast_to(rooted, factor.shape)
    keys = (dot(scaled[...], w_key[...]) * rooted).astype(bf16)
    values = (dot(scaled[...], w_value[...]) * rooted).astype(bf16)
    both = jnp.concatenate([keys, values], axis=1)
    turned = lax.dot_general(
        columns[...], both, (((1,), (1,)), ((), ())), preferred_element_type=f32
    ).astype(bf16)
    turned = dot(turned, order[...])
    each = turned.shape[0] // wide
    for dy in range(wide):
        sent[dy][...] = turned[dy * each : (dy + 1) * each].astype(bf16)


def query_body(scaled, factor, w_query, cosine, sine, query):
    raw = dot(scaled[...], w_query[...]) * factor[:, 0:1]
    for head in range(query.shape[1] // HEAD_DIM):
        span = slice(head * HEAD_DIM, (head + 1) * HEAD_DIM)
        one = raw[:, span]
        turned = one * cosine[...] + pltpu.roll(one, HEAD_DIM // 2, 1) * sine[...]
        query[:, span] = turned.astype(bf16)


def attend_body(plane, kv_local, *refs):
    tall = plane[0]
    arrived, rest = refs[:tall], refs[tall:]
    query, unmix, cosine, sine, key_pos, query_pos, w_output = rest[:7]
    parts, heads_out = rest[7:-1], rest[-1]
    half = HEAD_DIM // 2
    heads = query.shape[1] // HEAD_DIM
    mixed = jnp.concatenate([a[...].astype(f32) for a in arrived], axis=0).astype(bf16)
    both = dot(unmix[...], mixed)
    allowed = key_pos[...].astype(f32) <= query_pos[:, 0:1]
    for group in range(kv_local):
        base = group * HEAD_DIM
        first, second = both[base : base + half], both[base + half : base + HEAD_DIM]
        keys = jnp.concatenate(
            [first * cosine[...] - second * sine[...], second * cosine[...] + first * sine[...]],
            axis=0,
        ).astype(bf16)
        base += kv_local * HEAD_DIM
        values = both[base : base + HEAD_DIM].astype(bf16)
        for head in range(group * heads // kv_local, (group + 1) * heads // kv_local):
            span = slice(head * HEAD_DIM, (head + 1) * HEAD_DIM)
            scores = dot(query[:, span], keys) * HEAD_DIM ** (-0.5)
            scores = jnp.where(allowed, scores, -1e30)
            weights = jnp.exp(scores - jnp.max(scores, axis=1, keepdims=True))
            probs = (weights / jnp.sum(weights, axis=1, keepdims=True)).astype(bf16)
            heads_out[:, span] = lax.dot_general(
                probs, values, (((1,), (1,)), ((), ())), preferred_element_type=f32
            ).astype(bf16)
    spread(heads_out, w_output, parts, plane, False)


def spread(left, weight, parts, plane, back):
    width = weight.shape[1]
    tile = tile_of(width, 512)
    for start in range(0, width, tile):
        span = slice(start, start + tile)
        product = dot(left[...], weight[:, span]).astype(bf16)
        store_parts(parts, *plane, span, product, back)


def mlp_body(plane, *refs):
    count = plane[0] * plane[1]
    blocks, (w_gate, w_up, w_down) = refs[:count], refs[count : count + 3]
    parts, (piece, inner) = refs[count + 3 : -2], refs[-2:]
    share = blocks[0].shape[0]
    for index, block in enumerate(blocks):
        piece[index * share : (index + 1) * share, :] = block[...]
    width = w_gate.shape[1]
    tile = tile_of(width, 256)
    for start in range(0, width, tile):
        span = slice(start, start + tile)
        gate = dot(piece[...], w_gate[:, span])
        upward = dot(piece[...], w_up[:, span])
        inner[:, span] = (gate / (1.0 + jnp.exp(-gate)) * upward).astype(bf16)
    spread(inner, w_down, parts, plane, True)


def on_device(
    activations,
    routed,
    balance,
    w_query,
    w_key,
    w_value,
    w_output,
    attn_gain,
    mlp_gain,
    w_gate,
    w_up,
    w_down,
    w_router,
):
    count = lax.axis_size("ctx")
    plane = tall, wide = plane_of(count)
    me = lax.axis_index("ctx").astype(i32).reshape(1)
    tokens, model = activations.shape
    total = routed.shape[0]
    share = total // count
    capacity = 2 * share
    local_heads = w_query.shape[1] // HEAD_DIM
    group_size = HEADS // KV_HEADS
    kv_local = max(1, local_heads // group_size)
    key_cols = w_key.shape[1]
    depth = key_cols // KV_HEADS
    scalar = pl.BlockSpec(memory_space=pltpu.SMEM)
    in_hbm = pl.BlockSpec(memory_space=pl.ANY)
    routed, balance = routed.reshape(1, total), balance.reshape(1, total)

    (outgoing,) = kernel_call(
        send_body,
        [((capacity, model), bf16)],
        [me, from_hbm(routed), from_hbm(activations)],
        [
            pltpu.VMEM(routed.shape, i32),
            pltpu.VMEM(activations.shape, bf16),
            pltpu.SemaphoreType.DMA((2,)),
        ],
        specs=[scalar, in_hbm, in_hbm],
        flops=2 * capacity * tokens * model,
    )
    attn_gain, w_key, w_value, w_query, token_1 = load(
        outgoing, attn_gain.reshape(1, model), w_key, w_value, w_query
    )
    w_down, token_5 = load(token_1, w_down)

    each = kv_local * 2 * depth
    notes = np.zeros((max(count * each, 2 * kv_local * HEAD_DIM), 4), np.float32)
    block, local, side, entry = np.indices((count, kv_local, 2, depth)).reshape(4, -1)
    notes[: count * each, 0] = side * key_cols + entry * KV_HEADS + local
    notes[: count * each, 1] = block
    side, local, source, entry = np.indices((2, kv_local, count, depth)).reshape(4, -1)
    notes[: 2 * kv_local * HEAD_DIM, 2] = (local * 2 + side) * depth + entry
    notes[: 2 * kv_local * HEAD_DIM, 3] = source
    pick_rows, in_order, columns, unmix, positions = kernel_call(
        functools.partial(
            map_body, tall, wide, tokens, lambda peer: lax.div(peer * local_heads, group_size)
        ),
        [
            ((total, count * capacity), bf16),
            ((total, total), bf16),
            ((count * each, 2 * key_cols), bf16),
            ((2 * kv_local * HEAD_DIM, count * each), bf16),
            ((total, HEAD_DIM // 2), f32),
        ],
        [me, routed, balance, notes],
        specs=[scalar, VMEM, VMEM, VMEM],
    )
    blocks = gather_rows(outgoing, tall, wide, [token_1, token_5, positions])
    near = blocks[2 * wide]
    w_output, *token_2 = load(near, w_output)
    w_gate, *token_3 = load(near, w_gate)
    loaded = token_2 + token_3

    half = HEAD_DIM // 2
    steps_f = jnp.arange(half, dtype=f32)
    freqs = jnp.exp(-jnp.log(f32(rope_base)) * (2.0 * steps_f / HEAD_DIM))
    q_angles = positions * freqs[None, :]
    q_cos, q_sin = jnp.cos(q_angles), jnp.sin(q_angles)
    q_cos = jnp.concatenate([q_cos, q_cos], axis=1)
    q_sin = jnp.concatenate([-q_sin, q_sin], axis=1)
    k_angles = freqs[:, None] * routed.astype(f32)
    k_cos, k_sin = jnp.cos(k_angles), jnp.sin(k_angles)

    scaled, own, factor, *sent = kernel_call(
        functools.partial(kv_body, count, len(loaded)),
        [((total, model), bf16), ((share, model), bf16), ((total, 128), f32)]
        + [((tall * each, total), bf16)] * wide,
        [*blocks, pick_rows, in_order, columns, attn_gain, w_key, w_value, *loaded],
        flops=2 * total * model * 512,
    )
    arrived = exchange(sent, tall, wide)
    heads_wide = local_heads * HEAD_DIM
    (query,) = kernel_call(
        query_body,
        [((total, heads_wide), bf16)],
        [scaled, factor, w_query, q_cos, q_sin],
        flops=2 * total * model * heads_wide,
    )
    attn_parts = kernel_call(
        functools.partial(attend_body, plane, kv_local),
        [((share, model), bf16)] * count,
        [*arrived, query, unmix, k_cos, k_sin, routed, positions, w_output],
        [pltpu.VMEM((total, heads_wide), bf16)],
        flops=2 * total * model * heads_wide,
    )
    attn_own = scatter_sum(attn_parts, tall, wide)
    own_rows = own.astype(f32)
    hidden = own_rows + attn_own
    mean_sq = jnp.mean(hidden * hidden, axis=-1, keepdims=True)
    mnorm = (hidden * lax.rsqrt(mean_sq + norm_eps) * mlp_gain).astype(bf16)
    pieces = gather_blocks(mnorm, tall, wide)
    w_up, _ = load(mnorm, w_up)
    hidden_units = w_gate.shape[1]
    mlp_parts = kernel_call(
        functools.partial(mlp_body, plane),
        [((share, model), bf16)] * count,
        [*pieces, w_gate, w_up, w_down],
        [pltpu.VMEM((total, model), bf16), pltpu.VMEM((total, hidden_units), bf16)],
        flops=6 * total * model * hidden_units,
    )
    mlp_own = scatter_sum(mlp_parts, tall, wide)
    router_score = jnp.sum(own_rows * w_router[None, :], axis=1, keepdims=True)
    return (own_rows + router_score * (attn_own + mlp_own)).astype(bf16)


def solution(mesh):
    in_specs = (
        P(("dp", "ctx"), None),
        P("dp"),
        P("dp"),
        P(None, "ctx"),
        P(None, "ctx"),
        P(None, "ctx"),
        P("ctx", None),
        P(),
        P(),
        P(None, "ctx"),
        P(None, "ctx"),
        P("ctx", None),
        P(),
    )
    out_specs = P(("dp", "ctx"), None)
    return jax.shard_map(
        on_device, mesh=mesh, in_specs=in_specs, out_specs=out_specs, check_vma=False
    )
```

```python
import functools

import jax
import jax.numpy as jnp
import numpy as np
from jax import lax
from jax.experimental import pallas as pl
from jax.experimental.pallas import tpu as pltpu
from jax.sharding import PartitionSpec as P

HEADS = 32
KV_HEADS = 8
HEAD_DIM = 128

rope_base = 500000.0
norm_eps = 1e-05

bf16, f32, i32 = jnp.bfloat16, jnp.float32, jnp.int32
VMEM = pl.BlockSpec(memory_space=pltpu.VMEM)


def plane_of(count):
    wide = max(y for y in range(1, count + 1) if count % y == 0 and 2 * y * y <= max(count, 2))
    return count // wide, wide


def shift(block, tall, wide, dz, dy, keep=None):
    pairs = [
        (z * wide + y, (z + dz) % tall * wide + (y + dy) % wide)
        for z in range(tall)
        for y in range(wide)
        if keep is None or keep(z)
    ]
    return lax.ppermute(block, "ctx", pairs)


def tie_body(count, *refs):
    total = refs[0][...]
    for ref in refs[1:count]:
        total = total + ref[...]
    refs[-1][...] = total


def tie(blocks, tokens):
    return kernel_call(
        functools.partial(tie_body, len(blocks)),
        [(blocks[0].shape, blocks[0].dtype)],
        [*blocks, *tokens],
        specs=[VMEM] * len(blocks) + [pl.BlockSpec(memory_space=pl.ANY)] * len(tokens),
    )[0]


def gather_rows(block, tall, wide, tokens):
    blocks = {(0, 0): block}
    for dy in range(1, wide):
        blocks[0, dy] = shift(block, tall, wide, 0, dy)
    first = [*tokens, *(blocks[0, dy] for dy in range(1, wide))]
    for dz in range(tall - 1, 0, -1):
        if tall != 4 or dz != 2:
            blocks[dz, 0] = shift(block, tall, wide, dz, 0)
    blocks[tall - 1, 0] = tie([blocks[tall - 1, 0]], first)
    if tall == 4:
        for dy in range(1, wide):
            blocks[3, dy] = shift(blocks[3, 0], tall, wide, 0, dy)
        up = shift(blocks[1, 0], tall, wide, 1, 0, lambda z: z in (1, 2))
        down = shift(blocks[3, 0], tall, wide, -1, 0, lambda z: z in (1, 2))
        blocks[2, 0] = tie([up, down], [blocks[3, dy] for dy in range(1, wide)])
    for dz in range(1, tall):
        for dy in range(1, wide):
            if (dz, dy) not in blocks:
                blocks[dz, dy] = shift(blocks[dz, 0], tall, wide, 0, dy)
    return [blocks[dz, dy] for dz in range(tall) for dy in range(wide)]


def pack_body(tall, *refs):
    wide = len(refs) - tall
    each = refs[0].shape[0] // tall
    for dz in range(tall):
        values = [ref[...].astype(f32)[dz * each : (dz + 1) * each] for ref in refs[:wide]]
        refs[wide + dz][...] = jnp.concatenate(values, axis=0).astype(bf16)


def exchange(parts, tall, wide):
    shape = ((parts[0].shape[0] // tall * wide, parts[0].shape[1]), bf16)
    crossed = [parts[0]] + [shift(parts[dy], tall, wide, 0, dy) for dy in range(1, wide)]
    packed = kernel_call(functools.partial(pack_body, tall), [shape] * tall, crossed)
    pairs = [
        [(z * wide + y, (z ^ kz) * wide + y) for z in range(tall) for y in range(wide)]
        for kz in range(tall)
    ]
    return [packed[0]] + [lax.ppermute(packed[k], "ctx", pairs[k]) for k in range(1, tall)]


def gather_blocks(block, tall, wide):
    blocks = {(dz, 0): shift(block, tall, wide, dz, 0) if dz else block for dz in range(tall)}
    for dz in range(tall):
        for dy in range(1, wide):
            blocks[dz, dy] = shift(blocks[dz, 0], tall, wide, 0, dy)
    return [blocks[dz, dy] for dz in range(tall) for dy in range(wide)]


def sum_order(tall):
    return [tall // 2, *range(tall - 1, tall // 2, -1), *range(tall // 2 - 1, -1, -1)]


def store_parts(parts, tall, wide, span, product, back):
    share = parts[0].shape[0]
    sign = -1 if back else 1
    for dz in range(tall):
        for dy in range(wide):
            at = sign * dz % tall * wide + sign * dy % wide
            parts[dz * wide + dy][:, span] = product[at * share : (at + 1) * share, :]


def scatter_sum(parts, tall, wide):
    total = None
    for dz in sum_order(tall):
        lane = parts[dz * wide].astype(f32)
        for dy in range(1, wide):
            lane = lane + shift(parts[dz * wide + dy], tall, wide, 0, dy).astype(f32)
        if dz:
            lane = shift(lane.astype(bf16), tall, wide, dz, 0).astype(f32)
        total = lane if total is None else total + lane
    return total


def dot(a, b):
    return jnp.dot(a, b, preferred_element_type=f32)


def from_hbm(weight):
    return pltpu.with_memory_space_constraint(weight, pltpu.HBM)


def fetched(weight):
    return pltpu.with_memory_space_constraint(weight, pltpu.VMEM)


def kernel_call(body, outs, args, scratch=(), limit=14, flops=0, specs=None):
    return pl.pallas_call(
        body,
        out_shape=[jax.ShapeDtypeStruct(s, d) for s, d in outs],
        in_specs=specs or [VMEM] * len(args),
        out_specs=[VMEM] * len(outs),
        scratch_shapes=list(scratch),
        compiler_params=pltpu.CompilerParams(vmem_limit_bytes=limit << 20),
        cost_estimate=pl.CostEstimate(flops=flops, bytes_accessed=1 << 20, transcendentals=0),
    )(*args)


def load_body(count, *refs):
    sources, copies, sems = refs[1 : 1 + count], refs[1 + count : -2], refs[-1]
    moves = [
        pltpu.make_async_copy(a, b, sems.at[i]) for i, (a, b) in enumerate(zip(sources, copies))
    ]
    for move in moves:
        move.start()
    for move in moves:
        move.wait()
    refs[-2][...] = jnp.zeros_like(refs[-2])


def load(after, *arrays):
    size = sum(a.size * a.dtype.itemsize for a in arrays)
    *copies, token = pl.pallas_call(
        functools.partial(load_body, len(arrays)),
        out_shape=[pltpu.VMEM(a.shape, a.dtype) for a in arrays]
        + [jax.ShapeDtypeStruct((8, 128), f32)],
        in_specs=[pl.BlockSpec(memory_space=pl.ANY)] * (1 + len(arrays)),
        out_specs=[VMEM] * (1 + len(arrays)),
        scratch_shapes=[pltpu.SemaphoreType.DMA((len(arrays),))],
        compiler_params=pltpu.CompilerParams(vmem_limit_bytes=2 << 20),
        cost_estimate=pl.CostEstimate(flops=0, bytes_accessed=2 * size, transcendentals=0),
    )(after, *[from_hbm(a) for a in arrays])
    return [fetched(c) for c in copies] + [token]


def tile_of(width, most):
    return width if width <= most else most


def iota(shape, axis):
    return lax.broadcasted_iota(i32, shape, axis).astype(f32)


def pick(onehot, values):
    return dot(onehot, values).astype(values.dtype)


def send_body(me, routed_in, activations_in, outgoing, routed, activations, sems):
    first_move = pltpu.make_async_copy(routed_in, routed, sems.at[0])
    second_move = pltpu.make_async_copy(activations_in, activations, sems.at[1])
    first_move.start()
    second_move.start()
    first_move.wait()
    capacity, tokens, total = outgoing.shape[0], activations.shape[0], routed.shape[1]
    low = (me[0] * tokens).astype(f32)
    where = routed[...].astype(f32)
    first = jnp.sum(jnp.where(where < low, 1.0, 0.0), axis=1, keepdims=True)
    here = (where >= low) & (where < low + tokens)
    slot = jnp.where(here, iota((1, total), 1) - first, -1.0)
    hit = slot == iota((capacity, total), 0)
    token = jnp.sum(jnp.where(hit, where - low + 1.0, 0.0), axis=1, keepdims=True) - 1.0
    onehot = jnp.where(token == iota((capacity, tokens), 1), 1.0, 0.0).astype(bf16)
    second_move.wait()
    width = activations.shape[1]
    tile = tile_of(width, 1024)
    for start in range(0, width, tile):
        span = slice(start, start + tile)
        outgoing[:, span] = pick(onehot, activations[:, span])


def map_body(tall, wide, tokens, heads_of, me, routed, balance, notes, *outs):
    pick_rows, in_order, columns, unmix, positions = outs
    count, total = tall * wide, routed.shape[1]
    share, capacity = total // count, pick_rows.shape[1] // count
    outbound, inbound = columns.shape[0], unmix.shape[0]
    my_z, my_y = lax.div(me[0], wide), lax.rem(me[0], wide)
    where, owner = routed[...].astype(f32), balance[...].astype(f32)
    lane = iota((1, total), 1)
    slot, place = jnp.zeros((1, total), f32), jnp.zeros((1, total), f32)
    out_base, out_block = notes[:outbound, 0:1], notes[:outbound, 1:2]
    in_base, in_source = notes[:inbound, 2:3], notes[:inbound, 3:4]
    for s in range(count):
        z, y = divmod(s, wide)
        from_block = lax.rem(my_z - z + tall, tall) * wide + lax.rem(my_y - y + wide, wide)
        to_block = lax.rem(z - my_z + tall, tall) * wide + lax.rem(y - my_y + wide, wide)
        peer = (my_z ^ z) * wide + lax.rem(my_y + y, wide)
        lot = (my_z ^ z) * wide + lax.rem(my_y - y + wide, wide)
        before = where < s * tokens
        first = jnp.sum(jnp.where(before, 1.0, 0.0), axis=1, keepdims=True)
        inside = (where < (s + 1) * tokens) & jnp.logical_not(before)
        start = (from_block * capacity).astype(f32)
        slot += jnp.where(inside, lane - first + start, 0.0)
        place += jnp.where(owner == s, (to_block * share).astype(f32), 0.0)
        out_base += jnp.where(out_block == y * tall + z, heads_of(peer).astype(f32), 0.0)
        in_base += jnp.where(in_source == s, (lot * (outbound // count)).astype(f32), 0.0)
    mine = owner == iota((count, total), 0)
    earlier = jnp.where(iota((total, total), 0) < iota((total, total), 1), 1.0, 0.0)
    rank = dot(jnp.where(mine, 1.0, 0.0).astype(bf16), earlier.astype(bf16))
    place += jnp.sum(jnp.where(mine, rank, 0.0), axis=0, keepdims=True)
    placed = place == iota((total, total), 0)
    in_order[...] = jnp.where(placed, 1.0, 0.0).astype(bf16)
    at = jnp.sum(jnp.where(placed, where, 0.0), axis=1, keepdims=True)
    positions[...] = jnp.broadcast_to(at, positions.shape)
    slot_at = jnp.sum(jnp.where(placed, slot, 0.0), axis=1, keepdims=True)
    pick_rows[...] = jnp.where(slot_at == iota(pick_rows.shape, 1), 1.0, 0.0).astype(bf16)
    columns[...] = jnp.where(out_base == iota(columns.shape, 1), 1.0, 0.0).astype(bf16)
    unmix[...] = jnp.where(in_base == iota(unmix.shape, 1), 1.0, 0.0).astype(bf16)


def kv_body(count, extra, *refs):
    blocks = refs[:count]
    pick_rows, order, columns, gain, w_key, w_value = refs[count : count + 6]
    wide = len(refs) - count - 9 - extra
    scaled, own, factor, *sent = refs[-3 - wide :]
    total, width = scaled.shape
    tile = tile_of(width, 512)
    square = jnp.zeros((total, 1), f32)
    for start in range(0, width, tile):
        span = slice(start, start + tile)
        part = dot(pick_rows[...], jnp.concatenate([b[:, span] for b in blocks], axis=0))
        own[:, span] = part[: own.shape[0], :].astype(bf16)
        scaled[:, span] = (part * gain[:, span]).astype(bf16)
        square += jnp.sum(part * part, axis=1, keepdims=True)
    rooted = lax.rsqrt(square / width + norm_eps)
    factor[...] = jnp.broadcast_to(rooted, factor.shape)
    keys = (dot(scaled[...], w_key[...]) * rooted).astype(bf16)
    values = (dot(scaled[...], w_value[...]) * rooted).astype(bf16)
    both = jnp.concatenate([keys, values], axis=1)
    turned = lax.dot_general(
        columns[...], both, (((1,), (1,)), ((), ())), preferred_element_type=f32
    ).astype(bf16)
    turned = dot(turned, order[...])
    each = turned.shape[0] // wide
    for dy in range(wide):
        sent[dy][...] = turned[dy * each : (dy + 1) * each].astype(bf16)


def query_body(scaled, factor, w_query, cosine, sine, query):
    raw = dot(scaled[...], w_query[...]) * factor[:, 0:1]
    for head in range(query.shape[1] // HEAD_DIM):
        span = slice(head * HEAD_DIM, (head + 1) * HEAD_DIM)
        one = raw[:, span]
        turned = one * cosine[...] + pltpu.roll(one, HEAD_DIM // 2, 1) * sine[...]
        query[:, span] = turned.astype(bf16)


def attend_body(plane, kv_local, *refs):
    tall = plane[0]
    arrived, rest = refs[:tall], refs[tall:]
    query, unmix, cosine, sine, key_pos, query_pos, w_output = rest[:7]
    parts, heads_out = rest[7:-1], rest[-1]
    half = HEAD_DIM // 2
    heads = query.shape[1] // HEAD_DIM
    mixed = jnp.concatenate([a[...].astype(f32) for a in arrived], axis=0).astype(bf16)
    both = dot(unmix[...], mixed)
    allowed = key_pos[...].astype(f32) <= query_pos[:, 0:1]
    for group in range(kv_local):
        base = group * HEAD_DIM
        first, second = both[base : base + half], both[base + half : base + HEAD_DIM]
        keys = jnp.concatenate(
            [first * cosine[...] - second * sine[...], second * cosine[...] + first * sine[...]],
            axis=0,
        ).astype(bf16)
        base += kv_local * HEAD_DIM
        values = both[base : base + HEAD_DIM].astype(bf16)
        for head in range(group * heads // kv_local, (group + 1) * heads // kv_local):
            span = slice(head * HEAD_DIM, (head + 1) * HEAD_DIM)
            scores = dot(query[:, span], keys) * HEAD_DIM ** (-0.5)
            scores = jnp.where(allowed, scores, -1e30)
            weights = jnp.exp(scores - jnp.max(scores, axis=1, keepdims=True))
            probs = (weights / jnp.sum(weights, axis=1, keepdims=True)).astype(bf16)
            heads_out[:, span] = lax.dot_general(
                probs, values, (((1,), (1,)), ((), ())), preferred_element_type=f32
            ).astype(bf16)
    spread(heads_out, w_output, parts, plane, False)


def spread(left, weight, parts, plane, back):
    width = weight.shape[1]
    tile = tile_of(width, 512)
    for start in range(0, width, tile):
        span = slice(start, start + tile)
        product = dot(left[...], weight[:, span]).astype(bf16)
        store_parts(parts, *plane, span, product, back)


def mlp_body(plane, *refs):
    count = plane[0] * plane[1]
    blocks, (w_gate, w_up, w_down) = refs[:count], refs[count : count + 3]
    parts, (piece, inner) = refs[count + 3 : -2], refs[-2:]
    share = blocks[0].shape[0]
    for index, block in enumerate(blocks):
        piece[index * share : (index + 1) * share, :] = block[...]
    width = w_gate.shape[1]
    tile = tile_of(width, 256)
    for start in range(0, width, tile):
        span = slice(start, start + tile)
        gate = dot(piece[...], w_gate[:, span])
        upward = dot(piece[...], w_up[:, span])
        inner[:, span] = (gate / (1.0 + jnp.exp(-gate)) * upward).astype(bf16)
    spread(inner, w_down, parts, plane, True)


def on_device(
    activations,
    routed,
    balance,
    w_query,
    w_key,
    w_value,
    w_output,
    attn_gain,
    mlp_gain,
    w_gate,
    w_up,
    w_down,
    w_router,
):
    count = lax.axis_size("ctx")
    plane = tall, wide = plane_of(count)
    me = lax.axis_index("ctx").astype(i32).reshape(1)
    tokens, model = activations.shape
    total = routed.shape[0]
    share = total // count
    capacity = 2 * share
    local_heads = w_query.shape[1] // HEAD_DIM
    group_size = HEADS // KV_HEADS
    kv_local = max(1, local_heads // group_size)
    key_cols = w_key.shape[1]
    depth = key_cols // KV_HEADS
    scalar = pl.BlockSpec(memory_space=pltpu.SMEM)
    in_hbm = pl.BlockSpec(memory_space=pl.ANY)
    routed, balance = routed.reshape(1, total), balance.reshape(1, total)

    (outgoing,) = kernel_call(
        send_body,
        [((capacity, model), bf16)],
        [me, from_hbm(routed), from_hbm(activations)],
        [
            pltpu.VMEM(routed.shape, i32),
            pltpu.VMEM(activations.shape, bf16),
            pltpu.SemaphoreType.DMA((2,)),
        ],
        specs=[scalar, in_hbm, in_hbm],
        flops=2 * capacity * tokens * model,
    )
    attn_gain, w_key, w_value, w_query, token_1 = load(
        outgoing, attn_gain.reshape(1, model), w_key, w_value, w_query
    )
    w_down, token_5 = load(token_1, w_down)

    each = kv_local * 2 * depth
    notes = np.zeros((max(count * each, 2 * kv_local * HEAD_DIM), 4), np.float32)
    block, local, side, entry = np.indices((count, kv_local, 2, depth)).reshape(4, -1)
    notes[: count * each, 0] = side * key_cols + entry * KV_HEADS + local
    notes[: count * each, 1] = block
    side, local, source, entry = np.indices((2, kv_local, count, depth)).reshape(4, -1)
    notes[: 2 * kv_local * HEAD_DIM, 2] = (local * 2 + side) * depth + entry
    notes[: 2 * kv_local * HEAD_DIM, 3] = source
    pick_rows, in_order, columns, unmix, positions = kernel_call(
        functools.partial(
            map_body, tall, wide, tokens, lambda peer: lax.div(peer * local_heads, group_size)
        ),
        [
            ((total, count * capacity), bf16),
            ((total, total), bf16),
            ((count * each, 2 * key_cols), bf16),
            ((2 * kv_local * HEAD_DIM, count * each), bf16),
            ((total, HEAD_DIM // 2), f32),
        ],
        [me, routed, balance, notes],
        specs=[scalar, VMEM, VMEM, VMEM],
    )
    blocks = gather_rows(outgoing, tall, wide, [token_1, token_5, positions])
    near = blocks[2 * wide]
    w_output, *token_2 = load(near, w_output)
    w_gate, *token_3 = load(near, w_gate)
    loaded = token_2 + token_3

    half = HEAD_DIM // 2
    steps_f = jnp.arange(half, dtype=f32)
    freqs = jnp.exp(-jnp.log(f32(rope_base)) * (2.0 * steps_f / HEAD_DIM))
    q_angles = positions * freqs[None, :]
    q_cos, q_sin = jnp.cos(q_angles), jnp.sin(q_angles)
    q_cos = jnp.concatenate([q_cos, q_cos], axis=1)
    q_sin = jnp.concatenate([-q_sin, q_sin], axis=1)
    k_angles = freqs[:, None] * routed.astype(f32)
    k_cos, k_sin = jnp.cos(k_angles), jnp.sin(k_angles)

    scaled, own, factor, *sent = kernel_call(
        functools.partial(kv_body, count, len(loaded)),
        [((total, model), bf16), ((share, model), bf16), ((total, 128), f32)]
        + [((tall * each, total), bf16)] * wide,
        [*blocks, pick_rows, in_order, columns, attn_gain, w_key, w_value, *loaded],
        flops=2 * total * model * 512,
    )
    arrived = exchange(sent, tall, wide)
    heads_wide = local_heads * HEAD_DIM
    (query,) = kernel_call(
        query_body,
        [((total, heads_wide), bf16)],
        [scaled, factor, w_query, q_cos, q_sin],
        flops=2 * total * model * heads_wide,
    )
    attn_parts = kernel_call(
        functools.partial(attend_body, plane, kv_local),
        [((share, model), bf16)] * count,
        [*arrived, query, unmix, k_cos, k_sin, routed, positions, w_output],
        [pltpu.VMEM((total, heads_wide), bf16)],
        flops=2 * total * model * heads_wide,
    )
    attn_own = scatter_sum(attn_parts, tall, wide)
    own_rows = own.astype(f32)
    hidden = own_rows + attn_own
    mean_sq = jnp.mean(hidden * hidden, axis=-1, keepdims=True)
    mnorm = (hidden * lax.rsqrt(mean_sq + norm_eps) * mlp_gain).astype(bf16)
    pieces = gather_blocks(mnorm, tall, wide)
    w_up, _ = load(mnorm, w_up)
    hidden_units = w_gate.shape[1]
    mlp_parts = kernel_call(
        functools.partial(mlp_body, plane),
        [((share, model), bf16)] * count,
        [*pieces, w_gate, w_up, w_down],
        [pltpu.VMEM((total, model), bf16), pltpu.VMEM((total, hidden_units), bf16)],
        flops=6 * total * model * hidden_units,
    )
    mlp_own = scatter_sum(mlp_parts, tall, wide)
    router_score = jnp.sum(own_rows * w_router[None, :], axis=1, keepdims=True)
    return (own_rows + router_score * (attn_own + mlp_own)).astype(bf16)


def solution(mesh):
    in_specs = (
        P(("dp", "ctx"), None),
        P("dp"),
        P("dp"),
        P(None, "ctx"),
        P(None, "ctx"),
        P(None, "ctx"),
        P("ctx", None),
        P(),
        P(),
        P(None, "ctx"),
        P(None, "ctx"),
        P("ctx", None),
        P(),
    )
    out_specs = P(("dp", "ctx"), None)
    return jax.shard_map(
        on_device, mesh=mesh, in_specs=in_specs, out_specs=out_specs, check_vma=False
    )
```
